256 devices in a mesh: dp: 8 (over z), ctx: 32 (over x, y, core).
Axes of the slice: x: 4, y: 4, z: 8, core: 2. Of those that a mesh axis runs over, the one named last changes fastest.
Arguments:
- conv_input: bfloat16 [8, 4096, 5120], P('dp', 'ctx'), may hold values from -11 to 11
- conv_weight: float32 [4, 5120], replicated, may hold values from 0.2 to 0.6
- step_raw: float32 [8, 64, 4096], P('dp', None, 'ctx'), may hold values from -7 to -4.8
- decay_log: float32 [64], replicated, may hold values from -7 to 2.5
- skip_gain: float32 [64], replicated, may hold values from 0.25 to 1.75
- cotangent: bfloat16 [8, 4096, 4096], P('dp', 'ctx'), may hold values from -6 to 6
Outputs:
- layer_out: bfloat16 [8, 4096, 4096], P('dp', 'ctx')
- grad_input: bfloat16 [8, 4096, 5120], P('dp', 'ctx')
- grad_step: float32 [8, 64, 4096], P('dp', None, 'ctx')
- grad_conv: float32 [4, 5120], replicated
- grad_decay_log: float32 [64], replicated
- grad_skip: float32 [64], replicated
The draws below stay inside these ranges and needn't reach their ends.
All inputs are finite; a program needn't handle non-finite values.
Results may differ from the reference program's by a relative error of at most 0.0059.
Values may be sent and summed in bfloat16 or wider, within the bound.
No kernel may reach another device: no remote copies, remote signals or barrier semaphores. Data moves between devices by JAX's collectives and lax.ppermute only.
A program may use at most 320 MiB of HBM per device.

```python
import math
import jax
import jax.numpy as jnp
from jax import lax

HEADS = 64
HEAD_DIM = 64
GROUPS = 4
STATE = 128
TAPS = 4
SPAN = 128
T_DEV = 128
CH = 5120
SEQUENCE_LENGTH = 4096
BATCH_COUNT = 8


def tap_draws(key):
    return jax.random.uniform(key, (TAPS, CH), minval=0.2, maxval=0.6)


def head_magnitudes(key, slow_share, middle_share):
    class_key, level_key, middle_key, fast_key = jax.random.split(key, 4)
    chooser = jax.random.uniform(class_key, (HEADS,))
    slow_level = jnp.exp(jax.random.uniform(level_key, (HEADS,), minval=math.log(0.3), maxval=math.log(0.9))) / (SEQUENCE_LENGTH * 0.003)
    middle_level = jnp.exp(jax.random.uniform(middle_key, (HEADS,), minval=0.1, maxval=0.5))
    fast_level = jnp.exp(jax.random.uniform(fast_key, (HEADS,), minval=math.log(1.0 / 50.0), maxval=math.log(1.0 / 30.0))) / 0.003
    return jnp.where(chooser < slow_share, slow_level, jnp.where(chooser < slow_share + middle_share, middle_level, fast_level))


def draw_conv_weight(key, part):
    tap_values = tap_draws(key)
    return tap_values.astype(jnp.float32)


def draw_conv_input(key, part):
    tap_values = tap_draws(key)
    key = jax.random.fold_in(key, 11)
    tap_total = jnp.sum(tap_values, axis=0)
    tap_power = jnp.sum(tap_values * tap_values, axis=0)
    jitter_values = jax.random.truncated_normal(key, -4.0, 4.0, (BATCH_COUNT, SEQUENCE_LENGTH, CH))
    values = -0.5 / tap_total + jitter_values / jnp.sqrt(tap_power)
    return values.astype(jnp.bfloat16)


def draw_decay_log(key, part):
    magnitudes = head_magnitudes(key, 0.4, 0.3)
    return jnp.log(magnitudes).astype(jnp.float32)


def draw_step_raw(key, part):
    key = jax.random.fold_in(key, 5)
    block_key, token_key = jax.random.split(key, 2)
    blocks = SEQUENCE_LENGTH // T_DEV
    block_factor = jnp.exp(jax.random.uniform(block_key, (BATCH_COUNT, HEADS, blocks, 1), minval=math.log(0.6), maxval=math.log(1.6)))
    block_factor = jnp.broadcast_to(block_factor, (BATCH_COUNT, HEADS, blocks, T_DEV)).reshape(BATCH_COUNT, HEADS, SEQUENCE_LENGTH)
    token_factor = jnp.exp(jax.random.uniform(token_key, (BATCH_COUNT, HEADS, SEQUENCE_LENGTH), minval=math.log(0.6), maxval=math.log(1.6)))
    step_lengths = 0.003 * block_factor * token_factor
    return jnp.log(jnp.expm1(step_lengths)).astype(jnp.float32)


def shard_levels(rng, extent, shards, low, largest):
    gain, own = 1.0, jax.random.fold_in(rng, 6)
    for dim, blocks in shards:
        steps = jnp.exp(jax.random.uniform(jax.random.fold_in(own, dim), (blocks,), jnp.float32, low / len(shards), largest / len(shards)))
        gain = gain * jnp.repeat(steps, extent[dim] // blocks).reshape([-1 if axis == dim else 1 for axis in range(len(extent))])
    return gain


def centred(own_key, shape, width, bound, cuts=(), kind=jnp.bfloat16):
    drawn = width * jax.random.normal(own_key, shape, jnp.float32)
    if cuts:
        drawn = drawn * shard_levels(own_key, shape, cuts, -0.22, 0.18)
    return jnp.clip(drawn, -bound, bound).astype(kind)


def setup_inputs(seed: int = 0) -> dict:
    splits = jax.random.split(jax.random.key(seed), 7)
    conv_input = draw_conv_input(jax.random.fold_in(splits[6], 71), 0)
    conv_weight = draw_conv_weight(jax.random.fold_in(splits[6], 71), 0)
    step_raw = draw_step_raw(jax.random.fold_in(splits[6], 71), 0)
    decay_log = draw_decay_log(jax.random.fold_in(splits[6], 71), 0)
    skip_gain = jnp.clip(1.0 + 0.15 * jax.random.normal(splits[4], (HEADS,), jnp.float32), 0.25, 1.75)
    cotangent = centred(splits[5], (BATCH_COUNT, SEQUENCE_LENGTH, HEADS * HEAD_DIM), 1.0, 6.0, ((0, 8), (1, 32)))
    return dict(conv_input=conv_input, conv_weight=conv_weight, step_raw=step_raw, decay_log=decay_log, skip_gain=skip_gain, cotangent=cotangent)


exact_mode = lax.Precision.HIGHEST

def group_core(x_group, b_group, c_group, rate_group, decay_group, block_len):
    total_len, heads_here, head_dim = x_group.shape
    state_dim = b_group.shape[1]
    blocks = total_len // block_len
    x_blocks = x_group.reshape(blocks, block_len, heads_here, head_dim)
    b_blocks = b_group.reshape(blocks, block_len, state_dim)
    c_blocks = c_group.reshape(blocks, block_len, state_dim)
    rate_blocks = rate_group.reshape(heads_here, blocks, block_len).transpose(1, 0, 2)
    row_ids = lax.broadcasted_iota(jnp.int32, (block_len, block_len), 0)
    col_ids = lax.broadcasted_iota(jnp.int32, (block_len, block_len), 1)
    lower_mask = row_ids >= col_ids

    def advance(state_now, pieces):
        x_part, b_part, c_part, rate_part = pieces
        segment = jnp.cumsum(rate_part * decay_group[:, None], axis=1)
        spread = segment[:, :, None] - segment[:, None, :]
        kernel = jnp.where(lower_mask, jnp.exp(jnp.where(lower_mask, spread, 0.0)), 0.0) * rate_part[:, None, :]
        scores = jnp.dot(c_part, b_part.T, precision=exact_mode)
        inner_out = jnp.einsum('hts,shp->thp', kernel * scores[None], x_part, precision=exact_mode)
        from_state = jnp.einsum('tn,hpn->thp', c_part, state_now, precision=exact_mode) * jnp.exp(segment).T[:, :, None]
        weights = jnp.exp(segment[:, -1:] - segment) * rate_part
        fresh_state = jnp.einsum('shp,sn->hpn', x_part * weights.T[:, :, None], b_part, precision=exact_mode)
        next_state = jnp.exp(segment[:, -1])[:, None, None] * state_now + fresh_state
        return (next_state, inner_out + from_state)
    zero_state = jnp.zeros((heads_here, head_dim, state_dim), jnp.float32)
    final_state, outputs = lax.scan(jax.checkpoint(advance), zero_state, (x_blocks, b_blocks, c_blocks, rate_blocks))
    totals = jnp.exp(decay_group * lax.optimization_barrier(jnp.sum(rate_group, axis=1)))
    return (outputs.reshape(total_len, heads_here, head_dim), final_state, totals)

def ssd_core(x_all, b_all, c_all, step_rates, decay_rate, block_len):
    groups_here = b_all.shape[1]
    per_group = x_all.shape[1] // groups_here
    outputs = []
    states = []
    totals = []
    for member in range(groups_here):
        first_head = member * per_group
        last_head = first_head + per_group
        result = group_core(x_all[:, first_head:last_head], b_all[:, member], c_all[:, member], step_rates[first_head:last_head], decay_rate[first_head:last_head], block_len)
        outputs.append(result[0])
        states.append(result[1])
        totals.append(result[2])
    return (jnp.concatenate(outputs, axis=1), jnp.concatenate(states, axis=0), jnp.concatenate(totals, axis=0))

def silu_slope(values):
    sigmoid_v = jax.nn.sigmoid(values)
    return sigmoid_v * (1.0 + values * (1.0 - sigmoid_v))

def reference(conv_input, conv_weight, step_raw, decay_log, skip_gain, cotangent):
    decay_rate = -jnp.exp(decay_log)
    tap_count = TAPS
    width_x = HEADS * HEAD_DIM
    width_b = GROUPS * STATE

    def one_sequence(pieces):
        tokens_in, raw_rates, upstream = pieces
        padded = jnp.concatenate([jnp.zeros((tap_count - 1, tokens_in.shape[1]), jnp.float32), tokens_in.astype(jnp.float32)], axis=0)
        pre_conv = conv_weight[0] * padded[0:SEQUENCE_LENGTH]
        for offset in range(1, tap_count):
            pre_conv = pre_conv + conv_weight[offset] * padded[offset:offset + SEQUENCE_LENGTH]
        mixed_in = jax.nn.silu(pre_conv).astype(jnp.bfloat16)
        step_rates = jax.nn.softplus(raw_rates)

        def mixer(mixed_f, rate_in, decay_in, skip_in):
            x_all = mixed_f[:, :width_x].reshape(SEQUENCE_LENGTH, HEADS, HEAD_DIM)
            b_all = mixed_f[:, width_x:width_x + width_b].reshape(SEQUENCE_LENGTH, GROUPS, STATE)
            c_all = mixed_f[:, width_x + width_b:].reshape(SEQUENCE_LENGTH, GROUPS, STATE)
            core_out, _, _ = ssd_core(x_all, b_all, c_all, rate_in, decay_in, SPAN)
            return (core_out + skip_in[None, :, None] * x_all).reshape(SEQUENCE_LENGTH, width_x)
        mixer_out, pull_back = jax.vjp(mixer, mixed_in.astype(jnp.float32), step_rates, decay_rate, skip_gain)
        grad_mixed, grad_rates, grad_decay, grad_skip = pull_back(upstream.astype(jnp.float32))
        grad_mixed = grad_mixed.astype(jnp.bfloat16)
        grad_pre = grad_mixed.astype(jnp.float32) * silu_slope(pre_conv)
        extended = jnp.concatenate([grad_pre, jnp.zeros((tap_count - 1, grad_pre.shape[1]), jnp.float32)], axis=0)
        grad_tokens = conv_weight[0] * extended[tap_count - 1:tap_count - 1 + SEQUENCE_LENGTH]
        for offset in range(1, tap_count):
            start_row = tap_count - 1 - offset
            grad_tokens = grad_tokens + conv_weight[offset] * extended[start_row:start_row + SEQUENCE_LENGTH]
        conv_terms = jnp.stack([lax.optimization_barrier(jnp.sum(grad_pre * padded[offset:offset + SEQUENCE_LENGTH], axis=0)) for offset in range(tap_count)])
        return (mixer_out.astype(jnp.bfloat16), grad_tokens.astype(jnp.bfloat16), grad_rates * jax.nn.sigmoid(raw_rates), conv_terms, grad_decay, grad_skip)
    results = lax.map(one_sequence, (conv_input, step_raw, cotangent))
    return (results[0], results[1], results[2], lax.optimization_barrier(jnp.sum(results[3], axis=0)), lax.optimization_barrier(jnp.sum(results[4], axis=0)) * decay_rate, lax.optimization_barrier(jnp.sum(results[5], axis=0)))
```

```python
import functools

import jax
import jax.numpy as jnp
from jax import lax
from jax.experimental import pallas as pl
from jax.experimental.pallas import tpu as pltpu
from jax.sharding import Mesh
from jax.sharding import PartitionSpec as P

HEADS = 64
HEAD_DIM = 64
GROUPS = 4
STATE = 128
TAPS = 4
T = 128
LANES = 128
WIDTH_X = HEADS * HEAD_DIM
GROUP_X = WIDTH_X // GROUPS
PAIRS = HEADS // 2
GROUP_PAIRS = PAIRS // GROUPS
GROUP_HEADS = HEADS // GROUPS
HALF_PAIRS = PAIRS // 2
F32 = jnp.float32
BF16 = jnp.bfloat16
EXACT = lax.Precision.HIGHEST
NT = (((1,), (1,)), ((), ()))
TN = (((0,), (0,)), ((), ()))


def dot(a, b, dims=None):
    if dims is None:
        dims = (((1,), (0,)), ((), ()))
    return lax.dot_general(a, b, dims, preferred_element_type=F32)


def exact_dot(a, b):
    return lax.dot_general(
        a, b, (((1,), (0,)), ((), ())), precision=EXACT, preferred_element_type=F32
    )


def iota(shape, dim):
    return lax.broadcasted_iota(jnp.int32, shape, dim)


def sigmoid(v):
    return 1.0 / (1.0 + jnp.exp(-v))


def split_two(v):
    high = v.astype(BF16)
    return high, (v - high.astype(F32)).astype(BF16)


def rates_kernel(raw_ref, head_ref, dt_ref, seg_ref, cols_ref, rise_ref, keep_ref, tot_ref, skip_ref, decay_ref):
    raw = raw_ref[...]
    dt = jnp.log1p(jnp.exp(raw))
    decay = -jnp.exp(head_ref[:, 0:1])
    upper = (iota((T, T), 0) <= iota((T, T), 1)).astype(F32)
    seg = exact_dot(dt * decay, upper)
    total = seg[:, T - 1 : T]
    dt_ref[...] = dt
    seg_ref[...] = seg
    cols_ref[...] = jnp.transpose(jnp.concatenate([seg, dt], axis=0))

    def stacked(v):
        high = v.astype(BF16).astype(F32)
        return jnp.transpose(jnp.concatenate([high, v - high], axis=0)).astype(BF16)

    rise_ref[...] = stacked(jnp.exp(seg))
    keep_ref[...] = stacked(jnp.exp(total - seg) * dt)
    first = iota((PAIRS, LANES), 1) < HEAD_DIM
    even = (iota((PAIRS, HEADS), 1) == 2 * iota((PAIRS, HEADS), 0)).astype(F32)
    odd = (iota((PAIRS, HEADS), 1) == 2 * iota((PAIRS, HEADS), 0) + 1).astype(F32)

    def paired(col):
        wide = jnp.broadcast_to(col, (HEADS, LANES))
        return jnp.where(first, exact_dot(even, wide), exact_dot(odd, wide))

    tot_ref[...] = paired(total)
    skip_ref[...] = paired(head_ref[:, 1:2])
    decay_ref[...] = jnp.broadcast_to(decay, (HEADS, LANES))


def run_rates(raw, head_cols):
    shapes = [
        ((HEADS, T), F32),
        ((HEADS, T), F32),
        ((T, 2 * HEADS), F32),
        ((T, 2 * HEADS), BF16),
        ((T, 2 * HEADS), BF16),
        ((PAIRS, LANES), F32),
        ((PAIRS, LANES), F32),
        ((HEADS, LANES), F32),
    ]
    return pl.pallas_call(
        rates_kernel,
        out_shape=[jax.ShapeDtypeStruct(s, d) for s, d in shapes],
        name="rates",
    )(raw, head_cols)


def fill_window(tok_ref, halo_ref, win_ref):
    width = tok_ref.shape[1]
    win_ref[5:8, :width] = halo_ref[...].astype(F32)
    win_ref[8 : 8 + T, :width] = tok_ref[...].astype(F32)


def pre_conv(win_ref, weight_ref, lo, width):
    acc = weight_ref[0:1, lo : lo + width] * win_ref[5 : 5 + T, lo : lo + width]
    for k in range(1, TAPS):
        acc = acc + weight_ref[k : k + 1, lo : lo + width] * win_ref[5 + k : 5 + k + T, lo : lo + width]
    return acc


def expander(pair):
    rows = iota((2 * HEADS, LANES), 0) % HEADS
    return (rows == 2 * pair + iota((2 * HEADS, LANES), 1) // HEAD_DIM).astype(F32).astype(BF16)


def enter_kernel(core_ref, tx_ref, tb_ref, tc_ref, hx_ref, hb_ref, hc_ref, wx_ref, wb_ref, wc_ref,
                 g_ref, rise_ref, keep_ref, x_ref, b_ref, c_ref, own_ref, out_ref, win_ref):
    j = pl.program_id(0)

    def mixed(tok_ref, halo_ref, weight_ref, dst_ref):
        fill_window(tok_ref, halo_ref, win_ref)
        width = tok_ref.shape[1]
        for lo in range(0, width, LANES):
            pre = pre_conv(win_ref, weight_ref, lo, LANES)
            dst_ref[:, lo : lo + LANES] = (pre * sigmoid(pre)).astype(BF16)

    mixed(tb_ref, hb_ref, wb_ref, b_ref)
    mixed(tc_ref, hc_ref, wc_ref, c_ref)
    mixed(tx_ref, hx_ref, wx_ref, x_ref)
    b_flip = jnp.transpose(b_ref[...].astype(F32)).astype(BF16)
    c_flip = jnp.transpose(c_ref[...].astype(F32)).astype(BF16)
    rise = rise_ref[...]
    keep = keep_ref[...]
    mine = (j // 2) == core_ref[0]

    def fill(dst_ref):
        for i in range(GROUP_PAIRS):
            cols = slice(i * LANES, (i + 1) * LANES)
            spread = expander(j * GROUP_PAIRS + i)
            xw = (x_ref[:, cols].astype(F32) * dot(keep, spread)).astype(BF16)
            gw = (g_ref[:, cols].astype(F32) * dot(rise, spread)).astype(BF16)
            dst_ref[0, i] = dot(b_flip, xw).astype(BF16)
            dst_ref[1, i] = dot(c_flip, gw).astype(BF16)

    @pl.when(mine)
    def _():
        fill(own_ref)

    @pl.when(jnp.logical_not(mine))
    def _():
        fill(out_ref)


def group_specs(rows, width_rows=None):
    del width_rows
    return [
        pl.BlockSpec((rows, GROUP_X), lambda j, c: (0, j)),
        pl.BlockSpec((rows, STATE), lambda j, c: (0, WIDTH_X // STATE + j)),
        pl.BlockSpec((rows, STATE), lambda j, c: (0, WIDTH_X // STATE + GROUPS + j)),
    ]


def whole(shape):
    return pl.BlockSpec(shape, lambda j, c: (0,) * len(shape))


def params(mib=48):
    return pltpu.CompilerParams(vmem_limit_bytes=mib << 20)


def run_enter(core, tokens, halo, weight, cot, rise, keep):
    half = (2, HALF_PAIRS, STATE, LANES)
    half_block = (2, GROUP_PAIRS, STATE, LANES)
    return pl.pallas_call(
        enter_kernel,
        grid_spec=pltpu.PrefetchScalarGridSpec(
            num_scalar_prefetch=1,
            grid=(GROUPS,),
            in_specs=group_specs(T) + group_specs(TAPS - 1) + group_specs(TAPS)
            + [pl.BlockSpec((T, GROUP_X), lambda j, c: (0, j)), whole((T, LANES)), whole((T, LANES))],
            out_specs=[
                pl.BlockSpec((T, GROUP_X), lambda j, c: (0, j)),
                pl.BlockSpec((T, STATE), lambda j, c: (0, j)),
                pl.BlockSpec((T, STATE), lambda j, c: (0, j)),
                pl.BlockSpec(half_block, lambda j, c: (0, jnp.clip(j - 2 * c[0], 0, 1), 0, 0)),
                pl.BlockSpec(half_block, lambda j, c: (0, jnp.clip(j - 2 * (1 - c[0]), 0, 1), 0, 0)),
            ],
            scratch_shapes=[pltpu.VMEM((8 + T, GROUP_X), F32)],
        ),
        out_shape=[
            jax.ShapeDtypeStruct((T, WIDTH_X), BF16),
            jax.ShapeDtypeStruct((T, GROUPS * STATE), BF16),
            jax.ShapeDtypeStruct((T, GROUPS * STATE), BF16),
            jax.ShapeDtypeStruct(half, BF16),
            jax.ShapeDtypeStruct(half, BF16),
        ],
        compiler_params=params(),
        name="enter",
    )(core, tokens, tokens, tokens, halo, halo, halo, weight, weight, weight, cot, rise, keep)


STEP_PAIRS = 4
PACK_ROWS = 2 * STATE + 16


def pack_kernel(core_ref, own_ref, got_ref, tot_ref, other_ref, out_ref):
    second = core_ref[0] == 1
    start = core_ref[0] * HALF_PAIRS + pl.program_id(0) * STEP_PAIRS
    for i in range(STEP_PAIRS):
        tot = tot_ref[pl.ds(start + i, 1), :]
        other = other_ref[pl.ds(start + i, 1), :]
        one = jnp.ones_like(tot)
        by_own = jnp.exp(tot)
        by_other = jnp.exp(other)
        state = (
            jnp.where(second, one, by_other) * own_ref[0, i].astype(F32)
            + jnp.where(second, by_own, one) * got_ref[0, i].astype(F32)
        )
        grad = (
            jnp.where(second, by_other, one) * own_ref[1, i].astype(F32)
            + jnp.where(second, one, by_own) * got_ref[1, i].astype(F32)
        )
        out_ref[i, 0:STATE, :] = state.astype(BF16)
        out_ref[i, STATE : 2 * STATE, :] = grad.astype(BF16)
        both = tot + other
        high = both.astype(BF16).astype(F32)
        mid = (both - high).astype(BF16).astype(F32)
        low = both - high - mid
        row = iota((16, LANES), 0)
        wide = jnp.where(row == 0, high, jnp.where(row == 1, mid, jnp.where(row == 2, low, 0.0)))
        out_ref[i, 2 * STATE : PACK_ROWS, :] = wide.astype(BF16)


def run_pack(core, own, got, tot, other):
    block = pl.BlockSpec((2, STEP_PAIRS, STATE, LANES), lambda j, c: (0, j, 0, 0))
    return pl.pallas_call(
        pack_kernel,
        grid_spec=pltpu.PrefetchScalarGridSpec(
            num_scalar_prefetch=1,
            grid=(HALF_PAIRS // STEP_PAIRS,),
            in_specs=[block, block, whole((PAIRS, LANES)), whole((PAIRS, LANES))],
            out_specs=pl.BlockSpec((STEP_PAIRS, PACK_ROWS, LANES), lambda j, c: (j, 0, 0)),
        ),
        out_shape=jax.ShapeDtypeStruct((HALF_PAIRS, PACK_ROWS, LANES), BF16),
        compiler_params=params(),
        name="pack",
    )(core, own, got, tot, other)


def chain_kernel(chips, per, in_ref, out_ref):
    for q in range(per):
        def decay(k):
            rows = in_ref[k * per + q, 2 * STATE : PACK_ROWS, :].astype(F32)
            return jnp.exp(rows[0:1] + rows[1:2] + rows[2:3])

        carry = jnp.zeros((STATE, LANES), F32)
        for k in range(chips):
            out_ref[k * per + q, 0:STATE, :] = carry.astype(BF16)
            if k < chips - 1:
                carry = decay(k) * carry + in_ref[k * per + q, 0:STATE, :].astype(F32)
        carry = jnp.zeros((STATE, LANES), F32)
        for k in reversed(range(chips)):
            out_ref[k * per + q, STATE : 2 * STATE, :] = carry.astype(BF16)
            if k > 0:
                carry = decay(k) * carry + in_ref[k * per + q, STATE : 2 * STATE, :].astype(F32)


def run_chain(chips, packed):
    return pl.pallas_call(
        functools.partial(chain_kernel, chips, HALF_PAIRS // chips),
        out_shape=jax.ShapeDtypeStruct((HALF_PAIRS, 2 * STATE, LANES), BF16),
        compiler_params=params(),
        name="chain",
    )(packed)


def unpack_kernel(core_ref, back_ref, own_ref, got_ref, tot_ref, other_ref, mine_ref, send_ref):
    second = core_ref[0] == 1
    start = core_ref[0] * HALF_PAIRS + pl.program_id(0) * STEP_PAIRS
    for i in range(STEP_PAIRS):
        tot = tot_ref[pl.ds(start + i, 1), :]
        other = other_ref[pl.ds(start + i, 1), :]
        decay_zero = jnp.exp(jnp.where(second, other, tot))
        decay_one = jnp.exp(jnp.where(second, tot, other))
        state_zero = back_ref[i, 0:STATE, :].astype(F32)
        grad_one = back_ref[i, STATE : 2 * STATE, :].astype(F32)
        left = jnp.where(second, got_ref[0, i].astype(F32), own_ref[0, i].astype(F32))
        right = jnp.where(second, own_ref[1, i].astype(F32), got_ref[1, i].astype(F32))
        state_one = decay_zero * state_zero + left
        grad_zero = decay_one * grad_one + right
        mine_ref[0, i] = jnp.where(second, state_one, state_zero).astype(BF16)
        mine_ref[1, i] = jnp.where(second, grad_one, grad_zero).astype(BF16)
        send_ref[0, i] = jnp.where(second, state_zero, state_one).astype(BF16)
        send_ref[1, i] = jnp.where(second, grad_zero, grad_one).astype(BF16)


def run_unpack(core, back, own, got, tot, other):
    block = pl.BlockSpec((2, STEP_PAIRS, STATE, LANES), lambda j, c: (0, j, 0, 0))
    half = jax.ShapeDtypeStruct((2, HALF_PAIRS, STATE, LANES), BF16)
    return pl.pallas_call(
        unpack_kernel,
        grid_spec=pltpu.PrefetchScalarGridSpec(
            num_scalar_prefetch=1,
            grid=(HALF_PAIRS // STEP_PAIRS,),
            in_specs=[
                pl.BlockSpec((STEP_PAIRS, 2 * STATE, LANES), lambda j, c: (j, 0, 0)),
                block,
                block,
                whole((PAIRS, LANES)),
                whole((PAIRS, LANES)),
            ],
            out_specs=[block, block],
        ),
        out_shape=[half, half],
        compiler_params=params(),
        name="unpack",
    )(core, back, own, got, tot, other)


def by_lane_half(v):
    first = iota(v.shape, 1) < HEAD_DIM
    wide = v.astype(F32)
    return jnp.concatenate(
        [jnp.where(first, wide, 0.0).astype(BF16), jnp.where(first, 0.0, wide).astype(BF16)], axis=0
    )


def inner_kernel(core_ref, x_ref, b_ref, c_ref, g_ref, seg_ref, dt_ref, cols_ref, y_ref, gb_ref, gc_ref):
    j = pl.program_id(0)
    b = b_ref[...]
    c = c_ref[...]
    scores = dot(c, b, NT)
    lower = iota((T, T), 0) >= iota((T, T), 1)
    cols = pltpu.roll(cols_ref[...], (LANES - j * GROUP_HEADS) % LANES, 1)
    total = jnp.zeros((T, T), F32)
    for i in range(GROUP_PAIRS):
        lanes = slice(i * LANES, (i + 1) * LANES)
        x = x_ref[:, lanes]
        g_two = by_lane_half(g_ref[:, lanes])
        inner = dot(g_two, x, NT)
        weights = []
        for k in range(2):
            h = 2 * i + k
            spread = cols[:, h : h + 1] - seg_ref[h : h + 1, :]
            kernel = jnp.exp(jnp.where(lower, spread, -1e30)) * dt_ref[h : h + 1, :]
            total = total + kernel * inner[k * T : (k + 1) * T]
            weights.append((kernel * scores).astype(BF16))
        y_ref[:, lanes] = dot(jnp.concatenate(weights, axis=1), by_lane_half(x))
    total = total.astype(BF16)
    gc_ref[...] = dot(total, b)
    gb_ref[...] = dot(jnp.transpose(total.astype(F32)).astype(BF16), c)


def run_inner(core, x, b, c, cot, seg, dt, cols):
    wide = pl.BlockSpec((T, GROUP_X), lambda j, c: (0, j))
    slim = pl.BlockSpec((T, STATE), lambda j, c: (0, j))
    heads = pl.BlockSpec((GROUP_HEADS, T), lambda j, c: (j, 0))
    return pl.pallas_call(
        inner_kernel,
        grid_spec=pltpu.PrefetchScalarGridSpec(
            num_scalar_prefetch=1,
            grid=(GROUPS,),
            in_specs=[wide, slim, slim, wide, heads, heads, whole((T, 2 * HEADS))],
            out_specs=[wide, slim, slim],
        ),
        out_shape=[
            jax.ShapeDtypeStruct((T, WIDTH_X), F32),
            jax.ShapeDtypeStruct((T, GROUPS * STATE), F32),
            jax.ShapeDtypeStruct((T, GROUPS * STATE), F32),
        ],
        compiler_params=params(),
        name="inner",
    )(core, x, b, c, cot, seg, dt, cols)


def slopes_kernel(core_ref, b_ref, c_ref, g_ref, seg_ref, dt_ref, cols_ref, tx_ref, tb_ref, tc_ref,
                  hx_ref, hb_ref, hc_ref, wx_ref, wb_ref, wc_ref, gx_ref, sx_ref, sb_ref, sc_ref, win_ref):
    j = pl.program_id(0)
    scores = jnp.transpose(dot(c_ref[...], b_ref[...], NT))
    upper = iota((T, T), 0) <= iota((T, T), 1)
    rolled = pltpu.roll(cols_ref[...], (LANES - j * GROUP_HEADS) % LANES, 1)
    for i in range(GROUP_PAIRS):
        lanes = slice(i * LANES, (i + 1) * LANES)
        weights = []
        for k in range(2):
            h = 2 * i + k
            spread = seg_ref[h : h + 1, :] - rolled[:, h : h + 1]
            kernel = jnp.exp(jnp.where(upper, spread, -1e30)) * rolled[:, HEADS + h : HEADS + h + 1]
            weights.append((kernel * scores).astype(BF16))
        gx_ref[:, lanes] = dot(jnp.concatenate(weights, axis=1), by_lane_half(g_ref[:, lanes]))

    def slope(tok_ref, halo_ref, weight_ref, dst_ref):
        fill_window(tok_ref, halo_ref, win_ref)
        for lo in range(0, tok_ref.shape[1], LANES):
            pre = pre_conv(win_ref, weight_ref, lo, LANES)
            s = sigmoid(pre)
            dst_ref[:, lo : lo + LANES] = s * (1.0 + pre * (1.0 - s))

    slope(tx_ref, hx_ref, wx_ref, sx_ref)
    slope(tb_ref, hb_ref, wb_ref, sb_ref)
    slope(tc_ref, hc_ref, wc_ref, sc_ref)


def run_slopes(core, b, c, cot, seg, dt, cols, tokens, halo, weight):
    wide = pl.BlockSpec((T, GROUP_X), lambda j, c: (0, j))
    slim = pl.BlockSpec((T, STATE), lambda j, c: (0, j))
    heads = pl.BlockSpec((GROUP_HEADS, T), lambda j, c: (j, 0))
    return pl.pallas_call(
        slopes_kernel,
        grid_spec=pltpu.PrefetchScalarGridSpec(
            num_scalar_prefetch=1,
            grid=(GROUPS,),
            in_specs=[slim, slim, wide, heads, heads, whole((T, 2 * HEADS))]
            + group_specs(T) + group_specs(TAPS - 1) + group_specs(TAPS),
            out_specs=[wide, wide, slim, slim],
            scratch_shapes=[pltpu.VMEM((8 + T, GROUP_X), F32)],
        ),
        out_shape=[
            jax.ShapeDtypeStruct((T, WIDTH_X), F32),
            jax.ShapeDtypeStruct((T, WIDTH_X), F32),
            jax.ShapeDtypeStruct((T, GROUPS * STATE), F32),
            jax.ShapeDtypeStruct((T, GROUPS * STATE), F32),
        ],
        compiler_params=params(),
        name="slopes",
    )(core, b, c, cot, seg, dt, cols, tokens, tokens, tokens, halo, halo, halo, weight, weight, weight)


SUM_ROWS = 256


def leave_kernel(core_ref, x_ref, b_ref, c_ref, g_ref, y_ref, gx_ref, gb_ref, gc_ref, sx_ref, sb_ref, sc_ref,
                 tx_ref, tb_ref, tc_ref, hx_ref, hb_ref, hc_ref, mine_ref, got_ref, rise_ref, keep_ref,
                 tot_ref, skip_ref, dt_ref, raw_ref, decay_ref,
                 out_ref, px_ref, pbc_ref, step_ref, sum_ref, win_ref):
    j = pl.program_id(0)
    mine = (j // 2) == core_ref[0]
    b = b_ref[...]
    c = c_ref[...]
    rise_all = rise_ref[...]
    keep_all = keep_ref[...]
    grad_b = gb_ref[...]
    grad_c = gc_ref[...]
    seg_grad = jnp.zeros((GROUP_HEADS, T), F32)
    dt_grad = jnp.zeros((GROUP_HEADS, T), F32)
    last = iota((T, LANES), 0) == T - 1
    skips = []
    terms = []
    fill_window(tx_ref, hx_ref, win_ref)

    def tap_sums(grad_pre, lo):
        return [
            jnp.sum(grad_pre * win_ref[5 + k : 5 + k + T, lo : lo + LANES], axis=0, keepdims=True)
            for k in range(TAPS)
        ]

    for i in range(GROUP_PAIRS):
        lanes = slice(i * LANES, (i + 1) * LANES)
        spread = expander(j * GROUP_PAIRS + i)
        rise = dot(rise_all, spread)
        keep = dot(keep_all, spread)
        state = jnp.where(mine, mine_ref[0, i].astype(F32), got_ref[0, i].astype(F32))
        exits = jnp.where(mine, mine_ref[1, i].astype(F32), got_ref[1, i].astype(F32))
        state_b = state.astype(BF16)
        exits_b = exits.astype(BF16)
        x = x_ref[:, lanes].astype(F32)
        g = g_ref[:, lanes].astype(F32)
        skip = skip_ref[i : i + 1, :]
        y = y_ref[:, lanes] + rise * dot(c, state_b)
        through = keep * dot(b, exits_b)
        gx = gx_ref[:, lanes] + through
        grad_c = grad_c + dot((g * rise).astype(BF16), state_b, NT)
        grad_b = grad_b + dot((x * keep).astype(BF16), exits_b, NT)
        out_ref[:, lanes] = (y + skip * x).astype(BF16)
        grad_pre = (gx + skip * g) * sx_ref[:, lanes]
        px_ref[:, lanes] = grad_pre
        terms += tap_sums(grad_pre, i * LANES)
        skips.append(jnp.sum(g * x, axis=0, keepdims=True))
        x_gx = x * gx
        end = jnp.sum(x * through, axis=0, keepdims=True) + jnp.exp(tot_ref[i : i + 1, :]) * jnp.sum(
            exits * state, axis=0, keepdims=True
        )
        moved = g * y - x_gx + jnp.where(last, end, 0.0)
        pick = (
            iota((GROUP_HEADS, LANES), 0) == 2 * i + iota((GROUP_HEADS, LANES), 1) // HEAD_DIM
        ).astype(F32).astype(BF16)
        for high_low in split_two(moved):
            seg_grad = seg_grad + dot(pick, high_low, NT)
        for high_low in split_two(x_gx):
            dt_grad = dt_grad + dot(pick, high_low, NT)

    sum_ref[pl.ds(pl.multiple_of(j * 32, 32), 32), :] = jnp.concatenate(terms, axis=0)
    terms = []
    for grad, slope_ref, tok_ref, halo_ref, base in (
        (grad_b, sb_ref, tb_ref, hb_ref, 0),
        (grad_c, sc_ref, tc_ref, hc_ref, GROUPS * STATE),
    ):
        fill_window(tok_ref, halo_ref, win_ref)
        grad_pre = grad * slope_ref[...]
        pbc_ref[:, pl.ds(pl.multiple_of(base + j * STATE, STATE), STATE)] = grad_pre
        terms += tap_sums(grad_pre, 0)
    sum_ref[pl.ds(pl.multiple_of(128 + j * 8, 8), 8), :] = jnp.concatenate(terms, axis=0)
    sum_ref[pl.ds(pl.multiple_of(160 + j * 8, 8), 8), :] = jnp.concatenate(skips, axis=0)

    lower = (iota((T, T), 0) >= iota((T, T), 1)).astype(F32)
    behind = exact_dot(seg_grad, lower)
    dt = dt_ref[...]
    decay = decay_ref[...]
    step_ref[...] = (dt_grad / dt + decay * behind) * sigmoid(raw_ref[...])
    sum_ref[pl.ds(pl.multiple_of(192 + j * 16, 16), 16), :] = dt * behind * decay


def run_leave(core, x, b, c, cot, y, gx, gb, gc, sx, sb, sc, tokens, halo, mine, got, rise, keep, tot, skip, dt, raw, decay):
    wide = pl.BlockSpec((T, GROUP_X), lambda j, c: (0, j))
    slim = pl.BlockSpec((T, STATE), lambda j, c: (0, j))
    heads = pl.BlockSpec((GROUP_HEADS, T), lambda j, c: (j, 0))
    pairs = pl.BlockSpec((GROUP_PAIRS, LANES), lambda j, c: (j, 0))
    half_block = (2, GROUP_PAIRS, STATE, LANES)
    return pl.pallas_call(
        leave_kernel,
        grid_spec=pltpu.PrefetchScalarGridSpec(
            num_scalar_prefetch=1,
            grid=(GROUPS,),
            in_specs=[wide, slim, slim, wide, wide, wide, slim, slim, wide, slim, slim]
            + group_specs(T) + group_specs(TAPS - 1)
            + [
                pl.BlockSpec(half_block, lambda j, c: (0, jnp.clip(j - 2 * c[0], 0, 1), 0, 0)),
                pl.BlockSpec(half_block, lambda j, c: (0, jnp.clip(j - 2 * (1 - c[0]), 0, 1), 0, 0)),
                whole((T, 2 * HEADS)),
                whole((T, 2 * HEADS)),
                pairs,
                pairs,
                heads,
                heads,
                heads,
            ],
            out_specs=[
                wide,
                wide,
                whole((T, 2 * GROUPS * STATE)),
                heads,
                whole((SUM_ROWS, LANES)),
            ],
            scratch_shapes=[pltpu.VMEM((8 + T, GROUP_X), F32)],
        ),
        out_shape=[
            jax.ShapeDtypeStruct((T, WIDTH_X), BF16),
            jax.ShapeDtypeStruct((T, WIDTH_X), F32),
            jax.ShapeDtypeStruct((T, 2 * GROUPS * STATE), F32),
            jax.ShapeDtypeStruct((HEADS, T), F32),
            jax.ShapeDtypeStruct((SUM_ROWS, LANES), F32),
        ],
        compiler_params=params(),
        name="leave",
    )(core, x, b, c, cot, y, gx, gb, gc, sx, sb, sc, tokens, tokens, tokens, halo, halo, halo,
      mine, got, rise, keep, tot, skip, dt, raw, decay)


def spread_kernel(px_ref, pbc_ref, halo_ref, weight_ref, out_ref, win_ref):
    is_x = pl.program_id(0) < GROUPS

    @pl.when(is_x)
    def _():
        win_ref[0:T, :] = px_ref[...]

    @pl.when(jnp.logical_not(is_x))
    def _():
        win_ref[0:T, :] = pbc_ref[...]

    win_ref[T : T + 3, :] = halo_ref[...].astype(F32)
    for lo in range(0, GROUP_X, LANES):
        cols = slice(lo, lo + LANES)
        acc = weight_ref[0:1, cols] * win_ref[3 : 3 + T, cols]
        for k in range(1, TAPS):
            acc = acc + weight_ref[k : k + 1, cols] * win_ref[3 - k : 3 - k + T, cols]
        out_ref[:, cols] = acc.astype(BF16)


def run_spread(px, pbc, halo, weight):
    return pl.pallas_call(
        spread_kernel,
        grid=(GROUPS + 1,),
        in_specs=[
            pl.BlockSpec((T, GROUP_X), lambda j: (0, jnp.minimum(j, GROUPS - 1))),
            pl.BlockSpec((T, GROUP_X), lambda j: (0, 0)),
            pl.BlockSpec((TAPS - 1, GROUP_X), lambda j: (0, j)),
            pl.BlockSpec((TAPS, GROUP_X), lambda j: (0, j)),
        ],
        out_specs=pl.BlockSpec((T, GROUP_X), lambda j: (0, j)),
        out_shape=jax.ShapeDtypeStruct((T, WIDTH_X + 2 * GROUPS * STATE), BF16),
        scratch_shapes=[pltpu.VMEM((T + 8, GROUP_X), F32)],
        compiler_params=params(),
        name="spread",
    )(px, pbc, halo, weight)


CTX = ("chip", "core")
ALL = ("dp", "chip", "core")


def all_to_all(value, axis):
    return lax.all_to_all(value, axis, 0, 0, tiled=True)


def local(conv_input, conv_weight, step_raw, decay_log, skip_gain, cotangent):
    chips = lax.axis_size("chip")
    devices = 2 * chips
    tokens = conv_input[0]
    raw = step_raw[0]
    cot = cotangent[0]
    core = lax.axis_index("core").astype(jnp.int32).reshape(1)
    swap = [(0, 1), (1, 0)]
    halo = lax.ppermute(tokens[T - TAPS + 1 :], CTX, [(i, i + 1) for i in range(devices - 1)])
    dt, seg, cols, rise, keep, tot, skip, decay = run_rates(raw, jnp.stack([decay_log, skip_gain], axis=1))
    tot_other = lax.ppermute(tot, "core", swap)
    x, b, c, own, out = run_enter(core, tokens, halo, conv_weight, cot, rise, keep)
    got = lax.ppermute(out, "core", swap)
    packed = run_pack(core, own, got, tot, tot_other)
    chained = run_chain(chips, all_to_all(packed, "chip"))
    y, gb, gc = run_inner(core, x, b, c, cot, seg, dt, cols)
    back = all_to_all(chained, "chip")
    late_b, late_c, _ = lax.optimization_barrier((b, c, chained))
    gx, sx, sb, sc = run_slopes(core, late_b, late_c, cot, seg, dt, cols, tokens, halo, conv_weight)
    mine, send = run_unpack(core, back, own, got, tot, tot_other)
    theirs = lax.ppermute(send, "core", swap)
    out_tokens, px, pbc, grad_step, sums = run_leave(
        core, x, b, c, cot, y, gx, gb, gc, sx, sb, sc, tokens, halo, mine, theirs, rise, keep, tot, skip, dt, raw, decay
    )
    first = jnp.concatenate([px[: TAPS - 1], pbc[: TAPS - 1]], axis=1).astype(BF16)
    after = lax.ppermute(first, CTX, [(i + 1, i) for i in range(devices - 1)])
    count = lax.axis_size("dp") * devices
    shares = all_to_all(sums, ALL).reshape(count, SUM_ROWS // count, LANES)
    share = jnp.sum(shares, axis=0)
    total = all_to_all(jnp.broadcast_to(share[None], shares.shape).reshape(SUM_ROWS, LANES), ALL)
    grad_tokens = run_spread(px, pbc, after, conv_weight)
    conv_x = total[:128].reshape(PAIRS, TAPS, LANES)
    conv_bc = total[128:160].reshape(GROUPS, 2, TAPS, LANES)
    grad_conv = jnp.concatenate([conv_x, conv_bc[:, 0], conv_bc[:, 1]], axis=0)
    grad_conv = jnp.swapaxes(grad_conv, 0, 1).reshape(TAPS, WIDTH_X + 2 * GROUPS * STATE)
    grad_skip = jnp.sum(total[160:192].reshape(HEADS, HEAD_DIM), axis=1)
    grad_decay = jnp.sum(total[192:256], axis=1)
    return (
        out_tokens[None],
        grad_tokens[None],
        grad_step[None],
        grad_conv,
        grad_decay,
        grad_skip,
    )


def solution(mesh):
    dp, ctx = mesh.devices.shape
    fine = Mesh(mesh.devices.reshape(dp, ctx // 2, 2), ALL)
    seq = P("dp", CTX, None)
    rate = P("dp", None, CTX)
    in_specs = (seq, P(), rate, P(), P(), seq)
    out_specs = (seq, seq, rate, P(), P(), P())
    return jax.shard_map(local, mesh=fine, in_specs=in_specs, out_specs=out_specs, check_vma=False)
```

```python
import functools

import jax
import jax.numpy as jnp
from jax import lax
from jax.experimental import pallas as pl
from jax.experimental.pallas import tpu as pltpu
from jax.sharding import Mesh
from jax.sharding import PartitionSpec as P

HEADS = 64
HEAD_DIM = 64
GROUPS = 4
STATE = 128
TAPS = 4
T = 128
LANES = 128
WIDTH_X = HEADS * HEAD_DIM
WIDTH_B = GROUPS * STATE
CHANNELS = WIDTH_X + 2 * WIDTH_B
GROUP_X = WIDTH_X // GROUPS
PAIRS = HEADS // 2
GROUP_PAIRS = PAIRS // GROUPS
GROUP_HEADS = HEADS // GROUPS
HALF_PAIRS = PAIRS // 2
HALF_GROUPS = GROUPS // 2
F32 = jnp.float32
BF16 = jnp.bfloat16
EXACT = lax.Precision.HIGHEST
NN = (((1,), (0,)), ((), ()))
NT = (((1,), (1,)), ((), ()))
SUM_ROWS = 256
PACK_ROWS = 2 * STATE + 16


def dot(a, b, dims=NN):
    return lax.dot_general(a, b, dims, preferred_element_type=F32)


def exact_dot(a, b, dims=NN):
    return lax.dot_general(a, b, dims, precision=EXACT, preferred_element_type=F32)


def iota(shape, dim):
    return lax.broadcasted_iota(jnp.int32, shape, dim)


def sigmoid(v):
    return 0.5 + 0.5 * jnp.tanh(0.5 * v)


def split_two(v):
    high = v.astype(BF16)
    return high, (v - high.astype(F32)).astype(BF16)


def span(index, size):
    return pl.ds(pl.multiple_of(index * size, size), size)


def call(kernel, name, out_shape, specs, micros, scratch=(), mib=28):
    cost = pl.CostEstimate(
        flops=int(micros * 1e9), transcendentals=0, bytes_accessed=int(micros * 3.6e6)
    )
    places = {
        "s": pl.BlockSpec(memory_space=pltpu.SMEM),
        "v": pl.BlockSpec(memory_space=pltpu.VMEM),
        "h": pl.BlockSpec(memory_space=pltpu.HBM),
    }
    return pl.pallas_call(
        kernel,
        out_shape=[jax.ShapeDtypeStruct(s, d) for s, d in out_shape],
        in_specs=[places[p] for p in specs],
        out_specs=[places["v"]] * len(out_shape),
        scratch_shapes=list(scratch),
        cost_estimate=cost,
        compiler_params=pltpu.CompilerParams(vmem_limit_bytes=mib << 20),
        name=name,
    )


def fill_window(win_ref, tokens, halo):
    width = tokens.shape[1]
    win_ref[5:8, :width] = halo.astype(F32)
    win_ref[8 : 8 + T, :width] = tokens.astype(F32)


def pre_conv(win_ref, weights, lo):
    cols = slice(lo, lo + LANES)
    acc = weights[0:1, cols] * win_ref[5 : 5 + T, cols]
    for k in range(1, TAPS):
        acc = acc + weights[k : k + 1, cols] * win_ref[5 + k : 5 + k + T, cols]
    return acc


BLOCKS = CHANNELS // GROUP_X


def begin_kernel(raw_ref, decay_log_ref, skip_gain_ref, tok_ref, weight_ref,
                 dt_ref, seg_ref, cols_ref, scale_ref, tot_ref, skip_ref, decay_ref,
                 x_ref, bc_ref, head_ref, hold_ref, win_ref, sems):
    copies = [
        pltpu.make_async_copy(
            tok_ref.at[:, pl.ds(i * GROUP_X, GROUP_X)],
            hold_ref.at[:, pl.ds(i * GROUP_X, GROUP_X)],
            sems.at[i],
        )
        for i in range(BLOCKS)
    ]
    for copy in copies:
        copy.start()
    diagonal = iota((HEADS, HEADS), 0) == iota((HEADS, HEADS), 1)

    def column(row):
        return jnp.sum(jnp.where(diagonal, row, 0.0), axis=1, keepdims=True)

    raw = raw_ref[...]
    dt = jnp.log1p(jnp.exp(raw))
    decay = -jnp.exp(column(decay_log_ref[...]))
    upper = (iota((T, T), 0) <= iota((T, T), 1)).astype(F32)
    seg = exact_dot(dt * decay, upper)
    total = seg[:, T - 1 : T]
    dt_ref[...] = dt
    seg_ref[...] = seg
    cols_ref[...] = jnp.transpose(jnp.concatenate([seg, dt], axis=0))
    scale_ref[...] = jnp.transpose(
        jnp.concatenate([jnp.exp(seg), jnp.exp(total - seg) * dt], axis=0)
    )
    first = iota((PAIRS, LANES), 1) < HEAD_DIM
    even = (iota((PAIRS, HEADS), 1) == 2 * iota((PAIRS, HEADS), 0)).astype(F32)
    odd = (iota((PAIRS, HEADS), 1) == 2 * iota((PAIRS, HEADS), 0) + 1).astype(F32)

    def paired(col):
        wide = jnp.broadcast_to(col, (HEADS, LANES))
        return jnp.where(first, exact_dot(even, wide), exact_dot(odd, wide))

    tot_ref[...] = paired(total)
    skip_ref[...] = paired(column(skip_gain_ref[...]))
    decay_ref[...] = jnp.broadcast_to(decay, (HEADS, LANES))
    win_ref[0:8, :] = jnp.zeros((8, GROUP_X), F32)
    for i in range(BLOCKS):
        copies[i].wait()
        cols = slice(i * GROUP_X, (i + 1) * GROUP_X)
        win_ref[8 : 8 + T, :] = hold_ref[:, cols].astype(F32)
        for lo in range(0, GROUP_X, LANES):
            at = i * GROUP_X + lo
            pre = pre_conv(win_ref, weight_ref[:, cols], lo)
            mixed = (pre * sigmoid(pre)).astype(BF16)
            head_ref[:, at : at + LANES] = pre[0:8]
            if at < WIDTH_X:
                x_ref[:, at : at + LANES] = mixed
            else:
                bc_ref[:, at - WIDTH_X : at - WIDTH_X + LANES] = mixed


def run_begin(raw, decay_log, skip_gain, tokens, weight):
    out = [
        ((HEADS, T), F32),
        ((HEADS, T), F32),
        ((T, 2 * HEADS), F32),
        ((T, 2 * HEADS), F32),
        ((PAIRS, LANES), F32),
        ((PAIRS, LANES), F32),
        ((HEADS, LANES), F32),
        ((T, WIDTH_X), BF16),
        ((T, 2 * WIDTH_B), BF16),
        ((8, CHANNELS), F32),
    ]
    scratch = [
        pltpu.VMEM((T, CHANNELS), BF16),
        pltpu.VMEM((8 + T, GROUP_X), F32),
        pltpu.SemaphoreType.DMA((BLOCKS,)),
    ]
    return call(begin_kernel, "begin", out, "vvvhv", 5, scratch)(
        raw, decay_log, skip_gain, tokens, weight
    )


def rolled(ref, group):
    return pltpu.roll(ref[...], (LANES - group * GROUP_HEADS) % LANES, 1)


def widen(cols, base, pair):
    first = iota((T, LANES), 1) < HEAD_DIM
    at = base + 2 * pair
    return jnp.where(first, cols[:, at : at + 1], cols[:, at + 1 : at + 2])


def widen_two(cols, base, pair):
    return jnp.concatenate([widen(cols, base, pair), widen(cols, base, pair + 1)], axis=1)


def enter_kernel(core_ref, x0_ref, bc0_ref, head_ref, halo_ref, weight_ref, g_ref, scale_ref,
                 x_ref, bc_ref, own_ref, out_ref):
    row = iota((8, GROUP_X), 0)
    for i in range(BLOCKS):
        cols = slice(i * GROUP_X, (i + 1) * GROUP_X)
        halo = halo_ref[:, cols].astype(F32)
        weight = weight_ref[:, cols]
        pre = head_ref[:, cols]
        for t in range(TAPS - 1):
            extra = jnp.zeros((1, GROUP_X), F32)
            for k in range(TAPS - 1 - t):
                extra = extra + weight[k : k + 1] * halo[t + k : t + k + 1]
            pre = pre + jnp.where(row == t, extra, 0.0)
        fixed = pre * sigmoid(pre)
        src, dst, at = (x0_ref, x_ref, cols) if i < GROUPS else (bc0_ref, bc_ref, slice(0, GROUP_X))
        rest = src[0:16, at].astype(F32)
        dst[16:T, at] = src[16:T, at]
        dst[0:16, at] = jnp.concatenate([fixed, rest[8:16]], axis=0).astype(BF16)

    def fill(dst_ref, first):
        @pl.loop(0, HALF_GROUPS)
        def _(jj):
            j = first * HALF_GROUPS + jj
            b_flip = jnp.transpose(bc_ref[:, span(j, STATE)].astype(F32)).astype(BF16)
            c_flip = jnp.transpose(bc_ref[:, span(GROUPS + j, STATE)].astype(F32)).astype(BF16)
            cols = rolled(scale_ref, j)
            for q in range(0, GROUP_PAIRS, 2):
                lanes = pl.ds(pl.multiple_of(j * GROUP_X + q * LANES, 2 * LANES), 2 * LANES)
                xw = (x_ref[:, lanes].astype(F32) * widen_two(cols, HEADS, q)).astype(BF16)
                gw = (g_ref[:, lanes].astype(F32) * widen_two(cols, 0, q)).astype(BF16)
                state = dot(b_flip, xw).astype(BF16)
                grad = dot(c_flip, gw).astype(BF16)
                for k in range(2):
                    at = jj * GROUP_PAIRS + q + k
                    dst_ref[0, at] = state[:, k * LANES : (k + 1) * LANES]
                    dst_ref[1, at] = grad[:, k * LANES : (k + 1) * LANES]

    fill(out_ref, 1 - core_ref[0])
    fill(own_ref, core_ref[0])


def run_enter(core, x0, bc0, head, halo, weight, cot, scale):
    out = [
        ((T, WIDTH_X), BF16),
        ((T, 2 * WIDTH_B), BF16),
        ((2, HALF_PAIRS, STATE, LANES), BF16),
        ((2, HALF_PAIRS, STATE, LANES), BF16),
    ]
    return call(enter_kernel, "enter", out, "svvvvvvv", 4)(
        core, x0, bc0, head, halo, weight, cot, scale
    )


def pack_kernel(core_ref, own_ref, got_ref, tot_ref, other_ref, out_ref):
    second = core_ref[0] == 1

    @pl.loop(0, HALF_PAIRS)
    def _(i):
        at = core_ref[0] * HALF_PAIRS + i
        tot = tot_ref[pl.ds(at, 1), :]
        other = other_ref[pl.ds(at, 1), :]
        one = jnp.ones_like(tot)
        by_own = jnp.exp(tot)
        by_other = jnp.exp(other)
        state = (
            jnp.where(second, one, by_other) * own_ref[0, i].astype(F32)
            + jnp.where(second, by_own, one) * got_ref[0, i].astype(F32)
        )
        grad = (
            jnp.where(second, by_other, one) * own_ref[1, i].astype(F32)
            + jnp.where(second, one, by_own) * got_ref[1, i].astype(F32)
        )
        out_ref[i, 0:STATE, :] = state.astype(BF16)
        out_ref[i, STATE : 2 * STATE, :] = grad.astype(BF16)
        both = tot + other
        high = both.astype(BF16).astype(F32)
        mid = (both - high).astype(BF16).astype(F32)
        low = both - high - mid
        row = iota((16, LANES), 0)
        wide = jnp.where(row == 0, high, jnp.where(row == 1, mid, jnp.where(row == 2, low, 0.0)))
        out_ref[i, 2 * STATE : PACK_ROWS, :] = wide.astype(BF16)


def run_pack(core, own, got, tot, other):
    out = [((HALF_PAIRS, PACK_ROWS, LANES), BF16)]
    return call(pack_kernel, "pack", out, "svvvv", 1, mib=16)(core, own, got, tot, other)[0]


def chain_kernel(chips, per, in_ref, out_ref):
    for q in range(per):
        def decay(k):
            rows = in_ref[k * per + q, 2 * STATE : PACK_ROWS, :].astype(F32)
            return jnp.exp(rows[0:1] + rows[1:2] + rows[2:3])

        carry = jnp.zeros((STATE, LANES), F32)
        for k in range(chips):
            out_ref[k * per + q, 0:STATE, :] = carry.astype(BF16)
            if k < chips - 1:
                carry = decay(k) * carry + in_ref[k * per + q, 0:STATE, :].astype(F32)
        carry = jnp.zeros((STATE, LANES), F32)
        for k in reversed(range(chips)):
            out_ref[k * per + q, STATE : 2 * STATE, :] = carry.astype(BF16)
            if k > 0:
                carry = decay(k) * carry + in_ref[k * per + q, STATE : 2 * STATE, :].astype(F32)


def run_chain(chips, packed):
    kernel = functools.partial(chain_kernel, chips, HALF_PAIRS // chips)
    out = [((HALF_PAIRS, 2 * STATE, LANES), BF16)]
    return call(kernel, "chain", out, "v", 0.5, mib=16)(packed)[0]


def unpack_kernel(core_ref, back_ref, own_ref, got_ref, tot_ref, other_ref, mine_ref, send_ref):
    second = core_ref[0] == 1

    @pl.loop(0, HALF_PAIRS)
    def _(i):
        at = core_ref[0] * HALF_PAIRS + i
        tot = tot_ref[pl.ds(at, 1), :]
        other = other_ref[pl.ds(at, 1), :]
        decay_zero = jnp.exp(jnp.where(second, other, tot))
        decay_one = jnp.exp(jnp.where(second, tot, other))
        state_zero = back_ref[i, 0:STATE, :].astype(F32)
        grad_one = back_ref[i, STATE : 2 * STATE, :].astype(F32)
        left = jnp.where(second, got_ref[0, i].astype(F32), own_ref[0, i].astype(F32))
        right = jnp.where(second, own_ref[1, i].astype(F32), got_ref[1, i].astype(F32))
        state_one = decay_zero * state_zero + left
        grad_zero = decay_one * grad_one + right
        mine_ref[0, i] = jnp.where(second, state_one, state_zero).astype(BF16)
        mine_ref[1, i] = jnp.where(second, grad_one, grad_zero).astype(BF16)
        send_ref[0, i] = jnp.where(second, state_zero, state_one).astype(BF16)
        send_ref[1, i] = jnp.where(second, grad_zero, grad_one).astype(BF16)


def run_unpack(core, back, own, got, tot, other):
    out = [((2, HALF_PAIRS, STATE, LANES), BF16)] * 2
    return call(unpack_kernel, "unpack", out, "svvvvv", 1, mib=16)(core, back, own, got, tot, other)


def by_lane_half(v):
    first = iota(v.shape, 1) < HEAD_DIM
    wide = v.astype(F32)
    return jnp.concatenate(
        [jnp.where(first, wide, 0.0).astype(BF16), jnp.where(first, 0.0, wide).astype(BF16)], axis=0
    )


def inner_kernel(x_ref, bc_ref, g_ref, seg_ref, dt_ref, cols_ref, y_ref, gbc_ref):
    lower = iota((T, T), 0) >= iota((T, T), 1)

    @pl.loop(0, GROUPS)
    def _(j):
        b = bc_ref[:, span(j, STATE)]
        c = bc_ref[:, span(GROUPS + j, STATE)]
        seg = seg_ref[span(j, GROUP_HEADS), :]
        dt = dt_ref[span(j, GROUP_HEADS), :]
        scores = dot(c, b, NT)
        cols = rolled(cols_ref, j)
        total = jnp.zeros((T, T), F32)
        for i in range(GROUP_PAIRS):
            lanes = pl.ds(pl.multiple_of(j * GROUP_X + i * LANES, LANES), LANES)
            x = x_ref[:, lanes]
            inner = dot(by_lane_half(g_ref[:, lanes]), x, NT)
            weights = []
            for k in range(2):
                h = 2 * i + k
                spread = cols[:, h : h + 1] - seg[h : h + 1, :]
                kernel = jnp.exp(jnp.where(lower, spread, -1e30)) * dt[h : h + 1, :]
                total = total + kernel * inner[k * T : (k + 1) * T]
                weights.append((kernel * scores).astype(BF16))
            y_ref[:, lanes] = dot(jnp.concatenate(weights, axis=1), by_lane_half(x))
        gbc_ref[:, span(GROUPS + j, STATE)] = dot(total.astype(BF16), b)
        gbc_ref[:, span(j, STATE)] = dot(jnp.transpose(total).astype(BF16), c)


def run_inner(x, bc, cot, seg, dt, cols):
    out = [((T, WIDTH_X), F32), ((T, 2 * WIDTH_B), F32)]
    return call(inner_kernel, "inner", out, "vvvvvv", 3)(x, bc, cot, seg, dt, cols)


def slopes_kernel(bc_ref, g_ref, seg_ref, cols_ref, tok_ref, halo_ref, weight_ref,
                  gx_ref, slope_ref, win_ref):
    upper = iota((T, T), 0) <= iota((T, T), 1)

    @pl.loop(0, GROUPS)
    def _(j):
        b = bc_ref[:, span(j, STATE)]
        c = bc_ref[:, span(GROUPS + j, STATE)]
        seg = seg_ref[span(j, GROUP_HEADS), :]
        scores = jnp.transpose(dot(c, b, NT))
        cols = rolled(cols_ref, j)
        for i in range(GROUP_PAIRS):
            lanes = pl.ds(pl.multiple_of(j * GROUP_X + i * LANES, LANES), LANES)
            weights = []
            for k in range(2):
                h = 2 * i + k
                spread = seg[h : h + 1, :] - cols[:, h : h + 1]
                kernel = jnp.exp(jnp.where(upper, spread, -1e30)) * cols[:, HEADS + h : HEADS + h + 1]
                weights.append((kernel * scores).astype(BF16))
            gx_ref[:, lanes] = dot(jnp.concatenate(weights, axis=1), by_lane_half(g_ref[:, lanes]))

    @pl.loop(0, BLOCKS)
    def _(i):
        cols = span(i, GROUP_X)
        fill_window(win_ref, tok_ref[:, cols], halo_ref[:, cols])
        weights = weight_ref[:, cols]
        for lo in range(0, GROUP_X, LANES):
            pre = pre_conv(win_ref, weights, lo)
            s = sigmoid(pre)
            at = pl.ds(pl.multiple_of(i * GROUP_X + lo, LANES), LANES)
            slope_ref[:, at] = s * (1.0 + pre * (1.0 - s))


def run_slopes(bc, cot, seg, cols, tokens, halo, weight):
    out = [((T, WIDTH_X), F32), ((T, CHANNELS), F32)]
    scratch = [pltpu.VMEM((8 + T, GROUP_X), F32)]
    return call(slopes_kernel, "slopes", out, "vvvvvvv", 5, scratch)(
        bc, cot, seg, cols, tokens, halo, weight
    )


def leave_kernel(core_ref, x_ref, bc_ref, g_ref, y_ref, gx_ref, gbc_ref, slope_ref, tok_ref, halo_ref,
                 mine_ref, got_ref, scale_ref, tot_ref, skip_ref, dt_ref, raw_ref, decay_ref,
                 out_ref, pre_ref, first_ref, step_ref, sum_ref, win_ref):
    last = iota((T, 2 * LANES), 0) == T - 1
    lower = (iota((T, T), 0) >= iota((T, T), 1)).astype(F32)

    def tap_sums(grad_pre, lo):
        width = grad_pre.shape[1]
        return [
            jnp.sum(grad_pre * win_ref[5 + k : 5 + k + T, lo : lo + width], axis=0, keepdims=True)
            for k in range(TAPS)
        ]

    def by_rows(sums):
        return [s[:, lo : lo + LANES] for lo in range(0, sums[0].shape[1], LANES) for s in sums]

    def group(j, jj, state_ref):
        b = bc_ref[:, span(j, STATE)]
        c = bc_ref[:, span(GROUPS + j, STATE)]
        grad_b = gbc_ref[:, span(j, STATE)]
        grad_c = gbc_ref[:, span(GROUPS + j, STATE)]
        cols = rolled(scale_ref, j)
        skip_rows = skip_ref[span(j, GROUP_PAIRS), :]
        tot_rows = tot_ref[span(j, GROUP_PAIRS), :]
        seg_grad = jnp.zeros((GROUP_HEADS, T), F32)
        dt_grad = jnp.zeros((GROUP_HEADS, T), F32)
        skips = []
        terms = []
        wide = span(j, GROUP_X)
        fill_window(win_ref, tok_ref[:, wide], halo_ref[:, wide])
        for q in range(0, GROUP_PAIRS, 2):
            lanes = pl.ds(pl.multiple_of(j * GROUP_X + q * LANES, 2 * LANES), 2 * LANES)
            rise = widen_two(cols, 0, q)
            keep = widen_two(cols, HEADS, q)
            at = jj * GROUP_PAIRS + q
            state = jnp.concatenate([state_ref[0, at], state_ref[0, at + 1]], axis=1)
            exits = jnp.concatenate([state_ref[1, at], state_ref[1, at + 1]], axis=1)
            skip = jnp.concatenate([skip_rows[q : q + 1], skip_rows[q + 1 : q + 2]], axis=1)
            tot = jnp.concatenate([tot_rows[q : q + 1], tot_rows[q + 1 : q + 2]], axis=1)
            x = x_ref[:, lanes].astype(F32)
            g = g_ref[:, lanes].astype(F32)
            y = y_ref[:, lanes] + rise * dot(c, state)
            through = keep * dot(b, exits)
            gx = gx_ref[:, lanes] + through
            grad_c = grad_c + dot((g * rise).astype(BF16), state, NT)
            grad_b = grad_b + dot((x * keep).astype(BF16), exits, NT)
            out_ref[:, lanes] = (y + skip * x).astype(BF16)
            grad_pre = (gx + skip * g) * slope_ref[:, lanes]
            pre_ref[:, lanes] = grad_pre
            first_ref[:, lanes] = grad_pre[0 : TAPS - 1].astype(BF16)
            terms += by_rows(tap_sums(grad_pre, q * LANES))
            skips += by_rows([jnp.sum(g * x, axis=0, keepdims=True)])
            x_gx = x * gx
            end = jnp.sum(x * through, axis=0, keepdims=True) + jnp.exp(tot) * jnp.sum(
                exits.astype(F32) * state.astype(F32), axis=0, keepdims=True
            )
            moved = g * y - x_gx + jnp.where(last, end, 0.0)
            pick = (
                iota((GROUP_HEADS, 2 * LANES), 0)
                == 2 * q + iota((GROUP_HEADS, 2 * LANES), 1) // HEAD_DIM
            ).astype(F32).astype(BF16)
            for part in split_two(moved):
                seg_grad = seg_grad + dot(pick, part, NT)
            for part in split_two(x_gx):
                dt_grad = dt_grad + dot(pick, part, NT)
        sum_ref[span(j, 32), :] = jnp.concatenate(terms, axis=0)
        terms = []
        for grad, base in ((grad_b, 0), (grad_c, GROUPS)):
            at = span(WIDTH_X // STATE + base + j, STATE)
            fill_window(win_ref, tok_ref[:, at], halo_ref[:, at])
            grad_pre = grad * slope_ref[:, at]
            pre_ref[:, at] = grad_pre
            first_ref[:, at] = grad_pre[0 : TAPS - 1].astype(BF16)
            terms += tap_sums(grad_pre, 0)
        sum_ref[pl.ds(pl.multiple_of(128 + j * 8, 8), 8), :] = jnp.concatenate(terms, axis=0)
        sum_ref[pl.ds(pl.multiple_of(160 + j * 8, 8), 8), :] = jnp.concatenate(skips, axis=0)
        heads = span(j, GROUP_HEADS)
        behind = exact_dot(seg_grad, lower)
        dt = dt_ref[heads, :]
        decay = decay_ref[heads, :]
        step_ref[heads, :] = (dt_grad / dt + decay * behind) * sigmoid(raw_ref[heads, :])
        sum_ref[pl.ds(pl.multiple_of(192 + j * 16, 16), 16), :] = dt * behind * decay

    for state_ref, half in ((mine_ref, core_ref[0]), (got_ref, 1 - core_ref[0])):
        @pl.loop(0, HALF_GROUPS)
        def _(jj):
            group(half * HALF_GROUPS + jj, jj, state_ref)


def run_leave(*args):
    out = [
        ((T, WIDTH_X), BF16),
        ((T, CHANNELS), F32),
        ((TAPS - 1, CHANNELS), BF16),
        ((HEADS, T), F32),
        ((SUM_ROWS, LANES), F32),
    ]
    scratch = [pltpu.VMEM((8 + T, GROUP_X), F32)]
    return call(leave_kernel, "leave", out, "s" + "v" * 17, 8, scratch)(*args)


def spread_kernel(pre_ref, halo_ref, weight_ref, out_ref, win_ref):
    @pl.loop(0, BLOCKS)
    def _(i):
        cols = span(i, GROUP_X)
        win_ref[0:T, :] = pre_ref[:, cols]
        win_ref[T : T + TAPS - 1, :] = halo_ref[:, cols].astype(F32)
        weights = weight_ref[:, cols]
        for lo in range(0, GROUP_X, LANES):
            at = slice(lo, lo + LANES)
            acc = weights[0:1, at] * win_ref[3 : 3 + T, at]
            for k in range(1, TAPS):
                acc = acc + weights[k : k + 1, at] * win_ref[3 - k : 3 - k + T, at]
            out_ref[:, pl.ds(pl.multiple_of(i * GROUP_X + lo, LANES), LANES)] = acc.astype(BF16)


def run_spread(pre, halo, weight):
    out = [((T, CHANNELS), BF16)]
    scratch = [pltpu.VMEM((T + 8, GROUP_X), F32)]
    return call(spread_kernel, "spread", out, "vvv", 3, scratch, mib=16)(pre, halo, weight)[0]


def finish_kernel(sum_ref, conv_ref, decay_ref, skip_ref):
    for i in range(CHANNELS // LANES):
        if i < PAIRS:
            row = TAPS * i
        else:
            group = (i - PAIRS) % GROUPS
            row = 128 + 8 * group + TAPS * ((i - PAIRS) // GROUPS)
        conv_ref[:, i * LANES : (i + 1) * LANES] = sum_ref[row : row + TAPS, :]
    ones = jnp.ones((8, LANES), F32)
    decay_ref[...] = exact_dot(ones, sum_ref[192:256, :], NT)[0:1]
    first = iota((8, LANES), 1) < HEAD_DIM
    skips = sum_ref[160:192, :]
    even = exact_dot(jnp.where(first, 1.0, 0.0), skips, NT)
    odd = exact_dot(jnp.where(first, 0.0, 1.0), skips, NT)
    at_even = (iota((PAIRS, HEADS), 1) == 2 * iota((PAIRS, HEADS), 0)).astype(F32)
    at_odd = (iota((PAIRS, HEADS), 1) == 2 * iota((PAIRS, HEADS), 0) + 1).astype(F32)
    skip_ref[...] = (exact_dot(even, at_even) + exact_dot(odd, at_odd))[0:1]


def run_finish(sums):
    out = [((TAPS, CHANNELS), F32), ((1, HEADS), F32), ((1, HEADS), F32)]
    return call(finish_kernel, "finish", out, "v", 0.5, mib=16)(sums)


CTX = ("chip", "core")
ALL = ("dp", "chip", "core")


def all_to_all(value, axis):
    return lax.all_to_all(value, axis, 0, 0, tiled=True)


def tie(*values):
    return lax.optimization_barrier(values)


def sum_everywhere(sums, chips):
    share = SUM_ROWS // chips
    parts = all_to_all(sums, "chip").reshape(chips, share, LANES)
    total = jnp.sum(parts, axis=0)
    total = total + lax.ppermute(total, "core", [(0, 1), (1, 0)])
    count = lax.axis_size("dp")
    flip = 1
    while flip < count:
        mask = flip if 2 * flip < count else count - 1
        total = total + lax.ppermute(total, "dp", [(i, i ^ mask) for i in range(count)])
        flip *= 2
    return all_to_all(jnp.broadcast_to(total[None], (chips, share, LANES)).reshape(SUM_ROWS, LANES), "chip")


def local(conv_input, conv_weight, step_raw, decay_log, skip_gain, cotangent):
    chips = lax.axis_size("chip")
    devices = 2 * chips
    tokens = conv_input[0]
    raw = step_raw[0]
    cot = cotangent[0]
    core = lax.axis_index("core").astype(jnp.int32).reshape(1)
    swap = [(0, 1), (1, 0)]
    halo = lax.ppermute(tokens[T - TAPS + 1 :], CTX, [(i, i + 1) for i in range(devices - 1)])
    dt, seg, cols, scale, tot, skip, decay, x0, bc0, head = run_begin(
        raw, decay_log.reshape(1, HEADS), skip_gain.reshape(1, HEADS), tokens, conv_weight
    )
    other = lax.ppermute(tot, "core", swap)
    x, bc, own, out = run_enter(core, x0, bc0, head, halo, conv_weight, cot, scale)
    got = lax.ppermute(out, "core", swap)
    packed = run_pack(core, own, got, tot, other)
    heard = all_to_all(packed, "chip")
    y, gbc = run_inner(x, bc, cot, seg, dt, cols)
    heard, y, gbc = tie(heard, y, gbc)
    chained = run_chain(chips, heard)
    late, chained = tie(bc, chained)
    back = all_to_all(chained, "chip")
    gx, slope = run_slopes(late, cot, seg, cols, tokens, halo, conv_weight)
    back, gx, slope = tie(back, gx, slope)
    mine, send = run_unpack(core, back, own, got, tot, other)
    theirs = lax.ppermute(send, "core", swap)
    out_tokens, pre, first, grad_step, sums = run_leave(
        core, x, bc, cot, y, gx, gbc, slope, tokens, halo, mine, theirs, scale, tot, skip, dt, raw, decay
    )
    after = lax.ppermute(first, CTX, [(i + 1, i) for i in range(devices - 1)])
    grad_tokens = run_spread(pre, after, conv_weight)
    grad_conv, grad_decay, grad_skip = run_finish(sum_everywhere(sums, chips))
    return (
        out_tokens[None],
        grad_tokens[None],
        grad_step[None],
        grad_conv,
        grad_decay.reshape(HEADS),
        grad_skip.reshape(HEADS),
    )


def solution(mesh):
    dp, ctx = mesh.devices.shape
    fine = Mesh(mesh.devices.reshape(dp, ctx // 2, 2), ALL)
    seq = P("dp", CTX, None)
    rate = P("dp", None, CTX)
    in_specs = (seq, P(), rate, P(), P(), seq)
    out_specs = (seq, seq, rate, P(), P(), P())
    return jax.shard_map(local, mesh=fine, in_specs=in_specs, out_specs=out_specs, check_vma=False)
```

```python
import functools

import jax
import jax.numpy as jnp
from jax import lax
from jax.experimental import pallas as pl
from jax.experimental.pallas import tpu as pltpu
from jax.sharding import Mesh
from jax.sharding import PartitionSpec as P

HEADS = 64
HEAD_DIM = 64
GROUPS = 4
STATE = 128
TAPS = 4
T = 128
LANES = 128
WIDTH_X = HEADS * HEAD_DIM
WIDTH_B = GROUPS * STATE
CHANNELS = WIDTH_X + 2 * WIDTH_B
GROUP_X = WIDTH_X // GROUPS
PAIRS = HEADS // 2
GROUP_PAIRS = PAIRS // GROUPS
GROUP_HEADS = HEADS // GROUPS
HALF_PAIRS = PAIRS // 2
HALF_GROUPS = GROUPS // 2
F32 = jnp.float32
BF16 = jnp.bfloat16
EXACT = lax.Precision.HIGHEST
NN = (((1,), (0,)), ((), ()))
NT = (((1,), (1,)), ((), ()))
SUM_ROWS = 256
SUM_GROUP = SUM_ROWS // GROUPS
PACK_ROWS = 2 * STATE + 16


def dot(a, b, dims=NN):
    return lax.dot_general(a, b, dims, preferred_element_type=F32)


def exact_dot(a, b, dims=NN):
    return lax.dot_general(a, b, dims, precision=EXACT, preferred_element_type=F32)


def iota(shape, dim):
    return lax.broadcasted_iota(jnp.int32, shape, dim)


def sigmoid(v):
    return 0.5 + 0.5 * jnp.tanh(0.5 * v)


def split_two(v):
    high = v.astype(BF16)
    return high, (v - high.astype(F32)).astype(BF16)


def span(index, size):
    return pl.ds(pl.multiple_of(index * size, size), size)


def pin(value, space):
    return pltpu.with_memory_space_constraint(value, space)


def placed(space, shape, dtype):
    return space(shape, dtype)


def call(kernel, name, outs, specs, micros, scratch=(), mib=28, aliases=None):
    cost = pl.CostEstimate(
        flops=int(micros * 1e9), transcendentals=0, bytes_accessed=int(micros * 3.6e6)
    )
    blocks = {
        "s": pl.BlockSpec(memory_space=pltpu.SMEM),
        "v": pl.BlockSpec(memory_space=pltpu.VMEM),
        "V": pl.BlockSpec(memory_space=pltpu.VMEM),
        "h": pl.BlockSpec(memory_space=pltpu.HBM),
    }
    spaces = {"V": pltpu.VMEM, "h": pltpu.HBM}
    shapes = [
        placed(spaces[p], shape, dtype) if p in spaces else jax.ShapeDtypeStruct(shape, dtype)
        for p, shape, dtype in outs
    ]
    run = pl.pallas_call(
        kernel,
        out_shape=shapes,
        in_specs=[blocks[p] for p in specs],
        out_specs=[blocks[p] for p, _, _ in outs],
        scratch_shapes=list(scratch),
        input_output_aliases=aliases or {},
        cost_estimate=cost,
        compiler_params=pltpu.CompilerParams(vmem_limit_bytes=mib << 20),
        name=name,
    )

    def go(*args):
        return run(*[pin(a, spaces[p]) if p in spaces else a for a, p in zip(args, specs, strict=True)])

    return go


def start_all(pairs, sems):
    copies = [pltpu.make_async_copy(a, b, sems.at[i]) for i, (a, b) in enumerate(pairs)]
    for copy in copies:
        copy.start()
    return copies


def wait_all(copies):
    for copy in copies:
        copy.wait()


def DMA(*shape):
    return pltpu.SemaphoreType.DMA(shape)


def fill_window(win_ref, before, tokens):
    width = tokens.shape[1]
    win_ref[0:8, :width] = before
    win_ref[8 : 8 + T, :width] = tokens.astype(F32)


def pre_conv(win_ref, weights, lo):
    cols = slice(lo, lo + LANES)
    acc = weights[0:1, cols] * win_ref[5 : 5 + T, cols]
    for k in range(1, TAPS):
        acc = acc + weights[k : k + 1, cols] * win_ref[5 + k : 5 + k + T, cols]
    return acc


BLOCKS = CHANNELS // GROUP_X


ROW_DT, ROW_SEG, ROW_COLS, ROW_SCALE, ROW_TOT, ROW_SKIP, ROW_DECAY, SMALL_ROWS = (
    0, 64, 128, 256, 384, 416, 448, 512
)


def begin_kernel(raw_h, decay_log_h, skip_gain_h, tok_h, weight_h,
                 small_h, small_ref, tot_ref, x_ref, bc_ref, head_ref,
                 raw_ref, decay_log_ref, skip_gain_ref, weight_ref, hold_ref, win_ref, sems):
    first = start_all(
        [(raw_h, raw_ref), (decay_log_h, decay_log_ref), (skip_gain_h, skip_gain_ref), (weight_h, weight_ref)],
        sems.at[0],
    )
    blocks = [pl.ds(i * GROUP_X, GROUP_X) for i in range(BLOCKS)]
    copies = start_all([(tok_h.at[:, at], hold_ref.at[:, at]) for at in blocks], sems.at[1])
    diagonal = iota((HEADS, HEADS), 0) == iota((HEADS, HEADS), 1)

    def column(row):
        return jnp.sum(jnp.where(diagonal, row, 0.0), axis=1, keepdims=True)

    wait_all(first)
    raw = raw_ref[...]
    dt = jnp.log1p(jnp.exp(raw))
    decay = -jnp.exp(column(decay_log_ref[...]))
    upper = (iota((T, T), 0) <= iota((T, T), 1)).astype(F32)
    seg = exact_dot(dt * decay, upper)
    total = seg[:, T - 1 : T]
    small_ref[ROW_DT : ROW_DT + HEADS] = dt
    small_ref[ROW_SEG : ROW_SEG + HEADS] = seg
    small_ref[ROW_COLS : ROW_COLS + T] = jnp.transpose(jnp.concatenate([seg, dt], axis=0))
    small_ref[ROW_SCALE : ROW_SCALE + T] = jnp.transpose(
        jnp.concatenate([jnp.exp(seg), jnp.exp(total - seg) * dt], axis=0)
    )
    left = iota((PAIRS, LANES), 1) < HEAD_DIM
    even = (iota((PAIRS, HEADS), 1) == 2 * iota((PAIRS, HEADS), 0)).astype(F32)
    odd = (iota((PAIRS, HEADS), 1) == 2 * iota((PAIRS, HEADS), 0) + 1).astype(F32)

    def paired(col):
        wide = jnp.broadcast_to(col, (HEADS, LANES))
        return jnp.where(left, exact_dot(even, wide), exact_dot(odd, wide))

    tot = paired(total)
    tot_ref[...] = tot
    small_ref[ROW_TOT : ROW_TOT + PAIRS] = tot
    small_ref[ROW_SKIP : ROW_SKIP + PAIRS] = paired(column(skip_gain_ref[...]))
    small_ref[ROW_DECAY : ROW_DECAY + HEADS] = jnp.broadcast_to(decay, (HEADS, LANES))
    save = start_all([(small_ref, small_h)], sems.at[0])
    win_ref[0:8, :] = jnp.zeros((8, GROUP_X), F32)
    for i in range(BLOCKS):
        copies[i].wait()
        cols = slice(i * GROUP_X, (i + 1) * GROUP_X)
        win_ref[8 : 8 + T, :] = hold_ref[:, cols].astype(F32)
        for lo in range(0, GROUP_X, LANES):
            at = i * GROUP_X + lo
            pre = pre_conv(win_ref, weight_ref[:, cols], lo)
            mixed = (pre * sigmoid(pre)).astype(BF16)
            head_ref[:, at : at + LANES] = pre[0:8]
            if at < WIDTH_X:
                x_ref[:, at : at + LANES] = mixed
            else:
                bc_ref[:, at - WIDTH_X : at - WIDTH_X + LANES] = mixed
    wait_all(save)


def run_begin(raw, decay_log, skip_gain, tokens, weight):
    out = [
        ("h", (SMALL_ROWS, LANES), F32),
        ("V", (SMALL_ROWS, LANES), F32),
        ("V", (PAIRS, LANES), F32),
        ("V", (T, WIDTH_X), BF16),
        ("V", (T, 2 * WIDTH_B), BF16),
        ("V", (8, CHANNELS), F32),
    ]
    scratch = [
        pltpu.VMEM((HEADS, T), F32),
        pltpu.VMEM((1, HEADS), F32),
        pltpu.VMEM((1, HEADS), F32),
        pltpu.VMEM((TAPS, CHANNELS), F32),
        pltpu.VMEM((T, CHANNELS), BF16),
        pltpu.VMEM((8 + T, GROUP_X), F32),
        DMA(2, BLOCKS),
    ]
    return call(begin_kernel, "begin", out, "hhhhh", 4, scratch, mib=16)(
        raw, decay_log, skip_gain, tokens, weight
    )


def rolled(cols, group):
    return pltpu.roll(cols, (LANES - group * GROUP_HEADS) % LANES, 1)


def widen(cols, base, pair):
    first = iota((T, LANES), 1) < HEAD_DIM
    at = base + 2 * pair
    return jnp.where(first, cols[:, at : at + 1], cols[:, at + 1 : at + 2])


def widen_two(cols, base, pair):
    return jnp.concatenate([widen(cols, base, pair), widen(cols, base, pair + 1)], axis=1)


def fill_half(half, x_ref, bc_ref, g_ref, copies, scale, dst_ref):
    for jj in range(HALF_GROUPS):
        j = half * HALF_GROUPS + jj
        copies[jj].wait()
        b_flip = jnp.transpose(bc_ref[:, span(j, STATE)].astype(F32)).astype(BF16)
        c_flip = jnp.transpose(bc_ref[:, span(GROUPS + j, STATE)].astype(F32)).astype(BF16)
        cols = rolled(scale, j)
        for q in range(0, GROUP_PAIRS, 2):
            lanes = pl.ds(pl.multiple_of(j * GROUP_X + q * LANES, 2 * LANES), 2 * LANES)
            near = slice(jj * GROUP_X + q * LANES, jj * GROUP_X + (q + 2) * LANES)
            xw = (x_ref[:, lanes].astype(F32) * widen_two(cols, HEADS, q)).astype(BF16)
            gw = (g_ref[:, near].astype(F32) * widen_two(cols, 0, q)).astype(BF16)
            state = dot(b_flip, xw).astype(BF16)
            grad = dot(c_flip, gw).astype(BF16)
            for k in range(2):
                at = jj * GROUP_PAIRS + q + k
                dst_ref[0, at] = state[:, k * LANES : (k + 1) * LANES]
                dst_ref[1, at] = grad[:, k * LANES : (k + 1) * LANES]


def load_half(half, g_h, g_ref, sems):
    return start_all(
        [
            (g_h.at[:, span(half * HALF_GROUPS + jj, GROUP_X)], g_ref.at[:, pl.ds(jj * GROUP_X, GROUP_X)])
            for jj in range(HALF_GROUPS)
        ],
        sems,
    )


def enter_kernel(core_ref, x0_ref, bc0_ref, head_ref, halo_ref, weight_h, g_h, small_ref,
                 x_h, bc_h, before_h, x_ref, bc_ref, out_ref, g_ref, weight_ref, before_ref, sems):
    half = 1 - core_ref[0]
    weight_copy = start_all([(weight_h, weight_ref)], sems.at[0])
    copies = load_half(half, g_h, g_ref, sems.at[1])
    row = iota((8, GROUP_X), 0)
    wait_all(weight_copy)
    for i in range(BLOCKS):
        cols = slice(i * GROUP_X, (i + 1) * GROUP_X)
        halo = halo_ref[:, cols].astype(F32)
        weight = weight_ref[:, cols]
        pre = head_ref[:, cols]
        before = jnp.zeros((8, GROUP_X), F32)
        for t in range(TAPS - 1):
            extra = jnp.zeros((1, GROUP_X), F32)
            for k in range(TAPS - 1 - t):
                extra = extra + weight[k : k + 1] * halo[t + k : t + k + 1]
            pre = pre + jnp.where(row == t, extra, 0.0)
            before = before + jnp.where(row == t + 5, halo[t : t + 1], 0.0)
        before_ref[:, cols] = before
        fixed = pre * sigmoid(pre)
        src, dst, at = (x0_ref, x_ref, cols) if i < GROUPS else (bc0_ref, bc_ref, slice(0, GROUP_X))
        rest = src[0:16, at].astype(F32)
        dst[16:T, at] = src[16:T, at]
        dst[0:16, at] = jnp.concatenate([fixed, rest[8:16]], axis=0).astype(BF16)
    saves = start_all([(x_ref, x_h), (bc_ref, bc_h), (before_ref, before_h)], sems.at[0])
    fill_half(half, x_ref, bc_ref, g_ref, copies, small_ref[ROW_SCALE : ROW_SCALE + T], out_ref)
    wait_all(saves)


def run_enter(core, x0, bc0, head, halo, weight, cot, small):
    out = [
        ("h", (T, WIDTH_X), BF16),
        ("h", (T, 2 * WIDTH_B), BF16),
        ("h", (8, CHANNELS), F32),
        ("V", (T, WIDTH_X), BF16),
        ("V", (T, 2 * WIDTH_B), BF16),
        ("V", (2, HALF_PAIRS, STATE, LANES), BF16),
    ]
    scratch = [
        pltpu.VMEM((T, HALF_GROUPS * GROUP_X), BF16),
        pltpu.VMEM((TAPS, CHANNELS), F32),
        pltpu.VMEM((8, CHANNELS), F32),
        DMA(2, 3),
    ]
    return call(enter_kernel, "enter", out, "sVVVvhhV", 3, scratch, mib=16)(
        core, x0, bc0, head, halo, weight, cot, small
    )


def own_kernel(core_ref, x_ref, bc_ref, g_h, small_ref, own_ref, g_ref, sems):
    copies = load_half(core_ref[0], g_h, g_ref, sems)
    fill_half(core_ref[0], x_ref, bc_ref, g_ref, copies, small_ref[ROW_SCALE : ROW_SCALE + T], own_ref)


def run_own(core, x, bc, cot, small):
    out = [("V", (2, HALF_PAIRS, STATE, LANES), BF16)]
    scratch = [pltpu.VMEM((T, HALF_GROUPS * GROUP_X), BF16), DMA(HALF_GROUPS)]
    return call(own_kernel, "own", out, "sVVhV", 3, scratch, mib=16)(core, x, bc, cot, small)[0]


STEP_PAIRS = 4
STEPS = HALF_PAIRS // STEP_PAIRS


def pack_kernel(core_ref, own_ref, got_ref, tot_ref, other_ref,
                out_h, own_h, got_h, tots_h, out_ref, sems):
    saves = start_all(
        [
            (own_ref, own_h),
            (got_ref, got_h),
            (tot_ref, tots_h.at[pl.ds(0, PAIRS)]),
            (other_ref, tots_h.at[pl.ds(PAIRS, PAIRS)]),
        ],
        sems.at[0],
    )
    second = core_ref[0] == 1
    outs = []
    for i in range(HALF_PAIRS):
        at = core_ref[0] * HALF_PAIRS + i
        tot = tot_ref[pl.ds(at, 1), :]
        other = other_ref[pl.ds(at, 1), :]
        one = jnp.ones_like(tot)
        by_own = jnp.exp(tot)
        by_other = jnp.exp(other)
        state = (
            jnp.where(second, one, by_other) * own_ref[0, i].astype(F32)
            + jnp.where(second, by_own, one) * got_ref[0, i].astype(F32)
        )
        grad = (
            jnp.where(second, by_other, one) * own_ref[1, i].astype(F32)
            + jnp.where(second, one, by_own) * got_ref[1, i].astype(F32)
        )
        out_ref[i, 0:STATE, :] = state.astype(BF16)
        out_ref[i, STATE : 2 * STATE, :] = grad.astype(BF16)
        both = tot + other
        high = both.astype(BF16).astype(F32)
        mid = (both - high).astype(BF16).astype(F32)
        low = both - high - mid
        row = iota((16, LANES), 0)
        wide = jnp.where(row == 0, high, jnp.where(row == 1, mid, jnp.where(row == 2, low, 0.0)))
        out_ref[i, 2 * STATE : PACK_ROWS, :] = wide.astype(BF16)
        if i % STEP_PAIRS == STEP_PAIRS - 1:
            done = pl.ds(i + 1 - STEP_PAIRS, STEP_PAIRS)
            copy = pltpu.make_async_copy(out_ref.at[done], out_h.at[done], sems.at[1, i // STEP_PAIRS])
            copy.start()
            outs.append(copy)
    wait_all(outs + saves)


def run_pack(core, own, got, tot, other):
    half = (2, HALF_PAIRS, STATE, LANES)
    packed = (HALF_PAIRS, PACK_ROWS, LANES)
    out = [("h", packed, BF16), ("h", half, BF16), ("h", half, BF16), ("h", (2 * PAIRS, LANES), F32)]
    scratch = [pltpu.VMEM(packed, BF16), DMA(2, STEPS)]
    return call(pack_kernel, "pack", out, "sVvVv", 2, scratch, mib=16)(core, own, got, tot, other)


def chain_kernel(chips, per, in_ref, out_ref):
    for q in range(per):
        def decay(k):
            rows = in_ref[k * per + q, 2 * STATE : PACK_ROWS, :].astype(F32)
            return jnp.exp(rows[0:1] + rows[1:2] + rows[2:3])

        carry = jnp.zeros((STATE, LANES), F32)
        for k in range(chips):
            out_ref[k * per + q, 0:STATE, :] = carry.astype(BF16)
            if k < chips - 1:
                carry = decay(k) * carry + in_ref[k * per + q, 0:STATE, :].astype(F32)
        carry = jnp.zeros((STATE, LANES), F32)
        for k in reversed(range(chips)):
            out_ref[k * per + q, STATE : 2 * STATE, :] = carry.astype(BF16)
            if k > 0:
                carry = decay(k) * carry + in_ref[k * per + q, STATE : 2 * STATE, :].astype(F32)


def run_chain(chips, packed):
    kernel = functools.partial(chain_kernel, chips, HALF_PAIRS // chips)
    out = [("v", (HALF_PAIRS, 2 * STATE, LANES), BF16)]
    return call(kernel, "chain", out, "v", 1, mib=16)(packed)[0]


def unpack_kernel(core_ref, back_h, own_h, got_h, tots_h, mine_ref, send_ref,
                  back_ref, own_ref, got_ref, tots_ref, sems):
    first = start_all([(tots_h, tots_ref)], sems.at[STEPS])
    steps = []
    for step in range(STEPS):
        at = pl.ds(step * STEP_PAIRS, STEP_PAIRS)
        steps.append(
            start_all(
                [
                    (back_h.at[at], back_ref.at[at]),
                    (own_h.at[:, at], own_ref.at[:, at]),
                    (got_h.at[:, at], got_ref.at[:, at]),
                ],
                sems.at[step],
            )
        )
    wait_all(first)
    second = core_ref[0] == 1
    for i in range(HALF_PAIRS):
        if i % STEP_PAIRS == 0:
            wait_all(steps[i // STEP_PAIRS])
        at = core_ref[0] * HALF_PAIRS + i
        tot = tots_ref[pl.ds(at, 1), :]
        other = tots_ref[pl.ds(PAIRS + at, 1), :]
        decay_zero = jnp.exp(jnp.where(second, other, tot))
        decay_one = jnp.exp(jnp.where(second, tot, other))
        state_zero = back_ref[i, 0:STATE, :].astype(F32)
        grad_one = back_ref[i, STATE : 2 * STATE, :].astype(F32)
        left = jnp.where(second, got_ref[0, i].astype(F32), own_ref[0, i].astype(F32))
        right = jnp.where(second, own_ref[1, i].astype(F32), got_ref[1, i].astype(F32))
        state_one = decay_zero * state_zero + left
        grad_zero = decay_one * grad_one + right
        mine_ref[0, i] = jnp.where(second, state_one, state_zero).astype(BF16)
        mine_ref[1, i] = jnp.where(second, grad_one, grad_zero).astype(BF16)
        send_ref[0, i] = jnp.where(second, state_zero, state_one).astype(BF16)
        send_ref[1, i] = jnp.where(second, grad_zero, grad_one).astype(BF16)


def run_unpack(core, back, own, got, tots):
    half = (2, HALF_PAIRS, STATE, LANES)
    out = [("V", half, BF16)] * 2
    scratch = [
        pltpu.VMEM((HALF_PAIRS, 2 * STATE, LANES), BF16),
        pltpu.VMEM(half, BF16),
        pltpu.VMEM(half, BF16),
        pltpu.VMEM((2 * PAIRS, LANES), F32),
        DMA(STEPS + 1, 3),
    ]
    return call(unpack_kernel, "unpack", out, "shhhh", 2, scratch, mib=16)(core, back, own, got, tots)


def by_lane_half(v):
    first = iota(v.shape, 1) < HEAD_DIM
    wide = v.astype(F32)
    return jnp.concatenate(
        [jnp.where(first, wide, 0.0).astype(BF16), jnp.where(first, 0.0, wide).astype(BF16)], axis=0
    )


def inner_kernel(x_h, bc_h, g_h, small_h, y_h, gbc_h, x_ref, bc_ref, g_ref, small_ref, y_ref, gbc_ref, sems):
    first = start_all([(bc_h, bc_ref), (small_h, small_ref)], sems.at[0])

    def loads(j):
        at = span(j, GROUP_X)
        return [
            pltpu.make_async_copy(x_h.at[:, at], x_ref.at[:, at], sems.at[1, j]),
            pltpu.make_async_copy(g_h.at[:, at], g_ref.at[:, at], sems.at[2, j]),
        ]

    def store(j):
        at = span(j, GROUP_X)
        return pltpu.make_async_copy(y_ref.at[:, at], y_h.at[:, at], sems.at[3, j])

    for j in range(GROUPS):
        for copy in loads(j):
            copy.start()
    wait_all(first)
    lower = iota((T, T), 0) >= iota((T, T), 1)

    @pl.loop(0, GROUPS)
    def _(j):
        wait_all(loads(j))
        b = bc_ref[:, span(j, STATE)]
        c = bc_ref[:, span(GROUPS + j, STATE)]
        seg = small_ref[pl.ds(pl.multiple_of(ROW_SEG + j * GROUP_HEADS, GROUP_HEADS), GROUP_HEADS), :]
        dt = small_ref[pl.ds(pl.multiple_of(ROW_DT + j * GROUP_HEADS, GROUP_HEADS), GROUP_HEADS), :]
        scores = dot(c, b, NT)
        cols = rolled(small_ref[ROW_COLS : ROW_COLS + T], j)
        total = jnp.zeros((T, T), F32)
        for i in range(GROUP_PAIRS):
            lanes = pl.ds(pl.multiple_of(j * GROUP_X + i * LANES, LANES), LANES)
            x = x_ref[:, lanes]
            inner = dot(by_lane_half(g_ref[:, lanes]), x, NT)
            weights = []
            for k in range(2):
                h = 2 * i + k
                spread = cols[:, h : h + 1] - seg[h : h + 1, :]
                kernel = jnp.exp(jnp.where(lower, spread, -1e30)) * dt[h : h + 1, :]
                total = total + kernel * inner[k * T : (k + 1) * T]
                weights.append((kernel * scores).astype(BF16))
            y_ref[:, lanes] = dot(jnp.concatenate(weights, axis=1), by_lane_half(x))
        gbc_ref[:, span(GROUPS + j, STATE)] = dot(total.astype(BF16), b)
        gbc_ref[:, span(j, STATE)] = dot(jnp.transpose(total).astype(BF16), c)
        store(j).start()

    last = start_all([(gbc_ref, gbc_h)], sems.at[0])
    for j in range(GROUPS):
        store(j).wait()
    wait_all(last)


def run_inner(x, bc, cot, small):
    out = [("h", (T, WIDTH_X), F32), ("h", (T, 2 * WIDTH_B), F32)]
    scratch = [
        pltpu.VMEM((T, WIDTH_X), BF16),
        pltpu.VMEM((T, 2 * WIDTH_B), BF16),
        pltpu.VMEM((T, WIDTH_X), BF16),
        pltpu.VMEM((SMALL_ROWS, LANES), F32),
        pltpu.VMEM((T, WIDTH_X), F32),
        pltpu.VMEM((T, 2 * WIDTH_B), F32),
        DMA(4, GROUPS),
    ]
    return call(inner_kernel, "inner", out, "hhhh", 4, scratch, mib=24)(x, bc, cot, small)


def slopes_kernel(bc_h, g_h, small_h, tok_h, before_h, weight_h, gx_h, slope_h,
                  bc_ref, g_ref, small_ref, tok_ref, before_ref, weight_ref, gx_ref, slope_ref, win_ref, sems):
    first = start_all(
        [(bc_h, bc_ref), (small_h, small_ref), (before_h, before_ref), (weight_h, weight_ref), (tok_h, tok_ref)],
        sems.at[0],
    )

    def load(j):
        at = span(j, GROUP_X)
        return pltpu.make_async_copy(g_h.at[:, at], g_ref.at[:, at], sems.at[1, j])

    def store(j):
        at = span(j, GROUP_X)
        return pltpu.make_async_copy(gx_ref.at[:, at], gx_h.at[:, at], sems.at[2, j])

    def store_slope(i):
        at = span(i, GROUP_X)
        return pltpu.make_async_copy(slope_ref.at[:, at], slope_h.at[:, at], sems.at[3, i])

    for j in range(GROUPS):
        load(j).start()
    wait_all(first)
    upper = iota((T, T), 0) <= iota((T, T), 1)

    @pl.loop(0, GROUPS)
    def _(j):
        load(j).wait()
        b = bc_ref[:, span(j, STATE)]
        c = bc_ref[:, span(GROUPS + j, STATE)]
        seg = small_ref[pl.ds(pl.multiple_of(ROW_SEG + j * GROUP_HEADS, GROUP_HEADS), GROUP_HEADS), :]
        scores = jnp.transpose(dot(c, b, NT))
        cols = rolled(small_ref[ROW_COLS : ROW_COLS + T], j)
        for i in range(GROUP_PAIRS):
            lanes = pl.ds(pl.multiple_of(j * GROUP_X + i * LANES, LANES), LANES)
            weights = []
            for k in range(2):
                h = 2 * i + k
                spread = seg[h : h + 1, :] - cols[:, h : h + 1]
                kernel = jnp.exp(jnp.where(upper, spread, -1e30)) * cols[:, HEADS + h : HEADS + h + 1]
                weights.append((kernel * scores).astype(BF16))
            gx_ref[:, lanes] = dot(jnp.concatenate(weights, axis=1), by_lane_half(g_ref[:, lanes]))
        store(j).start()

    @pl.loop(0, BLOCKS)
    def _(i):
        cols = span(i, GROUP_X)
        fill_window(win_ref, before_ref[:, cols], tok_ref[:, cols])
        weights = weight_ref[:, cols]
        for lo in range(0, GROUP_X, LANES):
            pre = pre_conv(win_ref, weights, lo)
            s = sigmoid(pre)
            at = pl.ds(pl.multiple_of(i * GROUP_X + lo, LANES), LANES)
            slope_ref[:, at] = s * (1.0 + pre * (1.0 - s))
        store_slope(i).start()

    for j in range(GROUPS):
        store(j).wait()
    for i in range(BLOCKS):
        store_slope(i).wait()


def run_slopes(bc, cot, small, tokens, before, weight):
    out = [("h", (T, WIDTH_X), F32), ("h", (T, CHANNELS), F32)]
    scratch = [
        pltpu.VMEM((T, 2 * WIDTH_B), BF16),
        pltpu.VMEM((T, WIDTH_X), BF16),
        pltpu.VMEM((SMALL_ROWS, LANES), F32),
        pltpu.VMEM((T, CHANNELS), BF16),
        pltpu.VMEM((8, CHANNELS), F32),
        pltpu.VMEM((TAPS, CHANNELS), F32),
        pltpu.VMEM((T, WIDTH_X), F32),
        pltpu.VMEM((T, CHANNELS), F32),
        pltpu.VMEM((8 + T, GROUP_X), F32),
        DMA(4, BLOCKS),
    ]
    return call(slopes_kernel, "slopes", out, "hhhhhh", 6, scratch, mib=24)(
        bc, cot, small, tokens, before, weight
    )


def leave_kernel(theirs, core_ref, x_h, bc_h, g_h, y_h, gx_h, gbc_h, slope_h, tok_h, before_h, state_ref,
                 small_h, raw_h, *rest):
    (out_h, pre_h, step_h, sum_h, x_ref, bc_ref, g_ref, y_ref, gx_ref, gbc_ref, slope_ref, tok_ref,
     before_ref, small_ref, raw_ref, out_ref, pre_ref, step_ref, sum_ref, win_ref, sems) = rest[-21:]
    half = 1 - core_ref[0] if theirs else core_ref[0]

    def loads(jj):
        j = half * HALF_GROUPS + jj
        far, near = span(j, GROUP_X), span(jj, GROUP_X)
        pairs = [(h.at[:, far], v.at[:, near]) for h, v in (
            (x_h, x_ref), (g_h, g_ref), (y_h, y_ref), (gx_h, gx_ref), (slope_h, slope_ref), (tok_h, tok_ref)
        )]
        return [pltpu.make_async_copy(a, b, sems.at[1 + jj, i]) for i, (a, b) in enumerate(pairs)]

    def thin(jj):
        pairs = []
        for base in range(2):
            far = span(base * GROUPS + half * HALF_GROUPS + jj, STATE)
            wide = span(WIDTH_X // STATE + base * GROUPS + half * HALF_GROUPS + jj, STATE)
            near = span(base * HALF_GROUPS + jj, STATE)
            at = pl.ds(HALF_GROUPS * GROUP_X + (base * HALF_GROUPS + jj) * STATE, STATE)
            pairs += [
                (bc_h.at[:, far], bc_ref.at[:, near]),
                (gbc_h.at[:, far], gbc_ref.at[:, near]),
                (slope_h.at[:, wide], slope_ref.at[:, at]),
                (tok_h.at[:, wide], tok_ref.at[:, at]),
            ]
        return [pltpu.make_async_copy(a, b, sems.at[3 + jj, i]) for i, (a, b) in enumerate(pairs)]

    first = start_all([(small_h, small_ref), (before_h, before_ref), (raw_h, raw_ref)], sems.at[0])
    for jj in range(HALF_GROUPS):
        for copy in loads(jj) + thin(jj):
            copy.start()
    wait_all(first)
    last = iota((T, 2 * LANES), 0) == T - 1
    lower = (iota((T, T), 0) >= iota((T, T), 1)).astype(F32)

    def tap_sums(grad_pre, lo):
        width = grad_pre.shape[1]
        return [
            jnp.sum(grad_pre * win_ref[5 + k : 5 + k + T, lo : lo + width], axis=0, keepdims=True)
            for k in range(TAPS)
        ]

    def by_rows(sums):
        return [s[:, lo : lo + LANES] for lo in range(0, sums[0].shape[1], LANES) for s in sums]

    saves = []

    def save(src, dst):
        copy = pltpu.make_async_copy(src, dst, sems.at[5 + len(saves) // 8, len(saves) % 8])
        copy.start()
        saves.append(copy)

    for jj in range(HALF_GROUPS):
        j = half * HALF_GROUPS + jj
        wait_all(loads(jj) + thin(jj))
        near_b = slice(jj * STATE, (jj + 1) * STATE)
        near_c = slice((HALF_GROUPS + jj) * STATE, (HALF_GROUPS + jj + 1) * STATE)
        b = bc_ref[:, near_b]
        c = bc_ref[:, near_c]
        grad_b = gbc_ref[:, near_b]
        grad_c = gbc_ref[:, near_c]
        cols = rolled(small_ref[ROW_SCALE : ROW_SCALE + T], j)
        skip_rows = small_ref[pl.ds(pl.multiple_of(ROW_SKIP + j * GROUP_PAIRS, GROUP_PAIRS), GROUP_PAIRS), :]
        tot_rows = small_ref[pl.ds(pl.multiple_of(ROW_TOT + j * GROUP_PAIRS, GROUP_PAIRS), GROUP_PAIRS), :]
        seg_grad = jnp.zeros((GROUP_HEADS, T), F32)
        dt_grad = jnp.zeros((GROUP_HEADS, T), F32)
        skips = []
        terms = []
        near = slice(jj * GROUP_X, (jj + 1) * GROUP_X)
        fill_window(win_ref, before_ref[:, span(j, GROUP_X)], tok_ref[:, near])
        for q in range(0, GROUP_PAIRS, 2):
            lanes = slice(jj * GROUP_X + q * LANES, jj * GROUP_X + (q + 2) * LANES)
            rise = widen_two(cols, 0, q)
            keep = widen_two(cols, HEADS, q)
            at = jj * GROUP_PAIRS + q
            state = jnp.concatenate([state_ref[0, at], state_ref[0, at + 1]], axis=1)
            exits = jnp.concatenate([state_ref[1, at], state_ref[1, at + 1]], axis=1)
            skip = jnp.concatenate([skip_rows[q : q + 1], skip_rows[q + 1 : q + 2]], axis=1)
            tot = jnp.concatenate([tot_rows[q : q + 1], tot_rows[q + 1 : q + 2]], axis=1)
            x = x_ref[:, lanes].astype(F32)
            g = g_ref[:, lanes].astype(F32)
            y = y_ref[:, lanes] + rise * dot(c, state)
            through = keep * dot(b, exits)
            gx = gx_ref[:, lanes] + through
            grad_c = grad_c + dot((g * rise).astype(BF16), state, NT)
            grad_b = grad_b + dot((x * keep).astype(BF16), exits, NT)
            out_ref[:, lanes] = (y + skip * x).astype(BF16)
            grad_pre = (gx + skip * g) * slope_ref[:, lanes]
            pre_ref[:, lanes] = grad_pre
            terms += by_rows(tap_sums(grad_pre, q * LANES))
            skips += by_rows([jnp.sum(g * x, axis=0, keepdims=True)])
            x_gx = x * gx
            end = jnp.sum(x * through, axis=0, keepdims=True) + jnp.exp(tot) * jnp.sum(
                exits.astype(F32) * state.astype(F32), axis=0, keepdims=True
            )
            moved = g * y - x_gx + jnp.where(last, end, 0.0)
            pick = (
                iota((GROUP_HEADS, 2 * LANES), 0)
                == 2 * q + iota((GROUP_HEADS, 2 * LANES), 1) // HEAD_DIM
            ).astype(F32).astype(BF16)
            for part in split_two(moved):
                seg_grad = seg_grad + dot(pick, part, NT)
            for part in split_two(x_gx):
                dt_grad = dt_grad + dot(pick, part, NT)
        save(out_ref.at[:, pl.ds(jj * GROUP_X, GROUP_X)], out_h.at[:, span(j, GROUP_X)])
        save(pre_ref.at[:, pl.ds(jj * GROUP_X, GROUP_X)], pre_h.at[:, span(j, GROUP_X)])
        for grad, base in ((grad_b, 0), (grad_c, 1)):
            at = HALF_GROUPS * GROUP_X + (base * HALF_GROUPS + jj) * STATE
            far = span(WIDTH_X // STATE + base * GROUPS + j, STATE)
            fill_window(win_ref, before_ref[:, far], tok_ref[:, at : at + STATE])
            grad_pre = grad * slope_ref[:, at : at + STATE]
            pre_ref[:, at : at + STATE] = grad_pre
            terms += tap_sums(grad_pre, 0)
            save(pre_ref.at[:, pl.ds(at, STATE)], pre_h.at[:, far])
        heads = span(j, GROUP_HEADS)
        behind = exact_dot(seg_grad, lower)
        dt = small_ref[pl.ds(pl.multiple_of(ROW_DT + j * GROUP_HEADS, GROUP_HEADS), GROUP_HEADS), :]
        decay = small_ref[pl.ds(pl.multiple_of(ROW_DECAY + j * GROUP_HEADS, GROUP_HEADS), GROUP_HEADS), :]
        near = pl.ds(jj * GROUP_HEADS, GROUP_HEADS)
        step_ref[near, :] = (dt_grad / dt + decay * behind) * sigmoid(raw_ref[heads, :])
        save(step_ref.at[near], step_h.at[heads])
        rows = jj * SUM_GROUP
        sum_ref[rows : rows + SUM_GROUP, :] = jnp.concatenate(terms + skips + [dt * behind * decay], axis=0)
        save(sum_ref.at[pl.ds(rows, SUM_GROUP)], sum_h.at[span(j, SUM_GROUP)])
    wait_all(saves)


def run_leave(core, inputs, state, small, raw, before_out):
    out = [
        ("h", (T, WIDTH_X), BF16),
        ("h", (T, CHANNELS), F32),
        ("h", (HEADS, T), F32),
        ("h", (SUM_ROWS, LANES), F32),
    ]
    half_x = HALF_GROUPS * GROUP_X
    half_b = 2 * HALF_GROUPS * STATE
    scratch = [
        pltpu.VMEM((T, half_x), BF16),
        pltpu.VMEM((T, half_b), BF16),
        pltpu.VMEM((T, half_x), BF16),
        pltpu.VMEM((T, half_x), F32),
        pltpu.VMEM((T, half_x), F32),
        pltpu.VMEM((T, half_b), F32),
        pltpu.VMEM((T, half_x + half_b), F32),
        pltpu.VMEM((T, half_x + half_b), BF16),
        pltpu.VMEM((8, CHANNELS), F32),
        pltpu.VMEM((SMALL_ROWS, LANES), F32),
        pltpu.VMEM((HEADS, T), F32),
        pltpu.VMEM((T, half_x), BF16),
        pltpu.VMEM((T, half_x + half_b), F32),
        pltpu.VMEM((HALF_GROUPS * GROUP_HEADS, T), F32),
        pltpu.VMEM((HALF_GROUPS * SUM_GROUP, LANES), F32),
        pltpu.VMEM((8 + T, GROUP_X), F32),
        DMA(7, 8),
    ]
    args = [core, *inputs, state, small, raw]
    specs = "s" + "h" * 9 + ("V" if before_out is None else "v") + "hh"
    aliases = {}
    if before_out is not None:
        aliases = {len(args) + i: i for i in range(len(out))}
        args += before_out
        specs += "h" * len(out)
    kernel = functools.partial(leave_kernel, before_out is not None)
    return call(kernel, "leave", out, specs, 5, scratch, mib=24, aliases=aliases)(*args)


def spread_kernel(pre_h, halo_ref, weight_h, out_h, pre_ref, weight_ref, out_ref, win_ref, sems):
    first = start_all([(weight_h, weight_ref)], sems.at[0])

    def load(i):
        at = span(i, GROUP_X)
        return pltpu.make_async_copy(pre_h.at[:, at], pre_ref.at[:, at], sems.at[1, i])

    def store(i):
        at = span(i, GROUP_X)
        return pltpu.make_async_copy(out_ref.at[:, at], out_h.at[:, at], sems.at[2, i])

    for i in range(BLOCKS):
        load(i).start()
    wait_all(first)

    @pl.loop(0, BLOCKS)
    def _(i):
        load(i).wait()
        cols = span(i, GROUP_X)
        win_ref[0:T, :] = pre_ref[:, cols]
        win_ref[T : T + TAPS - 1, :] = halo_ref[:, cols].astype(F32)
        weights = weight_ref[:, cols]
        for lo in range(0, GROUP_X, LANES):
            at = slice(lo, lo + LANES)
            acc = weights[0:1, at] * win_ref[3 : 3 + T, at]
            for k in range(1, TAPS):
                acc = acc + weights[k : k + 1, at] * win_ref[3 - k : 3 - k + T, at]
            out_ref[:, pl.ds(pl.multiple_of(i * GROUP_X + lo, LANES), LANES)] = acc.astype(BF16)
        store(i).start()

    for i in range(BLOCKS):
        store(i).wait()


def run_spread(pre, halo, weight):
    out = [("h", (T, CHANNELS), BF16)]
    scratch = [
        pltpu.VMEM((T, CHANNELS), F32),
        pltpu.VMEM((TAPS, CHANNELS), F32),
        pltpu.VMEM((T, CHANNELS), BF16),
        pltpu.VMEM((T + 8, GROUP_X), F32),
        DMA(3, BLOCKS),
    ]
    return call(spread_kernel, "spread", out, "hvh", 4, scratch, mib=16)(pre, halo, weight)[0]


def finish_kernel(sum_ref, conv_ref, decay_ref, skip_ref):
    for i in range(CHANNELS // LANES):
        if i < PAIRS:
            row = SUM_GROUP * (i // GROUP_PAIRS) + TAPS * (i % GROUP_PAIRS)
        else:
            kind, group = divmod(i - PAIRS, GROUPS)
            row = SUM_GROUP * group + TAPS * (GROUP_PAIRS + kind)
        conv_ref[:, i * LANES : (i + 1) * LANES] = sum_ref[row : row + TAPS, :]
    skip_at, decay_at = TAPS * (GROUP_PAIRS + 2), SUM_GROUP - GROUP_HEADS
    skips = jnp.concatenate(
        [sum_ref[SUM_GROUP * j + skip_at : SUM_GROUP * j + decay_at, :] for j in range(GROUPS)], axis=0
    )
    decays = jnp.concatenate(
        [sum_ref[SUM_GROUP * j + decay_at : SUM_GROUP * (j + 1), :] for j in range(GROUPS)], axis=0
    )
    ones = jnp.ones((8, LANES), F32)
    decay_ref[...] = exact_dot(ones, decays, NT)[0:1]
    left = iota((8, LANES), 1) < HEAD_DIM
    even = exact_dot(jnp.where(left, 1.0, 0.0), skips, NT)
    odd = exact_dot(jnp.where(left, 0.0, 1.0), skips, NT)
    at_even = (iota((PAIRS, HEADS), 1) == 2 * iota((PAIRS, HEADS), 0)).astype(F32)
    at_odd = (iota((PAIRS, HEADS), 1) == 2 * iota((PAIRS, HEADS), 0) + 1).astype(F32)
    skip_ref[...] = (exact_dot(even, at_even) + exact_dot(odd, at_odd))[0:1]


def run_finish(sums):
    out = [("v", (TAPS, CHANNELS), F32), ("v", (1, HEADS), F32), ("v", (1, HEADS), F32)]
    return call(finish_kernel, "finish", out, "v", 1, mib=16)(sums)


CTX = ("chip", "core")
ALL = ("dp", "chip", "core")


def all_to_all(value, axis):
    return lax.all_to_all(value, axis, 0, 0, tiled=True)


def tie(*values):
    return lax.optimization_barrier(values)


def sum_everywhere(parts, chips):
    share = SUM_ROWS // chips
    total = jnp.sum(parts.reshape(chips, share, LANES), axis=0)
    total = total + lax.ppermute(total, "core", [(0, 1), (1, 0)])
    count = lax.axis_size("dp")
    flip = 1
    while flip < count:
        mask = flip if 2 * flip < count else count - 1
        total = total + lax.ppermute(total, "dp", [(i, i ^ mask) for i in range(count)])
        flip *= 2
    return all_to_all(jnp.broadcast_to(total[None], (chips, share, LANES)).reshape(SUM_ROWS, LANES), "chip")


def local(conv_input, conv_weight, step_raw, decay_log, skip_gain, cotangent):
    chips = lax.axis_size("chip")
    devices = 2 * chips
    tokens = conv_input[0]
    raw = step_raw[0]
    cot = cotangent[0]
    core = lax.axis_index("core").astype(jnp.int32).reshape(1)
    swap = [(0, 1), (1, 0)]
    halo = lax.ppermute(tokens[T - TAPS + 1 :], CTX, [(i, i + 1) for i in range(devices - 1)])
    small, small_near, tot, x0, bc0, head = run_begin(
        raw, decay_log.reshape(1, HEADS), skip_gain.reshape(1, HEADS), tokens, conv_weight
    )
    other = lax.ppermute(tot, "core", swap)
    x, bc, before, x_near, bc_near, out = run_enter(
        core, x0, bc0, head, halo, conv_weight, cot, small_near
    )
    got_near = lax.ppermute(out, "core", swap)
    own_near = run_own(core, x_near, bc_near, cot, small_near)
    packed, own, got, tots = run_pack(core, own_near, got_near, tot, other)
    heard = all_to_all(packed, "chip")
    y, gbc = run_inner(x, bc, cot, small)
    heard, y, gbc = tie(heard, y, gbc)
    chained = run_chain(chips, heard)
    late, chained = tie(bc, chained)
    back = all_to_all(chained, "chip")
    gx, slope = run_slopes(late, cot, small, tokens, before, conv_weight)
    back, gx, slope = tie(back, gx, slope)
    mine, send = run_unpack(core, back, own, got, tots)
    theirs = lax.ppermute(send, "core", swap)
    inputs = (x, bc, cot, y, gx, gbc, slope, tokens, before)
    half = run_leave(core, inputs, mine, small, raw, None)
    out_tokens, pre, grad_step, sums = run_leave(core, inputs, theirs, small, raw, half)
    parts = all_to_all(sums, "chip")
    first = pre[: TAPS - 1].astype(BF16)
    after = lax.ppermute(first, CTX, [(i + 1, i) for i in range(devices - 1)])
    parts, after = tie(parts, after)
    grad_conv, grad_decay, grad_skip = run_finish(sum_everywhere(parts, chips))
    grad_tokens = run_spread(pre, after, conv_weight)
    return (
        out_tokens[None],
        grad_tokens[None],
        grad_step[None],
        grad_conv,
        grad_decay.reshape(HEADS),
        grad_skip.reshape(HEADS),
    )


def solution(mesh):
    dp, ctx = mesh.devices.shape
    fine = Mesh(mesh.devices.reshape(dp, ctx // 2, 2), ALL)
    seq = P("dp", CTX, None)
    rate = P("dp", None, CTX)
    in_specs = (seq, P(), rate, P(), P(), seq)
    out_specs = (seq, seq, rate, P(), P(), P())
    return jax.shard_map(local, mesh=fine, in_specs=in_specs, out_specs=out_specs, check_vma=False)
```

```python
import functools

import jax
import jax.numpy as jnp
from jax import lax
from jax.experimental import pallas as pl
from jax.experimental.pallas import tpu as pltpu
from jax.sharding import Mesh
from jax.sharding import PartitionSpec as P

HEADS = 64
HEAD_DIM = 64
GROUPS = 4
STATE = 128
TAPS = 4
T = 128
LANES = 128
WIDTH_X = HEADS * HEAD_DIM
WIDTH_B = GROUPS * STATE
CHANNELS = WIDTH_X + 2 * WIDTH_B
GROUP_X = WIDTH_X // GROUPS
PAIRS = HEADS // 2
GROUP_PAIRS = PAIRS // GROUPS
GROUP_HEADS = HEADS // GROUPS
HALF_PAIRS = PAIRS // 2
HALF_GROUPS = GROUPS // 2
F32 = jnp.float32
BF16 = jnp.bfloat16
EXACT = lax.Precision.HIGHEST
NN = (((1,), (0,)), ((), ()))
NT = (((1,), (1,)), ((), ()))
SUM_ROWS = 256
SUM_GROUP = SUM_ROWS // GROUPS
PACK_ROWS = 2 * STATE + 16


def dot(a, b, dims=NN):
    return lax.dot_general(a, b, dims, preferred_element_type=F32)


def exact_dot(a, b, dims=NN):
    return lax.dot_general(a, b, dims, precision=EXACT, preferred_element_type=F32)


def iota(shape, dim):
    return lax.broadcasted_iota(jnp.int32, shape, dim)


def sigmoid(v):
    return 0.5 + 0.5 * jnp.tanh(0.5 * v)


def split_two(v):
    high = v.astype(BF16)
    return high, (v - high.astype(F32)).astype(BF16)


def span(index, size):
    return pl.ds(pl.multiple_of(index * size, size), size)


def pin(value, space):
    return pltpu.with_memory_space_constraint(value, space)


def placed(space, shape, dtype):
    return space(shape, dtype)


def call(kernel, name, outs, specs, micros, scratch=(), mib=28, aliases=None):
    cost = pl.CostEstimate(
        flops=int(micros * 1e9), transcendentals=0, bytes_accessed=int(micros * 3.6e6)
    )
    blocks = {
        "s": pl.BlockSpec(memory_space=pltpu.SMEM),
        "v": pl.BlockSpec(memory_space=pltpu.VMEM),
        "V": pl.BlockSpec(memory_space=pltpu.VMEM),
        "h": pl.BlockSpec(memory_space=pltpu.HBM),
    }
    spaces = {"V": pltpu.VMEM, "h": pltpu.HBM}
    shapes = [
        placed(spaces[p], shape, dtype) if p in spaces else jax.ShapeDtypeStruct(shape, dtype)
        for p, shape, dtype in outs
    ]
    run = pl.pallas_call(
        kernel,
        out_shape=shapes,
        in_specs=[blocks[p] for p in specs],
        out_specs=[blocks[p] for p, _, _ in outs],
        scratch_shapes=list(scratch),
        input_output_aliases=aliases or {},
        cost_estimate=cost,
        compiler_params=pltpu.CompilerParams(vmem_limit_bytes=mib << 20),
        name=name,
    )

    def go(*args):
        return run(*[pin(a, spaces[p]) if p in spaces else a for a, p in zip(args, specs, strict=True)])

    return go


def start_all(pairs, sems):
    copies = [pltpu.make_async_copy(a, b, sems.at[i]) for i, (a, b) in enumerate(pairs)]
    for copy in copies:
        copy.start()
    return copies


def wait_all(copies):
    for copy in copies:
        copy.wait()


def DMA(*shape):
    return pltpu.SemaphoreType.DMA(shape)


def fill_window(win_ref, before, tokens):
    width = tokens.shape[1]
    win_ref[0:8, :width] = before
    win_ref[8 : 8 + T, :width] = tokens.astype(F32)


def pre_conv(win_ref, weights, lo):
    cols = slice(lo, lo + LANES)
    acc = weights[0:1, cols] * win_ref[5 : 5 + T, cols]
    for k in range(1, TAPS):
        acc = acc + weights[k : k + 1, cols] * win_ref[5 + k : 5 + k + T, cols]
    return acc


BLOCKS = CHANNELS // GROUP_X


ROW_DT, ROW_SEG, ROW_COLS, ROW_SCALE, ROW_TOT, ROW_SKIP, ROW_DECAY, SMALL_ROWS = (
    0, 64, 128, 256, 384, 416, 448, 512
)


def begin_kernel(raw_h, decay_log_h, skip_gain_h, tok_h, weight_h, g_h,
                 small_h, small_ref, tot_ref, x_ref, bc_ref, head_ref, weight_ref, g_ref,
                 raw_ref, decay_log_ref, skip_gain_ref, hold_ref, win_ref, sems):
    first = start_all(
        [(raw_h, raw_ref), (decay_log_h, decay_log_ref), (skip_gain_h, skip_gain_ref), (weight_h, weight_ref)],
        sems.at[0],
    )
    blocks = [pl.ds(i * GROUP_X, GROUP_X) for i in range(BLOCKS)]
    copies = start_all([(tok_h.at[:, at], hold_ref.at[:, at]) for at in blocks], sems.at[1])
    later = start_all([(g_h, g_ref)], sems.at[2])
    diagonal = iota((HEADS, HEADS), 0) == iota((HEADS, HEADS), 1)

    def column(row):
        return jnp.sum(jnp.where(diagonal, row, 0.0), axis=1, keepdims=True)

    wait_all(first)
    raw = raw_ref[...]
    dt = jnp.log1p(jnp.exp(raw))
    decay = -jnp.exp(column(decay_log_ref[...]))
    upper = (iota((T, T), 0) <= iota((T, T), 1)).astype(F32)
    seg = exact_dot(dt * decay, upper)
    total = seg[:, T - 1 : T]
    small_ref[ROW_DT : ROW_DT + HEADS] = dt
    small_ref[ROW_SEG : ROW_SEG + HEADS] = seg
    small_ref[ROW_COLS : ROW_COLS + T] = jnp.transpose(jnp.concatenate([seg, dt], axis=0))
    small_ref[ROW_SCALE : ROW_SCALE + T] = jnp.transpose(
        jnp.concatenate([jnp.exp(seg), jnp.exp(total - seg) * dt], axis=0)
    )
    left = iota((PAIRS, LANES), 1) < HEAD_DIM
    even = (iota((PAIRS, HEADS), 1) == 2 * iota((PAIRS, HEADS), 0)).astype(F32)
    odd = (iota((PAIRS, HEADS), 1) == 2 * iota((PAIRS, HEADS), 0) + 1).astype(F32)

    def paired(col):
        wide = jnp.broadcast_to(col, (HEADS, LANES))
        return jnp.where(left, exact_dot(even, wide), exact_dot(odd, wide))

    tot = paired(total)
    tot_ref[...] = tot
    small_ref[ROW_TOT : ROW_TOT + PAIRS] = tot
    small_ref[ROW_SKIP : ROW_SKIP + PAIRS] = paired(column(skip_gain_ref[...]))
    small_ref[ROW_DECAY : ROW_DECAY + HEADS] = jnp.broadcast_to(decay, (HEADS, LANES))
    save = start_all([(small_ref, small_h)], sems.at[0])
    win_ref[0:8, :] = jnp.zeros((8, GROUP_X), F32)
    for i in range(BLOCKS):
        copies[i].wait()
        cols = slice(i * GROUP_X, (i + 1) * GROUP_X)
        win_ref[8 : 8 + T, :] = hold_ref[:, cols].astype(F32)
        for lo in range(0, GROUP_X, LANES):
            at = i * GROUP_X + lo
            pre = pre_conv(win_ref, weight_ref[:, cols], lo)
            mixed = (pre * sigmoid(pre)).astype(BF16)
            head_ref[:, at : at + LANES] = pre[0:8]
            if at < WIDTH_X:
                x_ref[:, at : at + LANES] = mixed
            else:
                bc_ref[:, at - WIDTH_X : at - WIDTH_X + LANES] = mixed
    wait_all(save + later)


def run_begin(raw, decay_log, skip_gain, tokens, weight, cot):
    out = [
        ("h", (SMALL_ROWS, LANES), F32),
        ("V", (SMALL_ROWS, LANES), F32),
        ("V", (PAIRS, LANES), F32),
        ("V", (T, WIDTH_X), BF16),
        ("V", (T, 2 * WIDTH_B), BF16),
        ("V", (8, CHANNELS), F32),
        ("V", (TAPS, CHANNELS), F32),
        ("V", (T, WIDTH_X), BF16),
    ]
    scratch = [
        pltpu.VMEM((HEADS, T), F32),
        pltpu.VMEM((1, HEADS), F32),
        pltpu.VMEM((1, HEADS), F32),
        pltpu.VMEM((T, CHANNELS), BF16),
        pltpu.VMEM((8 + T, GROUP_X), F32),
        DMA(3, BLOCKS),
    ]
    return call(begin_kernel, "begin", out, "hhhhhh", 4, scratch, mib=16)(
        raw, decay_log, skip_gain, tokens, weight, cot
    )


def rolled(cols, group):
    return pltpu.roll(cols, (LANES - group * GROUP_HEADS) % LANES, 1)


def widen(cols, base, pair):
    first = iota((T, LANES), 1) < HEAD_DIM
    at = base + 2 * pair
    return jnp.where(first, cols[:, at : at + 1], cols[:, at + 1 : at + 2])


def widen_two(cols, base, pair):
    return jnp.concatenate([widen(cols, base, pair), widen(cols, base, pair + 1)], axis=1)


def fill_half(half, x_ref, bc_ref, g_ref, scale, dst_ref):
    for jj in range(HALF_GROUPS):
        j = half * HALF_GROUPS + jj
        b_flip = jnp.transpose(bc_ref[:, span(j, STATE)].astype(F32)).astype(BF16)
        c_flip = jnp.transpose(bc_ref[:, span(GROUPS + j, STATE)].astype(F32)).astype(BF16)
        cols = rolled(scale, j)
        for q in range(0, GROUP_PAIRS, 2):
            lanes = pl.ds(pl.multiple_of(j * GROUP_X + q * LANES, 2 * LANES), 2 * LANES)
            xw = (x_ref[:, lanes].astype(F32) * widen_two(cols, HEADS, q)).astype(BF16)
            gw = (g_ref[:, lanes].astype(F32) * widen_two(cols, 0, q)).astype(BF16)
            state = dot(b_flip, xw).astype(BF16)
            grad = dot(c_flip, gw).astype(BF16)
            for k in range(2):
                at = jj * GROUP_PAIRS + q + k
                dst_ref[0, at] = state[:, k * LANES : (k + 1) * LANES]
                dst_ref[1, at] = grad[:, k * LANES : (k + 1) * LANES]


def enter_kernel(core_ref, x0_ref, bc0_ref, head_ref, halo_ref, weight_ref, g_ref, small_ref,
                 x_h, bc_h, before_h, x_ref, bc_ref, out_ref, before_ref, sems):
    half = 1 - core_ref[0]
    row = iota((8, GROUP_X), 0)
    for i in range(BLOCKS):
        cols = slice(i * GROUP_X, (i + 1) * GROUP_X)
        halo = halo_ref[:, cols].astype(F32)
        weight = weight_ref[:, cols]
        pre = head_ref[:, cols]
        before = jnp.zeros((8, GROUP_X), F32)
        for t in range(TAPS - 1):
            extra = jnp.zeros((1, GROUP_X), F32)
            for k in range(TAPS - 1 - t):
                extra = extra + weight[k : k + 1] * halo[t + k : t + k + 1]
            pre = pre + jnp.where(row == t, extra, 0.0)
            before = before + jnp.where(row == t + 5, halo[t : t + 1], 0.0)
        before_ref[:, cols] = before
        fixed = pre * sigmoid(pre)
        src, dst, at = (x0_ref, x_ref, cols) if i < GROUPS else (bc0_ref, bc_ref, slice(0, GROUP_X))
        rest = src[0:16, at].astype(F32)
        dst[16:T, at] = src[16:T, at]
        dst[0:16, at] = jnp.concatenate([fixed, rest[8:16]], axis=0).astype(BF16)
    saves = start_all([(x_ref, x_h), (bc_ref, bc_h), (before_ref, before_h)], sems)
    fill_half(half, x_ref, bc_ref, g_ref, small_ref[ROW_SCALE : ROW_SCALE + T], out_ref)
    wait_all(saves)


def run_enter(core, x0, bc0, head, halo, weight, cot, small):
    out = [
        ("h", (T, WIDTH_X), BF16),
        ("h", (T, 2 * WIDTH_B), BF16),
        ("h", (8, CHANNELS), F32),
        ("V", (T, WIDTH_X), BF16),
        ("V", (T, 2 * WIDTH_B), BF16),
        ("V", (2, HALF_PAIRS, STATE, LANES), BF16),
    ]
    scratch = [pltpu.VMEM((8, CHANNELS), F32), DMA(3)]
    return call(enter_kernel, "enter", out, "sVVVvVVV", 3, scratch, mib=16)(
        core, x0, bc0, head, halo, weight, cot, small
    )


def own_kernel(core_ref, x_ref, bc_ref, g_ref, small_ref, own_ref):
    fill_half(core_ref[0], x_ref, bc_ref, g_ref, small_ref[ROW_SCALE : ROW_SCALE + T], own_ref)


def run_own(core, x, bc, cot, small):
    out = [("V", (2, HALF_PAIRS, STATE, LANES), BF16)]
    return call(own_kernel, "own", out, "sVVVV", 3, mib=16)(core, x, bc, cot, small)[0]


STEP_PAIRS = 4
STEPS = HALF_PAIRS // STEP_PAIRS


def pack_kernel(core_ref, own_ref, got_ref, tot_ref, other_ref,
                out_h, own_h, got_h, tots_h, out_ref, sems):
    saves = start_all(
        [
            (own_ref, own_h),
            (got_ref, got_h),
            (tot_ref, tots_h.at[pl.ds(0, PAIRS)]),
            (other_ref, tots_h.at[pl.ds(PAIRS, PAIRS)]),
        ],
        sems.at[0],
    )
    second = core_ref[0] == 1
    outs = []
    for i in range(HALF_PAIRS):
        at = core_ref[0] * HALF_PAIRS + i
        tot = tot_ref[pl.ds(at, 1), :]
        other = other_ref[pl.ds(at, 1), :]
        one = jnp.ones_like(tot)
        by_own = jnp.exp(tot)
        by_other = jnp.exp(other)
        state = (
            jnp.where(second, one, by_other) * own_ref[0, i].astype(F32)
            + jnp.where(second, by_own, one) * got_ref[0, i].astype(F32)
        )
        grad = (
            jnp.where(second, by_other, one) * own_ref[1, i].astype(F32)
            + jnp.where(second, one, by_own) * got_ref[1, i].astype(F32)
        )
        out_ref[i, 0:STATE, :] = state.astype(BF16)
        out_ref[i, STATE : 2 * STATE, :] = grad.astype(BF16)
        both = tot + other
        high = both.astype(BF16).astype(F32)
        mid = (both - high).astype(BF16).astype(F32)
        low = both - high - mid
        row = iota((16, LANES), 0)
        wide = jnp.where(row == 0, high, jnp.where(row == 1, mid, jnp.where(row == 2, low, 0.0)))
        out_ref[i, 2 * STATE : PACK_ROWS, :] = wide.astype(BF16)
        if i % STEP_PAIRS == STEP_PAIRS - 1:
            done = pl.ds(i + 1 - STEP_PAIRS, STEP_PAIRS)
            copy = pltpu.make_async_copy(out_ref.at[done], out_h.at[done], sems.at[1, i // STEP_PAIRS])
            copy.start()
            outs.append(copy)
    wait_all(outs + saves)


def run_pack(core, own, got, tot, other):
    half = (2, HALF_PAIRS, STATE, LANES)
    packed = (HALF_PAIRS, PACK_ROWS, LANES)
    out = [("h", packed, BF16), ("h", half, BF16), ("h", half, BF16), ("h", (2 * PAIRS, LANES), F32)]
    scratch = [pltpu.VMEM(packed, BF16), DMA(2, STEPS)]
    return call(pack_kernel, "pack", out, "sVvVv", 2, scratch, mib=16)(core, own, got, tot, other)


def chain_kernel(chips, per, in_ref, out_ref):
    for q in range(per):
        def decay(k):
            rows = in_ref[k * per + q, 2 * STATE : PACK_ROWS, :].astype(F32)
            return jnp.exp(rows[0:1] + rows[1:2] + rows[2:3])

        carry = jnp.zeros((STATE, LANES), F32)
        for k in range(chips):
            out_ref[k * per + q, 0:STATE, :] = carry.astype(BF16)
            if k < chips - 1:
                carry = decay(k) * carry + in_ref[k * per + q, 0:STATE, :].astype(F32)
        carry = jnp.zeros((STATE, LANES), F32)
        for k in reversed(range(chips)):
            out_ref[k * per + q, STATE : 2 * STATE, :] = carry.astype(BF16)
            if k > 0:
                carry = decay(k) * carry + in_ref[k * per + q, STATE : 2 * STATE, :].astype(F32)


def run_chain(chips, packed):
    kernel = functools.partial(chain_kernel, chips, HALF_PAIRS // chips)
    out = [("v", (HALF_PAIRS, 2 * STATE, LANES), BF16)]
    return call(kernel, "chain", out, "v", 1, mib=16)(packed)[0]


HALF_X = HALF_GROUPS * GROUP_X
HALF_B = 2 * HALF_GROUPS * STATE

NEAR = [
    ("V", (T, HALF_X), BF16),
    ("V", (T, HALF_X), BF16),
    ("V", (T, HALF_X), F32),
    ("V", (T, HALF_X), F32),
    ("V", (T, HALF_X + HALF_B), F32),
    ("V", (T, HALF_X + HALF_B), BF16),
    ("V", (T, HALF_B), BF16),
    ("V", (T, HALF_B), F32),
]
COMMON = [
    ("V", (8, CHANNELS), F32),
    ("V", (SMALL_ROWS, LANES), F32),
    ("V", (HEADS, T), F32),
    ("V", (PAIRS, LANES), F32),
]
FETCHES = 6 + 8


def fetch_half(half, far, near, sems):
    x_h, g_h, y_h, gx_h, slope_h, tok_h, bc_h, gbc_h = far
    x_v, g_v, y_v, gx_v, slope_v, tok_v, bc_v, gbc_v = near
    wide = pl.ds(0, HALF_X)
    pairs = [
        (a.at[:, span(half, HALF_X)], b.at[:, wide])
        for a, b in ((x_h, x_v), (g_h, g_v), (y_h, y_v), (gx_h, gx_v), (slope_h, slope_v), (tok_h, tok_v))
    ]
    size = HALF_GROUPS * STATE
    for base in range(2):
        at = span(base * 2 + half, size)
        off = span(WIDTH_X // size + base * 2 + half, size)
        pairs += [
            (bc_h.at[:, at], bc_v.at[:, pl.ds(base * size, size)]),
            (gbc_h.at[:, at], gbc_v.at[:, pl.ds(base * size, size)]),
            (slope_h.at[:, off], slope_v.at[:, pl.ds(HALF_X + base * size, size)]),
            (tok_h.at[:, off], tok_v.at[:, pl.ds(HALF_X + base * size, size)]),
        ]
    return start_all(pairs, sems)


def unpack_kernel(core_ref, back_ref, own_h, got_h, tots_h, *rest):
    far, rest = rest[: len(NEAR)], rest[len(NEAR) :]
    common_far, rest = rest[: len(COMMON)], rest[len(COMMON) :]
    mine_ref, send_ref, *rest = rest
    near, rest = rest[: len(NEAR)], rest[len(NEAR) :]
    common, rest = rest[: len(COMMON)], rest[len(COMMON) :]
    own_ref, got_ref, tots_ref, sems, fetch_sems = rest
    first = start_all([(tots_h, tots_ref)], sems.at[STEPS])
    steps = []
    for step in range(STEPS):
        at = pl.ds(step * STEP_PAIRS, STEP_PAIRS)
        steps.append(
            start_all([(own_h.at[:, at], own_ref.at[:, at]), (got_h.at[:, at], got_ref.at[:, at])], sems.at[step])
        )
    fetches = start_all(list(zip(common_far, common)), fetch_sems.at[1])
    fetches += fetch_half(core_ref[0], far, near, fetch_sems.at[0])
    wait_all(first)
    second = core_ref[0] == 1
    for i in range(HALF_PAIRS):
        if i % STEP_PAIRS == 0:
            wait_all(steps[i // STEP_PAIRS])
        at = core_ref[0] * HALF_PAIRS + i
        tot = tots_ref[pl.ds(at, 1), :]
        other = tots_ref[pl.ds(PAIRS + at, 1), :]
        decay_zero = jnp.exp(jnp.where(second, other, tot))
        decay_one = jnp.exp(jnp.where(second, tot, other))
        state_zero = back_ref[i, 0:STATE, :].astype(F32)
        grad_one = back_ref[i, STATE : 2 * STATE, :].astype(F32)
        left = jnp.where(second, got_ref[0, i].astype(F32), own_ref[0, i].astype(F32))
        right = jnp.where(second, own_ref[1, i].astype(F32), got_ref[1, i].astype(F32))
        state_one = decay_zero * state_zero + left
        grad_zero = decay_one * grad_one + right
        mine_ref[0, i] = jnp.where(second, state_one, state_zero).astype(BF16)
        mine_ref[1, i] = jnp.where(second, grad_one, grad_zero).astype(BF16)
        send_ref[0, i] = jnp.where(second, state_zero, state_one).astype(BF16)
        send_ref[1, i] = jnp.where(second, grad_zero, grad_one).astype(BF16)
    wait_all(fetches)


def run_unpack(core, back, own, got, tots, far, common):
    half = (2, HALF_PAIRS, STATE, LANES)
    out = [("V", half, BF16)] * 2 + NEAR + COMMON
    scratch = [
        pltpu.VMEM(half, BF16),
        pltpu.VMEM(half, BF16),
        pltpu.VMEM((2 * PAIRS, LANES), F32),
        DMA(STEPS + 1, 2),
        DMA(2, FETCHES),
    ]
    specs = "svhhh" + "h" * (len(NEAR) + len(COMMON))
    outs = call(unpack_kernel, "unpack", out, specs, 3, scratch, mib=16)(
        core, back, own, got, tots, *far, *common
    )
    return outs[0], outs[1], outs[2 : 2 + len(NEAR)], outs[2 + len(NEAR) :]


def by_lane_half(v):
    first = iota(v.shape, 1) < HEAD_DIM
    wide = v.astype(F32)
    return jnp.concatenate(
        [jnp.where(first, wide, 0.0).astype(BF16), jnp.where(first, 0.0, wide).astype(BF16)], axis=0
    )


def inner_kernel(x_h, bc_h, g_h, small_h, y_h, gbc_h, skips_h,
                 x_ref, bc_ref, g_ref, small_ref, y_ref, gbc_ref, skips_ref, sems):
    first = start_all([(bc_h, bc_ref), (small_h, small_ref)], sems.at[0])

    def loads(j):
        at = span(j, GROUP_X)
        return [
            pltpu.make_async_copy(x_h.at[:, at], x_ref.at[:, at], sems.at[1, j]),
            pltpu.make_async_copy(g_h.at[:, at], g_ref.at[:, at], sems.at[2, j]),
        ]

    def store(j):
        at = span(j, GROUP_X)
        return pltpu.make_async_copy(y_ref.at[:, at], y_h.at[:, at], sems.at[3, j])

    for j in range(GROUPS):
        for copy in loads(j):
            copy.start()
    wait_all(first)
    lower = iota((T, T), 0) >= iota((T, T), 1)

    @pl.loop(0, GROUPS)
    def _(j):
        wait_all(loads(j))
        b = bc_ref[:, span(j, STATE)]
        c = bc_ref[:, span(GROUPS + j, STATE)]
        seg = small_ref[pl.ds(pl.multiple_of(ROW_SEG + j * GROUP_HEADS, GROUP_HEADS), GROUP_HEADS), :]
        dt = small_ref[pl.ds(pl.multiple_of(ROW_DT + j * GROUP_HEADS, GROUP_HEADS), GROUP_HEADS), :]
        scores = dot(c, b, NT)
        cols = rolled(small_ref[ROW_COLS : ROW_COLS + T], j)
        total = jnp.zeros((T, T), F32)
        skips = []
        for i in range(GROUP_PAIRS):
            lanes = pl.ds(pl.multiple_of(j * GROUP_X + i * LANES, LANES), LANES)
            x = x_ref[:, lanes]
            g = g_ref[:, lanes]
            skips.append(jnp.sum(g.astype(F32) * x.astype(F32), axis=0, keepdims=True))
            inner = dot(by_lane_half(g), x, NT)
            weights = []
            for k in range(2):
                h = 2 * i + k
                spread = cols[:, h : h + 1] - seg[h : h + 1, :]
                kernel = jnp.exp(jnp.where(lower, spread, -1e30)) * dt[h : h + 1, :]
                total = total + kernel * inner[k * T : (k + 1) * T]
                weights.append((kernel * scores).astype(BF16))
            y_ref[:, lanes] = dot(jnp.concatenate(weights, axis=1), by_lane_half(x))
        skips_ref[span(j, GROUP_PAIRS), :] = jnp.concatenate(skips, axis=0)
        gbc_ref[:, span(GROUPS + j, STATE)] = dot(total.astype(BF16), b)
        gbc_ref[:, span(j, STATE)] = dot(jnp.transpose(total).astype(BF16), c)
        store(j).start()

    last = start_all([(gbc_ref, gbc_h), (skips_ref, skips_h)], sems.at[0])
    for j in range(GROUPS):
        store(j).wait()
    wait_all(last)


def run_inner(x, bc, cot, small):
    out = [("h", (T, WIDTH_X), F32), ("h", (T, 2 * WIDTH_B), F32), ("h", (PAIRS, LANES), F32)]
    scratch = [
        pltpu.VMEM((T, WIDTH_X), BF16),
        pltpu.VMEM((T, 2 * WIDTH_B), BF16),
        pltpu.VMEM((T, WIDTH_X), BF16),
        pltpu.VMEM((SMALL_ROWS, LANES), F32),
        pltpu.VMEM((T, WIDTH_X), F32),
        pltpu.VMEM((T, 2 * WIDTH_B), F32),
        pltpu.VMEM((PAIRS, LANES), F32),
        DMA(4, GROUPS),
    ]
    return call(inner_kernel, "inner", out, "hhhh", 4, scratch, mib=24)(x, bc, cot, small)


def slopes_kernel(bc_h, g_h, small_h, tok_h, before_h, weight_h, gx_h, slope_h,
                  bc_ref, g_ref, small_ref, tok_ref, before_ref, weight_ref, gx_ref, slope_ref, win_ref, sems):
    first = start_all(
        [(bc_h, bc_ref), (small_h, small_ref), (before_h, before_ref), (weight_h, weight_ref), (tok_h, tok_ref)],
        sems.at[0],
    )

    def load(j):
        at = span(j, GROUP_X)
        return pltpu.make_async_copy(g_h.at[:, at], g_ref.at[:, at], sems.at[1, j])

    def store(j):
        at = span(j, GROUP_X)
        return pltpu.make_async_copy(gx_ref.at[:, at], gx_h.at[:, at], sems.at[2, j])

    def store_slope(i):
        at = span(i, GROUP_X)
        return pltpu.make_async_copy(slope_ref.at[:, at], slope_h.at[:, at], sems.at[3, i])

    for j in range(GROUPS):
        load(j).start()
    wait_all(first)
    upper = iota((T, T), 0) <= iota((T, T), 1)

    @pl.loop(0, GROUPS)
    def _(j):
        load(j).wait()
        b = bc_ref[:, span(j, STATE)]
        c = bc_ref[:, span(GROUPS + j, STATE)]
        seg = small_ref[pl.ds(pl.multiple_of(ROW_SEG + j * GROUP_HEADS, GROUP_HEADS), GROUP_HEADS), :]
        scores = jnp.transpose(dot(c, b, NT))
        cols = rolled(small_ref[ROW_COLS : ROW_COLS + T], j)
        for i in range(GROUP_PAIRS):
            lanes = pl.ds(pl.multiple_of(j * GROUP_X + i * LANES, LANES), LANES)
            weights = []
            for k in range(2):
                h = 2 * i + k
                spread = seg[h : h + 1, :] - cols[:, h : h + 1]
                kernel = jnp.exp(jnp.where(upper, spread, -1e30)) * cols[:, HEADS + h : HEADS + h + 1]
                weights.append((kernel * scores).astype(BF16))
            gx_ref[:, lanes] = dot(jnp.concatenate(weights, axis=1), by_lane_half(g_ref[:, lanes]))
        store(j).start()

    @pl.loop(0, BLOCKS)
    def _(i):
        cols = span(i, GROUP_X)
        fill_window(win_ref, before_ref[:, cols], tok_ref[:, cols])
        weights = weight_ref[:, cols]
        for lo in range(0, GROUP_X, LANES):
            pre = pre_conv(win_ref, weights, lo)
            s = sigmoid(pre)
            at = pl.ds(pl.multiple_of(i * GROUP_X + lo, LANES), LANES)
            slope_ref[:, at] = s * (1.0 + pre * (1.0 - s))
        store_slope(i).start()

    for j in range(GROUPS):
        store(j).wait()
    for i in range(BLOCKS):
        store_slope(i).wait()


def run_slopes(bc, cot, small, tokens, before, weight):
    out = [("h", (T, WIDTH_X), F32), ("h", (T, CHANNELS), F32)]
    scratch = [
        pltpu.VMEM((T, 2 * WIDTH_B), BF16),
        pltpu.VMEM((T, WIDTH_X), BF16),
        pltpu.VMEM((SMALL_ROWS, LANES), F32),
        pltpu.VMEM((T, CHANNELS), BF16),
        pltpu.VMEM((8, CHANNELS), F32),
        pltpu.VMEM((TAPS, CHANNELS), F32),
        pltpu.VMEM((T, WIDTH_X), F32),
        pltpu.VMEM((T, CHANNELS), F32),
        pltpu.VMEM((8 + T, GROUP_X), F32),
        DMA(4, BLOCKS),
    ]
    return call(slopes_kernel, "slopes", out, "hhhhhh", 6, scratch, mib=24)(
        bc, cot, small, tokens, before, weight
    )


def leave_kernel(theirs, core_ref, state_ref, *rest):
    near, rest = rest[: len(NEAR)], rest[len(NEAR) :]
    x_ref, g_ref, y_ref, gx_ref, slope_ref, tok_ref, bc_ref, gbc_ref = near
    (before_ref, small_ref, raw_ref, skips_ref), rest = rest[: len(COMMON)], rest[len(COMMON) :]
    far, rest = rest[: len(NEAR)], rest[len(NEAR) :]
    out_ref, pre_ref, step_ref, sum_ref, win_ref, sems = rest[-6:]
    if theirs:
        far, rest = (), far[4:] + rest
    out_h, pre_h, step_h, sum_h = rest[:4]
    half = 1 - core_ref[0] if theirs else core_ref[0]
    fetches = [] if theirs else fetch_half(1 - core_ref[0], far, rest[4 : 4 + len(NEAR)], sems.at[2])
    last = iota((8, 2 * LANES), 0) == 7
    lower = (iota((T, T), 0) >= iota((T, T), 1)).astype(F32)

    def tap_sums(grad_pre, lo):
        width = grad_pre.shape[1]
        return [
            jnp.sum(grad_pre * win_ref[5 + k : 5 + k + T, lo : lo + width], axis=0, keepdims=True)
            for k in range(TAPS)
        ]

    def by_rows(sums):
        return [s[:, lo : lo + LANES] for lo in range(0, sums[0].shape[1], LANES) for s in sums]

    saves = []

    def save(src, dst):
        copy = pltpu.make_async_copy(src, dst, sems.at[len(saves) // 8, len(saves) % 8])
        copy.start()
        saves.append(copy)

    for jj in range(HALF_GROUPS):
        j = half * HALF_GROUPS + jj
        near_b = slice(jj * STATE, (jj + 1) * STATE)
        near_c = slice((HALF_GROUPS + jj) * STATE, (HALF_GROUPS + jj + 1) * STATE)
        b = bc_ref[:, near_b]
        c = bc_ref[:, near_c]
        grad_b = gbc_ref[:, near_b]
        grad_c = gbc_ref[:, near_c]
        cols = rolled(small_ref[ROW_SCALE : ROW_SCALE + T], j)
        skip_rows = small_ref[pl.ds(pl.multiple_of(ROW_SKIP + j * GROUP_PAIRS, GROUP_PAIRS), GROUP_PAIRS), :]
        tot_rows = small_ref[pl.ds(pl.multiple_of(ROW_TOT + j * GROUP_PAIRS, GROUP_PAIRS), GROUP_PAIRS), :]
        seg_grad = jnp.zeros((GROUP_HEADS, T), F32)
        dt_grad = jnp.zeros((GROUP_HEADS, T), F32)
        skips = [skips_ref[span(j, GROUP_PAIRS), :]]
        terms = []
        near = slice(jj * GROUP_X, (jj + 1) * GROUP_X)
        fill_window(win_ref, before_ref[:, span(j, GROUP_X)], tok_ref[:, near])
        for q in range(0, GROUP_PAIRS, 2):
            lanes = slice(jj * GROUP_X + q * LANES, jj * GROUP_X + (q + 2) * LANES)
            rise = widen_two(cols, 0, q)
            keep = widen_two(cols, HEADS, q)
            at = jj * GROUP_PAIRS + q
            state = jnp.concatenate([state_ref[0, at], state_ref[0, at + 1]], axis=1)
            exits = jnp.concatenate([state_ref[1, at], state_ref[1, at + 1]], axis=1)
            skip = jnp.concatenate([skip_rows[q : q + 1], skip_rows[q + 1 : q + 2]], axis=1)
            tot = jnp.concatenate([tot_rows[q : q + 1], tot_rows[q + 1 : q + 2]], axis=1)
            x = x_ref[:, lanes].astype(F32)
            g = g_ref[:, lanes].astype(F32)
            y = y_ref[:, lanes] + rise * dot(c, state)
            through = keep * dot(b, exits)
            gx = gx_ref[:, lanes] + through
            grad_c = grad_c + dot((g * rise).astype(BF16), state, NT)
            grad_b = grad_b + dot((x * keep).astype(BF16), exits, NT)
            out_ref[:, lanes] = (y + skip * x).astype(BF16)
            grad_pre = (gx + skip * g) * slope_ref[:, lanes]
            pre_ref[:, lanes] = grad_pre
            terms += by_rows(tap_sums(grad_pre, q * LANES))
            x_gx = x * gx
            end = jnp.sum(x * through, axis=0, keepdims=True) + jnp.exp(tot) * jnp.sum(
                exits.astype(F32) * state.astype(F32), axis=0, keepdims=True
            )
            moved = g * y - x_gx
            moved = jnp.concatenate([moved[: T - 8], moved[T - 8 :] + jnp.where(last, end, 0.0)], axis=0)
            pick = (
                iota((GROUP_HEADS, 2 * LANES), 0)
                == 2 * q + iota((GROUP_HEADS, 2 * LANES), 1) // HEAD_DIM
            ).astype(F32).astype(BF16)
            for part in split_two(moved):
                seg_grad = seg_grad + dot(pick, part, NT)
            for part in split_two(x_gx):
                dt_grad = dt_grad + dot(pick, part, NT)
        save(out_ref.at[:, pl.ds(jj * GROUP_X, GROUP_X)], out_h.at[:, span(j, GROUP_X)])
        save(pre_ref.at[:, pl.ds(jj * GROUP_X, GROUP_X)], pre_h.at[:, span(j, GROUP_X)])
        for grad, base in ((grad_b, 0), (grad_c, 1)):
            at = HALF_X + (base * HALF_GROUPS + jj) * STATE
            far = span(WIDTH_X // STATE + base * GROUPS + j, STATE)
            fill_window(win_ref, before_ref[:, far], tok_ref[:, at : at + STATE])
            grad_pre = grad * slope_ref[:, at : at + STATE]
            pre_ref[:, at : at + STATE] = grad_pre
            terms += tap_sums(grad_pre, 0)
            save(pre_ref.at[:, pl.ds(at, STATE)], pre_h.at[:, far])
        heads = span(j, GROUP_HEADS)
        behind = exact_dot(seg_grad, lower)
        dt = small_ref[pl.ds(pl.multiple_of(ROW_DT + j * GROUP_HEADS, GROUP_HEADS), GROUP_HEADS), :]
        decay = small_ref[pl.ds(pl.multiple_of(ROW_DECAY + j * GROUP_HEADS, GROUP_HEADS), GROUP_HEADS), :]
        near = pl.ds(jj * GROUP_HEADS, GROUP_HEADS)
        step_ref[near, :] = (dt_grad / dt + decay * behind) * sigmoid(raw_ref[heads, :])
        save(step_ref.at[near], step_h.at[heads])
        rows = jj * SUM_GROUP
        sum_ref[rows : rows + SUM_GROUP, :] = jnp.concatenate(terms + skips + [dt * behind * decay], axis=0)
        save(sum_ref.at[pl.ds(rows, SUM_GROUP)], sum_h.at[span(j, SUM_GROUP)])
    wait_all(saves + fetches)


def run_leave(core, state, near, common, far, before_out):
    theirs = before_out is not None
    out = [
        ("h", (T, WIDTH_X), BF16),
        ("h", (T, CHANNELS), F32),
        ("h", (HEADS, T), F32),
        ("h", (SUM_ROWS, LANES), F32),
    ]
    scratch = [
        pltpu.VMEM((T, HALF_X), BF16),
        pltpu.VMEM((T, HALF_X + HALF_B), F32),
        pltpu.VMEM((HALF_GROUPS * GROUP_HEADS, T), F32),
        pltpu.VMEM((HALF_GROUPS * SUM_GROUP, LANES), F32),
        pltpu.VMEM((8 + T, GROUP_X), F32),
        DMA(3, FETCHES),
    ]
    args = [core, state, *near, *common, *far]
    specs = "s" + ("v" if theirs else "V") + "V" * (len(NEAR) + len(COMMON)) + "h" * len(far)
    aliases = {}
    if theirs:
        aliases = {len(args) + i: i for i in range(len(out))}
        args += before_out
        specs += "h" * len(out)
    kernel = functools.partial(leave_kernel, theirs)
    outs = call(kernel, "leave", out + ([] if theirs else NEAR), specs, 5, scratch, mib=16, aliases=aliases)(*args)
    return outs[:4], outs[4:]


def spread_kernel(pre_h, halo_ref, weight_h, out_h, pre_ref, weight_ref, out_ref, win_ref, sems):
    first = start_all([(weight_h, weight_ref)], sems.at[0])

    def load(i):
        at = span(i, GROUP_X)
        return pltpu.make_async_copy(pre_h.at[:, at], pre_ref.at[:, at], sems.at[1, i])

    def store(i):
        at = span(i, GROUP_X)
        return pltpu.make_async_copy(out_ref.at[:, at], out_h.at[:, at], sems.at[2, i])

    for i in range(BLOCKS):
        load(i).start()
    wait_all(first)

    @pl.loop(0, BLOCKS)
    def _(i):
        load(i).wait()
        cols = span(i, GROUP_X)
        win_ref[0:T, :] = pre_ref[:, cols]
        win_ref[T : T + TAPS - 1, :] = halo_ref[:, cols].astype(F32)
        weights = weight_ref[:, cols]
        for lo in range(0, GROUP_X, LANES):
            at = slice(lo, lo + LANES)
            acc = weights[0:1, at] * win_ref[3 : 3 + T, at]
            for k in range(1, TAPS):
                acc = acc + weights[k : k + 1, at] * win_ref[3 - k : 3 - k + T, at]
            out_ref[:, pl.ds(pl.multiple_of(i * GROUP_X + lo, LANES), LANES)] = acc.astype(BF16)
        store(i).start()

    for i in range(BLOCKS):
        store(i).wait()


def run_spread(pre, halo, weight):
    out = [("h", (T, CHANNELS), BF16)]
    scratch = [
        pltpu.VMEM((T, CHANNELS), F32),
        pltpu.VMEM((TAPS, CHANNELS), F32),
        pltpu.VMEM((T, CHANNELS), BF16),
        pltpu.VMEM((T + 8, GROUP_X), F32),
        DMA(3, BLOCKS),
    ]
    return call(spread_kernel, "spread", out, "hvh", 4, scratch, mib=16)(pre, halo, weight)[0]


def finish_kernel(sum_ref, conv_ref, decay_ref, skip_ref):
    for i in range(CHANNELS // LANES):
        if i < PAIRS:
            row = SUM_GROUP * (i // GROUP_PAIRS) + TAPS * (i % GROUP_PAIRS)
        else:
            kind, group = divmod(i - PAIRS, GROUPS)
            row = SUM_GROUP * group + TAPS * (GROUP_PAIRS + kind)
        conv_ref[:, i * LANES : (i + 1) * LANES] = sum_ref[row : row + TAPS, :]
    skip_at, decay_at = TAPS * (GROUP_PAIRS + 2), SUM_GROUP - GROUP_HEADS
    skips = jnp.concatenate(
        [sum_ref[SUM_GROUP * j + skip_at : SUM_GROUP * j + decay_at, :] for j in range(GROUPS)], axis=0
    )
    decays = jnp.concatenate(
        [sum_ref[SUM_GROUP * j + decay_at : SUM_GROUP * (j + 1), :] for j in range(GROUPS)], axis=0
    )
    ones = jnp.ones((8, LANES), F32)
    decay_ref[...] = exact_dot(ones, decays, NT)[0:1]
    left = iota((8, LANES), 1) < HEAD_DIM
    even = exact_dot(jnp.where(left, 1.0, 0.0), skips, NT)
    odd = exact_dot(jnp.where(left, 0.0, 1.0), skips, NT)
    at_even = (iota((PAIRS, HEADS), 1) == 2 * iota((PAIRS, HEADS), 0)).astype(F32)
    at_odd = (iota((PAIRS, HEADS), 1) == 2 * iota((PAIRS, HEADS), 0) + 1).astype(F32)
    skip_ref[...] = (exact_dot(even, at_even) + exact_dot(odd, at_odd))[0:1]


def run_finish(sums):
    out = [("v", (TAPS, CHANNELS), F32), ("v", (1, HEADS), F32), ("v", (1, HEADS), F32)]
    return call(finish_kernel, "finish", out, "v", 1, mib=16)(sums)


CTX = ("chip", "core")
ALL = ("dp", "chip", "core")


def all_to_all(value, axis):
    return lax.all_to_all(value, axis, 0, 0, tiled=True)


def tie(*values):
    return lax.optimization_barrier(values)


def fold_kernel(parts, copies, in_ref, out_ref):
    share = in_ref.shape[0] // parts
    total = in_ref[0:share, :]
    for i in range(1, parts):
        total = total + in_ref[i * share : (i + 1) * share, :]
    for i in range(copies):
        out_ref[i * share : (i + 1) * share, :] = total


def run_fold(value, parts, copies):
    out = [("v", (value.shape[0] // parts * copies, LANES), F32)]
    return call(functools.partial(fold_kernel, parts, copies), "fold", out, "v", 1, mib=16)(value)[0]


def local(conv_input, conv_weight, step_raw, decay_log, skip_gain, cotangent):
    chips = lax.axis_size("chip")
    devices = 2 * chips
    across = 2 * lax.axis_size("dp")
    tokens = conv_input[0]
    raw = step_raw[0]
    cot = cotangent[0]
    core = lax.axis_index("core").astype(jnp.int32).reshape(1)
    swap = [(0, 1), (1, 0)]
    halo = lax.ppermute(tokens[T - TAPS + 1 :], CTX, [(i, i + 1) for i in range(devices - 1)])
    small, small_near, tot, x0, bc0, head, weight_near, cot_near = run_begin(
        raw, decay_log.reshape(1, HEADS), skip_gain.reshape(1, HEADS), tokens, conv_weight, cot
    )
    other = lax.ppermute(tot, "core", swap)
    x, bc, before, x_near, bc_near, out = run_enter(
        core, x0, bc0, head, halo, weight_near, cot_near, small_near
    )
    got_near = lax.ppermute(out, "core", swap)
    own_near = run_own(core, x_near, bc_near, cot_near, small_near)
    packed, own, got, tots = run_pack(core, own_near, got_near, tot, other)
    heard = all_to_all(packed, "chip")
    y, gbc, skips = run_inner(x, bc, cot, small)
    heard, y, gbc, skips = tie(heard, y, gbc, skips)
    chained = run_chain(chips, heard)
    late, chained = tie(bc, chained)
    back = all_to_all(chained, "chip")
    gx, slope = run_slopes(late, cot, small, tokens, before, conv_weight)
    back, gx, slope = tie(back, gx, slope)
    far = (x, cot, y, gx, slope, tokens, bc, gbc)
    mine, send, near, common = run_unpack(core, back, own, got, tots, far, (before, small, raw, skips))
    theirs = lax.ppermute(send, "core", swap)
    half, near = run_leave(core, mine, near, common, far, None)
    (out_tokens, pre, grad_step, sums), _ = run_leave(core, theirs, near, common, (), half)
    parts = all_to_all(sums, "chip")
    first = pre[: TAPS - 1].astype(BF16)
    after = lax.ppermute(first, CTX, [(i + 1, i) for i in range(devices - 1)])
    parts = all_to_all(run_fold(parts, chips, across), ("dp", "core"))
    parts, after = tie(parts, after)
    sums = all_to_all(run_fold(parts, across, chips), "chip")
    grad_tokens = run_spread(pre, after, conv_weight)
    grad_conv, grad_decay, grad_skip = run_finish(sums)
    return (
        out_tokens[None],
        grad_tokens[None],
        grad_step[None],
        grad_conv,
        grad_decay.reshape(HEADS),
        grad_skip.reshape(HEADS),
    )


def solution(mesh):
    dp, ctx = mesh.devices.shape
    fine = Mesh(mesh.devices.reshape(dp, ctx // 2, 2), ALL)
    seq = P("dp", CTX, None)
    rate = P("dp", None, CTX)
    in_specs = (seq, P(), rate, P(), P(), seq)
    out_specs = (seq, seq, rate, P(), P(), P())
    return jax.shard_map(local, mesh=fine, in_specs=in_specs, out_specs=out_specs, check_vma=False)
```

```python
import functools

import jax
import jax.numpy as jnp
from jax import lax
from jax.experimental import pallas as pl
from jax.experimental.pallas import tpu as pltpu
from jax.sharding import Mesh
from jax.sharding import PartitionSpec as P

HEADS = 64
HEAD_DIM = 64
GROUPS = 4
STATE = 128
TAPS = 4
T = 128
LANES = 128
WIDTH_X = HEADS * HEAD_DIM
WIDTH_B = GROUPS * STATE
CHANNELS = WIDTH_X + 2 * WIDTH_B
GROUP_X = WIDTH_X // GROUPS
PAIRS = HEADS // 2
GROUP_PAIRS = PAIRS // GROUPS
GROUP_HEADS = HEADS // GROUPS
HALF_PAIRS = PAIRS // 2
HALF_GROUPS = GROUPS // 2
F32 = jnp.float32
BF16 = jnp.bfloat16
EXACT = lax.Precision.HIGHEST
NN = (((1,), (0,)), ((), ()))
NT = (((1,), (1,)), ((), ()))
SUM_ROWS = 256
SUM_GROUP = SUM_ROWS // GROUPS
PACK_ROWS = 2 * STATE + 16


def dot(a, b, dims=NN):
    return lax.dot_general(a, b, dims, preferred_element_type=F32)


def exact_dot(a, b, dims=NN):
    return lax.dot_general(a, b, dims, precision=EXACT, preferred_element_type=F32)


def iota(shape, dim):
    return lax.broadcasted_iota(jnp.int32, shape, dim)


def sigmoid(v):
    return 0.5 + 0.5 * jnp.tanh(0.5 * v)


def split_two(v):
    high = v.astype(BF16)
    return high, (v - high.astype(F32)).astype(BF16)


def span(index, size):
    return pl.ds(pl.multiple_of(index * size, size), size)


def pin(value, space):
    return pltpu.with_memory_space_constraint(value, space)


def placed(space, shape, dtype):
    return space(shape, dtype)


def call(kernel, name, outs, specs, micros, scratch=(), mib=28, aliases=None):
    cost = pl.CostEstimate(
        flops=int(micros * 1e9), transcendentals=0, bytes_accessed=int(micros * 3.6e6)
    )
    blocks = {
        "s": pl.BlockSpec(memory_space=pltpu.SMEM),
        "v": pl.BlockSpec(memory_space=pltpu.VMEM),
        "V": pl.BlockSpec(memory_space=pltpu.VMEM),
        "h": pl.BlockSpec(memory_space=pltpu.HBM),
    }
    spaces = {"V": pltpu.VMEM, "h": pltpu.HBM}
    shapes = [
        placed(spaces[p], shape, dtype) if p in spaces else jax.ShapeDtypeStruct(shape, dtype)
        for p, shape, dtype in outs
    ]
    run = pl.pallas_call(
        kernel,
        out_shape=shapes,
        in_specs=[blocks[p] for p in specs],
        out_specs=[blocks[p] for p, _, _ in outs],
        scratch_shapes=list(scratch),
        input_output_aliases=aliases or {},
        cost_estimate=cost,
        compiler_params=pltpu.CompilerParams(vmem_limit_bytes=mib << 20),
        name=name,
    )

    def go(*args):
        return run(*[pin(a, spaces[p]) if p in spaces else a for a, p in zip(args, specs, strict=True)])

    return go


def start_all(pairs, sems):
    copies = [pltpu.make_async_copy(a, b, sems.at[i]) for i, (a, b) in enumerate(pairs)]
    for copy in copies:
        copy.start()
    return copies


def wait_all(copies):
    for copy in copies:
        copy.wait()


def DMA(*shape):
    return pltpu.SemaphoreType.DMA(shape)


def fill_window(win_ref, before, tokens):
    width = tokens.shape[1]
    win_ref[0:8, :width] = before
    win_ref[8 : 8 + T, :width] = tokens.astype(F32)


def pre_conv(win_ref, weights, lo):
    cols = slice(lo, lo + LANES)
    acc = weights[0:1, cols] * win_ref[5 : 5 + T, cols]
    for k in range(1, TAPS):
        acc = acc + weights[k : k + 1, cols] * win_ref[5 + k : 5 + k + T, cols]
    return acc


BLOCKS = CHANNELS // GROUP_X


ROW_DT, ROW_SEG, ROW_COLS, ROW_SCALE, ROW_TOT, ROW_SKIP, ROW_DECAY, SMALL_ROWS = (
    0, 64, 128, 256, 384, 416, 448, 512
)


def begin_kernel(raw_h, decay_log_h, skip_gain_h, tok_h, weight_h, g_h,
                 small_h, small_ref, tot_ref, x_ref, bc_ref, head_ref, weight_ref, g_ref,
                 raw_ref, decay_log_ref, skip_gain_ref, hold_ref, win_ref, sems):
    first = start_all(
        [(raw_h, raw_ref), (decay_log_h, decay_log_ref), (skip_gain_h, skip_gain_ref), (weight_h, weight_ref)],
        sems.at[0],
    )
    blocks = [pl.ds(i * GROUP_X, GROUP_X) for i in range(BLOCKS)]
    copies = start_all([(tok_h.at[:, at], hold_ref.at[:, at]) for at in blocks], sems.at[1])
    later = start_all([(g_h, g_ref)], sems.at[2])
    win_ref[0:8, :] = jnp.zeros((8, GROUP_X), F32)
    copies[0].wait()
    diagonal = iota((HEADS, HEADS), 0) == iota((HEADS, HEADS), 1)

    def column(row):
        return jnp.sum(jnp.where(diagonal, row, 0.0), axis=1, keepdims=True)

    wait_all(first)
    raw = raw_ref[...]
    dt = jnp.log1p(jnp.exp(raw))
    decay = -jnp.exp(column(decay_log_ref[...]))
    upper = (iota((T, T), 0) <= iota((T, T), 1)).astype(F32)
    seg = exact_dot(dt * decay, upper)
    total = seg[:, T - 1 : T]
    small_ref[ROW_DT : ROW_DT + HEADS] = dt
    small_ref[ROW_SEG : ROW_SEG + HEADS] = seg
    small_ref[ROW_COLS : ROW_COLS + T] = jnp.transpose(jnp.concatenate([seg, dt], axis=0))
    small_ref[ROW_SCALE : ROW_SCALE + T] = jnp.transpose(
        jnp.concatenate([jnp.exp(seg), jnp.exp(total - seg) * dt], axis=0)
    )
    left = iota((PAIRS, LANES), 1) < HEAD_DIM
    even = (iota((PAIRS, HEADS), 1) == 2 * iota((PAIRS, HEADS), 0)).astype(F32)
    odd = (iota((PAIRS, HEADS), 1) == 2 * iota((PAIRS, HEADS), 0) + 1).astype(F32)

    def paired(col):
        wide = jnp.broadcast_to(col, (HEADS, LANES))
        return jnp.where(left, exact_dot(even, wide), exact_dot(odd, wide))

    tot = paired(total)
    tot_ref[...] = tot
    small_ref[ROW_TOT : ROW_TOT + PAIRS] = tot
    small_ref[ROW_SKIP : ROW_SKIP + PAIRS] = paired(column(skip_gain_ref[...]))
    small_ref[ROW_DECAY : ROW_DECAY + HEADS] = jnp.broadcast_to(decay, (HEADS, LANES))
    save = start_all([(small_ref, small_h)], sems.at[0])
    for i in range(BLOCKS):
        if i:
            copies[i].wait()
        cols = slice(i * GROUP_X, (i + 1) * GROUP_X)
        win_ref[8 : 8 + T, :] = hold_ref[:, cols].astype(F32)
        for lo in range(0, GROUP_X, LANES):
            at = i * GROUP_X + lo
            pre = pre_conv(win_ref, weight_ref[:, cols], lo)
            mixed = (pre * sigmoid(pre)).astype(BF16)
            head_ref[:, at : at + LANES] = pre[0:8]
            if at < WIDTH_X:
                x_ref[:, at : at + LANES] = mixed
            else:
                bc_ref[:, at - WIDTH_X : at - WIDTH_X + LANES] = mixed
    wait_all(save + later)


def run_begin(raw, decay_log, skip_gain, tokens, weight, cot):
    out = [
        ("h", (SMALL_ROWS, LANES), F32),
        ("V", (SMALL_ROWS, LANES), F32),
        ("V", (PAIRS, LANES), F32),
        ("V", (T, WIDTH_X), BF16),
        ("V", (T, 2 * WIDTH_B), BF16),
        ("V", (8, CHANNELS), F32),
        ("V", (TAPS, CHANNELS), F32),
        ("V", (T, WIDTH_X), BF16),
    ]
    scratch = [
        pltpu.VMEM((HEADS, T), F32),
        pltpu.VMEM((1, HEADS), F32),
        pltpu.VMEM((1, HEADS), F32),
        pltpu.VMEM((T, CHANNELS), BF16),
        pltpu.VMEM((8 + T, GROUP_X), F32),
        DMA(3, BLOCKS),
    ]
    return call(begin_kernel, "begin", out, "hhhhhh", 4, scratch, mib=16)(
        raw, decay_log, skip_gain, tokens, weight, cot
    )


def rolled(cols, group):
    return pltpu.roll(cols, (LANES - group * GROUP_HEADS) % LANES, 1)


def widen(cols, base, pair):
    first = iota((T, LANES), 1) < HEAD_DIM
    at = base + 2 * pair
    return jnp.where(first, cols[:, at : at + 1], cols[:, at + 1 : at + 2])


def widen_two(cols, base, pair):
    return jnp.concatenate([widen(cols, base, pair), widen(cols, base, pair + 1)], axis=1)


def fill_half(half, x_ref, bc_ref, g_ref, scale, dst_ref):
    for jj in range(HALF_GROUPS):
        j = half * HALF_GROUPS + jj
        b_flip = jnp.transpose(bc_ref[:, span(j, STATE)].astype(F32)).astype(BF16)
        c_flip = jnp.transpose(bc_ref[:, span(GROUPS + j, STATE)].astype(F32)).astype(BF16)
        cols = rolled(scale, j)
        for q in range(0, GROUP_PAIRS, 2):
            lanes = pl.ds(pl.multiple_of(j * GROUP_X + q * LANES, 2 * LANES), 2 * LANES)
            xw = (x_ref[:, lanes].astype(F32) * widen_two(cols, HEADS, q)).astype(BF16)
            gw = (g_ref[:, lanes].astype(F32) * widen_two(cols, 0, q)).astype(BF16)
            state = dot(b_flip, xw).astype(BF16)
            grad = dot(c_flip, gw).astype(BF16)
            for k in range(2):
                at = jj * GROUP_PAIRS + q + k
                dst_ref[0, at] = state[:, k * LANES : (k + 1) * LANES]
                dst_ref[1, at] = grad[:, k * LANES : (k + 1) * LANES]


def enter_kernel(core_ref, x0_ref, bc0_ref, head_ref, halo_ref, weight_ref, g_ref, small_ref,
                 x_h, bc_h, before_h, x_ref, bc_ref, out_ref, before_ref, sems):
    half = 1 - core_ref[0]
    row = iota((8, GROUP_X), 0)
    for i in range(BLOCKS):
        cols = slice(i * GROUP_X, (i + 1) * GROUP_X)
        halo = halo_ref[:, cols].astype(F32)
        weight = weight_ref[:, cols]
        pre = head_ref[:, cols]
        before = jnp.zeros((8, GROUP_X), F32)
        for t in range(TAPS - 1):
            extra = jnp.zeros((1, GROUP_X), F32)
            for k in range(TAPS - 1 - t):
                extra = extra + weight[k : k + 1] * halo[t + k : t + k + 1]
            pre = pre + jnp.where(row == t, extra, 0.0)
            before = before + jnp.where(row == t + 5, halo[t : t + 1], 0.0)
        before_ref[:, cols] = before
        fixed = pre * sigmoid(pre)
        src, dst, at = (x0_ref, x_ref, cols) if i < GROUPS else (bc0_ref, bc_ref, slice(0, GROUP_X))
        rest = src[0:16, at].astype(F32)
        dst[16:T, at] = src[16:T, at]
        dst[0:16, at] = jnp.concatenate([fixed, rest[8:16]], axis=0).astype(BF16)
    saves = start_all([(x_ref, x_h), (bc_ref, bc_h), (before_ref, before_h)], sems)
    fill_half(half, x_ref, bc_ref, g_ref, small_ref[ROW_SCALE : ROW_SCALE + T], out_ref)
    wait_all(saves)


def run_enter(core, x0, bc0, head, halo, weight, cot, small):
    out = [
        ("h", (T, WIDTH_X), BF16),
        ("h", (T, 2 * WIDTH_B), BF16),
        ("h", (8, CHANNELS), F32),
        ("V", (T, WIDTH_X), BF16),
        ("V", (T, 2 * WIDTH_B), BF16),
        ("V", (2, HALF_PAIRS, STATE, LANES), BF16),
    ]
    scratch = [pltpu.VMEM((8, CHANNELS), F32), DMA(3)]
    return call(enter_kernel, "enter", out, "sVVVvVVV", 3, scratch, mib=16)(
        core, x0, bc0, head, halo, weight, cot, small
    )


def own_kernel(core_ref, x_ref, bc_ref, g_ref, small_ref, own_ref):
    fill_half(core_ref[0], x_ref, bc_ref, g_ref, small_ref[ROW_SCALE : ROW_SCALE + T], own_ref)


def run_own(core, x, bc, cot, small):
    out = [("V", (2, HALF_PAIRS, STATE, LANES), BF16)]
    return call(own_kernel, "own", out, "sVVVV", 3, mib=16)(core, x, bc, cot, small)[0]


STEP_PAIRS = 4
STEPS = HALF_PAIRS // STEP_PAIRS


def pack_kernel(core_ref, own_ref, got_ref, tot_ref, other_ref,
                out_h, own_h, got_h, tots_h, out_ref, sems):
    saves = start_all(
        [
            (own_ref, own_h),
            (got_ref, got_h),
            (tot_ref, tots_h.at[pl.ds(0, PAIRS)]),
            (other_ref, tots_h.at[pl.ds(PAIRS, PAIRS)]),
        ],
        sems.at[0],
    )
    second = core_ref[0] == 1
    outs = []
    for i in range(HALF_PAIRS):
        at = core_ref[0] * HALF_PAIRS + i
        tot = tot_ref[pl.ds(at, 1), :]
        other = other_ref[pl.ds(at, 1), :]
        one = jnp.ones_like(tot)
        by_own = jnp.exp(tot)
        by_other = jnp.exp(other)
        state = (
            jnp.where(second, one, by_other) * own_ref[0, i].astype(F32)
            + jnp.where(second, by_own, one) * got_ref[0, i].astype(F32)
        )
        grad = (
            jnp.where(second, by_other, one) * own_ref[1, i].astype(F32)
            + jnp.where(second, one, by_own) * got_ref[1, i].astype(F32)
        )
        out_ref[i, 0:STATE, :] = state.astype(BF16)
        out_ref[i, STATE : 2 * STATE, :] = grad.astype(BF16)
        both = tot + other
        high = both.astype(BF16).astype(F32)
        mid = (both - high).astype(BF16).astype(F32)
        low = both - high - mid
        row = iota((16, LANES), 0)
        wide = jnp.where(row == 0, high, jnp.where(row == 1, mid, jnp.where(row == 2, low, 0.0)))
        out_ref[i, 2 * STATE : PACK_ROWS, :] = wide.astype(BF16)
        if i % STEP_PAIRS == STEP_PAIRS - 1:
            done = pl.ds(i + 1 - STEP_PAIRS, STEP_PAIRS)
            copy = pltpu.make_async_copy(out_ref.at[done], out_h.at[done], sems.at[1, i // STEP_PAIRS])
            copy.start()
            outs.append(copy)
    wait_all(outs + saves)


def run_pack(core, own, got, tot, other):
    half = (2, HALF_PAIRS, STATE, LANES)
    packed = (HALF_PAIRS, PACK_ROWS, LANES)
    out = [("h", packed, BF16), ("h", half, BF16), ("h", half, BF16), ("h", (2 * PAIRS, LANES), F32)]
    scratch = [pltpu.VMEM(packed, BF16), DMA(2, STEPS)]
    return call(pack_kernel, "pack", out, "sVvVv", 2, scratch, mib=16)(core, own, got, tot, other)


def chain_kernel(chips, per, in_ref, out_ref):
    for q in range(per):
        def decay(k):
            rows = in_ref[k * per + q, 2 * STATE : PACK_ROWS, :].astype(F32)
            return jnp.exp(rows[0:1] + rows[1:2] + rows[2:3])

        carry = jnp.zeros((STATE, LANES), F32)
        for k in range(chips):
            out_ref[k * per + q, 0:STATE, :] = carry.astype(BF16)
            if k < chips - 1:
                carry = decay(k) * carry + in_ref[k * per + q, 0:STATE, :].astype(F32)
        carry = jnp.zeros((STATE, LANES), F32)
        for k in reversed(range(chips)):
            out_ref[k * per + q, STATE : 2 * STATE, :] = carry.astype(BF16)
            if k > 0:
                carry = decay(k) * carry + in_ref[k * per + q, STATE : 2 * STATE, :].astype(F32)


def run_chain(chips, packed):
    kernel = functools.partial(chain_kernel, chips, HALF_PAIRS // chips)
    out = [("v", (HALF_PAIRS, 2 * STATE, LANES), BF16)]
    return call(kernel, "chain", out, "v", 1, mib=16)(packed)[0]


HALF_X = HALF_GROUPS * GROUP_X
HALF_B = 2 * HALF_GROUPS * STATE

NEAR = [
    ("V", (T, GROUP_X), BF16),
    ("V", (T, GROUP_X), BF16),
    ("V", (T, GROUP_X), F32),
    ("V", (T, GROUP_X), F32),
    ("V", (T, GROUP_X + 2 * STATE), F32),
    ("V", (T, GROUP_X + 2 * STATE), BF16),
    ("V", (T, 2 * STATE), BF16),
    ("V", (T, 2 * STATE), F32),
]
COMMON = [
    ("V", (8, CHANNELS), F32),
    ("V", (SMALL_ROWS, LANES), F32),
    ("V", (HEADS, T), F32),
    ("V", (PAIRS, LANES), F32),
]
FETCHES = 6 + 8


def fetch_group(j, far, near, sems):
    x_h, g_h, y_h, gx_h, slope_h, tok_h, bc_h, gbc_h = far
    x_v, g_v, y_v, gx_v, slope_v, tok_v, bc_v, gbc_v = near
    wide = pl.ds(0, GROUP_X)
    pairs = [
        (a.at[:, span(j, GROUP_X)], b.at[:, wide])
        for a, b in ((x_h, x_v), (g_h, g_v), (y_h, y_v), (gx_h, gx_v), (slope_h, slope_v), (tok_h, tok_v))
    ]
    for base in range(2):
        at = span(base * GROUPS + j, STATE)
        off = span(WIDTH_X // STATE + base * GROUPS + j, STATE)
        thin = pl.ds(base * STATE, STATE)
        tail = pl.ds(GROUP_X + base * STATE, STATE)
        pairs += [
            (bc_h.at[:, at], bc_v.at[:, thin]),
            (gbc_h.at[:, at], gbc_v.at[:, thin]),
            (slope_h.at[:, off], slope_v.at[:, tail]),
            (tok_h.at[:, off], tok_v.at[:, tail]),
        ]
    return start_all(pairs, sems)


def unpack_kernel(core_ref, back_ref, own_h, got_h, tots_h, *rest):
    far, rest = rest[: len(NEAR)], rest[len(NEAR) :]
    common_far, rest = rest[: len(COMMON)], rest[len(COMMON) :]
    mine_ref, send_ref, *rest = rest
    near, rest = rest[: len(NEAR)], rest[len(NEAR) :]
    common, rest = rest[: len(COMMON)], rest[len(COMMON) :]
    own_ref, got_ref, tots_ref, sems, fetch_sems = rest
    first = start_all([(tots_h, tots_ref)], sems.at[STEPS])
    steps = []
    for step in range(STEPS):
        at = pl.ds(step * STEP_PAIRS, STEP_PAIRS)
        steps.append(
            start_all([(own_h.at[:, at], own_ref.at[:, at]), (got_h.at[:, at], got_ref.at[:, at])], sems.at[step])
        )
    fetches = start_all(list(zip(common_far, common)), fetch_sems.at[1])
    fetches += fetch_group(core_ref[0] * HALF_GROUPS, far, near, fetch_sems.at[0])
    wait_all(first)
    second = core_ref[0] == 1
    for i in range(HALF_PAIRS):
        if i % STEP_PAIRS == 0:
            wait_all(steps[i // STEP_PAIRS])
        at = core_ref[0] * HALF_PAIRS + i
        tot = tots_ref[pl.ds(at, 1), :]
        other = tots_ref[pl.ds(PAIRS + at, 1), :]
        decay_zero = jnp.exp(jnp.where(second, other, tot))
        decay_one = jnp.exp(jnp.where(second, tot, other))
        state_zero = back_ref[i, 0:STATE, :].astype(F32)
        grad_one = back_ref[i, STATE : 2 * STATE, :].astype(F32)
        left = jnp.where(second, got_ref[0, i].astype(F32), own_ref[0, i].astype(F32))
        right = jnp.where(second, own_ref[1, i].astype(F32), got_ref[1, i].astype(F32))
        state_one = decay_zero * state_zero + left
        grad_zero = decay_one * grad_one + right
        mine_ref[0, i] = jnp.where(second, state_one, state_zero).astype(BF16)
        mine_ref[1, i] = jnp.where(second, grad_one, grad_zero).astype(BF16)
        send_ref[0, i] = jnp.where(second, state_zero, state_one).astype(BF16)
        send_ref[1, i] = jnp.where(second, grad_zero, grad_one).astype(BF16)
    wait_all(fetches)


def run_unpack(core, back, own, got, tots, far, common):
    half = (2, HALF_PAIRS, STATE, LANES)
    out = [("V", half, BF16)] * 2 + NEAR + COMMON
    scratch = [
        pltpu.VMEM(half, BF16),
        pltpu.VMEM(half, BF16),
        pltpu.VMEM((2 * PAIRS, LANES), F32),
        DMA(STEPS + 1, 2),
        DMA(2, FETCHES),
    ]
    specs = "svhhh" + "h" * (len(NEAR) + len(COMMON))
    outs = call(unpack_kernel, "unpack", out, specs, 3, scratch, mib=16)(
        core, back, own, got, tots, *far, *common
    )
    return outs[0], outs[1], outs[2 : 2 + len(NEAR)], outs[2 + len(NEAR) :]


def by_lane_half(v):
    first = iota(v.shape, 1) < HEAD_DIM
    wide = v.astype(F32)
    return jnp.concatenate(
        [jnp.where(first, wide, 0.0).astype(BF16), jnp.where(first, 0.0, wide).astype(BF16)], axis=0
    )


def inner_kernel(x_h, bc_h, g_h, small_h, y_h, gbc_h, skips_h,
                 x_ref, bc_ref, g_ref, small_ref, y_ref, gbc_ref, skips_ref, sems):
    first = start_all([(bc_h, bc_ref), (small_h, small_ref)], sems.at[0])

    def loads(j):
        at = span(j, GROUP_X)
        return [
            pltpu.make_async_copy(x_h.at[:, at], x_ref.at[:, at], sems.at[1, j]),
            pltpu.make_async_copy(g_h.at[:, at], g_ref.at[:, at], sems.at[2, j]),
        ]

    def store(j):
        at = span(j, GROUP_X)
        return pltpu.make_async_copy(y_ref.at[:, at], y_h.at[:, at], sems.at[3, j])

    for j in range(GROUPS):
        for copy in loads(j):
            copy.start()
    wait_all(first)
    lower = iota((T, T), 0) >= iota((T, T), 1)

    @pl.loop(0, GROUPS)
    def _(j):
        wait_all(loads(j))
        b = bc_ref[:, span(j, STATE)]
        c = bc_ref[:, span(GROUPS + j, STATE)]
        seg = small_ref[pl.ds(pl.multiple_of(ROW_SEG + j * GROUP_HEADS, GROUP_HEADS), GROUP_HEADS), :]
        dt = small_ref[pl.ds(pl.multiple_of(ROW_DT + j * GROUP_HEADS, GROUP_HEADS), GROUP_HEADS), :]
        scores = dot(c, b, NT)
        cols = rolled(small_ref[ROW_COLS : ROW_COLS + T], j)
        total = jnp.zeros((T, T), F32)
        skips = []
        for i in range(GROUP_PAIRS):
            lanes = pl.ds(pl.multiple_of(j * GROUP_X + i * LANES, LANES), LANES)
            x = x_ref[:, lanes]
            g = g_ref[:, lanes]
            skips.append(jnp.sum(g.astype(F32) * x.astype(F32), axis=0, keepdims=True))
            inner = dot(by_lane_half(g), x, NT)
            weights = []
            for k in range(2):
                h = 2 * i + k
                spread = cols[:, h : h + 1] - seg[h : h + 1, :]
                kernel = jnp.exp(jnp.where(lower, spread, -1e30)) * dt[h : h + 1, :]
                total = total + kernel * inner[k * T : (k + 1) * T]
                weights.append((kernel * scores).astype(BF16))
            y_ref[:, lanes] = dot(jnp.concatenate(weights, axis=1), by_lane_half(x))
        skips_ref[span(j, GROUP_PAIRS), :] = jnp.concatenate(skips, axis=0)
        gbc_ref[:, span(GROUPS + j, STATE)] = dot(total.astype(BF16), b)
        gbc_ref[:, span(j, STATE)] = dot(jnp.transpose(total).astype(BF16), c)
        store(j).start()

    last = start_all([(gbc_ref, gbc_h), (skips_ref, skips_h)], sems.at[0])
    for j in range(GROUPS):
        store(j).wait()
    wait_all(last)


def run_inner(x, bc, cot, small):
    out = [("h", (T, WIDTH_X), F32), ("h", (T, 2 * WIDTH_B), F32), ("h", (PAIRS, LANES), F32)]
    scratch = [
        pltpu.VMEM((T, WIDTH_X), BF16),
        pltpu.VMEM((T, 2 * WIDTH_B), BF16),
        pltpu.VMEM((T, WIDTH_X), BF16),
        pltpu.VMEM((SMALL_ROWS, LANES), F32),
        pltpu.VMEM((T, WIDTH_X), F32),
        pltpu.VMEM((T, 2 * WIDTH_B), F32),
        pltpu.VMEM((PAIRS, LANES), F32),
        DMA(4, GROUPS),
    ]
    return call(inner_kernel, "inner", out, "hhhh", 4, scratch, mib=24)(x, bc, cot, small)


def slopes_kernel(bc_h, g_h, small_h, tok_h, before_h, weight_h, gx_h, slope_h,
                  bc_ref, g_ref, small_ref, tok_ref, before_ref, weight_ref, gx_ref, slope_ref, win_ref, sems):
    first = start_all(
        [(bc_h, bc_ref), (small_h, small_ref), (before_h, before_ref), (weight_h, weight_ref), (tok_h, tok_ref)],
        sems.at[0],
    )

    def load(j):
        at = span(j, GROUP_X)
        return pltpu.make_async_copy(g_h.at[:, at], g_ref.at[:, at], sems.at[1, j])

    def store(j):
        at = span(j, GROUP_X)
        return pltpu.make_async_copy(gx_ref.at[:, at], gx_h.at[:, at], sems.at[2, j])

    def store_slope(i):
        at = span(i, GROUP_X)
        return pltpu.make_async_copy(slope_ref.at[:, at], slope_h.at[:, at], sems.at[3, i])

    for j in range(GROUPS):
        load(j).start()
    wait_all(first)
    upper = iota((T, T), 0) <= iota((T, T), 1)

    @pl.loop(0, GROUPS)
    def _(j):
        load(j).wait()
        b = bc_ref[:, span(j, STATE)]
        c = bc_ref[:, span(GROUPS + j, STATE)]
        seg = small_ref[pl.ds(pl.multiple_of(ROW_SEG + j * GROUP_HEADS, GROUP_HEADS), GROUP_HEADS), :]
        scores = jnp.transpose(dot(c, b, NT))
        cols = rolled(small_ref[ROW_COLS : ROW_COLS + T], j)
        for i in range(GROUP_PAIRS):
            lanes = pl.ds(pl.multiple_of(j * GROUP_X + i * LANES, LANES), LANES)
            weights = []
            for k in range(2):
                h = 2 * i + k
                spread = seg[h : h + 1, :] - cols[:, h : h + 1]
                kernel = jnp.exp(jnp.where(upper, spread, -1e30)) * cols[:, HEADS + h : HEADS + h + 1]
                weights.append((kernel * scores).astype(BF16))
            gx_ref[:, lanes] = dot(jnp.concatenate(weights, axis=1), by_lane_half(g_ref[:, lanes]))
        store(j).start()

    @pl.loop(0, BLOCKS)
    def _(i):
        cols = span(i, GROUP_X)
        fill_window(win_ref, before_ref[:, cols], tok_ref[:, cols])
        weights = weight_ref[:, cols]
        for lo in range(0, GROUP_X, LANES):
            pre = pre_conv(win_ref, weights, lo)
            s = sigmoid(pre)
            at = pl.ds(pl.multiple_of(i * GROUP_X + lo, LANES), LANES)
            slope_ref[:, at] = s * (1.0 + pre * (1.0 - s))
        store_slope(i).start()

    for j in range(GROUPS):
        store(j).wait()
    for i in range(BLOCKS):
        store_slope(i).wait()


def run_slopes(bc, cot, small, tokens, before, weight):
    out = [("h", (T, WIDTH_X), F32), ("h", (T, CHANNELS), F32)]
    scratch = [
        pltpu.VMEM((T, 2 * WIDTH_B), BF16),
        pltpu.VMEM((T, WIDTH_X), BF16),
        pltpu.VMEM((SMALL_ROWS, LANES), F32),
        pltpu.VMEM((T, CHANNELS), BF16),
        pltpu.VMEM((8, CHANNELS), F32),
        pltpu.VMEM((TAPS, CHANNELS), F32),
        pltpu.VMEM((T, WIDTH_X), F32),
        pltpu.VMEM((T, CHANNELS), F32),
        pltpu.VMEM((8 + T, GROUP_X), F32),
        DMA(4, BLOCKS),
    ]
    return call(slopes_kernel, "slopes", out, "hhhhhh", 6, scratch, mib=24)(
        bc, cot, small, tokens, before, weight
    )


def leave_kernel(theirs, core_ref, state_ref, *rest):
    rest = list(rest)

    def take(count):
        taken = rest[:count]
        del rest[:count]
        return taken

    sets = [take(len(NEAR))]
    if theirs:
        sets.append(take(len(NEAR)))
    before_ref, small_ref, raw_ref, skips_ref = take(len(COMMON))
    far = take(4 if theirs else len(NEAR))
    out_h, pre_h, step_h, sum_h = take(4)
    half = 1 - core_ref[0] if theirs else core_ref[0]
    arrivals, fetches = [], []
    if theirs:
        first_ref, = take(1)
        head_ref, = take(1)
    else:
        after = [take(len(NEAR)) for _ in range(HALF_GROUPS)]
        sets.append(take(len(NEAR)))
    out_ref, pre_ref, step_ref, sum_ref, win_ref, sems = rest
    if theirs:
        own = core_ref[0]
        pieces = [span(own, HALF_X)] + [
            span(WIDTH_X // (HALF_GROUPS * STATE) + 2 * base + own, HALF_GROUPS * STATE) for base in range(2)
        ]
        fetches = start_all([(pre_h.at[pl.ds(0, 8), at], head_ref.at[:, at]) for at in pieces], sems.at[2])
    else:
        arrivals = fetch_group(half * HALF_GROUPS + 1, far, sets[1], sems.at[2])
        for jj in range(HALF_GROUPS):
            fetches += fetch_group((1 - half) * HALF_GROUPS + jj, far, after[jj], sems.at[3 + jj])
    last = iota((8, 2 * LANES), 0) == 7
    lower = (iota((T, T), 0) >= iota((T, T), 1)).astype(F32)

    def tap_sums(grad_pre, lo):
        width = grad_pre.shape[1]
        return [
            jnp.sum(grad_pre * win_ref[5 + k : 5 + k + T, lo : lo + width], axis=0, keepdims=True)
            for k in range(TAPS)
        ]

    def by_rows(sums):
        return [s[:, lo : lo + LANES] for lo in range(0, sums[0].shape[1], LANES) for s in sums]

    saves = []

    def save(src, dst):
        copy = pltpu.make_async_copy(src, dst, sems.at[len(saves) // 8, len(saves) % 8])
        copy.start()
        saves.append(copy)

    for jj in range(HALF_GROUPS):
        j = half * HALF_GROUPS + jj
        x_ref, g_ref, y_ref, gx_ref, slope_ref, tok_ref, bc_ref, gbc_ref = sets[jj]
        if jj:
            wait_all(arrivals)
        b = bc_ref[:, 0:STATE]
        c = bc_ref[:, STATE:]
        grad_b = gbc_ref[:, 0:STATE]
        grad_c = gbc_ref[:, STATE:]
        cols = rolled(small_ref[ROW_SCALE : ROW_SCALE + T], j)
        skip_rows = small_ref[pl.ds(pl.multiple_of(ROW_SKIP + j * GROUP_PAIRS, GROUP_PAIRS), GROUP_PAIRS), :]
        tot_rows = small_ref[pl.ds(pl.multiple_of(ROW_TOT + j * GROUP_PAIRS, GROUP_PAIRS), GROUP_PAIRS), :]
        seg_grad = jnp.zeros((GROUP_HEADS, T), F32)
        dt_grad = jnp.zeros((GROUP_HEADS, T), F32)
        skips = [skips_ref[span(j, GROUP_PAIRS), :]]
        terms = []
        fill_window(win_ref, before_ref[:, span(j, GROUP_X)], tok_ref[:, 0:GROUP_X])
        for q in range(0, GROUP_PAIRS, 2):
            lanes = slice(q * LANES, (q + 2) * LANES)
            wide = slice(jj * GROUP_X + q * LANES, jj * GROUP_X + (q + 2) * LANES)
            rise = widen_two(cols, 0, q)
            keep = widen_two(cols, HEADS, q)
            at = jj * GROUP_PAIRS + q
            state = jnp.concatenate([state_ref[0, at], state_ref[0, at + 1]], axis=1)
            exits = jnp.concatenate([state_ref[1, at], state_ref[1, at + 1]], axis=1)
            skip = jnp.concatenate([skip_rows[q : q + 1], skip_rows[q + 1 : q + 2]], axis=1)
            tot = jnp.concatenate([tot_rows[q : q + 1], tot_rows[q + 1 : q + 2]], axis=1)
            x = x_ref[:, lanes].astype(F32)
            g = g_ref[:, lanes].astype(F32)
            y = y_ref[:, lanes] + rise * dot(c, state)
            through = keep * dot(b, exits)
            gx = gx_ref[:, lanes] + through
            grad_c = grad_c + dot((g * rise).astype(BF16), state, NT)
            grad_b = grad_b + dot((x * keep).astype(BF16), exits, NT)
            out_ref[:, wide] = (y + skip * x).astype(BF16)
            grad_pre = (gx + skip * g) * slope_ref[:, lanes]
            pre_ref[:, wide] = grad_pre
            if theirs:
                at = pl.ds(pl.multiple_of(j * GROUP_X + q * LANES, 2 * LANES), 2 * LANES)
                head_ref[:, at] = grad_pre[0:8]
            terms += by_rows(tap_sums(grad_pre, q * LANES))
            x_gx = x * gx
            end = jnp.sum(x * through, axis=0, keepdims=True) + jnp.exp(tot) * jnp.sum(
                exits.astype(F32) * state.astype(F32), axis=0, keepdims=True
            )
            moved = g * y - x_gx
            moved = jnp.concatenate([moved[: T - 8], moved[T - 8 :] + jnp.where(last, end, 0.0)], axis=0)
            pick = (
                iota((GROUP_HEADS, 2 * LANES), 0)
                == 2 * q + iota((GROUP_HEADS, 2 * LANES), 1) // HEAD_DIM
            ).astype(F32).astype(BF16)
            for part in split_two(moved):
                seg_grad = seg_grad + dot(pick, part, NT)
            for part in split_two(x_gx):
                dt_grad = dt_grad + dot(pick, part, NT)
            if q % 4 == 2:
                size = GROUP_X // 2
                near_at = pl.ds(jj * GROUP_X + (q // 4) * size, size)
                far_at = span(2 * j + q // 4, size)
                save(out_ref.at[:, near_at], out_h.at[:, far_at])
                save(pre_ref.at[:, near_at], pre_h.at[:, far_at])
        for grad, base in ((grad_b, 0), (grad_c, 1)):
            at = HALF_X + (base * HALF_GROUPS + jj) * STATE
            tail = slice(GROUP_X + base * STATE, GROUP_X + (base + 1) * STATE)
            far_at = span(WIDTH_X // STATE + base * GROUPS + j, STATE)
            fill_window(win_ref, before_ref[:, far_at], tok_ref[:, tail])
            grad_pre = grad * slope_ref[:, tail]
            pre_ref[:, at : at + STATE] = grad_pre
            if theirs:
                head_ref[:, far_at] = grad_pre[0:8]
            terms += tap_sums(grad_pre, 0)
            save(pre_ref.at[:, pl.ds(at, STATE)], pre_h.at[:, far_at])
        heads = span(j, GROUP_HEADS)
        behind = exact_dot(seg_grad, lower)
        dt = small_ref[pl.ds(pl.multiple_of(ROW_DT + j * GROUP_HEADS, GROUP_HEADS), GROUP_HEADS), :]
        decay = small_ref[pl.ds(pl.multiple_of(ROW_DECAY + j * GROUP_HEADS, GROUP_HEADS), GROUP_HEADS), :]
        near = pl.ds(jj * GROUP_HEADS, GROUP_HEADS)
        step_ref[near, :] = (dt_grad / dt + decay * behind) * sigmoid(raw_ref[heads, :])
        save(step_ref.at[near], step_h.at[heads])
        rows = jj * SUM_GROUP
        sum_ref[rows : rows + SUM_GROUP, :] = jnp.concatenate(terms + skips + [dt * behind * decay], axis=0)
        save(sum_ref.at[pl.ds(rows, SUM_GROUP)], sum_h.at[span(j, SUM_GROUP)])
    wait_all(fetches)
    if theirs:
        first_ref[...] = head_ref[0 : TAPS - 1, :].astype(BF16)
    wait_all(saves)


def run_leave(core, state, near, common, far, before_out):
    theirs = before_out is not None
    out = [
        ("h", (T, WIDTH_X), BF16),
        ("h", (T, CHANNELS), F32),
        ("h", (HEADS, T), F32),
        ("h", (SUM_ROWS, LANES), F32),
    ]
    scratch = [
        pltpu.VMEM((T, HALF_X), BF16),
        pltpu.VMEM((T, HALF_X + HALF_B), F32),
        pltpu.VMEM((HALF_GROUPS * GROUP_HEADS, T), F32),
        pltpu.VMEM((HALF_GROUPS * SUM_GROUP, LANES), F32),
        pltpu.VMEM((8 + T, GROUP_X), F32),
        DMA(3 + HALF_GROUPS, FETCHES + 2),
    ]
    args = [core, state, *near, *common, *far]
    specs = "s" + ("v" if theirs else "V") + "V" * (len(near) + len(COMMON)) + "h" * len(far)
    aliases = {}
    if theirs:
        aliases = {len(args) + i: i for i in range(len(out))}
        args += before_out
        specs += "h" * len(out)
        more = [("V", (TAPS - 1, CHANNELS), BF16)]
        scratch = [pltpu.VMEM((8, CHANNELS), F32)] + scratch
    else:
        more = NEAR * HALF_GROUPS
        scratch = [pltpu.VMEM(shape, dtype) for _, shape, dtype in NEAR] + scratch
    kernel = functools.partial(leave_kernel, theirs)
    outs = call(kernel, "leave", out + more, specs, 5, scratch, mib=16, aliases=aliases)(*args)
    return outs[:4], outs[4:]


def spread_kernel(pre_h, halo_ref, weight_h, out_h, pre_ref, weight_ref, out_ref, win_ref, sems):
    first = start_all([(weight_h, weight_ref)], sems.at[0])

    def load(i):
        at = span(i, GROUP_X)
        return pltpu.make_async_copy(pre_h.at[:, at], pre_ref.at[:, at], sems.at[1, i])

    def store(i):
        at = span(i, GROUP_X)
        return pltpu.make_async_copy(out_ref.at[:, at], out_h.at[:, at], sems.at[2, i])

    for i in range(BLOCKS):
        load(i).start()
    wait_all(first)

    @pl.loop(0, BLOCKS)
    def _(i):
        load(i).wait()
        cols = span(i, GROUP_X)
        win_ref[0:T, :] = pre_ref[:, cols]
        win_ref[T : T + TAPS - 1, :] = halo_ref[:, cols].astype(F32)
        weights = weight_ref[:, cols]
        for lo in range(0, GROUP_X, LANES):
            at = slice(lo, lo + LANES)
            acc = weights[0:1, at] * win_ref[3 : 3 + T, at]
            for k in range(1, TAPS):
                acc = acc + weights[k : k + 1, at] * win_ref[3 - k : 3 - k + T, at]
            out_ref[:, pl.ds(pl.multiple_of(i * GROUP_X + lo, LANES), LANES)] = acc.astype(BF16)
        store(i).start()

    for i in range(BLOCKS):
        store(i).wait()


def run_spread(pre, halo, weight):
    out = [("h", (T, CHANNELS), BF16)]
    scratch = [
        pltpu.VMEM((T, CHANNELS), F32),
        pltpu.VMEM((TAPS, CHANNELS), F32),
        pltpu.VMEM((T, CHANNELS), BF16),
        pltpu.VMEM((T + 8, GROUP_X), F32),
        DMA(3, BLOCKS),
    ]
    return call(spread_kernel, "spread", out, "hvh", 4, scratch, mib=16)(pre, halo, weight)[0]


def finish_kernel(sum_ref, conv_ref, decay_ref, skip_ref):
    for i in range(CHANNELS // LANES):
        if i < PAIRS:
            row = SUM_GROUP * (i // GROUP_PAIRS) + TAPS * (i % GROUP_PAIRS)
        else:
            kind, group = divmod(i - PAIRS, GROUPS)
            row = SUM_GROUP * group + TAPS * (GROUP_PAIRS + kind)
        conv_ref[:, i * LANES : (i + 1) * LANES] = sum_ref[row : row + TAPS, :]
    skip_at, decay_at = TAPS * (GROUP_PAIRS + 2), SUM_GROUP - GROUP_HEADS
    skips = jnp.concatenate(
        [sum_ref[SUM_GROUP * j + skip_at : SUM_GROUP * j + decay_at, :] for j in range(GROUPS)], axis=0
    )
    decays = jnp.concatenate(
        [sum_ref[SUM_GROUP * j + decay_at : SUM_GROUP * (j + 1), :] for j in range(GROUPS)], axis=0
    )
    ones = jnp.ones((8, LANES), F32)
    decay_ref[...] = exact_dot(ones, decays, NT)[0:1]
    left = iota((8, LANES), 1) < HEAD_DIM
    even = exact_dot(jnp.where(left, 1.0, 0.0), skips, NT)
    odd = exact_dot(jnp.where(left, 0.0, 1.0), skips, NT)
    at_even = (iota((PAIRS, HEADS), 1) == 2 * iota((PAIRS, HEADS), 0)).astype(F32)
    at_odd = (iota((PAIRS, HEADS), 1) == 2 * iota((PAIRS, HEADS), 0) + 1).astype(F32)
    skip_ref[...] = (exact_dot(even, at_even) + exact_dot(odd, at_odd))[0:1]


def run_finish(sums):
    out = [("v", (TAPS, CHANNELS), F32), ("v", (1, HEADS), F32), ("v", (1, HEADS), F32)]
    return call(finish_kernel, "finish", out, "v", 1, mib=16)(sums)


CTX = ("chip", "core")
ALL = ("dp", "chip", "core")


def all_to_all(value, axis):
    return lax.all_to_all(value, axis, 0, 0, tiled=True)


def tie(*values):
    return lax.optimization_barrier(values)


def fold_kernel(parts, copies, in_ref, out_ref):
    share = in_ref.shape[0] // parts
    total = in_ref[0:share, :]
    for i in range(1, parts):
        total = total + in_ref[i * share : (i + 1) * share, :]
    for i in range(copies):
        out_ref[i * share : (i + 1) * share, :] = total


def run_fold(value, parts, copies):
    out = [("v", (value.shape[0] // parts * copies, LANES), F32)]
    return call(functools.partial(fold_kernel, parts, copies), "fold", out, "v", 1, mib=16)(value)[0]


def local(conv_input, conv_weight, step_raw, decay_log, skip_gain, cotangent):
    chips = lax.axis_size("chip")
    devices = 2 * chips
    across = 2 * lax.axis_size("dp")
    tokens = conv_input[0]
    raw = step_raw[0]
    cot = cotangent[0]
    core = lax.axis_index("core").astype(jnp.int32).reshape(1)
    swap = [(0, 1), (1, 0)]
    halo = lax.ppermute(tokens[T - TAPS + 1 :], CTX, [(i, i + 1) for i in range(devices - 1)])
    small, small_near, tot, x0, bc0, head, weight_near, cot_near = run_begin(
        raw, decay_log.reshape(1, HEADS), skip_gain.reshape(1, HEADS), tokens, conv_weight, cot
    )
    other = lax.ppermute(tot, "core", swap)
    x, bc, before, x_near, bc_near, out = run_enter(
        core, x0, bc0, head, halo, weight_near, cot_near, small_near
    )
    got_near = lax.ppermute(out, "core", swap)
    own_near = run_own(core, x_near, bc_near, cot_near, small_near)
    packed, own, got, tots = run_pack(core, own_near, got_near, tot, other)
    heard = all_to_all(packed, "chip")
    y, gbc, skips = run_inner(x, bc, cot, small)
    heard, y, gbc, skips = tie(heard, y, gbc, skips)
    chained = run_chain(chips, heard)
    late, chained = tie(bc, chained)
    back = all_to_all(chained, "chip")
    gx, slope = run_slopes(late, cot, small, tokens, before, conv_weight)
    back, gx, slope = tie(back, gx, slope)
    far = (x, cot, y, gx, slope, tokens, bc, gbc)
    mine, send, near, common = run_unpack(core, back, own, got, tots, far, (before, small, raw, skips))
    theirs = lax.ppermute(send, "core", swap)
    half, near = run_leave(core, mine, near, common, far, None)
    (out_tokens, pre, grad_step, sums), (first,) = run_leave(core, theirs, near, common, (), half)
    parts = all_to_all(sums, "chip")
    after = lax.ppermute(first, CTX, [(i + 1, i) for i in range(devices - 1)])
    parts, after = tie(parts, after)
    parts = all_to_all(run_fold(parts, chips, across), ("dp", "core"))
    grad_tokens = run_spread(pre, after, conv_weight)
    parts, grad_tokens = tie(parts, grad_tokens)
    sums = all_to_all(run_fold(parts, across, chips), "chip")
    grad_conv, grad_decay, grad_skip = run_finish(sums)
    return (
        out_tokens[None],
        grad_tokens[None],
        grad_step[None],
        grad_conv,
        grad_decay.reshape(HEADS),
        grad_skip.reshape(HEADS),
    )


def solution(mesh):
    dp, ctx = mesh.devices.shape
    fine = Mesh(mesh.devices.reshape(dp, ctx // 2, 2), ALL)
    seq = P("dp", CTX, None)
    rate = P("dp", None, CTX)
    in_specs = (seq, P(), rate, P(), P(), seq)
    out_specs = (seq, seq, rate, P(), P(), P())
    return jax.shard_map(local, mesh=fine, in_specs=in_specs, out_specs=out_specs, check_vma=False)
```

```python
import functools

import jax
import jax.numpy as jnp
from jax import lax
from jax.experimental import pallas as pl
from jax.experimental.pallas import tpu as pltpu
from jax.sharding import Mesh
from jax.sharding import PartitionSpec as P

HEADS = 64
HEAD_DIM = 64
GROUPS = 4
STATE = 128
TAPS = 4
T = 128
LANES = 128
WIDTH_X = HEADS * HEAD_DIM
WIDTH_B = GROUPS * STATE
CHANNELS = WIDTH_X + 2 * WIDTH_B
GROUP_X = WIDTH_X // GROUPS
PAIRS = HEADS // 2
GROUP_PAIRS = PAIRS // GROUPS
GROUP_HEADS = HEADS // GROUPS
HALF_PAIRS = PAIRS // 2
HALF_GROUPS = GROUPS // 2
F32 = jnp.float32
BF16 = jnp.bfloat16
EXACT = lax.Precision.HIGHEST
NN = (((1,), (0,)), ((), ()))
NT = (((1,), (1,)), ((), ()))
SUM_GROUP = 64
PACK_ROWS = 2 * STATE + 16


def dot(a, b, dims=NN):
    return lax.dot_general(a, b, dims, preferred_element_type=F32)


def exact_dot(a, b, dims=NN):
    return lax.dot_general(a, b, dims, precision=EXACT, preferred_element_type=F32)


def iota(shape, dim):
    return lax.broadcasted_iota(jnp.int32, shape, dim)


def sigmoid(v):
    return 0.5 + 0.5 * jnp.tanh(0.5 * v)


def split_two(v):
    high = v.astype(BF16)
    return high, (v - high.astype(F32)).astype(BF16)


def span(index, size):
    return pl.ds(pl.multiple_of(index * size, size), size)


def pin(value, space):
    return pltpu.with_memory_space_constraint(value, space)


def placed(space, shape, dtype):
    return space(shape, dtype)


def call(kernel, name, outs, specs, micros, scratch=(), mib=28, aliases=None):
    cost = pl.CostEstimate(
        flops=int(micros * 1e9), transcendentals=0, bytes_accessed=int(micros * 3.6e6)
    )
    blocks = {
        "s": pl.BlockSpec(memory_space=pltpu.SMEM),
        "v": pl.BlockSpec(memory_space=pltpu.VMEM),
        "V": pl.BlockSpec(memory_space=pltpu.VMEM),
        "h": pl.BlockSpec(memory_space=pltpu.HBM),
    }
    spaces = {"V": pltpu.VMEM, "h": pltpu.HBM}
    shapes = [
        placed(spaces[p], shape, dtype) if p in spaces else jax.ShapeDtypeStruct(shape, dtype)
        for p, shape, dtype in outs
    ]
    run = pl.pallas_call(
        kernel,
        out_shape=shapes,
        in_specs=[blocks[p] for p in specs],
        out_specs=[blocks[p] for p, _, _ in outs],
        scratch_shapes=list(scratch),
        input_output_aliases=aliases or {},
        cost_estimate=cost,
        compiler_params=pltpu.CompilerParams(vmem_limit_bytes=mib << 20),
        name=name,
    )

    def go(*args):
        return run(*[pin(a, spaces[p]) if p in spaces else a for a, p in zip(args, specs, strict=True)])

    return go


def start_all(pairs, sems):
    copies = [pltpu.make_async_copy(a, b, sems.at[i]) for i, (a, b) in enumerate(pairs)]
    for copy in copies:
        copy.start()
    return copies


def wait_all(copies):
    for copy in copies:
        copy.wait()


def DMA(*shape):
    return pltpu.SemaphoreType.DMA(shape)


def fill_window(win_ref, before, tokens):
    width = tokens.shape[1]
    win_ref[0:8, :width] = before
    win_ref[8 : 8 + T, :width] = tokens.astype(F32)


def pre_conv(win_ref, weights, lo):
    cols = slice(lo, lo + LANES)
    acc = weights[0:1, cols] * win_ref[5 : 5 + T, cols]
    for k in range(1, TAPS):
        acc = acc + weights[k : k + 1, cols] * win_ref[5 + k : 5 + k + T, cols]
    return acc


BLOCKS = CHANNELS // GROUP_X


ROW_DT, ROW_SEG, ROW_COLS, ROW_SCALE, ROW_TOT, ROW_SKIP, ROW_DECAY, SMALL_ROWS = (
    0, 64, 128, 256, 384, 416, 448, 512
)


def begin_kernel(raw_h, decay_log_h, skip_gain_h, tok_h, weight_h, g_h,
                 small_h, small_ref, tot_ref, x_ref, bc_ref, head_ref, weight_ref, g_ref,
                 raw_ref, decay_log_ref, skip_gain_ref, hold_ref, win_ref, sems):
    first = start_all(
        [(raw_h, raw_ref), (decay_log_h, decay_log_ref), (skip_gain_h, skip_gain_ref), (weight_h, weight_ref)],
        sems.at[0],
    )
    blocks = [pl.ds(i * GROUP_X, GROUP_X) for i in range(BLOCKS)]
    copies = start_all([(tok_h.at[:, at], hold_ref.at[:, at]) for at in blocks], sems.at[1])
    later = start_all([(g_h, g_ref)], sems.at[2])
    win_ref[0:8, :] = jnp.zeros((8, GROUP_X), F32)
    copies[0].wait()
    diagonal = iota((HEADS, HEADS), 0) == iota((HEADS, HEADS), 1)

    def column(row):
        return jnp.sum(jnp.where(diagonal, row, 0.0), axis=1, keepdims=True)

    wait_all(first)
    raw = raw_ref[...]
    dt = jnp.log1p(jnp.exp(raw))
    decay = -jnp.exp(column(decay_log_ref[...]))
    upper = (iota((T, T), 0) <= iota((T, T), 1)).astype(F32)
    seg = exact_dot(dt * decay, upper)
    total = seg[:, T - 1 : T]
    small_ref[ROW_DT : ROW_DT + HEADS] = dt
    small_ref[ROW_SEG : ROW_SEG + HEADS] = seg
    small_ref[ROW_COLS : ROW_COLS + T] = jnp.transpose(jnp.concatenate([seg, dt], axis=0))
    small_ref[ROW_SCALE : ROW_SCALE + T] = jnp.transpose(
        jnp.concatenate([jnp.exp(seg), jnp.exp(total - seg) * dt], axis=0)
    )
    left = iota((PAIRS, LANES), 1) < HEAD_DIM
    even = (iota((PAIRS, HEADS), 1) == 2 * iota((PAIRS, HEADS), 0)).astype(F32)
    odd = (iota((PAIRS, HEADS), 1) == 2 * iota((PAIRS, HEADS), 0) + 1).astype(F32)

    def paired(col):
        wide = jnp.broadcast_to(col, (HEADS, LANES))
        return jnp.where(left, exact_dot(even, wide), exact_dot(odd, wide))

    tot = paired(total)
    tot_ref[...] = tot
    small_ref[ROW_TOT : ROW_TOT + PAIRS] = tot
    small_ref[ROW_SKIP : ROW_SKIP + PAIRS] = paired(column(skip_gain_ref[...]))
    small_ref[ROW_DECAY : ROW_DECAY + HEADS] = jnp.broadcast_to(decay, (HEADS, LANES))
    save = start_all([(small_ref, small_h)], sems.at[0])
    for i in range(BLOCKS):
        if i:
            copies[i].wait()
        cols = slice(i * GROUP_X, (i + 1) * GROUP_X)
        win_ref[8 : 8 + T, :] = hold_ref[:, cols].astype(F32)
        for lo in range(0, GROUP_X, LANES):
            at = i * GROUP_X + lo
            pre = pre_conv(win_ref, weight_ref[:, cols], lo)
            mixed = (pre * sigmoid(pre)).astype(BF16)
            head_ref[:, at : at + LANES] = pre[0:8]
            if at < WIDTH_X:
                x_ref[:, at : at + LANES] = mixed
            else:
                bc_ref[:, at - WIDTH_X : at - WIDTH_X + LANES] = mixed
    wait_all(save + later)


def run_begin(raw, decay_log, skip_gain, tokens, weight, cot):
    out = [
        ("h", (SMALL_ROWS, LANES), F32),
        ("V", (SMALL_ROWS, LANES), F32),
        ("V", (PAIRS, LANES), F32),
        ("V", (T, WIDTH_X), BF16),
        ("V", (T, 2 * WIDTH_B), BF16),
        ("V", (8, CHANNELS), F32),
        ("V", (TAPS, CHANNELS), F32),
        ("V", (T, WIDTH_X), BF16),
    ]
    scratch = [
        pltpu.VMEM((HEADS, T), F32),
        pltpu.VMEM((1, HEADS), F32),
        pltpu.VMEM((1, HEADS), F32),
        pltpu.VMEM((T, CHANNELS), BF16),
        pltpu.VMEM((8 + T, GROUP_X), F32),
        DMA(3, BLOCKS),
    ]
    return call(begin_kernel, "begin", out, "hhhhhh", 4, scratch, mib=16)(
        raw, decay_log, skip_gain, tokens, weight, cot
    )


def rolled(cols, group):
    return pltpu.roll(cols, (LANES - group * GROUP_HEADS) % LANES, 1)


def widen(cols, base, pair):
    first = iota((T, LANES), 1) < HEAD_DIM
    at = base + 2 * pair
    return jnp.where(first, cols[:, at : at + 1], cols[:, at + 1 : at + 2])


def widen_two(cols, base, pair):
    return jnp.concatenate([widen(cols, base, pair), widen(cols, base, pair + 1)], axis=1)


def fill_half(half, x_ref, bc_ref, g_ref, scale, dst_ref):
    for jj in range(HALF_GROUPS):
        j = half * HALF_GROUPS + jj
        b_flip = jnp.transpose(bc_ref[:, span(j, STATE)].astype(F32)).astype(BF16)
        c_flip = jnp.transpose(bc_ref[:, span(GROUPS + j, STATE)].astype(F32)).astype(BF16)
        cols = rolled(scale, j)
        for q in range(0, GROUP_PAIRS, 2):
            lanes = pl.ds(pl.multiple_of(j * GROUP_X + q * LANES, 2 * LANES), 2 * LANES)
            xw = (x_ref[:, lanes].astype(F32) * widen_two(cols, HEADS, q)).astype(BF16)
            gw = (g_ref[:, lanes].astype(F32) * widen_two(cols, 0, q)).astype(BF16)
            state = dot(b_flip, xw).astype(BF16)
            grad = dot(c_flip, gw).astype(BF16)
            for k in range(2):
                at = jj * GROUP_PAIRS + q + k
                dst_ref[0, at] = state[:, k * LANES : (k + 1) * LANES]
                dst_ref[1, at] = grad[:, k * LANES : (k + 1) * LANES]


def enter_kernel(core_ref, x0_ref, bc0_ref, head_ref, halo_ref, weight_ref, g_ref, small_ref,
                 x_h, bc_h, before_h, x_ref, bc_ref, out_ref, before_ref, sems):
    half = 1 - core_ref[0]
    row = iota((8, GROUP_X), 0)
    for i in range(BLOCKS):
        cols = slice(i * GROUP_X, (i + 1) * GROUP_X)
        halo = halo_ref[:, cols].astype(F32)
        weight = weight_ref[:, cols]
        pre = head_ref[:, cols]
        before = jnp.zeros((8, GROUP_X), F32)
        for t in range(TAPS - 1):
            extra = jnp.zeros((1, GROUP_X), F32)
            for k in range(TAPS - 1 - t):
                extra = extra + weight[k : k + 1] * halo[t + k : t + k + 1]
            pre = pre + jnp.where(row == t, extra, 0.0)
            before = before + jnp.where(row == t + 5, halo[t : t + 1], 0.0)
        before_ref[:, cols] = before
        fixed = pre * sigmoid(pre)
        src, dst, at = (x0_ref, x_ref, cols) if i < GROUPS else (bc0_ref, bc_ref, slice(0, GROUP_X))
        rest = src[0:16, at].astype(F32)
        dst[16:T, at] = src[16:T, at]
        dst[0:16, at] = jnp.concatenate([fixed, rest[8:16]], axis=0).astype(BF16)
    saves = start_all([(x_ref, x_h), (bc_ref, bc_h), (before_ref, before_h)], sems)
    fill_half(half, x_ref, bc_ref, g_ref, small_ref[ROW_SCALE : ROW_SCALE + T], out_ref)
    wait_all(saves)


def run_enter(core, x0, bc0, head, halo, weight, cot, small):
    out = [
        ("h", (T, WIDTH_X), BF16),
        ("h", (T, 2 * WIDTH_B), BF16),
        ("h", (8, CHANNELS), F32),
        ("V", (T, WIDTH_X), BF16),
        ("V", (T, 2 * WIDTH_B), BF16),
        ("V", (2, HALF_PAIRS, STATE, LANES), BF16),
    ]
    scratch = [pltpu.VMEM((8, CHANNELS), F32), DMA(3)]
    return call(enter_kernel, "enter", out, "sVVVvVVV", 3, scratch, mib=16)(
        core, x0, bc0, head, halo, weight, cot, small
    )


def own_kernel(core_ref, x_ref, bc_ref, g_ref, small_ref, own_ref):
    fill_half(core_ref[0], x_ref, bc_ref, g_ref, small_ref[ROW_SCALE : ROW_SCALE + T], own_ref)


def run_own(core, x, bc, cot, small):
    out = [("V", (2, HALF_PAIRS, STATE, LANES), BF16)]
    return call(own_kernel, "own", out, "sVVVV", 3, mib=16)(core, x, bc, cot, small)[0]


STEP_PAIRS = 4
STEPS = HALF_PAIRS // STEP_PAIRS


def pack_kernel(core_ref, own_ref, got_ref, tot_ref, other_ref,
                out_h, own_h, got_h, tots_h, out_ref, sems):
    saves = start_all(
        [
            (own_ref, own_h),
            (got_ref, got_h),
            (tot_ref, tots_h.at[pl.ds(0, PAIRS)]),
            (other_ref, tots_h.at[pl.ds(PAIRS, PAIRS)]),
        ],
        sems.at[0],
    )
    second = core_ref[0] == 1
    outs = []
    for i in range(HALF_PAIRS):
        at = core_ref[0] * HALF_PAIRS + i
        tot = tot_ref[pl.ds(at, 1), :]
        other = other_ref[pl.ds(at, 1), :]
        one = jnp.ones_like(tot)
        by_own = jnp.exp(tot)
        by_other = jnp.exp(other)
        state = (
            jnp.where(second, one, by_other) * own_ref[0, i].astype(F32)
            + jnp.where(second, by_own, one) * got_ref[0, i].astype(F32)
        )
        grad = (
            jnp.where(second, by_other, one) * own_ref[1, i].astype(F32)
            + jnp.where(second, one, by_own) * got_ref[1, i].astype(F32)
        )
        out_ref[i, 0:STATE, :] = state.astype(BF16)
        out_ref[i, STATE : 2 * STATE, :] = grad.astype(BF16)
        both = tot + other
        high = both.astype(BF16).astype(F32)
        mid = (both - high).astype(BF16).astype(F32)
        low = both - high - mid
        row = iota((16, LANES), 0)
        wide = jnp.where(row == 0, high, jnp.where(row == 1, mid, jnp.where(row == 2, low, 0.0)))
        out_ref[i, 2 * STATE : PACK_ROWS, :] = wide.astype(BF16)
        if i % STEP_PAIRS == STEP_PAIRS - 1:
            done = pl.ds(i + 1 - STEP_PAIRS, STEP_PAIRS)
            copy = pltpu.make_async_copy(out_ref.at[done], out_h.at[done], sems.at[1, i // STEP_PAIRS])
            copy.start()
            outs.append(copy)
    wait_all(outs + saves)


def run_pack(core, own, got, tot, other):
    half = (2, HALF_PAIRS, STATE, LANES)
    packed = (HALF_PAIRS, PACK_ROWS, LANES)
    out = [("h", packed, BF16), ("h", half, BF16), ("h", half, BF16), ("h", (2 * PAIRS, LANES), F32)]
    scratch = [pltpu.VMEM(packed, BF16), DMA(2, STEPS)]
    return call(pack_kernel, "pack", out, "sVvVv", 2, scratch, mib=16)(core, own, got, tot, other)


def chain_kernel(chips, per, in_ref, out_ref):
    for q in range(per):
        def decay(k):
            rows = in_ref[k * per + q, 2 * STATE : PACK_ROWS, :].astype(F32)
            return jnp.exp(rows[0:1] + rows[1:2] + rows[2:3])

        carry = jnp.zeros((STATE, LANES), F32)
        for k in range(chips):
            out_ref[k * per + q, 0:STATE, :] = carry.astype(BF16)
            if k < chips - 1:
                carry = decay(k) * carry + in_ref[k * per + q, 0:STATE, :].astype(F32)
        carry = jnp.zeros((STATE, LANES), F32)
        for k in reversed(range(chips)):
            out_ref[k * per + q, STATE : 2 * STATE, :] = carry.astype(BF16)
            if k > 0:
                carry = decay(k) * carry + in_ref[k * per + q, STATE : 2 * STATE, :].astype(F32)


def run_chain(chips, packed):
    kernel = functools.partial(chain_kernel, chips, HALF_PAIRS // chips)
    out = [("v", (HALF_PAIRS, 2 * STATE, LANES), BF16)]
    return call(kernel, "chain", out, "v", 1, mib=16)(packed)[0]


HALF_X = HALF_GROUPS * GROUP_X
HALF_B = 2 * HALF_GROUPS * STATE

NEAR = [
    ("V", (T, GROUP_X), BF16),
    ("V", (T, GROUP_X), BF16),
    ("V", (T, GROUP_X), F32),
    ("V", (T, GROUP_X), F32),
    ("V", (T, GROUP_X + 2 * STATE), F32),
    ("V", (T, GROUP_X + 2 * STATE), BF16),
    ("V", (T, 2 * STATE), BF16),
    ("V", (T, 2 * STATE), F32),
]
COMMON = [
    ("V", (8, CHANNELS), F32),
    ("V", (SMALL_ROWS, LANES), F32),
    ("V", (HEADS, T), F32),
    ("V", (PAIRS, LANES), F32),
    ("V", (TAPS, CHANNELS), F32),
]
FETCHES = 6 + 8


def fetch_group(j, far, near, sems):
    x_h, g_h, y_h, gx_h, slope_h, tok_h, bc_h, gbc_h = far
    x_v, g_v, y_v, gx_v, slope_v, tok_v, bc_v, gbc_v = near
    wide = pl.ds(0, GROUP_X)
    pairs = [
        (a.at[:, span(j, GROUP_X)], b.at[:, wide])
        for a, b in ((x_h, x_v), (g_h, g_v), (y_h, y_v), (gx_h, gx_v), (slope_h, slope_v), (tok_h, tok_v))
    ]
    for base in range(2):
        at = span(base * GROUPS + j, STATE)
        off = span(WIDTH_X // STATE + base * GROUPS + j, STATE)
        thin = pl.ds(base * STATE, STATE)
        tail = pl.ds(GROUP_X + base * STATE, STATE)
        pairs += [
            (bc_h.at[:, at], bc_v.at[:, thin]),
            (gbc_h.at[:, at], gbc_v.at[:, thin]),
            (slope_h.at[:, off], slope_v.at[:, tail]),
            (tok_h.at[:, off], tok_v.at[:, tail]),
        ]
    return start_all(pairs, sems)


def unpack_kernel(core_ref, back_ref, own_h, got_h, tots_h, *rest):
    far, rest = rest[: len(NEAR)], rest[len(NEAR) :]
    common_far, rest = rest[: len(COMMON)], rest[len(COMMON) :]
    mine_ref, send_ref, *rest = rest
    near = [rest[i * len(NEAR) : (i + 1) * len(NEAR)] for i in range(HALF_GROUPS)]
    rest = rest[HALF_GROUPS * len(NEAR) :]
    common, rest = rest[: len(COMMON)], rest[len(COMMON) :]
    own_ref, got_ref, tots_ref, sems, fetch_sems = rest
    first = start_all([(tots_h, tots_ref)], sems.at[STEPS])
    steps = []
    for step in range(STEPS):
        at = pl.ds(step * STEP_PAIRS, STEP_PAIRS)
        steps.append(
            start_all([(own_h.at[:, at], own_ref.at[:, at]), (got_h.at[:, at], got_ref.at[:, at])], sems.at[step])
        )
    fetches = start_all(list(zip(common_far, common)), fetch_sems.at[HALF_GROUPS])
    for jj in range(HALF_GROUPS):
        fetches += fetch_group(core_ref[0] * HALF_GROUPS + jj, far, near[jj], fetch_sems.at[jj])
    wait_all(first)
    second = core_ref[0] == 1
    for i in range(HALF_PAIRS):
        if i % STEP_PAIRS == 0:
            wait_all(steps[i // STEP_PAIRS])
        at = core_ref[0] * HALF_PAIRS + i
        tot = tots_ref[pl.ds(at, 1), :]
        other = tots_ref[pl.ds(PAIRS + at, 1), :]
        decay_zero = jnp.exp(jnp.where(second, other, tot))
        decay_one = jnp.exp(jnp.where(second, tot, other))
        state_zero = back_ref[i, 0:STATE, :].astype(F32)
        grad_one = back_ref[i, STATE : 2 * STATE, :].astype(F32)
        left = jnp.where(second, got_ref[0, i].astype(F32), own_ref[0, i].astype(F32))
        right = jnp.where(second, own_ref[1, i].astype(F32), got_ref[1, i].astype(F32))
        state_one = decay_zero * state_zero + left
        grad_zero = decay_one * grad_one + right
        mine_ref[0, i] = jnp.where(second, state_one, state_zero).astype(BF16)
        mine_ref[1, i] = jnp.where(second, grad_one, grad_zero).astype(BF16)
        send_ref[0, i] = jnp.where(second, state_zero, state_one).astype(BF16)
        send_ref[1, i] = jnp.where(second, grad_zero, grad_one).astype(BF16)
    wait_all(fetches)


def run_unpack(core, back, own, got, tots, far, common):
    half = (2, HALF_PAIRS, STATE, LANES)
    out = [("V", half, BF16)] * 2 + NEAR * HALF_GROUPS + COMMON
    scratch = [
        pltpu.VMEM(half, BF16),
        pltpu.VMEM(half, BF16),
        pltpu.VMEM((2 * PAIRS, LANES), F32),
        DMA(STEPS + 1, 2),
        DMA(HALF_GROUPS + 1, FETCHES),
    ]
    specs = "svhhh" + "h" * (len(NEAR) + len(COMMON))
    outs = call(unpack_kernel, "unpack", out, specs, 3, scratch, mib=16)(
        core, back, own, got, tots, *far, *common
    )
    at = 2 + HALF_GROUPS * len(NEAR)
    return outs[0], outs[1], outs[2:at], outs[at:]


def by_lane_half(v):
    first = iota(v.shape, 1) < HEAD_DIM
    wide = v.astype(F32)
    return jnp.concatenate(
        [jnp.where(first, wide, 0.0).astype(BF16), jnp.where(first, 0.0, wide).astype(BF16)], axis=0
    )


def inner_kernel(x_h, bc_h, g_h, small_h, y_h, gbc_h, skips_h,
                 x_ref, bc_ref, g_ref, small_ref, y_ref, gbc_ref, skips_ref, sems):
    first = start_all([(bc_h, bc_ref), (small_h, small_ref)], sems.at[0])

    def loads(j):
        at = span(j, GROUP_X)
        return [
            pltpu.make_async_copy(x_h.at[:, at], x_ref.at[:, at], sems.at[1, j]),
            pltpu.make_async_copy(g_h.at[:, at], g_ref.at[:, at], sems.at[2, j]),
        ]

    def store(j):
        at = span(j, GROUP_X)
        return pltpu.make_async_copy(y_ref.at[:, at], y_h.at[:, at], sems.at[3, j])

    for j in range(GROUPS):
        for copy in loads(j):
            copy.start()
    wait_all(first)
    lower = iota((T, T), 0) >= iota((T, T), 1)

    @pl.loop(0, GROUPS)
    def _(j):
        wait_all(loads(j))
        b = bc_ref[:, span(j, STATE)]
        c = bc_ref[:, span(GROUPS + j, STATE)]
        seg = small_ref[pl.ds(pl.multiple_of(ROW_SEG + j * GROUP_HEADS, GROUP_HEADS), GROUP_HEADS), :]
        dt = small_ref[pl.ds(pl.multiple_of(ROW_DT + j * GROUP_HEADS, GROUP_HEADS), GROUP_HEADS), :]
        scores = dot(c, b, NT)
        cols = rolled(small_ref[ROW_COLS : ROW_COLS + T], j)
        total = jnp.zeros((T, T), F32)
        skips = []
        for i in range(GROUP_PAIRS):
            lanes = pl.ds(pl.multiple_of(j * GROUP_X + i * LANES, LANES), LANES)
            x = x_ref[:, lanes]
            g = g_ref[:, lanes]
            skips.append(jnp.sum(g.astype(F32) * x.astype(F32), axis=0, keepdims=True))
            inner = dot(by_lane_half(g), x, NT)
            weights = []
            for k in range(2):
                h = 2 * i + k
                spread = cols[:, h : h + 1] - seg[h : h + 1, :]
                kernel = jnp.exp(jnp.where(lower, spread, -1e30)) * dt[h : h + 1, :]
                total = total + kernel * inner[k * T : (k + 1) * T]
                weights.append((kernel * scores).astype(BF16))
            y_ref[:, lanes] = dot(jnp.concatenate(weights, axis=1), by_lane_half(x))
        skips_ref[span(j, GROUP_PAIRS), :] = jnp.concatenate(skips, axis=0)
        gbc_ref[:, span(GROUPS + j, STATE)] = dot(total.astype(BF16), b)
        gbc_ref[:, span(j, STATE)] = dot(jnp.transpose(total).astype(BF16), c)
        store(j).start()

    last = start_all([(gbc_ref, gbc_h), (skips_ref, skips_h)], sems.at[0])
    for j in range(GROUPS):
        store(j).wait()
    wait_all(last)


def run_inner(x, bc, cot, small):
    out = [("h", (T, WIDTH_X), F32), ("h", (T, 2 * WIDTH_B), F32), ("h", (PAIRS, LANES), F32)]
    scratch = [
        pltpu.VMEM((T, WIDTH_X), BF16),
        pltpu.VMEM((T, 2 * WIDTH_B), BF16),
        pltpu.VMEM((T, WIDTH_X), BF16),
        pltpu.VMEM((SMALL_ROWS, LANES), F32),
        pltpu.VMEM((T, WIDTH_X), F32),
        pltpu.VMEM((T, 2 * WIDTH_B), F32),
        pltpu.VMEM((PAIRS, LANES), F32),
        DMA(4, GROUPS),
    ]
    return call(inner_kernel, "inner", out, "hhhh", 4, scratch, mib=24)(x, bc, cot, small)


def slopes_kernel(bc_h, g_h, small_h, tok_h, before_h, weight_h, gx_h, slope_h,
                  bc_ref, g_ref, small_ref, tok_ref, before_ref, weight_ref, gx_ref, slope_ref, win_ref, sems):
    first = start_all(
        [(bc_h, bc_ref), (small_h, small_ref), (before_h, before_ref), (weight_h, weight_ref), (tok_h, tok_ref)],
        sems.at[0],
    )

    def load(j):
        at = span(j, GROUP_X)
        return pltpu.make_async_copy(g_h.at[:, at], g_ref.at[:, at], sems.at[1, j])

    def store(j):
        at = span(j, GROUP_X)
        return pltpu.make_async_copy(gx_ref.at[:, at], gx_h.at[:, at], sems.at[2, j])

    def store_slope(i):
        at = span(i, GROUP_X)
        return pltpu.make_async_copy(slope_ref.at[:, at], slope_h.at[:, at], sems.at[3, i])

    for j in range(GROUPS):
        load(j).start()
    wait_all(first)
    upper = iota((T, T), 0) <= iota((T, T), 1)

    @pl.loop(0, GROUPS)
    def _(j):
        load(j).wait()
        b = bc_ref[:, span(j, STATE)]
        c = bc_ref[:, span(GROUPS + j, STATE)]
        seg = small_ref[pl.ds(pl.multiple_of(ROW_SEG + j * GROUP_HEADS, GROUP_HEADS), GROUP_HEADS), :]
        scores = jnp.transpose(dot(c, b, NT))
        cols = rolled(small_ref[ROW_COLS : ROW_COLS + T], j)
        for i in range(GROUP_PAIRS):
            lanes = pl.ds(pl.multiple_of(j * GROUP_X + i * LANES, LANES), LANES)
            weights = []
            for k in range(2):
                h = 2 * i + k
                spread = seg[h : h + 1, :] - cols[:, h : h + 1]
                kernel = jnp.exp(jnp.where(upper, spread, -1e30)) * cols[:, HEADS + h : HEADS + h + 1]
                weights.append((kernel * scores).astype(BF16))
            gx_ref[:, lanes] = dot(jnp.concatenate(weights, axis=1), by_lane_half(g_ref[:, lanes]))
        store(j).start()

    @pl.loop(0, BLOCKS)
    def _(i):
        cols = span(i, GROUP_X)
        fill_window(win_ref, before_ref[:, cols], tok_ref[:, cols])
        weights = weight_ref[:, cols]
        for lo in range(0, GROUP_X, LANES):
            pre = pre_conv(win_ref, weights, lo)
            s = sigmoid(pre)
            at = pl.ds(pl.multiple_of(i * GROUP_X + lo, LANES), LANES)
            slope_ref[:, at] = s * (1.0 + pre * (1.0 - s))
        store_slope(i).start()

    for j in range(GROUPS):
        store(j).wait()
    for i in range(BLOCKS):
        store_slope(i).wait()


def run_slopes(bc, cot, small, tokens, before, weight):
    out = [("h", (T, WIDTH_X), F32), ("h", (T, CHANNELS), F32)]
    scratch = [
        pltpu.VMEM((T, 2 * WIDTH_B), BF16),
        pltpu.VMEM((T, WIDTH_X), BF16),
        pltpu.VMEM((SMALL_ROWS, LANES), F32),
        pltpu.VMEM((T, CHANNELS), BF16),
        pltpu.VMEM((8, CHANNELS), F32),
        pltpu.VMEM((TAPS, CHANNELS), F32),
        pltpu.VMEM((T, WIDTH_X), F32),
        pltpu.VMEM((T, CHANNELS), F32),
        pltpu.VMEM((8 + T, GROUP_X), F32),
        DMA(4, BLOCKS),
    ]
    return call(slopes_kernel, "slopes", out, "hhhhhh", 6, scratch, mib=24)(
        bc, cot, small, tokens, before, weight
    )


def leave_kernel(theirs, core_ref, state_ref, *rest):
    rest = list(rest)

    def take(count):
        taken = rest[:count]
        del rest[:count]
        return taken

    sets = [take(len(NEAR)) for _ in range(HALF_GROUPS)]
    before_ref, small_ref, raw_ref, skips_ref, _ = take(len(COMMON))
    half = 1 - core_ref[0] if theirs else core_ref[0]
    fetches = []
    if theirs:
        pre_own_ref, _, _ = take(3)
        out_h, step_h, pre_ref, sum_ref, first_ref = take(5)
        head_ref, out_ref, step_ref, win_ref, sems = rest
        own = core_ref[0]
        head_ref[:, span(own, HALF_X)] = pre_own_ref[0:8, 0:HALF_X]
        size = HALF_GROUPS * STATE
        for base in range(2):
            at = HALF_X + base * size
            head_ref[:, span(WIDTH_X // size + 2 * base + own, size)] = pre_own_ref[0:8, at : at + size]
    else:
        far = take(len(NEAR))
        out_h, step_h, pre_ref, sum_ref = take(4)
        after = [take(len(NEAR)) for _ in range(HALF_GROUPS)]
        out_ref, step_ref, win_ref, sems = rest
        for jj in range(HALF_GROUPS):
            fetches += fetch_group((1 - half) * HALF_GROUPS + jj, far, after[jj], sems.at[2 + jj])
    last = iota((8, 2 * LANES), 0) == 7
    lower = (iota((T, T), 0) >= iota((T, T), 1)).astype(F32)

    def tap_sums(grad_pre, lo):
        width = grad_pre.shape[1]
        return [
            jnp.sum(grad_pre * win_ref[5 + k : 5 + k + T, lo : lo + width], axis=0, keepdims=True)
            for k in range(TAPS)
        ]

    def by_rows(sums):
        return [s[:, lo : lo + LANES] for lo in range(0, sums[0].shape[1], LANES) for s in sums]

    saves = []

    def save(src, dst):
        copy = pltpu.make_async_copy(src, dst, sems.at[len(saves) // 8, len(saves) % 8])
        copy.start()
        saves.append(copy)

    for jj in range(HALF_GROUPS):
        j = half * HALF_GROUPS + jj
        x_ref, g_ref, y_ref, gx_ref, slope_ref, tok_ref, bc_ref, gbc_ref = sets[jj]
        b = bc_ref[:, 0:STATE]
        c = bc_ref[:, STATE:]
        grad_b = gbc_ref[:, 0:STATE]
        grad_c = gbc_ref[:, STATE:]
        cols = rolled(small_ref[ROW_SCALE : ROW_SCALE + T], j)
        skip_rows = small_ref[pl.ds(pl.multiple_of(ROW_SKIP + j * GROUP_PAIRS, GROUP_PAIRS), GROUP_PAIRS), :]
        tot_rows = small_ref[pl.ds(pl.multiple_of(ROW_TOT + j * GROUP_PAIRS, GROUP_PAIRS), GROUP_PAIRS), :]
        seg_grad = jnp.zeros((GROUP_HEADS, T), F32)
        dt_grad = jnp.zeros((GROUP_HEADS, T), F32)
        skips = [skips_ref[span(j, GROUP_PAIRS), :]]
        terms = []
        fill_window(win_ref, before_ref[:, span(j, GROUP_X)], tok_ref[:, 0:GROUP_X])
        for q in range(0, GROUP_PAIRS, 2):
            lanes = slice(q * LANES, (q + 2) * LANES)
            wide = slice(jj * GROUP_X + q * LANES, jj * GROUP_X + (q + 2) * LANES)
            rise = widen_two(cols, 0, q)
            keep = widen_two(cols, HEADS, q)
            at = jj * GROUP_PAIRS + q
            state = jnp.concatenate([state_ref[0, at], state_ref[0, at + 1]], axis=1)
            exits = jnp.concatenate([state_ref[1, at], state_ref[1, at + 1]], axis=1)
            skip = jnp.concatenate([skip_rows[q : q + 1], skip_rows[q + 1 : q + 2]], axis=1)
            tot = jnp.concatenate([tot_rows[q : q + 1], tot_rows[q + 1 : q + 2]], axis=1)
            x = x_ref[:, lanes].astype(F32)
            g = g_ref[:, lanes].astype(F32)
            y = y_ref[:, lanes] + rise * dot(c, state)
            through = keep * dot(b, exits)
            gx = gx_ref[:, lanes] + through
            grad_c = grad_c + dot((g * rise).astype(BF16), state, NT)
            grad_b = grad_b + dot((x * keep).astype(BF16), exits, NT)
            out_ref[:, wide] = (y + skip * x).astype(BF16)
            grad_pre = (gx + skip * g) * slope_ref[:, lanes]
            pre_ref[:, wide] = grad_pre
            if theirs:
                at = pl.ds(pl.multiple_of(j * GROUP_X + q * LANES, 2 * LANES), 2 * LANES)
                head_ref[:, at] = grad_pre[0:8]
            terms += by_rows(tap_sums(grad_pre, q * LANES))
            x_gx = x * gx
            end = jnp.sum(x * through, axis=0, keepdims=True) + jnp.exp(tot) * jnp.sum(
                exits.astype(F32) * state.astype(F32), axis=0, keepdims=True
            )
            moved = g * y - x_gx
            moved = jnp.concatenate([moved[: T - 8], moved[T - 8 :] + jnp.where(last, end, 0.0)], axis=0)
            pick = (
                iota((GROUP_HEADS, 2 * LANES), 0)
                == 2 * q + iota((GROUP_HEADS, 2 * LANES), 1) // HEAD_DIM
            ).astype(F32).astype(BF16)
            for part in split_two(moved):
                seg_grad = seg_grad + dot(pick, part, NT)
            for part in split_two(x_gx):
                dt_grad = dt_grad + dot(pick, part, NT)
            if q % 4 == 2:
                size = GROUP_X // 2
                near_at = pl.ds(jj * GROUP_X + (q // 4) * size, size)
                far_at = span(2 * j + q // 4, size)
                save(out_ref.at[:, near_at], out_h.at[:, far_at])
        for grad, base in ((grad_b, 0), (grad_c, 1)):
            at = HALF_X + (base * HALF_GROUPS + jj) * STATE
            tail = slice(GROUP_X + base * STATE, GROUP_X + (base + 1) * STATE)
            far_at = span(WIDTH_X // STATE + base * GROUPS + j, STATE)
            fill_window(win_ref, before_ref[:, far_at], tok_ref[:, tail])
            grad_pre = grad * slope_ref[:, tail]
            pre_ref[:, at : at + STATE] = grad_pre
            if theirs:
                head_ref[:, far_at] = grad_pre[0:8]
            terms += tap_sums(grad_pre, 0)
        heads = span(j, GROUP_HEADS)
        behind = exact_dot(seg_grad, lower)
        dt = small_ref[pl.ds(pl.multiple_of(ROW_DT + j * GROUP_HEADS, GROUP_HEADS), GROUP_HEADS), :]
        decay = small_ref[pl.ds(pl.multiple_of(ROW_DECAY + j * GROUP_HEADS, GROUP_HEADS), GROUP_HEADS), :]
        near = pl.ds(jj * GROUP_HEADS, GROUP_HEADS)
        step_ref[near, :] = (dt_grad / dt + decay * behind) * sigmoid(raw_ref[heads, :])
        save(step_ref.at[near], step_h.at[heads])
        rows = jj * SUM_GROUP
        sum_ref[rows : rows + SUM_GROUP, :] = jnp.concatenate(terms + skips + [dt * behind * decay], axis=0)
    wait_all(fetches)
    if theirs:
        first_ref[...] = head_ref[0 : TAPS - 1, :].astype(BF16)
    wait_all(saves)


def run_leave(core, state, near, common, far, before_out):
    theirs = before_out is not None
    out = [
        ("h", (T, WIDTH_X), BF16),
        ("h", (HEADS, T), F32),
        ("V", (T, HALF_X + HALF_B), F32),
        ("V", (HALF_GROUPS * SUM_GROUP, LANES), F32),
    ]
    scratch = [
        pltpu.VMEM((T, HALF_X), BF16),
        pltpu.VMEM((HALF_GROUPS * GROUP_HEADS, T), F32),
        pltpu.VMEM((8 + T, GROUP_X), F32),
        DMA(2 + HALF_GROUPS, FETCHES),
    ]
    args = [core, state, *near, *common, *far]
    specs = "s" + ("v" if theirs else "V") + "V" * (len(near) + len(COMMON)) + "h" * len(far)
    aliases = {}
    if theirs:
        done, pre_own = before_out
        args += [pre_own]
        aliases = {len(args) + i: i for i in range(2)}
        args += done
        specs += "Vhh"
        out += [("V", (TAPS - 1, CHANNELS), BF16)]
        scratch = [pltpu.VMEM((8, CHANNELS), F32)] + scratch
    else:
        out += NEAR * HALF_GROUPS
    kernel = functools.partial(leave_kernel, theirs)
    outs = call(kernel, "leave", out, specs, 5, scratch, mib=16, aliases=aliases)(*args)
    return outs[:2], outs[2], outs[3], outs[4:]


def spread_kernel(core_ref, own_ref, theirs_ref, halo_ref, weight_ref, out_h, out_ref, win_ref, sems):
    saves = []
    size = HALF_GROUPS * STATE
    for side, pre_ref in enumerate((own_ref, theirs_ref)):
        half = 1 - core_ref[0] if side else core_ref[0]
        blocks = [(jj * GROUP_X, span(half * HALF_GROUPS + jj, GROUP_X), GROUP_X) for jj in range(HALF_GROUPS)]
        blocks += [
            (HALF_X + base * size, span(WIDTH_X // size + 2 * base + half, size), size) for base in range(2)
        ]
        for near, far, width in blocks:
            win_ref[0:T, 0:width] = pre_ref[:, near : near + width]
            win_ref[T : T + TAPS - 1, 0:width] = halo_ref[:, far].astype(F32)
            weights = weight_ref[:, far]
            base = side * (HALF_X + HALF_B) + near
            for lo in range(0, width, LANES):
                at = slice(lo, lo + LANES)
                acc = weights[0:1, at] * win_ref[3 : 3 + T, at]
                for k in range(1, TAPS):
                    acc = acc + weights[k : k + 1, at] * win_ref[3 - k : 3 - k + T, at]
                out_ref[:, base + lo : base + lo + LANES] = acc.astype(BF16)
            copy = pltpu.make_async_copy(out_ref.at[:, pl.ds(base, width)], out_h.at[:, far], sems.at[len(saves)])
            copy.start()
            saves.append(copy)
    wait_all(saves)


def run_spread(core, own, theirs, halo, weight):
    out = [("h", (T, CHANNELS), BF16)]
    scratch = [pltpu.VMEM((T, CHANNELS), BF16), pltpu.VMEM((T + 8, GROUP_X), F32), DMA(8)]
    return call(spread_kernel, "spread", out, "sVVvV", 3, scratch, mib=16)(core, own, theirs, halo, weight)[0]


CONV_ROWS = TAPS * (CHANNELS // LANES)
CONV_GROUP = CONV_ROWS // GROUPS
SEND_ROWS = CONV_ROWS + 16


def write_send(out_ref, conv, thin):
    high = thin.astype(BF16).astype(F32)
    low = thin - high
    row = iota((16, LANES), 0)
    out_ref[0:CONV_ROWS, :] = conv.astype(BF16)
    out_ref[CONV_ROWS:SEND_ROWS, :] = jnp.where(row == 0, high, jnp.where(row == 1, low, 0.0)).astype(BF16)


def read_send(value):
    wide = value.astype(F32)
    return wide[0:CONV_ROWS], wide[CONV_ROWS : CONV_ROWS + 1] + wide[CONV_ROWS + 1 : CONV_ROWS + 2]


def merge_kernel(core_ref, own_ref, own_got_ref, theirs_ref, theirs_got_ref, out_ref):
    thin = jnp.zeros((8, LANES), F32)
    left = iota((8, LANES), 1) < HEAD_DIM
    count = HEADS // 2
    parts = []
    for side, (mine, other) in enumerate(((own_ref, theirs_got_ref), (theirs_ref, own_got_ref))):
        half = 1 - core_ref[0] if side else core_ref[0]
        total = mine[...] + other[...]
        rows, skips, decays = [], [], []
        for jj in range(HALF_GROUPS):
            at = jj * SUM_GROUP
            rows.append(total[at : at + CONV_GROUP])
            skips.append(total[at + CONV_GROUP : at + SUM_GROUP - GROUP_HEADS])
            decays.append(total[at + SUM_GROUP - GROUP_HEADS : at + SUM_GROUP])
        skips = jnp.concatenate(skips, axis=0)
        even = exact_dot(jnp.where(left, 1.0, 0.0), skips, NT)
        odd = exact_dot(jnp.where(left, 0.0, 1.0), skips, NT)
        decay = exact_dot(jnp.ones((8, LANES), F32), jnp.concatenate(decays, axis=0), NT)
        for part, step, shift in ((even, 2, 0), (odd, 2, 1), (decay, 1, HEADS)):
            size = part.shape[1]
            spot = (iota((size, LANES), 1) == step * iota((size, LANES), 0) + shift + half * count).astype(F32)
            thin = thin + exact_dot(part, spot)
        parts.append(jnp.concatenate(rows, axis=0))
    first = core_ref[0] == 0
    conv = jnp.concatenate(
        [jnp.where(first, parts[0], parts[1]), jnp.where(first, parts[1], parts[0])], axis=0
    )
    write_send(out_ref, conv, thin[0:1])


def run_merge(core, own, own_got, theirs, theirs_got):
    out = [("v", (SEND_ROWS, LANES), BF16)]
    return call(merge_kernel, "merge", out, "svvvv", 1, mib=16)(core, own, own_got, theirs, theirs_got)[0]


def ring_sum(me_ref, refs, hold_ref):
    count = len(refs)
    for d in range(count):
        hold_ref[d] = refs[d][...]
    conv, thin = read_send(hold_ref[lax.rem(me_ref[0], count)])
    for k in range(1, count):
        more, little = read_send(hold_ref[lax.rem(me_ref[0] + count - k, count)])
        conv, thin = conv + more, thin + little
    return conv, thin


def fold_kernel(me_ref, *rest):
    *refs, out_ref, hold_ref = rest
    write_send(out_ref, *ring_sum(me_ref, refs, hold_ref))


def run_fold(me, values):
    out = [("v", (SEND_ROWS, LANES), BF16)]
    scratch = [pltpu.VMEM((len(values), SEND_ROWS, LANES), BF16)]
    return call(fold_kernel, "fold", out, "s" + "v" * len(values), 1, scratch, mib=16)(me, *values)[0]


def finish_kernel(me_ref, *rest):
    *refs, conv_ref, decay_ref, skip_ref, hold_ref = rest
    conv, thin = ring_sum(me_ref, refs, hold_ref)
    for i in range(CHANNELS // LANES):
        if i < PAIRS:
            row = CONV_GROUP * (i // GROUP_PAIRS) + TAPS * (i % GROUP_PAIRS)
        else:
            kind, group = divmod(i - PAIRS, GROUPS)
            row = CONV_GROUP * group + TAPS * (GROUP_PAIRS + kind)
        conv_ref[:, i * LANES : (i + 1) * LANES] = conv[row : row + TAPS]
    skip_ref[...] = thin[:, 0:HEADS]
    decay_ref[...] = thin[:, HEADS:]


def run_finish(me, values):
    out = [("v", (TAPS, CHANNELS), F32), ("v", (1, HEADS), F32), ("v", (1, HEADS), F32)]
    scratch = [pltpu.VMEM((len(values), SEND_ROWS, LANES), BF16)]
    return call(finish_kernel, "finish", out, "s" + "v" * len(values), 1, scratch, mib=16)(me, *values)


CTX = ("chip", "core")
ALL = ("dp", "chip", "core")


def all_to_all(value, axis):
    return lax.all_to_all(value, axis, 0, 0, tiled=True)


def tie(*values):
    return lax.optimization_barrier(values)


SIDE = 4


def around(value, axis, count, ring, move):
    return [value] + [
        lax.ppermute(value, axis, [(i, move(i, d)) for i in range(count)]) for d in range(1, ring)
    ]


def scalar(value):
    return value.astype(jnp.int32).reshape(1)


def local(conv_input, conv_weight, step_raw, decay_log, skip_gain, cotangent):
    chips = lax.axis_size("chip")
    devices = 2 * chips
    sequences = lax.axis_size("dp")
    tokens = conv_input[0]
    raw = step_raw[0]
    cot = cotangent[0]
    core = lax.axis_index("core").astype(jnp.int32).reshape(1)
    swap = [(0, 1), (1, 0)]
    halo = lax.ppermute(tokens[T - TAPS + 1 :], CTX, [(i, i + 1) for i in range(devices - 1)])
    small, small_near, tot, x0, bc0, head, weight_near, cot_near = run_begin(
        raw, decay_log.reshape(1, HEADS), skip_gain.reshape(1, HEADS), tokens, conv_weight, cot
    )
    other = lax.ppermute(tot, "core", swap)
    x, bc, before, x_near, bc_near, out = run_enter(
        core, x0, bc0, head, halo, weight_near, cot_near, small_near
    )
    got_near = lax.ppermute(out, "core", swap)
    own_near = run_own(core, x_near, bc_near, cot_near, small_near)
    packed, own, got, tots = run_pack(core, own_near, got_near, tot, other)
    heard = all_to_all(packed, "chip")
    y, gbc, skips = run_inner(x, bc, cot, small)
    heard, y, gbc, skips = tie(heard, y, gbc, skips)
    chained = run_chain(chips, heard)
    late, chained = tie(bc, chained)
    back = all_to_all(chained, "chip")
    gx, slope = run_slopes(late, cot, small, tokens, before, conv_weight)
    back, gx, slope = tie(back, gx, slope)
    far = (x, cot, y, gx, slope, tokens, bc, gbc)
    mine, send, near, common = run_unpack(
        core, back, own, got, tots, far, (before, small, raw, skips, conv_weight)
    )
    theirs = lax.ppermute(send, "core", swap)
    half, pre_own, sum_own, near = run_leave(core, mine, near, common, far, None)
    sum_own_got = lax.ppermute(sum_own, "core", swap)
    (out_tokens, grad_step), pre_theirs, sum_theirs, (first,) = run_leave(
        core, theirs, near, common, (), (half, pre_own)
    )
    sum_theirs_got = lax.ppermute(sum_theirs, "core", swap)
    after = lax.ppermute(first, CTX, [(i + 1, i) for i in range(devices - 1)])
    sums = run_merge(core, sum_own, sum_own_got, sum_theirs, sum_theirs_got)
    chip = lax.axis_index("chip")
    values = around(sums, "chip", chips, SIDE, lambda i, d: i // SIDE * SIDE + (i % SIDE + d) % SIDE)
    grad_tokens = run_spread(core, pre_own, pre_theirs, after, common[4])
    values, grad_tokens = tie(values, grad_tokens)
    sums = run_fold(scalar(lax.rem(chip, SIDE)), values)
    values = around(sums, "chip", chips, chips // SIDE, lambda i, d: (i + d * SIDE) % chips)
    sums = run_fold(scalar(lax.div(chip, SIDE)), values)
    values = around(sums, "dp", sequences, sequences, lambda i, d: (i + d) % sequences)
    grad_conv, grad_decay, grad_skip = run_finish(scalar(lax.axis_index("dp")), values)
    return (
        out_tokens[None],
        grad_tokens[None],
        grad_step[None],
        grad_conv,
        grad_decay.reshape(HEADS),
        grad_skip.reshape(HEADS),
    )


def solution(mesh):
    dp, ctx = mesh.devices.shape
    fine = Mesh(mesh.devices.reshape(dp, ctx // 2, 2), ALL)
    seq = P("dp", CTX, None)
    rate = P("dp", None, CTX)
    in_specs = (seq, P(), rate, P(), P(), seq)
    out_specs = (seq, seq, rate, P(), P(), P())
    return jax.shard_map(local, mesh=fine, in_specs=in_specs, out_specs=out_specs, check_vma=False)
```

```python
import functools

import jax
import jax.numpy as jnp
from jax import lax
from jax.experimental import pallas as pl
from jax.experimental.pallas import tpu as pltpu
from jax.sharding import Mesh
from jax.sharding import PartitionSpec as P

HEADS = 64
HEAD_DIM = 64
GROUPS = 4
STATE = 128
TAPS = 4
T = 128
LANES = 128
WIDTH_X = HEADS * HEAD_DIM
WIDTH_B = GROUPS * STATE
CHANNELS = WIDTH_X + 2 * WIDTH_B
GROUP_X = WIDTH_X // GROUPS
PAIRS = HEADS // 2
GROUP_PAIRS = PAIRS // GROUPS
GROUP_HEADS = HEADS // GROUPS
HALF_PAIRS = PAIRS // 2
HALF_GROUPS = GROUPS // 2
F32 = jnp.float32
BF16 = jnp.bfloat16
EXACT = lax.Precision.HIGHEST
NN = (((1,), (0,)), ((), ()))
NT = (((1,), (1,)), ((), ()))
SUM_GROUP = 64
PACK_ROWS = 2 * STATE + 16


def dot(a, b, dims=NN):
    return lax.dot_general(a, b, dims, preferred_element_type=F32)


def exact_dot(a, b, dims=NN):
    return lax.dot_general(a, b, dims, precision=EXACT, preferred_element_type=F32)


def iota(shape, dim):
    return lax.broadcasted_iota(jnp.int32, shape, dim)


def sigmoid(v):
    return 0.5 + 0.5 * jnp.tanh(0.5 * v)


def split_two(v):
    high = v.astype(BF16)
    return high, (v - high.astype(F32)).astype(BF16)


def span(index, size):
    return pl.ds(pl.multiple_of(index * size, size), size)


def pin(value, space):
    return pltpu.with_memory_space_constraint(value, space)


def placed(space, shape, dtype):
    return space(shape, dtype)


def call(kernel, name, outs, specs, micros, scratch=(), mib=28, aliases=None):
    cost = pl.CostEstimate(
        flops=int(micros * 1e9), transcendentals=0, bytes_accessed=int(micros * 3.6e6)
    )
    blocks = {
        "s": pl.BlockSpec(memory_space=pltpu.SMEM),
        "v": pl.BlockSpec(memory_space=pltpu.VMEM),
        "V": pl.BlockSpec(memory_space=pltpu.VMEM),
        "h": pl.BlockSpec(memory_space=pltpu.HBM),
    }
    spaces = {"V": pltpu.VMEM, "h": pltpu.HBM}
    shapes = [
        placed(spaces[p], shape, dtype) if p in spaces else jax.ShapeDtypeStruct(shape, dtype)
        for p, shape, dtype in outs
    ]
    run = pl.pallas_call(
        kernel,
        out_shape=shapes,
        in_specs=[blocks[p] for p in specs],
        out_specs=[blocks[p] for p, _, _ in outs],
        scratch_shapes=list(scratch),
        input_output_aliases=aliases or {},
        cost_estimate=cost,
        compiler_params=pltpu.CompilerParams(vmem_limit_bytes=mib << 20),
        name=name,
    )

    def go(*args):
        return run(*[pin(a, spaces[p]) if p in spaces else a for a, p in zip(args, specs, strict=True)])

    return go


def start_all(pairs, sems):
    copies = [pltpu.make_async_copy(a, b, sems.at[i]) for i, (a, b) in enumerate(pairs)]
    for copy in copies:
        copy.start()
    return copies


def wait_all(copies):
    for copy in copies:
        copy.wait()


def DMA(*shape):
    return pltpu.SemaphoreType.DMA(shape)


def fill_window(win_ref, before, tokens):
    width = tokens.shape[1]
    win_ref[0:8, :width] = before
    win_ref[8 : 8 + T, :width] = tokens.astype(F32)


def pre_conv(win_ref, weights, lo):
    cols = slice(lo, lo + LANES)
    acc = weights[0:1, cols] * win_ref[5 : 5 + T, cols]
    for k in range(1, TAPS):
        acc = acc + weights[k : k + 1, cols] * win_ref[5 + k : 5 + k + T, cols]
    return acc


BLOCKS = CHANNELS // GROUP_X


ROW_DT, ROW_SEG, ROW_COLS, ROW_SCALE, ROW_TOT, ROW_SKIP, ROW_DECAY, SMALL_ROWS = (
    0, 64, 128, 256, 384, 416, 448, 512
)


def begin_kernel(raw_h, decay_log_h, skip_gain_h, tok_h, weight_h, g_h,
                 small_h, small_ref, tot_ref, x_ref, bc_ref, head_ref, weight_ref, g_ref,
                 raw_ref, decay_log_ref, skip_gain_ref, wide_ref, hold_ref, win_ref, sems):
    first = start_all(
        [(raw_h, raw_ref), (decay_log_h, decay_log_ref), (skip_gain_h, skip_gain_ref), (weight_h, weight_ref)],
        sems.at[0],
    )
    blocks = [pl.ds(i * GROUP_X, GROUP_X) for i in range(BLOCKS)]
    copies = start_all([(tok_h.at[:, at], hold_ref.at[:, at]) for at in blocks], sems.at[1])
    later = start_all([(g_h, g_ref)], sems.at[2])
    win_ref[0:8, :] = jnp.zeros((8, GROUP_X), F32)
    copies[0].wait()
    diagonal = iota((HEADS, HEADS), 0) == iota((HEADS, HEADS), 1)

    def column(row):
        return jnp.sum(jnp.where(diagonal, row, 0.0), axis=1, keepdims=True)

    wait_all(first)
    raw = raw_ref[...]
    dt = jnp.log1p(jnp.exp(raw))
    decay = -jnp.exp(column(decay_log_ref[...]))
    upper = (iota((T, T), 0) <= iota((T, T), 1)).astype(F32)
    seg = exact_dot(dt * decay, upper)
    total = seg[:, T - 1 : T]
    small_ref[ROW_DT : ROW_DT + HEADS] = dt
    small_ref[ROW_SEG : ROW_SEG + HEADS] = seg
    small_ref[ROW_COLS : ROW_COLS + T] = jnp.transpose(jnp.concatenate([seg, dt], axis=0))
    small_ref[ROW_SCALE : ROW_SCALE + T] = jnp.transpose(
        jnp.concatenate([jnp.exp(seg), jnp.exp(total - seg) * dt], axis=0)
    )
    left = iota((PAIRS, LANES), 1) < HEAD_DIM

    def paired(col):
        wide_ref[...] = jnp.broadcast_to(col, (HEADS, LANES))
        return jnp.where(left, wide_ref[pl.ds(0, PAIRS, 2), :], wide_ref[pl.ds(1, PAIRS, 2), :])

    tot = paired(total)
    tot_ref[...] = tot
    small_ref[ROW_TOT : ROW_TOT + PAIRS] = tot
    small_ref[ROW_SKIP : ROW_SKIP + PAIRS] = paired(column(skip_gain_ref[...]))
    small_ref[ROW_DECAY : ROW_DECAY + HEADS] = jnp.broadcast_to(decay, (HEADS, LANES))
    save = start_all([(small_ref, small_h)], sems.at[0])
    for i in range(BLOCKS):
        if i:
            copies[i].wait()
        cols = slice(i * GROUP_X, (i + 1) * GROUP_X)
        win_ref[8 : 8 + T, :] = hold_ref[:, cols].astype(F32)
        for lo in range(0, GROUP_X, LANES):
            at = i * GROUP_X + lo
            pre = pre_conv(win_ref, weight_ref[:, cols], lo)
            mixed = (pre * sigmoid(pre)).astype(BF16)
            head_ref[:, at : at + LANES] = pre[0:8]
            if at < WIDTH_X:
                x_ref[:, at : at + LANES] = mixed
            else:
                bc_ref[:, at - WIDTH_X : at - WIDTH_X + LANES] = mixed
    wait_all(save + later)


def run_begin(raw, decay_log, skip_gain, tokens, weight, cot):
    out = [
        ("h", (SMALL_ROWS, LANES), F32),
        ("V", (SMALL_ROWS, LANES), F32),
        ("V", (PAIRS, LANES), F32),
        ("V", (T, WIDTH_X), BF16),
        ("V", (T, 2 * WIDTH_B), BF16),
        ("V", (8, CHANNELS), F32),
        ("V", (TAPS, CHANNELS), F32),
        ("V", (T, WIDTH_X), BF16),
    ]
    scratch = [
        pltpu.VMEM((HEADS, T), F32),
        pltpu.VMEM((1, HEADS), F32),
        pltpu.VMEM((1, HEADS), F32),
        pltpu.VMEM((HEADS, LANES), F32),
        pltpu.VMEM((T, CHANNELS), BF16),
        pltpu.VMEM((8 + T, GROUP_X), F32),
        DMA(3, BLOCKS),
    ]
    return call(begin_kernel, "begin", out, "hhhhhh", 4, scratch, mib=8)(
        raw, decay_log, skip_gain, tokens, weight, cot
    )


def rolled(cols, group):
    return pltpu.roll(cols, (LANES - group * GROUP_HEADS) % LANES, 1)


def widen(cols, base, pair):
    first = iota((T, LANES), 1) < HEAD_DIM
    at = base + 2 * pair
    return jnp.where(first, cols[:, at : at + 1], cols[:, at + 1 : at + 2])


def widen_two(cols, base, pair):
    return jnp.concatenate([widen(cols, base, pair), widen(cols, base, pair + 1)], axis=1)


def fill_half(half, x_ref, bc_ref, g_ref, scale, dst_ref):
    for jj in range(HALF_GROUPS):
        j = half * HALF_GROUPS + jj
        b_flip = jnp.transpose(bc_ref[:, span(j, STATE)].astype(F32)).astype(BF16)
        c_flip = jnp.transpose(bc_ref[:, span(GROUPS + j, STATE)].astype(F32)).astype(BF16)
        cols = rolled(scale, j)
        for q in range(0, GROUP_PAIRS, 2):
            lanes = pl.ds(pl.multiple_of(j * GROUP_X + q * LANES, 2 * LANES), 2 * LANES)
            xw = (x_ref[:, lanes].astype(F32) * widen_two(cols, HEADS, q)).astype(BF16)
            gw = (g_ref[:, lanes].astype(F32) * widen_two(cols, 0, q)).astype(BF16)
            state = dot(b_flip, xw).astype(BF16)
            grad = dot(c_flip, gw).astype(BF16)
            for k in range(2):
                at = jj * GROUP_PAIRS + q + k
                dst_ref[0, at] = state[:, k * LANES : (k + 1) * LANES]
                dst_ref[1, at] = grad[:, k * LANES : (k + 1) * LANES]


def enter_kernel(core_ref, x0_ref, bc0_ref, head_ref, halo_ref, weight_ref, g_ref, small_ref,
                 x_h, bc_h, before_h, x_ref, bc_ref, out_ref, before_ref, sems):
    half = 1 - core_ref[0]
    row = iota((8, GROUP_X), 0)
    for i in range(BLOCKS):
        cols = slice(i * GROUP_X, (i + 1) * GROUP_X)
        halo = halo_ref[:, cols].astype(F32)
        weight = weight_ref[:, cols]
        pre = head_ref[:, cols]
        before = jnp.zeros((8, GROUP_X), F32)
        for t in range(TAPS - 1):
            extra = jnp.zeros((1, GROUP_X), F32)
            for k in range(TAPS - 1 - t):
                extra = extra + weight[k : k + 1] * halo[t + k : t + k + 1]
            pre = pre + jnp.where(row == t, extra, 0.0)
            before = before + jnp.where(row == t + 5, halo[t : t + 1], 0.0)
        before_ref[:, cols] = before
        fixed = pre * sigmoid(pre)
        src, dst, at = (x0_ref, x_ref, cols) if i < GROUPS else (bc0_ref, bc_ref, slice(0, GROUP_X))
        rest = src[0:16, at].astype(F32)
        dst[16:T, at] = src[16:T, at]
        dst[0:16, at] = jnp.concatenate([fixed, rest[8:16]], axis=0).astype(BF16)
    saves = start_all([(x_ref, x_h), (bc_ref, bc_h), (before_ref, before_h)], sems)
    fill_half(half, x_ref, bc_ref, g_ref, small_ref[ROW_SCALE : ROW_SCALE + T], out_ref)
    wait_all(saves)


def run_enter(core, x0, bc0, head, halo, weight, cot, small):
    out = [
        ("h", (T, WIDTH_X), BF16),
        ("h", (T, 2 * WIDTH_B), BF16),
        ("h", (8, CHANNELS), F32),
        ("V", (T, WIDTH_X), BF16),
        ("V", (T, 2 * WIDTH_B), BF16),
        ("V", (2, HALF_PAIRS, STATE, LANES), BF16),
    ]
    scratch = [pltpu.VMEM((8, CHANNELS), F32), DMA(3)]
    return call(enter_kernel, "enter", out, "sVVVvVVV", 3, scratch, mib=6)(
        core, x0, bc0, head, halo, weight, cot, small
    )


def own_kernel(core_ref, x_ref, bc_ref, g_ref, small_ref, own_ref):
    fill_half(core_ref[0], x_ref, bc_ref, g_ref, small_ref[ROW_SCALE : ROW_SCALE + T], own_ref)


def run_own(core, x, bc, cot, small):
    out = [("V", (2, HALF_PAIRS, STATE, LANES), BF16)]
    return call(own_kernel, "own", out, "sVVVV", 3, mib=6)(core, x, bc, cot, small)[0]


STEP_PAIRS = 4
STEPS = HALF_PAIRS // STEP_PAIRS


def pack_kernel(core_ref, own_ref, got_ref, tot_ref, other_ref,
                out_h, left_h, right_h, tots_h, out_ref, sems):
    saves = start_all(
        [(tot_ref, tots_h.at[pl.ds(0, PAIRS)]), (other_ref, tots_h.at[pl.ds(PAIRS, PAIRS)])], sems.at[0]
    )
    second = core_ref[0] == 1

    def keep(first_ref, last_ref):
        return [
            pltpu.make_async_copy(first_ref.at[0], left_h, sems.at[0, 2]),
            pltpu.make_async_copy(last_ref.at[1], right_h, sems.at[0, 3]),
        ]

    @pl.when(second)
    def _():
        for copy in keep(got_ref, own_ref):
            copy.start()

    @pl.when(jnp.logical_not(second))
    def _():
        for copy in keep(own_ref, got_ref):
            copy.start()

    saves += keep(own_ref, got_ref)
    outs = []
    for i in range(HALF_PAIRS):
        at = core_ref[0] * HALF_PAIRS + i
        tot = tot_ref[pl.ds(at, 1), :]
        other = other_ref[pl.ds(at, 1), :]
        one = jnp.ones_like(tot)
        by_own = jnp.exp(tot)
        by_other = jnp.exp(other)
        state = (
            jnp.where(second, one, by_other) * own_ref[0, i].astype(F32)
            + jnp.where(second, by_own, one) * got_ref[0, i].astype(F32)
        )
        grad = (
            jnp.where(second, by_other, one) * own_ref[1, i].astype(F32)
            + jnp.where(second, one, by_own) * got_ref[1, i].astype(F32)
        )
        out_ref[i, 0:STATE, :] = state.astype(BF16)
        out_ref[i, STATE : 2 * STATE, :] = grad.astype(BF16)
        both = tot + other
        high = both.astype(BF16).astype(F32)
        mid = (both - high).astype(BF16).astype(F32)
        low = both - high - mid
        row = iota((16, LANES), 0)
        wide = jnp.where(row == 0, high, jnp.where(row == 1, mid, jnp.where(row == 2, low, 0.0)))
        out_ref[i, 2 * STATE : PACK_ROWS, :] = wide.astype(BF16)
        if i % STEP_PAIRS == STEP_PAIRS - 1:
            done = pl.ds(i + 1 - STEP_PAIRS, STEP_PAIRS)
            copy = pltpu.make_async_copy(out_ref.at[done], out_h.at[done], sems.at[1, i // STEP_PAIRS])
            copy.start()
            outs.append(copy)
    wait_all(outs + saves)


def run_pack(core, own, got, tot, other):
    half = (HALF_PAIRS, STATE, LANES)
    packed = (HALF_PAIRS, PACK_ROWS, LANES)
    out = [("h", packed, BF16), ("h", half, BF16), ("h", half, BF16), ("h", (2 * PAIRS, LANES), F32)]
    scratch = [pltpu.VMEM(packed, BF16), DMA(2, STEPS)]
    return call(pack_kernel, "pack", out, "sVvVv", 2, scratch, mib=8)(core, own, got, tot, other)


def chain_kernel(chips, per, in_ref, out_ref):
    for q in range(per):
        def decay(k):
            rows = in_ref[k * per + q, 2 * STATE : PACK_ROWS, :].astype(F32)
            return jnp.exp(rows[0:1] + rows[1:2] + rows[2:3])

        carry = jnp.zeros((STATE, LANES), F32)
        for k in range(chips):
            out_ref[k * per + q, 0:STATE, :] = carry.astype(BF16)
            if k < chips - 1:
                carry = decay(k) * carry + in_ref[k * per + q, 0:STATE, :].astype(F32)
        carry = jnp.zeros((STATE, LANES), F32)
        for k in reversed(range(chips)):
            out_ref[k * per + q, STATE : 2 * STATE, :] = carry.astype(BF16)
            if k > 0:
                carry = decay(k) * carry + in_ref[k * per + q, STATE : 2 * STATE, :].astype(F32)


def run_chain(chips, packed):
    kernel = functools.partial(chain_kernel, chips, HALF_PAIRS // chips)
    out = [("v", (HALF_PAIRS, 2 * STATE, LANES), BF16)]
    return call(kernel, "chain", out, "v", 1, mib=8)(packed)[0]


HALF_X = HALF_GROUPS * GROUP_X
HALF_B = 2 * HALF_GROUPS * STATE

NEAR = [
    ("V", (T, GROUP_X), BF16),
    ("V", (T, GROUP_X), BF16),
    ("V", (T, GROUP_X), F32),
    ("V", (T, GROUP_X), F32),
    ("V", (T, GROUP_X + 2 * STATE), F32),
    ("V", (T, GROUP_X + 2 * STATE), BF16),
    ("V", (T, 2 * STATE), BF16),
    ("V", (T, 2 * STATE), F32),
]
COMMON = [
    ("V", (8, CHANNELS), F32),
    ("V", (SMALL_ROWS, LANES), F32),
    ("V", (HEADS, T), F32),
    ("V", (PAIRS, LANES), F32),
    ("V", (TAPS, CHANNELS), F32),
]
FETCHES = 6 + 8


def fetch_group(j, far, near, sems):
    x_h, g_h, y_h, gx_h, slope_h, tok_h, bc_h, gbc_h = far
    x_v, g_v, y_v, gx_v, slope_v, tok_v, bc_v, gbc_v = near
    wide = pl.ds(0, GROUP_X)
    pairs = [
        (a.at[:, span(j, GROUP_X)], b.at[:, wide])
        for a, b in ((x_h, x_v), (g_h, g_v), (y_h, y_v), (gx_h, gx_v), (slope_h, slope_v), (tok_h, tok_v))
    ]
    for base in range(2):
        at = span(base * GROUPS + j, STATE)
        off = span(WIDTH_X // STATE + base * GROUPS + j, STATE)
        thin = pl.ds(base * STATE, STATE)
        tail = pl.ds(GROUP_X + base * STATE, STATE)
        pairs += [
            (bc_h.at[:, at], bc_v.at[:, thin]),
            (gbc_h.at[:, at], gbc_v.at[:, thin]),
            (slope_h.at[:, off], slope_v.at[:, tail]),
            (tok_h.at[:, off], tok_v.at[:, tail]),
        ]
    return start_all(pairs, sems)


def unpack_kernel(core_ref, back_ref, left_h, right_h, tots_h, *rest):
    far, rest = rest[: len(NEAR)], rest[len(NEAR) :]
    common_far, rest = rest[: len(COMMON)], rest[len(COMMON) :]
    mine_ref, send_ref, *rest = rest
    near = [rest[i * len(NEAR) : (i + 1) * len(NEAR)] for i in range(HALF_GROUPS)]
    rest = rest[HALF_GROUPS * len(NEAR) :]
    common, rest = rest[: len(COMMON)], rest[len(COMMON) :]
    left_ref, right_ref, tots_ref, sems, fetch_sems = rest
    first = start_all([(tots_h, tots_ref)], sems.at[STEPS])
    steps = []
    for step in range(STEPS):
        at = pl.ds(step * STEP_PAIRS, STEP_PAIRS)
        steps.append(
            start_all([(left_h.at[at], left_ref.at[at]), (right_h.at[at], right_ref.at[at])], sems.at[step])
        )
    fetches = start_all(list(zip(common_far, common)), fetch_sems.at[HALF_GROUPS])
    for jj in range(HALF_GROUPS):
        fetches += fetch_group(core_ref[0] * HALF_GROUPS + jj, far, near[jj], fetch_sems.at[jj])
    wait_all(first)
    second = core_ref[0] == 1
    for i in range(HALF_PAIRS):
        if i % STEP_PAIRS == 0:
            wait_all(steps[i // STEP_PAIRS])
        at = core_ref[0] * HALF_PAIRS + i
        tot = tots_ref[pl.ds(at, 1), :]
        other = tots_ref[pl.ds(PAIRS + at, 1), :]
        decay_zero = jnp.exp(jnp.where(second, other, tot))
        decay_one = jnp.exp(jnp.where(second, tot, other))
        state_zero = back_ref[i, 0:STATE, :].astype(F32)
        grad_one = back_ref[i, STATE : 2 * STATE, :].astype(F32)
        state_one = decay_zero * state_zero + left_ref[i].astype(F32)
        grad_zero = decay_one * grad_one + right_ref[i].astype(F32)
        mine_ref[0, i] = jnp.where(second, state_one, state_zero).astype(BF16)
        mine_ref[1, i] = jnp.where(second, grad_one, grad_zero).astype(BF16)
        send_ref[0, i] = jnp.where(second, state_zero, state_one).astype(BF16)
        send_ref[1, i] = jnp.where(second, grad_zero, grad_one).astype(BF16)
    wait_all(fetches)


def run_unpack(core, back, left, right, tots, far, common):
    half = (2, HALF_PAIRS, STATE, LANES)
    out = [("V", half, BF16)] * 2 + NEAR * HALF_GROUPS + COMMON
    scratch = [
        pltpu.VMEM(half[1:], BF16),
        pltpu.VMEM(half[1:], BF16),
        pltpu.VMEM((2 * PAIRS, LANES), F32),
        DMA(STEPS + 1, 2),
        DMA(HALF_GROUPS + 1, FETCHES),
    ]
    specs = "svhhh" + "h" * (len(NEAR) + len(COMMON))
    outs = call(unpack_kernel, "unpack", out, specs, 3, scratch, mib=8)(
        core, back, left, right, tots, *far, *common
    )
    at = 2 + HALF_GROUPS * len(NEAR)
    return outs[0], outs[1], outs[2:at], outs[at:]


def by_lane_half(v):
    first = iota(v.shape, 1) < HEAD_DIM
    wide = v.astype(F32)
    return jnp.concatenate(
        [jnp.where(first, wide, 0.0).astype(BF16), jnp.where(first, 0.0, wide).astype(BF16)], axis=0
    )


def inner_kernel(x_h, bc_h, g_h, small_h, y_h, gbc_h, skips_h,
                 x_ref, bc_ref, g_ref, small_ref, y_ref, gbc_ref, skips_ref, sems):
    first = start_all([(bc_h, bc_ref), (small_h, small_ref)], sems.at[0])

    def loads(j):
        at = span(j, GROUP_X)
        return [
            pltpu.make_async_copy(x_h.at[:, at], x_ref.at[:, at], sems.at[1, j]),
            pltpu.make_async_copy(g_h.at[:, at], g_ref.at[:, at], sems.at[2, j]),
        ]

    def store(j):
        at = span(j, GROUP_X)
        return pltpu.make_async_copy(y_ref.at[:, at], y_h.at[:, at], sems.at[3, j])

    for j in range(GROUPS):
        for copy in loads(j):
            copy.start()
    wait_all(first)
    lower = iota((T, T), 0) >= iota((T, T), 1)

    @pl.loop(0, GROUPS)
    def _(j):
        wait_all(loads(j))
        b = bc_ref[:, span(j, STATE)]
        c = bc_ref[:, span(GROUPS + j, STATE)]
        seg = small_ref[pl.ds(pl.multiple_of(ROW_SEG + j * GROUP_HEADS, GROUP_HEADS), GROUP_HEADS), :]
        dt = small_ref[pl.ds(pl.multiple_of(ROW_DT + j * GROUP_HEADS, GROUP_HEADS), GROUP_HEADS), :]
        scores = dot(c, b, NT)
        cols = rolled(small_ref[ROW_COLS : ROW_COLS + T], j)
        total = jnp.zeros((T, T), F32)
        skips = []
        for i in range(GROUP_PAIRS):
            lanes = pl.ds(pl.multiple_of(j * GROUP_X + i * LANES, LANES), LANES)
            x = x_ref[:, lanes]
            g = g_ref[:, lanes]
            skips.append(jnp.sum(g.astype(F32) * x.astype(F32), axis=0, keepdims=True))
            inner = dot(by_lane_half(g), x, NT)
            weights = []
            for k in range(2):
                h = 2 * i + k
                spread = cols[:, h : h + 1] - seg[h : h + 1, :]
                kernel = jnp.exp(jnp.where(lower, spread, -1e30)) * dt[h : h + 1, :]
                total = total + kernel * inner[k * T : (k + 1) * T]
                weights.append((kernel * scores).astype(BF16))
            y_ref[:, lanes] = dot(jnp.concatenate(weights, axis=1), by_lane_half(x))
        skips_ref[span(j, GROUP_PAIRS), :] = jnp.concatenate(skips, axis=0)
        gbc_ref[:, span(GROUPS + j, STATE)] = dot(total.astype(BF16), b)
        gbc_ref[:, span(j, STATE)] = dot(jnp.transpose(total).astype(BF16), c)
        store(j).start()

    last = start_all([(gbc_ref, gbc_h), (skips_ref, skips_h)], sems.at[0])
    for j in range(GROUPS):
        store(j).wait()
    wait_all(last)


def run_inner(x, bc, cot, small):
    out = [("h", (T, WIDTH_X), F32), ("h", (T, 2 * WIDTH_B), F32), ("h", (PAIRS, LANES), F32)]
    scratch = [
        pltpu.VMEM((T, WIDTH_X), BF16),
        pltpu.VMEM((T, 2 * WIDTH_B), BF16),
        pltpu.VMEM((T, WIDTH_X), BF16),
        pltpu.VMEM((SMALL_ROWS, LANES), F32),
        pltpu.VMEM((T, WIDTH_X), F32),
        pltpu.VMEM((T, 2 * WIDTH_B), F32),
        pltpu.VMEM((PAIRS, LANES), F32),
        DMA(4, GROUPS),
    ]
    return call(inner_kernel, "inner", out, "hhhh", 4, scratch, mib=16)(x, bc, cot, small)


def slopes_kernel(bc_h, g_h, small_h, tok_h, before_h, weight_h, gx_h, slope_h,
                  bc_ref, g_ref, small_ref, tok_ref, before_ref, weight_ref, gx_ref, slope_ref, win_ref, sems):
    first = start_all(
        [(bc_h, bc_ref), (small_h, small_ref), (before_h, before_ref), (weight_h, weight_ref), (tok_h, tok_ref)],
        sems.at[0],
    )

    def load(j):
        at = span(j, GROUP_X)
        return pltpu.make_async_copy(g_h.at[:, at], g_ref.at[:, at], sems.at[1, j])

    def store(j):
        at = span(j, GROUP_X)
        return pltpu.make_async_copy(gx_ref.at[:, at], gx_h.at[:, at], sems.at[2, j])

    def store_slope(i):
        at = span(i, GROUP_X)
        return pltpu.make_async_copy(slope_ref.at[:, at], slope_h.at[:, at], sems.at[3, i])

    for j in range(GROUPS):
        load(j).start()
    wait_all(first)
    upper = iota((T, T), 0) <= iota((T, T), 1)

    @pl.loop(0, GROUPS)
    def _(j):
        load(j).wait()
        b = bc_ref[:, span(j, STATE)]
        c = bc_ref[:, span(GROUPS + j, STATE)]
        seg = small_ref[pl.ds(pl.multiple_of(ROW_SEG + j * GROUP_HEADS, GROUP_HEADS), GROUP_HEADS), :]
        scores = jnp.transpose(dot(c, b, NT))
        cols = rolled(small_ref[ROW_COLS : ROW_COLS + T], j)
        for i in range(GROUP_PAIRS):
            lanes = pl.ds(pl.multiple_of(j * GROUP_X + i * LANES, LANES), LANES)
            weights = []
            for k in range(2):
                h = 2 * i + k
                spread = seg[h : h + 1, :] - cols[:, h : h + 1]
                kernel = jnp.exp(jnp.where(upper, spread, -1e30)) * cols[:, HEADS + h : HEADS + h + 1]
                weights.append((kernel * scores).astype(BF16))
            gx_ref[:, lanes] = dot(jnp.concatenate(weights, axis=1), by_lane_half(g_ref[:, lanes]))
        store(j).start()

    @pl.loop(0, BLOCKS)
    def _(i):
        cols = span(i, GROUP_X)
        fill_window(win_ref, before_ref[:, cols], tok_ref[:, cols])
        weights = weight_ref[:, cols]
        for lo in range(0, GROUP_X, LANES):
            pre = pre_conv(win_ref, weights, lo)
            s = sigmoid(pre)
            at = pl.ds(pl.multiple_of(i * GROUP_X + lo, LANES), LANES)
            slope_ref[:, at] = s * (1.0 + pre * (1.0 - s))
        store_slope(i).start()

    for j in range(GROUPS):
        store(j).wait()
    for i in range(BLOCKS):
        store_slope(i).wait()


def run_slopes(bc, cot, small, tokens, before, weight):
    out = [("h", (T, WIDTH_X), F32), ("h", (T, CHANNELS), F32)]
    scratch = [
        pltpu.VMEM((T, 2 * WIDTH_B), BF16),
        pltpu.VMEM((T, WIDTH_X), BF16),
        pltpu.VMEM((SMALL_ROWS, LANES), F32),
        pltpu.VMEM((T, CHANNELS), BF16),
        pltpu.VMEM((8, CHANNELS), F32),
        pltpu.VMEM((TAPS, CHANNELS), F32),
        pltpu.VMEM((T, WIDTH_X), F32),
        pltpu.VMEM((T, CHANNELS), F32),
        pltpu.VMEM((8 + T, GROUP_X), F32),
        DMA(4, BLOCKS),
    ]
    return call(slopes_kernel, "slopes", out, "hhhhhh", 6, scratch, mib=16)(
        bc, cot, small, tokens, before, weight
    )


def leave_kernel(theirs, core_ref, state_ref, *rest):
    rest = list(rest)

    def take(count):
        taken = rest[:count]
        del rest[:count]
        return taken

    sets = [take(len(NEAR)) for _ in range(HALF_GROUPS)]
    before_ref, small_ref, raw_ref, skips_ref, _ = take(len(COMMON))
    half = 1 - core_ref[0] if theirs else core_ref[0]
    fetches = []
    if theirs:
        pre_own_ref, _, _ = take(3)
        out_h, step_h, pre_ref, sum_ref, first_ref = take(5)
        head_ref, out_ref, step_ref, win_ref, sems = rest
        own = core_ref[0]
        head_ref[:, span(own, HALF_X)] = pre_own_ref[0:8, 0:HALF_X]
        size = HALF_GROUPS * STATE
        for base in range(2):
            at = HALF_X + base * size
            head_ref[:, span(WIDTH_X // size + 2 * base + own, size)] = pre_own_ref[0:8, at : at + size]
    else:
        far = take(len(NEAR))
        out_h, step_h, pre_ref, sum_ref = take(4)
        after = [take(len(NEAR)) for _ in range(HALF_GROUPS)]
        out_ref, step_ref, win_ref, sems = rest
        for jj in range(HALF_GROUPS):
            fetches += fetch_group((1 - half) * HALF_GROUPS + jj, far, after[jj], sems.at[2 + jj])
    last = iota((8, 2 * LANES), 0) == 7
    lower = (iota((T, T), 0) >= iota((T, T), 1)).astype(F32)

    def tap_sums(grad_pre, lo):
        width = grad_pre.shape[1]
        return [
            jnp.sum(grad_pre * win_ref[5 + k : 5 + k + T, lo : lo + width], axis=0, keepdims=True)
            for k in range(TAPS)
        ]

    def by_rows(sums):
        return [s[:, lo : lo + LANES] for lo in range(0, sums[0].shape[1], LANES) for s in sums]

    saves = []

    def save(src, dst):
        copy = pltpu.make_async_copy(src, dst, sems.at[len(saves) // 8, len(saves) % 8])
        copy.start()
        saves.append(copy)

    for jj in range(HALF_GROUPS):
        j = half * HALF_GROUPS + jj
        x_ref, g_ref, y_ref, gx_ref, slope_ref, tok_ref, bc_ref, gbc_ref = sets[jj]
        b = bc_ref[:, 0:STATE]
        c = bc_ref[:, STATE:]
        grad_b = gbc_ref[:, 0:STATE]
        grad_c = gbc_ref[:, STATE:]
        cols = rolled(small_ref[ROW_SCALE : ROW_SCALE + T], j)
        skip_rows = small_ref[pl.ds(pl.multiple_of(ROW_SKIP + j * GROUP_PAIRS, GROUP_PAIRS), GROUP_PAIRS), :]
        tot_rows = small_ref[pl.ds(pl.multiple_of(ROW_TOT + j * GROUP_PAIRS, GROUP_PAIRS), GROUP_PAIRS), :]
        seg_grad = jnp.zeros((GROUP_HEADS, T), F32)
        dt_grad = jnp.zeros((GROUP_HEADS, T), F32)
        skips = [skips_ref[span(j, GROUP_PAIRS), :]]
        terms = []
        fill_window(win_ref, before_ref[:, span(j, GROUP_X)], tok_ref[:, 0:GROUP_X])
        for q in range(0, GROUP_PAIRS, 2):
            lanes = slice(q * LANES, (q + 2) * LANES)
            wide = slice(jj * GROUP_X + q * LANES, jj * GROUP_X + (q + 2) * LANES)
            rise = widen_two(cols, 0, q)
            keep = widen_two(cols, HEADS, q)
            at = jj * GROUP_PAIRS + q
            state = jnp.concatenate([state_ref[0, at], state_ref[0, at + 1]], axis=1)
            exits = jnp.concatenate([state_ref[1, at], state_ref[1, at + 1]], axis=1)
            skip = jnp.concatenate([skip_rows[q : q + 1], skip_rows[q + 1 : q + 2]], axis=1)
            tot = jnp.concatenate([tot_rows[q : q + 1], tot_rows[q + 1 : q + 2]], axis=1)
            x = x_ref[:, lanes].astype(F32)
            g = g_ref[:, lanes].astype(F32)
            y = y_ref[:, lanes] + rise * dot(c, state)
            through = keep * dot(b, exits)
            gx = gx_ref[:, lanes] + through
            grad_c = grad_c + dot((g * rise).astype(BF16), state, NT)
            grad_b = grad_b + dot((x * keep).astype(BF16), exits, NT)
            out_ref[:, wide] = (y + skip * x).astype(BF16)
            grad_pre = (gx + skip * g) * slope_ref[:, lanes]
            pre_ref[:, wide] = grad_pre
            if theirs:
                at = pl.ds(pl.multiple_of(j * GROUP_X + q * LANES, 2 * LANES), 2 * LANES)
                head_ref[:, at] = grad_pre[0:8]
            terms += by_rows(tap_sums(grad_pre, q * LANES))
            x_gx = x * gx
            end = jnp.sum(x * through, axis=0, keepdims=True) + jnp.exp(tot) * jnp.sum(
                exits.astype(F32) * state.astype(F32), axis=0, keepdims=True
            )
            moved = g * y - x_gx
            moved = jnp.concatenate([moved[: T - 8], moved[T - 8 :] + jnp.where(last, end, 0.0)], axis=0)
            pick = (
                iota((GROUP_HEADS, 2 * LANES), 0)
                == 2 * q + iota((GROUP_HEADS, 2 * LANES), 1) // HEAD_DIM
            ).astype(F32).astype(BF16)
            for part in split_two(moved):
                seg_grad = seg_grad + dot(pick, part, NT)
            for part in split_two(x_gx):
                dt_grad = dt_grad + dot(pick, part, NT)
            if q % 4 == 2:
                size = GROUP_X // 2
                near_at = pl.ds(jj * GROUP_X + (q // 4) * size, size)
                far_at = span(2 * j + q // 4, size)
                save(out_ref.at[:, near_at], out_h.at[:, far_at])
        for grad, base in ((grad_b, 0), (grad_c, 1)):
            at = HALF_X + (base * HALF_GROUPS + jj) * STATE
            tail = slice(GROUP_X + base * STATE, GROUP_X + (base + 1) * STATE)
            far_at = span(WIDTH_X // STATE + base * GROUPS + j, STATE)
            fill_window(win_ref, before_ref[:, far_at], tok_ref[:, tail])
            grad_pre = grad * slope_ref[:, tail]
            pre_ref[:, at : at + STATE] = grad_pre
            if theirs:
                head_ref[:, far_at] = grad_pre[0:8]
            terms += tap_sums(grad_pre, 0)
        heads = span(j, GROUP_HEADS)
        behind = exact_dot(seg_grad, lower)
        dt = small_ref[pl.ds(pl.multiple_of(ROW_DT + j * GROUP_HEADS, GROUP_HEADS), GROUP_HEADS), :]
        decay = small_ref[pl.ds(pl.multiple_of(ROW_DECAY + j * GROUP_HEADS, GROUP_HEADS), GROUP_HEADS), :]
        near = pl.ds(jj * GROUP_HEADS, GROUP_HEADS)
        step_ref[near, :] = (dt_grad / dt + decay * behind) * sigmoid(raw_ref[heads, :])
        save(step_ref.at[near], step_h.at[heads])
        rows = jj * SUM_GROUP
        sum_ref[rows : rows + SUM_GROUP, :] = jnp.concatenate(terms + skips + [dt * behind * decay], axis=0)
    wait_all(fetches)
    if theirs:
        first_ref[...] = head_ref[0 : TAPS - 1, :].astype(BF16)
    wait_all(saves)


def run_leave(core, state, near, common, far, before_out):
    theirs = before_out is not None
    out = [
        ("h", (T, WIDTH_X), BF16),
        ("h", (HEADS, T), F32),
        ("V", (T, HALF_X + HALF_B), F32),
        ("V", (HALF_GROUPS * SUM_GROUP, LANES), F32),
    ]
    scratch = [
        pltpu.VMEM((T, HALF_X), BF16),
        pltpu.VMEM((HALF_GROUPS * GROUP_HEADS, T), F32),
        pltpu.VMEM((8 + T, GROUP_X), F32),
        DMA(2 + HALF_GROUPS, FETCHES),
    ]
    args = [core, state, *near, *common, *far]
    specs = "s" + ("v" if theirs else "V") + "V" * (len(near) + len(COMMON)) + "h" * len(far)
    aliases = {}
    if theirs:
        done, pre_own = before_out
        args += [pre_own]
        aliases = {len(args) + i: i for i in range(2)}
        args += done
        specs += "Vhh"
        out += [("V", (TAPS - 1, CHANNELS), BF16)]
        scratch = [pltpu.VMEM((8, CHANNELS), F32)] + scratch
    else:
        out += NEAR * HALF_GROUPS
    kernel = functools.partial(leave_kernel, theirs)
    outs = call(kernel, "leave", out, specs, 5, scratch, mib=8, aliases=aliases)(*args)
    return outs[:2], outs[2], outs[3], outs[4:]


def spread_kernel(core_ref, own_ref, theirs_ref, halo_ref, weight_ref, out_h, out_ref, win_ref, sems):
    saves = []
    size = HALF_GROUPS * STATE
    for side, pre_ref in enumerate((own_ref, theirs_ref)):
        half = 1 - core_ref[0] if side else core_ref[0]
        blocks = [(jj * GROUP_X, span(half * HALF_GROUPS + jj, GROUP_X), GROUP_X) for jj in range(HALF_GROUPS)]
        blocks += [
            (HALF_X + base * size, span(WIDTH_X // size + 2 * base + half, size), size) for base in range(2)
        ]
        for near, far, width in blocks:
            win_ref[0:T, 0:width] = pre_ref[:, near : near + width]
            win_ref[T : T + TAPS - 1, 0:width] = halo_ref[:, far].astype(F32)
            weights = weight_ref[:, far]
            base = side * (HALF_X + HALF_B) + near
            for lo in range(0, width, LANES):
                at = slice(lo, lo + LANES)
                acc = weights[0:1, at] * win_ref[3 : 3 + T, at]
                for k in range(1, TAPS):
                    acc = acc + weights[k : k + 1, at] * win_ref[3 - k : 3 - k + T, at]
                out_ref[:, base + lo : base + lo + LANES] = acc.astype(BF16)
            copy = pltpu.make_async_copy(out_ref.at[:, pl.ds(base, width)], out_h.at[:, far], sems.at[len(saves)])
            copy.start()
            saves.append(copy)
    wait_all(saves)


def run_spread(core, own, theirs, halo, weight):
    out = [("h", (T, CHANNELS), BF16)]
    scratch = [pltpu.VMEM((T, CHANNELS), BF16), pltpu.VMEM((T + 8, GROUP_X), F32), DMA(8)]
    return call(spread_kernel, "spread", out, "sVVvV", 3, scratch, mib=6)(core, own, theirs, halo, weight)[0]


CONV_ROWS = TAPS * (CHANNELS // LANES)
CONV_GROUP = CONV_ROWS // GROUPS
SEND_ROWS = CONV_ROWS + 16


def write_send(out_ref, conv, thin):
    high = thin.astype(BF16).astype(F32)
    low = thin - high
    row = iota((16, LANES), 0)
    out_ref[0:CONV_ROWS, :] = conv.astype(BF16)
    out_ref[CONV_ROWS:SEND_ROWS, :] = jnp.where(row == 0, high, jnp.where(row == 1, low, 0.0)).astype(BF16)


def read_send(value):
    wide = value.astype(F32)
    return wide[0:CONV_ROWS], wide[CONV_ROWS : CONV_ROWS + 1] + wide[CONV_ROWS + 1 : CONV_ROWS + 2]


def merge_kernel(core_ref, own_ref, own_got_ref, theirs_ref, theirs_got_ref, out_ref):
    thin = jnp.zeros((8, LANES), F32)
    left = iota((8, LANES), 1) < HEAD_DIM
    count = HEADS // 2
    parts = []
    for side, (mine, other) in enumerate(((own_ref, theirs_got_ref), (theirs_ref, own_got_ref))):
        half = 1 - core_ref[0] if side else core_ref[0]
        total = mine[...] + other[...]
        rows, skips, decays = [], [], []
        for jj in range(HALF_GROUPS):
            at = jj * SUM_GROUP
            rows.append(total[at : at + CONV_GROUP])
            skips.append(total[at + CONV_GROUP : at + SUM_GROUP - GROUP_HEADS])
            decays.append(total[at + SUM_GROUP - GROUP_HEADS : at + SUM_GROUP])
        skips = jnp.concatenate(skips, axis=0)
        even = exact_dot(jnp.where(left, 1.0, 0.0), skips, NT)
        odd = exact_dot(jnp.where(left, 0.0, 1.0), skips, NT)
        decay = exact_dot(jnp.ones((8, LANES), F32), jnp.concatenate(decays, axis=0), NT)
        for part, step, shift in ((even, 2, 0), (odd, 2, 1), (decay, 1, HEADS)):
            size = part.shape[1]
            spot = (iota((size, LANES), 1) == step * iota((size, LANES), 0) + shift + half * count).astype(F32)
            thin = thin + exact_dot(part, spot)
        parts.append(jnp.concatenate(rows, axis=0))
    first = core_ref[0] == 0
    conv = jnp.concatenate(
        [jnp.where(first, parts[0], parts[1]), jnp.where(first, parts[1], parts[0])], axis=0
    )
    write_send(out_ref, conv, thin[0:1])


def run_merge(core, own, own_got, theirs, theirs_got):
    out = [("v", (SEND_ROWS, LANES), BF16)]
    return call(merge_kernel, "merge", out, "svvvv", 1, mib=4)(core, own, own_got, theirs, theirs_got)[0]


def ring_sum(me_ref, hold_ref):
    count = hold_ref.shape[0]
    conv, thin = read_send(hold_ref[lax.rem(me_ref[0], count)])
    for k in range(1, count):
        more, little = read_send(hold_ref[lax.rem(me_ref[0] + count - k, count)])
        conv, thin = conv + more, thin + little
    return conv, thin


def fold_kernel(me_ref, *rest):
    *refs, out_ref, hold_ref = rest
    for d, ref in enumerate(refs):
        hold_ref[d] = ref[...]
    write_send(out_ref, *ring_sum(me_ref, hold_ref))


def run_fold(me, values):
    out = [("v", (SEND_ROWS, LANES), BF16)]
    scratch = [pltpu.VMEM((len(values), SEND_ROWS, LANES), BF16)]
    return call(fold_kernel, "fold", out, "s" + "v" * len(values), 1, scratch, mib=4)(me, *values)[0]


def finish_kernel(core_ref, me_ref, *rest):
    *refs, conv_ref, decay_ref, skip_ref, hold_ref = rest
    count = len(refs)
    sides = (count - 1) // 2
    hold_ref[0] = refs[0][...]
    for k in range(1, sides + 1):
        mine = jnp.where(core_ref[0] == 0, k, count - k)
        hold_ref[mine] = refs[k][...]
        hold_ref[count - mine] = refs[sides + k][...]
    if count % 2 == 0:
        hold_ref[count // 2] = refs[count - 1][...]
    conv, thin = ring_sum(me_ref, hold_ref)
    for i in range(CHANNELS // LANES):
        if i < PAIRS:
            row = CONV_GROUP * (i // GROUP_PAIRS) + TAPS * (i % GROUP_PAIRS)
        else:
            kind, group = divmod(i - PAIRS, GROUPS)
            row = CONV_GROUP * group + TAPS * (GROUP_PAIRS + kind)
        conv_ref[:, i * LANES : (i + 1) * LANES] = conv[row : row + TAPS]
    skip_ref[...] = thin[:, 0:HEADS]
    decay_ref[...] = thin[:, HEADS:]


def run_finish(core, me, values):
    out = [("v", (TAPS, CHANNELS), F32), ("v", (1, HEADS), F32), ("v", (1, HEADS), F32)]
    scratch = [pltpu.VMEM((len(values), SEND_ROWS, LANES), BF16)]
    return call(finish_kernel, "finish", out, "ss" + "v" * len(values), 1, scratch, mib=4)(core, me, *values)


CTX = ("chip", "core")
ALL = ("dp", "chip", "core")


def all_to_all(value, axis):
    return lax.all_to_all(value, axis, 0, 0, tiled=True)


def tie(*values):
    return lax.optimization_barrier(values)


SIDE = 4


def around(value, axis, count, ring, move):
    return [value] + [
        lax.ppermute(value, axis, [(i, move(i, d)) for i in range(count)]) for d in range(1, ring)
    ]


def around_by_sides(value, count):
    def shifts(first, second):
        return [
            (2 * i + side, 2 * ((i + move) % count) + side)
            for i in range(count)
            for side, move in enumerate((first, second))
        ]

    def hear(first, second):
        return lax.ppermute(value, ("dp", "core"), shifts(first, second))

    middle = [hear(count // 2, count // 2)] if count % 2 == 0 else []
    heard = [hear(k, -k) for k in range((count - 1) // 2, 0, -1)][::-1]
    swapped = [lax.ppermute(part, "core", [(0, 1), (1, 0)]) for part in heard]
    return [value] + heard + swapped + middle


def scalar(value):
    return value.astype(jnp.int32).reshape(1)


def local(conv_input, conv_weight, step_raw, decay_log, skip_gain, cotangent):
    chips = lax.axis_size("chip")
    devices = 2 * chips
    sequences = lax.axis_size("dp")
    tokens = conv_input[0]
    raw = step_raw[0]
    cot = cotangent[0]
    core = lax.axis_index("core").astype(jnp.int32).reshape(1)
    swap = [(0, 1), (1, 0)]
    halo = lax.ppermute(tokens[T - TAPS + 1 :], CTX, [(i, i + 1) for i in range(devices - 1)])
    small, small_near, tot, x0, bc0, head, weight_near, cot_near = run_begin(
        raw, decay_log.reshape(1, HEADS), skip_gain.reshape(1, HEADS), tokens, conv_weight, cot
    )
    other = lax.ppermute(tot, "core", swap)
    x, bc, before, x_near, bc_near, out = run_enter(
        core, x0, bc0, head, halo, weight_near, cot_near, small_near
    )
    got_near = lax.ppermute(out, "core", swap)
    own_near = run_own(core, x_near, bc_near, cot_near, small_near)
    packed, left, right, tots = run_pack(core, own_near, got_near, tot, other)
    heard = all_to_all(packed, "chip")
    y, gbc, skips = run_inner(x, bc, cot, small)
    heard, y, gbc, skips = tie(heard, y, gbc, skips)
    chained = run_chain(chips, heard)
    late, chained = tie(bc, chained)
    back = all_to_all(chained, "chip")
    gx, slope = run_slopes(late, cot, small, tokens, before, conv_weight)
    back, gx, slope = tie(back, gx, slope)
    far = (x, cot, y, gx, slope, tokens, bc, gbc)
    mine, send, near, common = run_unpack(
        core, back, left, right, tots, far, (before, small, raw, skips, conv_weight)
    )
    theirs = lax.ppermute(send, "core", swap)
    half, pre_own, sum_own, near = run_leave(core, mine, near, common, far, None)
    sum_own_got = lax.ppermute(sum_own, "core", swap)
    (out_tokens, grad_step), pre_theirs, sum_theirs, (first,) = run_leave(
        core, theirs, near, common, (), (half, pre_own)
    )
    sum_theirs_got = lax.ppermute(sum_theirs, "core", swap)
    sums = run_merge(core, sum_own, sum_own_got, sum_theirs, sum_theirs_got)
    chip = lax.axis_index("chip")
    values = around(sums, "chip", chips, SIDE, lambda i, d: i // SIDE * SIDE + (i % SIDE + d) % SIDE)
    sums, first = tie(run_fold(scalar(lax.rem(chip, SIDE)), values), first)
    after = lax.ppermute(first, CTX, [(i + 1, i) for i in range(devices - 1)])
    values = around(sums, "chip", chips, chips // SIDE, lambda i, d: (i + d * SIDE) % chips)
    sums, after = tie(run_fold(scalar(lax.div(chip, SIDE)), values), after)
    values = around_by_sides(sums, sequences)
    grad_tokens = run_spread(core, pre_own, pre_theirs, after, common[4])
    values, grad_tokens = tie(values, grad_tokens)
    grad_conv, grad_decay, grad_skip = run_finish(core, scalar(lax.axis_index("dp")), values)
    return (
        out_tokens[None],
        grad_tokens[None],
        grad_step[None],
        grad_conv,
        grad_decay.reshape(HEADS),
        grad_skip.reshape(HEADS),
    )


def solution(mesh):
    dp, ctx = mesh.devices.shape
    fine = Mesh(mesh.devices.reshape(dp, ctx // 2, 2), ALL)
    seq = P("dp", CTX, None)
    rate = P("dp", None, CTX)
    in_specs = (seq, P(), rate, P(), P(), seq)
    out_specs = (seq, seq, rate, P(), P(), P())
    return jax.shard_map(local, mesh=fine, in_specs=in_specs, out_specs=out_specs, check_vma=False)
```

```python
import functools

import jax
import jax.numpy as jnp
from jax import lax
from jax.experimental import pallas as pl
from jax.experimental.pallas import tpu as pltpu
from jax.sharding import Mesh
from jax.sharding import PartitionSpec as P

HEADS = 64
HEAD_DIM = 64
GROUPS = 4
STATE = 128
TAPS = 4
T = 128
LANES = 128
WIDTH_X = HEADS * HEAD_DIM
WIDTH_B = GROUPS * STATE
CHANNELS = WIDTH_X + 2 * WIDTH_B
GROUP_X = WIDTH_X // GROUPS
PAIRS = HEADS // 2
GROUP_PAIRS = PAIRS // GROUPS
GROUP_HEADS = HEADS // GROUPS
HALF_PAIRS = PAIRS // 2
HALF_GROUPS = GROUPS // 2
F32 = jnp.float32
BF16 = jnp.bfloat16
EXACT = lax.Precision.HIGHEST
NN = (((1,), (0,)), ((), ()))
NT = (((1,), (1,)), ((), ()))
SUM_GROUP = 64
PACK_ROWS = 2 * STATE + 16


def dot(a, b, dims=NN):
    return lax.dot_general(a, b, dims, preferred_element_type=F32)


def exact_dot(a, b, dims=NN):
    return lax.dot_general(a, b, dims, precision=EXACT, preferred_element_type=F32)


def iota(shape, dim):
    return lax.broadcasted_iota(jnp.int32, shape, dim)


def sigmoid(v):
    return 0.5 + 0.5 * jnp.tanh(0.5 * v)


def split_two(v):
    high = v.astype(BF16)
    return high, (v - high.astype(F32)).astype(BF16)


def span(index, size):
    return pl.ds(pl.multiple_of(index * size, size), size)


def pin(value, space):
    return pltpu.with_memory_space_constraint(value, space)


def placed(space, shape, dtype):
    return space(shape, dtype)


def call(kernel, name, outs, specs, micros, scratch=(), mib=28, aliases=None):
    cost = pl.CostEstimate(
        flops=int(micros * 1e9), transcendentals=0, bytes_accessed=int(micros * 3.6e6)
    )
    blocks = {
        "s": pl.BlockSpec(memory_space=pltpu.SMEM),
        "v": pl.BlockSpec(memory_space=pltpu.VMEM),
        "V": pl.BlockSpec(memory_space=pltpu.VMEM),
        "h": pl.BlockSpec(memory_space=pltpu.HBM),
    }
    spaces = {"V": pltpu.VMEM, "h": pltpu.HBM}
    shapes = [
        placed(spaces[p], shape, dtype) if p in spaces else jax.ShapeDtypeStruct(shape, dtype)
        for p, shape, dtype in outs
    ]
    run = pl.pallas_call(
        kernel,
        out_shape=shapes,
        in_specs=[blocks[p] for p in specs],
        out_specs=[blocks[p] for p, _, _ in outs],
        scratch_shapes=list(scratch),
        input_output_aliases=aliases or {},
        cost_estimate=cost,
        compiler_params=pltpu.CompilerParams(vmem_limit_bytes=mib << 20),
        name=name,
    )

    def go(*args):
        return run(*[pin(a, spaces[p]) if p in spaces else a for a, p in zip(args, specs, strict=True)])

    return go


def start_all(pairs, sems):
    copies = [pltpu.make_async_copy(a, b, sems.at[i]) for i, (a, b) in enumerate(pairs)]
    for copy in copies:
        copy.start()
    return copies


def wait_all(copies):
    for copy in copies:
        copy.wait()


def DMA(*shape):
    return pltpu.SemaphoreType.DMA(shape)


def fill_window(win_ref, before, tokens):
    width = tokens.shape[1]
    win_ref[0:8, :width] = before
    win_ref[8 : 8 + T, :width] = tokens.astype(F32)


def pre_conv(win_ref, weights, lo):
    cols = slice(lo, lo + LANES)
    acc = weights[0:1, cols] * win_ref[5 : 5 + T, cols]
    for k in range(1, TAPS):
        acc = acc + weights[k : k + 1, cols] * win_ref[5 + k : 5 + k + T, cols]
    return acc


BLOCKS = CHANNELS // GROUP_X


ROW_DT, ROW_SEG, ROW_COLS, ROW_SCALE, ROW_TOT, ROW_SKIP, ROW_DECAY, SMALL_ROWS = (
    0, 64, 128, 256, 384, 416, 448, 512
)


def begin_kernel(raw_h, decay_log_h, skip_gain_h, tok_h, weight_h, g_h,
                 small_h, small_ref, tot_ref, x_ref, bc_ref, head_ref, weight_ref, g_ref,
                 raw_ref, decay_log_ref, skip_gain_ref, wide_ref, hold_ref, win_ref, sems):
    first = start_all(
        [(raw_h, raw_ref), (decay_log_h, decay_log_ref), (skip_gain_h, skip_gain_ref), (weight_h, weight_ref)],
        sems.at[0],
    )
    blocks = [pl.ds(i * GROUP_X, GROUP_X) for i in range(BLOCKS)]
    copies = start_all([(tok_h.at[:, at], hold_ref.at[:, at]) for at in blocks], sems.at[1])
    later = start_all([(g_h, g_ref)], sems.at[2])
    win_ref[0:8, :] = jnp.zeros((8, GROUP_X), F32)
    copies[0].wait()
    diagonal = iota((HEADS, HEADS), 0) == iota((HEADS, HEADS), 1)

    def column(row):
        return jnp.sum(jnp.where(diagonal, row, 0.0), axis=1, keepdims=True)

    wait_all(first)
    raw = raw_ref[...]
    dt = jnp.log1p(jnp.exp(raw))
    decay = -jnp.exp(column(decay_log_ref[...]))
    upper = (iota((T, T), 0) <= iota((T, T), 1)).astype(F32)
    seg = exact_dot(dt * decay, upper)
    total = seg[:, T - 1 : T]
    small_ref[ROW_DT : ROW_DT + HEADS] = dt
    small_ref[ROW_SEG : ROW_SEG + HEADS] = seg
    small_ref[ROW_COLS : ROW_COLS + T] = jnp.transpose(jnp.concatenate([seg, dt], axis=0))
    small_ref[ROW_SCALE : ROW_SCALE + T] = jnp.transpose(
        jnp.concatenate([jnp.exp(seg), jnp.exp(total - seg) * dt], axis=0)
    )
    left = iota((PAIRS, LANES), 1) < HEAD_DIM

    def paired(col):
        wide_ref[...] = jnp.broadcast_to(col, (HEADS, LANES))
        return jnp.where(left, wide_ref[pl.ds(0, PAIRS, 2), :], wide_ref[pl.ds(1, PAIRS, 2), :])

    tot = paired(total)
    tot_ref[...] = tot
    small_ref[ROW_TOT : ROW_TOT + PAIRS] = tot
    small_ref[ROW_SKIP : ROW_SKIP + PAIRS] = paired(column(skip_gain_ref[...]))
    small_ref[ROW_DECAY : ROW_DECAY + HEADS] = jnp.broadcast_to(decay, (HEADS, LANES))
    save = start_all([(small_ref, small_h)], sems.at[0])
    for i in range(BLOCKS):
        if i:
            copies[i].wait()
        cols = slice(i * GROUP_X, (i + 1) * GROUP_X)
        win_ref[8 : 8 + T, :] = hold_ref[:, cols].astype(F32)
        for lo in range(0, GROUP_X, LANES):
            at = i * GROUP_X + lo
            pre = pre_conv(win_ref, weight_ref[:, cols], lo)
            mixed = (pre * sigmoid(pre)).astype(BF16)
            head_ref[:, at : at + LANES] = pre[0:8]
            if at < WIDTH_X:
                x_ref[:, at : at + LANES] = mixed
            else:
                bc_ref[:, at - WIDTH_X : at - WIDTH_X + LANES] = mixed
    wait_all(save + later)


def run_begin(raw, decay_log, skip_gain, tokens, weight, cot):
    out = [
        ("h", (SMALL_ROWS, LANES), F32),
        ("V", (SMALL_ROWS, LANES), F32),
        ("V", (PAIRS, LANES), F32),
        ("V", (T, WIDTH_X), BF16),
        ("V", (T, 2 * WIDTH_B), BF16),
        ("V", (8, CHANNELS), F32),
        ("V", (TAPS, CHANNELS), F32),
        ("V", (T, WIDTH_X), BF16),
    ]
    scratch = [
        pltpu.VMEM((HEADS, T), F32),
        pltpu.VMEM((1, HEADS), F32),
        pltpu.VMEM((1, HEADS), F32),
        pltpu.VMEM((HEADS, LANES), F32),
        pltpu.VMEM((T, CHANNELS), BF16),
        pltpu.VMEM((8 + T, GROUP_X), F32),
        DMA(3, BLOCKS),
    ]
    return call(begin_kernel, "begin", out, "hhhhhh", 4, scratch, mib=8)(
        raw, decay_log, skip_gain, tokens, weight, cot
    )


def rolled(cols, group):
    return pltpu.roll(cols, (LANES - group * GROUP_HEADS) % LANES, 1)


def widen(cols, base, pair):
    first = iota((T, LANES), 1) < HEAD_DIM
    at = base + 2 * pair
    return jnp.where(first, cols[:, at : at + 1], cols[:, at + 1 : at + 2])


def widen_two(cols, base, pair):
    return jnp.concatenate([widen(cols, base, pair), widen(cols, base, pair + 1)], axis=1)


def fill_half(half, x_ref, bc_ref, g_ref, scale, dst_ref):
    for jj in range(HALF_GROUPS):
        j = half * HALF_GROUPS + jj
        b_flip = jnp.transpose(bc_ref[:, span(j, STATE)].astype(F32)).astype(BF16)
        c_flip = jnp.transpose(bc_ref[:, span(GROUPS + j, STATE)].astype(F32)).astype(BF16)
        cols = rolled(scale, j)
        for q in range(0, GROUP_PAIRS, 2):
            lanes = pl.ds(pl.multiple_of(j * GROUP_X + q * LANES, 2 * LANES), 2 * LANES)
            xw = (x_ref[:, lanes].astype(F32) * widen_two(cols, HEADS, q)).astype(BF16)
            gw = (g_ref[:, lanes].astype(F32) * widen_two(cols, 0, q)).astype(BF16)
            state = dot(b_flip, xw).astype(BF16)
            grad = dot(c_flip, gw).astype(BF16)
            for k in range(2):
                at = jj * GROUP_PAIRS + q + k
                dst_ref[0, at] = state[:, k * LANES : (k + 1) * LANES]
                dst_ref[1, at] = grad[:, k * LANES : (k + 1) * LANES]


def enter_kernel(core_ref, x0_ref, bc0_ref, head_ref, halo_ref, weight_ref, g_ref, small_ref,
                 x_h, bc_h, before_h, x_ref, bc_ref, out_ref, before_ref, sems):
    half = 1 - core_ref[0]
    row = iota((8, GROUP_X), 0)
    for i in range(BLOCKS):
        cols = slice(i * GROUP_X, (i + 1) * GROUP_X)
        halo = halo_ref[:, cols].astype(F32)
        weight = weight_ref[:, cols]
        pre = head_ref[:, cols]
        before = jnp.zeros((8, GROUP_X), F32)
        for t in range(TAPS - 1):
            extra = jnp.zeros((1, GROUP_X), F32)
            for k in range(TAPS - 1 - t):
                extra = extra + weight[k : k + 1] * halo[t + k : t + k + 1]
            pre = pre + jnp.where(row == t, extra, 0.0)
            before = before + jnp.where(row == t + 5, halo[t : t + 1], 0.0)
        before_ref[:, cols] = before
        fixed = pre * sigmoid(pre)
        src, dst, at = (x0_ref, x_ref, cols) if i < GROUPS else (bc0_ref, bc_ref, slice(0, GROUP_X))
        rest = src[0:16, at].astype(F32)
        dst[16:T, at] = src[16:T, at]
        dst[0:16, at] = jnp.concatenate([fixed, rest[8:16]], axis=0).astype(BF16)
    saves = start_all([(x_ref, x_h), (bc_ref, bc_h), (before_ref, before_h)], sems)
    fill_half(half, x_ref, bc_ref, g_ref, small_ref[ROW_SCALE : ROW_SCALE + T], out_ref)
    wait_all(saves)


def run_enter(core, x0, bc0, head, halo, weight, cot, small):
    out = [
        ("h", (T, WIDTH_X), BF16),
        ("h", (T, 2 * WIDTH_B), BF16),
        ("h", (8, CHANNELS), F32),
        ("V", (T, WIDTH_X), BF16),
        ("V", (T, 2 * WIDTH_B), BF16),
        ("V", (2, HALF_PAIRS, STATE, LANES), BF16),
    ]
    scratch = [pltpu.VMEM((8, CHANNELS), F32), DMA(3)]
    return call(enter_kernel, "enter", out, "sVVVvVVV", 3, scratch, mib=6)(
        core, x0, bc0, head, halo, weight, cot, small
    )


def own_kernel(core_ref, x_ref, bc_ref, g_ref, small_ref, own_ref):
    fill_half(core_ref[0], x_ref, bc_ref, g_ref, small_ref[ROW_SCALE : ROW_SCALE + T], own_ref)


def run_own(core, x, bc, cot, small):
    out = [("V", (2, HALF_PAIRS, STATE, LANES), BF16)]
    return call(own_kernel, "own", out, "sVVVV", 3, mib=6)(core, x, bc, cot, small)[0]


STEP_PAIRS = 4
STEPS = HALF_PAIRS // STEP_PAIRS


def pack_kernel(core_ref, own_ref, got_ref, tot_ref, other_ref,
                out_h, left_h, right_h, tots_h, out_ref, sems):
    saves = start_all(
        [(tot_ref, tots_h.at[pl.ds(0, PAIRS)]), (other_ref, tots_h.at[pl.ds(PAIRS, PAIRS)])], sems.at[0]
    )
    second = core_ref[0] == 1

    def keep(first_ref, last_ref):
        return [
            pltpu.make_async_copy(first_ref.at[0], left_h, sems.at[0, 2]),
            pltpu.make_async_copy(last_ref.at[1], right_h, sems.at[0, 3]),
        ]

    @pl.when(second)
    def _():
        for copy in keep(got_ref, own_ref):
            copy.start()

    @pl.when(jnp.logical_not(second))
    def _():
        for copy in keep(own_ref, got_ref):
            copy.start()

    saves += keep(own_ref, got_ref)
    outs = []
    for i in range(HALF_PAIRS):
        at = core_ref[0] * HALF_PAIRS + i
        tot = tot_ref[pl.ds(at, 1), :]
        other = other_ref[pl.ds(at, 1), :]
        one = jnp.ones_like(tot)
        by_own = jnp.exp(tot)
        by_other = jnp.exp(other)
        state = (
            jnp.where(second, one, by_other) * own_ref[0, i].astype(F32)
            + jnp.where(second, by_own, one) * got_ref[0, i].astype(F32)
        )
        grad = (
            jnp.where(second, by_other, one) * own_ref[1, i].astype(F32)
            + jnp.where(second, one, by_own) * got_ref[1, i].astype(F32)
        )
        out_ref[i, 0:STATE, :] = state.astype(BF16)
        out_ref[i, STATE : 2 * STATE, :] = grad.astype(BF16)
        both = tot + other
        high = both.astype(BF16).astype(F32)
        mid = (both - high).astype(BF16).astype(F32)
        low = both - high - mid
        row = iota((16, LANES), 0)
        wide = jnp.where(row == 0, high, jnp.where(row == 1, mid, jnp.where(row == 2, low, 0.0)))
        out_ref[i, 2 * STATE : PACK_ROWS, :] = wide.astype(BF16)
        if i % STEP_PAIRS == STEP_PAIRS - 1:
            done = pl.ds(i + 1 - STEP_PAIRS, STEP_PAIRS)
            copy = pltpu.make_async_copy(out_ref.at[done], out_h.at[done], sems.at[1, i // STEP_PAIRS])
            copy.start()
            outs.append(copy)
    wait_all(outs + saves)


def run_pack(core, own, got, tot, other):
    half = (HALF_PAIRS, STATE, LANES)
    packed = (HALF_PAIRS, PACK_ROWS, LANES)
    out = [("h", packed, BF16), ("h", half, BF16), ("h", half, BF16), ("h", (2 * PAIRS, LANES), F32)]
    scratch = [pltpu.VMEM(packed, BF16), DMA(2, STEPS)]
    return call(pack_kernel, "pack", out, "sVvVv", 2, scratch, mib=8)(core, own, got, tot, other)


def chain_kernel(chips, per, in_ref, out_ref):
    for q in range(per):
        def decay(k):
            rows = in_ref[k * per + q, 2 * STATE : PACK_ROWS, :].astype(F32)
            return jnp.exp(rows[0:1] + rows[1:2] + rows[2:3])

        carry = jnp.zeros((STATE, LANES), F32)
        for k in range(chips):
            out_ref[k * per + q, 0:STATE, :] = carry.astype(BF16)
            if k < chips - 1:
                carry = decay(k) * carry + in_ref[k * per + q, 0:STATE, :].astype(F32)
        carry = jnp.zeros((STATE, LANES), F32)
        for k in reversed(range(chips)):
            out_ref[k * per + q, STATE : 2 * STATE, :] = carry.astype(BF16)
            if k > 0:
                carry = decay(k) * carry + in_ref[k * per + q, STATE : 2 * STATE, :].astype(F32)


def run_chain(chips, packed):
    kernel = functools.partial(chain_kernel, chips, HALF_PAIRS // chips)
    out = [("v", (HALF_PAIRS, 2 * STATE, LANES), BF16)]
    return call(kernel, "chain", out, "v", 1, mib=8)(packed)[0]


HALF_X = HALF_GROUPS * GROUP_X
HALF_B = 2 * HALF_GROUPS * STATE

NEAR = [
    ("V", (T, GROUP_X), BF16),
    ("V", (T, GROUP_X), BF16),
    ("V", (T, GROUP_X), F32),
    ("V", (T, GROUP_X), F32),
    ("V", (T, GROUP_X + 2 * STATE), F32),
    ("V", (T, GROUP_X + 2 * STATE), BF16),
    ("V", (T, 2 * STATE), BF16),
    ("V", (T, 2 * STATE), F32),
]
COMMON = [
    ("V", (8, CHANNELS), F32),
    ("V", (SMALL_ROWS, LANES), F32),
    ("V", (HEADS, T), F32),
    ("V", (PAIRS, LANES), F32),
    ("V", (TAPS, CHANNELS), F32),
]
FETCHES = 6 + 8


def fetch_group(j, far, near, sems):
    x_h, g_h, y_h, gx_h, slope_h, tok_h, bc_h, gbc_h = far
    x_v, g_v, y_v, gx_v, slope_v, tok_v, bc_v, gbc_v = near
    wide = pl.ds(0, GROUP_X)
    pairs = [
        (a.at[:, span(j, GROUP_X)], b.at[:, wide])
        for a, b in ((x_h, x_v), (g_h, g_v), (y_h, y_v), (gx_h, gx_v), (slope_h, slope_v), (tok_h, tok_v))
    ]
    for base in range(2):
        at = span(base * GROUPS + j, STATE)
        off = span(WIDTH_X // STATE + base * GROUPS + j, STATE)
        thin = pl.ds(base * STATE, STATE)
        tail = pl.ds(GROUP_X + base * STATE, STATE)
        pairs += [
            (bc_h.at[:, at], bc_v.at[:, thin]),
            (gbc_h.at[:, at], gbc_v.at[:, thin]),
            (slope_h.at[:, off], slope_v.at[:, tail]),
            (tok_h.at[:, off], tok_v.at[:, tail]),
        ]
    return start_all(pairs, sems)


def unpack_kernel(core_ref, back_ref, left_h, right_h, tots_h, *rest):
    far, rest = rest[: len(NEAR)], rest[len(NEAR) :]
    common_far, rest = rest[: len(COMMON)], rest[len(COMMON) :]
    mine_ref, send_ref, *rest = rest
    near, rest = rest[: len(NEAR)], rest[len(NEAR) :]
    common, rest = rest[: len(COMMON)], rest[len(COMMON) :]
    left_ref, right_ref, tots_ref, sems, fetch_sems = rest
    first = start_all([(tots_h, tots_ref)], sems.at[STEPS])
    steps = []
    for step in range(STEPS):
        at = pl.ds(step * STEP_PAIRS, STEP_PAIRS)
        steps.append(
            start_all([(left_h.at[at], left_ref.at[at]), (right_h.at[at], right_ref.at[at])], sems.at[step])
        )
    fetches = start_all(list(zip(common_far, common)), fetch_sems.at[1])
    fetches += fetch_group(core_ref[0] * HALF_GROUPS, far, near, fetch_sems.at[0])
    wait_all(first)
    second = core_ref[0] == 1
    for i in range(HALF_PAIRS):
        if i % STEP_PAIRS == 0:
            wait_all(steps[i // STEP_PAIRS])
        at = core_ref[0] * HALF_PAIRS + i
        tot = tots_ref[pl.ds(at, 1), :]
        other = tots_ref[pl.ds(PAIRS + at, 1), :]
        decay_zero = jnp.exp(jnp.where(second, other, tot))
        decay_one = jnp.exp(jnp.where(second, tot, other))
        state_zero = back_ref[i, 0:STATE, :].astype(F32)
        grad_one = back_ref[i, STATE : 2 * STATE, :].astype(F32)
        state_one = decay_zero * state_zero + left_ref[i].astype(F32)
        grad_zero = decay_one * grad_one + right_ref[i].astype(F32)
        mine_ref[0, i] = jnp.where(second, state_one, state_zero).astype(BF16)
        mine_ref[1, i] = jnp.where(second, grad_one, grad_zero).astype(BF16)
        send_ref[0, i] = jnp.where(second, state_zero, state_one).astype(BF16)
        send_ref[1, i] = jnp.where(second, grad_zero, grad_one).astype(BF16)
    wait_all(fetches)


def run_unpack(core, back, left, right, tots, far, common):
    half = (2, HALF_PAIRS, STATE, LANES)
    out = [("V", half, BF16)] * 2 + NEAR + COMMON
    scratch = [
        pltpu.VMEM(half[1:], BF16),
        pltpu.VMEM(half[1:], BF16),
        pltpu.VMEM((2 * PAIRS, LANES), F32),
        DMA(STEPS + 1, 2),
        DMA(2, FETCHES),
    ]
    specs = "svhhh" + "h" * (len(NEAR) + len(COMMON))
    outs = call(unpack_kernel, "unpack", out, specs, 3, scratch, mib=8)(
        core, back, left, right, tots, *far, *common
    )
    at = 2 + len(NEAR)
    return outs[0], outs[1], outs[2:at], outs[at:]


def by_lane_half(v):
    first = iota(v.shape, 1) < HEAD_DIM
    wide = v.astype(F32)
    return jnp.concatenate(
        [jnp.where(first, wide, 0.0).astype(BF16), jnp.where(first, 0.0, wide).astype(BF16)], axis=0
    )


def inner_kernel(x_h, bc_h, g_h, small_h, y_h, gbc_h, skips_h,
                 x_ref, bc_ref, g_ref, small_ref, y_ref, gbc_ref, skips_ref, sems):
    first = start_all([(bc_h, bc_ref), (small_h, small_ref)], sems.at[0])

    def loads(j):
        at = span(j, GROUP_X)
        return [
            pltpu.make_async_copy(x_h.at[:, at], x_ref.at[:, at], sems.at[1, j]),
            pltpu.make_async_copy(g_h.at[:, at], g_ref.at[:, at], sems.at[2, j]),
        ]

    def store(j):
        at = span(j, GROUP_X)
        return pltpu.make_async_copy(y_ref.at[:, at], y_h.at[:, at], sems.at[3, j])

    for j in range(GROUPS):
        for copy in loads(j):
            copy.start()
    wait_all(first)
    lower = iota((T, T), 0) >= iota((T, T), 1)

    @pl.loop(0, GROUPS)
    def _(j):
        wait_all(loads(j))
        b = bc_ref[:, span(j, STATE)]
        c = bc_ref[:, span(GROUPS + j, STATE)]
        seg = small_ref[pl.ds(pl.multiple_of(ROW_SEG + j * GROUP_HEADS, GROUP_HEADS), GROUP_HEADS), :]
        dt = small_ref[pl.ds(pl.multiple_of(ROW_DT + j * GROUP_HEADS, GROUP_HEADS), GROUP_HEADS), :]
        scores = dot(c, b, NT)
        cols = rolled(small_ref[ROW_COLS : ROW_COLS + T], j)
        total = jnp.zeros((T, T), F32)
        skips = []
        for i in range(GROUP_PAIRS):
            lanes = pl.ds(pl.multiple_of(j * GROUP_X + i * LANES, LANES), LANES)
            x = x_ref[:, lanes]
            g = g_ref[:, lanes]
            skips.append(jnp.sum(g.astype(F32) * x.astype(F32), axis=0, keepdims=True))
            inner = dot(by_lane_half(g), x, NT)
            weights = []
            for k in range(2):
                h = 2 * i + k
                spread = cols[:, h : h + 1] - seg[h : h + 1, :]
                kernel = jnp.exp(jnp.where(lower, spread, -1e30)) * dt[h : h + 1, :]
                total = total + kernel * inner[k * T : (k + 1) * T]
                weights.append((kernel * scores).astype(BF16))
            y_ref[:, lanes] = dot(jnp.concatenate(weights, axis=1), by_lane_half(x))
        skips_ref[span(j, GROUP_PAIRS), :] = jnp.concatenate(skips, axis=0)
        gbc_ref[:, span(GROUPS + j, STATE)] = dot(total.astype(BF16), b)
        gbc_ref[:, span(j, STATE)] = dot(jnp.transpose(total).astype(BF16), c)
        store(j).start()

    last = start_all([(gbc_ref, gbc_h), (skips_ref, skips_h)], sems.at[0])
    for j in range(GROUPS):
        store(j).wait()
    wait_all(last)


def run_inner(x, bc, cot, small):
    out = [("h", (T, WIDTH_X), F32), ("h", (T, 2 * WIDTH_B), F32), ("h", (PAIRS, LANES), F32)]
    scratch = [
        pltpu.VMEM((T, WIDTH_X), BF16),
        pltpu.VMEM((T, 2 * WIDTH_B), BF16),
        pltpu.VMEM((T, WIDTH_X), BF16),
        pltpu.VMEM((SMALL_ROWS, LANES), F32),
        pltpu.VMEM((T, WIDTH_X), F32),
        pltpu.VMEM((T, 2 * WIDTH_B), F32),
        pltpu.VMEM((PAIRS, LANES), F32),
        DMA(4, GROUPS),
    ]
    return call(inner_kernel, "inner", out, "hhhh", 4, scratch, mib=16)(x, bc, cot, small)


def slopes_kernel(bc_h, g_h, small_h, tok_h, before_h, weight_h, gx_h, slope_h,
                  bc_ref, g_ref, small_ref, tok_ref, before_ref, weight_ref, gx_ref, slope_ref, win_ref, sems):
    first = start_all(
        [(bc_h, bc_ref), (small_h, small_ref), (before_h, before_ref), (weight_h, weight_ref), (tok_h, tok_ref)],
        sems.at[0],
    )

    def load(j):
        at = span(j, GROUP_X)
        return pltpu.make_async_copy(g_h.at[:, at], g_ref.at[:, at], sems.at[1, j])

    def store(j):
        at = span(j, GROUP_X)
        return pltpu.make_async_copy(gx_ref.at[:, at], gx_h.at[:, at], sems.at[2, j])

    def store_slope(i):
        at = span(i, GROUP_X)
        return pltpu.make_async_copy(slope_ref.at[:, at], slope_h.at[:, at], sems.at[3, i])

    for j in range(GROUPS):
        load(j).start()
    wait_all(first)
    upper = iota((T, T), 0) <= iota((T, T), 1)

    @pl.loop(0, GROUPS)
    def _(j):
        load(j).wait()
        b = bc_ref[:, span(j, STATE)]
        c = bc_ref[:, span(GROUPS + j, STATE)]
        seg = small_ref[pl.ds(pl.multiple_of(ROW_SEG + j * GROUP_HEADS, GROUP_HEADS), GROUP_HEADS), :]
        scores = jnp.transpose(dot(c, b, NT))
        cols = rolled(small_ref[ROW_COLS : ROW_COLS + T], j)
        for i in range(GROUP_PAIRS):
            lanes = pl.ds(pl.multiple_of(j * GROUP_X + i * LANES, LANES), LANES)
            weights = []
            for k in range(2):
                h = 2 * i + k
                spread = seg[h : h + 1, :] - cols[:, h : h + 1]
                kernel = jnp.exp(jnp.where(upper, spread, -1e30)) * cols[:, HEADS + h : HEADS + h + 1]
                weights.append((kernel * scores).astype(BF16))
            gx_ref[:, lanes] = dot(jnp.concatenate(weights, axis=1), by_lane_half(g_ref[:, lanes]))
        store(j).start()

    @pl.loop(0, BLOCKS)
    def _(i):
        cols = span(i, GROUP_X)
        fill_window(win_ref, before_ref[:, cols], tok_ref[:, cols])
        weights = weight_ref[:, cols]
        for lo in range(0, GROUP_X, LANES):
            pre = pre_conv(win_ref, weights, lo)
            s = sigmoid(pre)
            at = pl.ds(pl.multiple_of(i * GROUP_X + lo, LANES), LANES)
            slope_ref[:, at] = s * (1.0 + pre * (1.0 - s))
        store_slope(i).start()

    for j in range(GROUPS):
        store(j).wait()
    for i in range(BLOCKS):
        store_slope(i).wait()


def run_slopes(bc, cot, small, tokens, before, weight):
    out = [("h", (T, WIDTH_X), F32), ("h", (T, CHANNELS), F32)]
    scratch = [
        pltpu.VMEM((T, 2 * WIDTH_B), BF16),
        pltpu.VMEM((T, WIDTH_X), BF16),
        pltpu.VMEM((SMALL_ROWS, LANES), F32),
        pltpu.VMEM((T, CHANNELS), BF16),
        pltpu.VMEM((8, CHANNELS), F32),
        pltpu.VMEM((TAPS, CHANNELS), F32),
        pltpu.VMEM((T, WIDTH_X), F32),
        pltpu.VMEM((T, CHANNELS), F32),
        pltpu.VMEM((8 + T, GROUP_X), F32),
        DMA(4, BLOCKS),
    ]
    return call(slopes_kernel, "slopes", out, "hhhhhh", 6, scratch, mib=16)(
        bc, cot, small, tokens, before, weight
    )


def leave_kernel(theirs, core_ref, state_ref, *rest):
    rest = list(rest)

    def take(count):
        taken = rest[:count]
        del rest[:count]
        return taken

    sets = [take(len(NEAR))]
    before_ref, small_ref, raw_ref, skips_ref, _ = take(len(COMMON))
    far = take(len(NEAR))
    half = 1 - core_ref[0] if theirs else core_ref[0]
    if theirs:
        take(3)
        out_h, pre_h, step_h, sum_ref, first_ref = take(5)
        head_ref, = take(1)
    else:
        out_h, pre_h, step_h, sum_ref = take(4)
        after = take(len(NEAR))
    sets.append(take(len(NEAR)))
    out_ref, pre_ref, step_ref, win_ref, sems = rest
    arrivals = fetch_group(half * HALF_GROUPS + 1, far, sets[1], sems.at[2])
    if theirs:
        own = core_ref[0]
        size = HALF_GROUPS * STATE
        pieces = [span(own, HALF_X)] + [span(WIDTH_X // size + 2 * base + own, size) for base in range(2)]
        fetches = start_all([(pre_h.at[pl.ds(0, 8), at], head_ref.at[:, at]) for at in pieces], sems.at[3])
    else:
        fetches = fetch_group((1 - half) * HALF_GROUPS, far, after, sems.at[3])
    last = iota((8, 2 * LANES), 0) == 7
    lower = (iota((T, T), 0) >= iota((T, T), 1)).astype(F32)

    def tap_sums(grad_pre, lo):
        width = grad_pre.shape[1]
        return [
            jnp.sum(grad_pre * win_ref[5 + k : 5 + k + T, lo : lo + width], axis=0, keepdims=True)
            for k in range(TAPS)
        ]

    def by_rows(sums):
        return [s[:, lo : lo + LANES] for lo in range(0, sums[0].shape[1], LANES) for s in sums]

    saves = []

    def save(src, dst):
        copy = pltpu.make_async_copy(src, dst, sems.at[len(saves) // 8, len(saves) % 8])
        copy.start()
        saves.append(copy)

    for jj in range(HALF_GROUPS):
        j = half * HALF_GROUPS + jj
        x_ref, g_ref, y_ref, gx_ref, slope_ref, tok_ref, bc_ref, gbc_ref = sets[jj]
        if jj:
            wait_all(arrivals)
        b = bc_ref[:, 0:STATE]
        c = bc_ref[:, STATE:]
        grad_b = gbc_ref[:, 0:STATE]
        grad_c = gbc_ref[:, STATE:]
        cols = rolled(small_ref[ROW_SCALE : ROW_SCALE + T], j)
        skip_rows = small_ref[pl.ds(pl.multiple_of(ROW_SKIP + j * GROUP_PAIRS, GROUP_PAIRS), GROUP_PAIRS), :]
        tot_rows = small_ref[pl.ds(pl.multiple_of(ROW_TOT + j * GROUP_PAIRS, GROUP_PAIRS), GROUP_PAIRS), :]
        seg_grad = jnp.zeros((GROUP_HEADS, T), F32)
        dt_grad = jnp.zeros((GROUP_HEADS, T), F32)
        skips = [skips_ref[span(j, GROUP_PAIRS), :]]
        terms = []
        fill_window(win_ref, before_ref[:, span(j, GROUP_X)], tok_ref[:, 0:GROUP_X])
        for q in range(0, GROUP_PAIRS, 2):
            lanes = slice(q * LANES, (q + 2) * LANES)
            wide = slice(jj * GROUP_X + q * LANES, jj * GROUP_X + (q + 2) * LANES)
            rise = widen_two(cols, 0, q)
            keep = widen_two(cols, HEADS, q)
            at = jj * GROUP_PAIRS + q
            state = jnp.concatenate([state_ref[0, at], state_ref[0, at + 1]], axis=1)
            exits = jnp.concatenate([state_ref[1, at], state_ref[1, at + 1]], axis=1)
            skip = jnp.concatenate([skip_rows[q : q + 1], skip_rows[q + 1 : q + 2]], axis=1)
            tot = jnp.concatenate([tot_rows[q : q + 1], tot_rows[q + 1 : q + 2]], axis=1)
            x = x_ref[:, lanes].astype(F32)
            g = g_ref[:, lanes].astype(F32)
            y = y_ref[:, lanes] + rise * dot(c, state)
            through = keep * dot(b, exits)
            gx = gx_ref[:, lanes] + through
            grad_c = grad_c + dot((g * rise).astype(BF16), state, NT)
            grad_b = grad_b + dot((x * keep).astype(BF16), exits, NT)
            out_ref[:, wide] = (y + skip * x).astype(BF16)
            grad_pre = (gx + skip * g) * slope_ref[:, lanes]
            pre_ref[:, wide] = grad_pre
            if theirs:
                at = pl.ds(pl.multiple_of(j * GROUP_X + q * LANES, 2 * LANES), 2 * LANES)
                head_ref[:, at] = grad_pre[0:8]
            terms += by_rows(tap_sums(grad_pre, q * LANES))
            x_gx = x * gx
            end = jnp.sum(x * through, axis=0, keepdims=True) + jnp.exp(tot) * jnp.sum(
                exits.astype(F32) * state.astype(F32), axis=0, keepdims=True
            )
            moved = g * y - x_gx
            moved = jnp.concatenate([moved[: T - 8], moved[T - 8 :] + jnp.where(last, end, 0.0)], axis=0)
            pick = (
                iota((GROUP_HEADS, 2 * LANES), 0)
                == 2 * q + iota((GROUP_HEADS, 2 * LANES), 1) // HEAD_DIM
            ).astype(F32).astype(BF16)
            for part in split_two(moved):
                seg_grad = seg_grad + dot(pick, part, NT)
            for part in split_two(x_gx):
                dt_grad = dt_grad + dot(pick, part, NT)
            if q % 4 == 2:
                size = GROUP_X // 2
                near_at = pl.ds(jj * GROUP_X + (q // 4) * size, size)
                far_at = span(2 * j + q // 4, size)
                save(out_ref.at[:, near_at], out_h.at[:, far_at])
                save(pre_ref.at[:, near_at], pre_h.at[:, far_at])
        for grad, base in ((grad_b, 0), (grad_c, 1)):
            at = HALF_X + (base * HALF_GROUPS + jj) * STATE
            tail = slice(GROUP_X + base * STATE, GROUP_X + (base + 1) * STATE)
            far_at = span(WIDTH_X // STATE + base * GROUPS + j, STATE)
            fill_window(win_ref, before_ref[:, far_at], tok_ref[:, tail])
            grad_pre = grad * slope_ref[:, tail]
            pre_ref[:, at : at + STATE] = grad_pre
            if theirs:
                head_ref[:, far_at] = grad_pre[0:8]
            terms += tap_sums(grad_pre, 0)
            save(pre_ref.at[:, pl.ds(at, STATE)], pre_h.at[:, far_at])
        heads = span(j, GROUP_HEADS)
        behind = exact_dot(seg_grad, lower)
        dt = small_ref[pl.ds(pl.multiple_of(ROW_DT + j * GROUP_HEADS, GROUP_HEADS), GROUP_HEADS), :]
        decay = small_ref[pl.ds(pl.multiple_of(ROW_DECAY + j * GROUP_HEADS, GROUP_HEADS), GROUP_HEADS), :]
        near = pl.ds(jj * GROUP_HEADS, GROUP_HEADS)
        step_ref[near, :] = (dt_grad / dt + decay * behind) * sigmoid(raw_ref[heads, :])
        save(step_ref.at[near], step_h.at[heads])
        rows = jj * SUM_GROUP
        sum_ref[rows : rows + SUM_GROUP, :] = jnp.concatenate(terms + skips + [dt * behind * decay], axis=0)
    wait_all(fetches)
    if theirs:
        first_ref[...] = head_ref[0 : TAPS - 1, :].astype(BF16)
    wait_all(saves)


def run_leave(core, state, near, common, far, done):
    theirs = done is not None
    out = [
        ("h", (T, WIDTH_X), BF16),
        ("h", (T, CHANNELS), F32),
        ("h", (HEADS, T), F32),
        ("V", (HALF_GROUPS * SUM_GROUP, LANES), F32),
    ]
    scratch = [pltpu.VMEM(shape, dtype) for _, shape, dtype in NEAR] + [
        pltpu.VMEM((T, HALF_X), BF16),
        pltpu.VMEM((T, HALF_X + HALF_B), F32),
        pltpu.VMEM((HALF_GROUPS * GROUP_HEADS, T), F32),
        pltpu.VMEM((8 + T, GROUP_X), F32),
        DMA(4, FETCHES),
    ]
    args = [core, state, *near, *common, *far]
    specs = "s" + ("v" if theirs else "V") + "V" * (len(near) + len(COMMON)) + "h" * len(far)
    aliases = {}
    if theirs:
        aliases = {len(args) + i: i for i in range(3)}
        args += done
        specs += "hhh"
        out += [("V", (TAPS - 1, CHANNELS), BF16)]
        scratch = [pltpu.VMEM((8, CHANNELS), F32)] + scratch
    else:
        out += NEAR
    kernel = functools.partial(leave_kernel, theirs)
    outs = call(kernel, "leave", out, specs, 5, scratch, mib=12, aliases=aliases)(*args)
    return outs[:3], outs[3], outs[4:]


def spread_kernel(pre_h, halo_ref, weight_ref, out_h, pre_ref, out_ref, win_ref, sems):
    blocks = [pl.ds(i * GROUP_X, GROUP_X) for i in range(BLOCKS)]
    loads = start_all([(pre_h.at[:, at], pre_ref.at[:, at]) for at in blocks], sems.at[0])
    saves = []
    for i, load in enumerate(loads):
        load.wait()
        cols = slice(i * GROUP_X, (i + 1) * GROUP_X)
        win_ref[0:T, :] = pre_ref[:, cols]
        win_ref[T : T + TAPS - 1, :] = halo_ref[:, cols].astype(F32)
        weights = weight_ref[:, cols]
        for lo in range(0, GROUP_X, LANES):
            at = slice(lo, lo + LANES)
            acc = weights[0:1, at] * win_ref[3 : 3 + T, at]
            for k in range(1, TAPS):
                acc = acc + weights[k : k + 1, at] * win_ref[3 - k : 3 - k + T, at]
            out_ref[:, i * GROUP_X + lo : i * GROUP_X + lo + LANES] = acc.astype(BF16)
        saves.append(pltpu.make_async_copy(out_ref.at[:, blocks[i]], out_h.at[:, blocks[i]], sems.at[1, i]))
        saves[-1].start()
    wait_all(saves)


def run_spread(pre, halo, weight):
    out = [("h", (T, CHANNELS), BF16)]
    scratch = [
        pltpu.VMEM((T, CHANNELS), F32),
        pltpu.VMEM((T, CHANNELS), BF16),
        pltpu.VMEM((T + 8, GROUP_X), F32),
        DMA(2, BLOCKS),
    ]
    return call(spread_kernel, "spread", out, "hvV", 3, scratch, mib=8)(pre, halo, weight)[0]


CONV_ROWS = TAPS * (CHANNELS // LANES)
CONV_GROUP = CONV_ROWS // GROUPS
SEND_ROWS = CONV_ROWS + 16


def write_send(out_ref, conv, thin):
    high = thin.astype(BF16).astype(F32)
    low = thin - high
    row = iota((16, LANES), 0)
    out_ref[0:CONV_ROWS, :] = conv.astype(BF16)
    out_ref[CONV_ROWS:SEND_ROWS, :] = jnp.where(row == 0, high, jnp.where(row == 1, low, 0.0)).astype(BF16)


def read_send(value):
    wide = value.astype(F32)
    return wide[0:CONV_ROWS], wide[CONV_ROWS : CONV_ROWS + 1] + wide[CONV_ROWS + 1 : CONV_ROWS + 2]


def merge_kernel(core_ref, own_ref, own_got_ref, theirs_ref, theirs_got_ref, out_ref):
    thin = jnp.zeros((8, LANES), F32)
    left = iota((8, LANES), 1) < HEAD_DIM
    count = HEADS // 2
    parts = []
    for side, (mine, other) in enumerate(((own_ref, theirs_got_ref), (theirs_ref, own_got_ref))):
        half = 1 - core_ref[0] if side else core_ref[0]
        total = mine[...] + other[...]
        rows, skips, decays = [], [], []
        for jj in range(HALF_GROUPS):
            at = jj * SUM_GROUP
            rows.append(total[at : at + CONV_GROUP])
            skips.append(total[at + CONV_GROUP : at + SUM_GROUP - GROUP_HEADS])
            decays.append(total[at + SUM_GROUP - GROUP_HEADS : at + SUM_GROUP])
        skips = jnp.concatenate(skips, axis=0)
        even = exact_dot(jnp.where(left, 1.0, 0.0), skips, NT)
        odd = exact_dot(jnp.where(left, 0.0, 1.0), skips, NT)
        decay = exact_dot(jnp.ones((8, LANES), F32), jnp.concatenate(decays, axis=0), NT)
        for part, step, shift in ((even, 2, 0), (odd, 2, 1), (decay, 1, HEADS)):
            size = part.shape[1]
            spot = (iota((size, LANES), 1) == step * iota((size, LANES), 0) + shift + half * count).astype(F32)
            thin = thin + exact_dot(part, spot)
        parts.append(jnp.concatenate(rows, axis=0))
    first = core_ref[0] == 0
    conv = jnp.concatenate(
        [jnp.where(first, parts[0], parts[1]), jnp.where(first, parts[1], parts[0])], axis=0
    )
    write_send(out_ref, conv, thin[0:1])


def run_merge(core, own, own_got, theirs, theirs_got):
    out = [("v", (SEND_ROWS, LANES), BF16)]
    return call(merge_kernel, "merge", out, "svvvv", 1, mib=4)(core, own, own_got, theirs, theirs_got)[0]


def ring_sum(me_ref, hold_ref):
    count = hold_ref.shape[0]
    conv, thin = read_send(hold_ref[lax.rem(me_ref[0], count)])
    for k in range(1, count):
        more, little = read_send(hold_ref[lax.rem(me_ref[0] + count - k, count)])
        conv, thin = conv + more, thin + little
    return conv, thin


def fold_kernel(me_ref, *rest):
    *refs, out_ref, hold_ref = rest
    for d, ref in enumerate(refs):
        hold_ref[d] = ref[...]
    write_send(out_ref, *ring_sum(me_ref, hold_ref))


def run_fold(me, values):
    out = [("v", (SEND_ROWS, LANES), BF16)]
    scratch = [pltpu.VMEM((len(values), SEND_ROWS, LANES), BF16)]
    return call(fold_kernel, "fold", out, "s" + "v" * len(values), 1, scratch, mib=4)(me, *values)[0]


def finish_kernel(core_ref, me_ref, *rest):
    *refs, conv_ref, decay_ref, skip_ref, hold_ref = rest
    count = len(refs)
    sides = (count - 1) // 2
    hold_ref[0] = refs[0][...]
    for k in range(1, sides + 1):
        mine = jnp.where(core_ref[0] == 0, k, count - k)
        hold_ref[mine] = refs[k][...]
        hold_ref[count - mine] = refs[sides + k][...]
    if count % 2 == 0:
        hold_ref[count // 2] = refs[count - 1][...]
    conv, thin = ring_sum(me_ref, hold_ref)
    for i in range(CHANNELS // LANES):
        if i < PAIRS:
            row = CONV_GROUP * (i // GROUP_PAIRS) + TAPS * (i % GROUP_PAIRS)
        else:
            kind, group = divmod(i - PAIRS, GROUPS)
            row = CONV_GROUP * group + TAPS * (GROUP_PAIRS + kind)
        conv_ref[:, i * LANES : (i + 1) * LANES] = conv[row : row + TAPS]
    skip_ref[...] = thin[:, 0:HEADS]
    decay_ref[...] = thin[:, HEADS:]


def run_finish(core, me, values):
    out = [("v", (TAPS, CHANNELS), F32), ("v", (1, HEADS), F32), ("v", (1, HEADS), F32)]
    scratch = [pltpu.VMEM((len(values), SEND_ROWS, LANES), BF16)]
    return call(finish_kernel, "finish", out, "ss" + "v" * len(values), 1, scratch, mib=4)(core, me, *values)


CTX = ("chip", "core")
ALL = ("dp", "chip", "core")


def all_to_all(value, axis):
    return lax.all_to_all(value, axis, 0, 0, tiled=True)


def tie(*values):
    return lax.optimization_barrier(values)


SIDE = 4


def around(value, axis, count, ring, move):
    return [value] + [
        lax.ppermute(value, axis, [(i, move(i, d)) for i in range(count)]) for d in range(1, ring)
    ]


def around_by_sides(value, count):
    def shifts(first, second):
        return [
            (2 * i + side, 2 * ((i + move) % count) + side)
            for i in range(count)
            for side, move in enumerate((first, second))
        ]

    def hear(first, second):
        return lax.ppermute(value, ("dp", "core"), shifts(first, second))

    middle = [hear(count // 2, count // 2)] if count % 2 == 0 else []
    heard = [hear(k, -k) for k in range((count - 1) // 2, 0, -1)][::-1]
    swapped = [lax.ppermute(part, "core", [(0, 1), (1, 0)]) for part in heard]
    return [value] + heard + swapped + middle


def scalar(value):
    return value.astype(jnp.int32).reshape(1)


def local(conv_input, conv_weight, step_raw, decay_log, skip_gain, cotangent):
    chips = lax.axis_size("chip")
    devices = 2 * chips
    sequences = lax.axis_size("dp")
    tokens = conv_input[0]
    raw = step_raw[0]
    cot = cotangent[0]
    core = lax.axis_index("core").astype(jnp.int32).reshape(1)
    swap = [(0, 1), (1, 0)]
    halo = lax.ppermute(tokens[T - TAPS + 1 :], CTX, [(i, i + 1) for i in range(devices - 1)])
    small, small_near, tot, x0, bc0, head, weight_near, cot_near = run_begin(
        raw, decay_log.reshape(1, HEADS), skip_gain.reshape(1, HEADS), tokens, conv_weight, cot
    )
    other = lax.ppermute(tot, "core", swap)
    x, bc, before, x_near, bc_near, out = run_enter(
        core, x0, bc0, head, halo, weight_near, cot_near, small_near
    )
    got_near = lax.ppermute(out, "core", swap)
    own_near = run_own(core, x_near, bc_near, cot_near, small_near)
    packed, left, right, tots = run_pack(core, own_near, got_near, tot, other)
    heard = all_to_all(packed, "chip")
    y, gbc, skips = run_inner(x, bc, cot, small)
    heard, y, gbc, skips = tie(heard, y, gbc, skips)
    chained = run_chain(chips, heard)
    late, chained = tie(bc, chained)
    back = all_to_all(chained, "chip")
    gx, slope = run_slopes(late, cot, small, tokens, before, conv_weight)
    back, gx, slope = tie(back, gx, slope)
    far = (x, cot, y, gx, slope, tokens, bc, gbc)
    mine, send, near, common = run_unpack(
        core, back, left, right, tots, far, (before, small, raw, skips, conv_weight)
    )
    theirs = lax.ppermute(send, "core", swap)
    half, sum_own, near = run_leave(core, mine, near, common, far, None)
    sum_own_got = lax.ppermute(sum_own, "core", swap)
    (out_tokens, pre, grad_step), sum_theirs, (first,) = run_leave(core, theirs, near, common, far, half)
    sum_theirs_got = lax.ppermute(sum_theirs, "core", swap)
    after = lax.ppermute(first, CTX, [(i + 1, i) for i in range(devices - 1)])
    sums = run_merge(core, sum_own, sum_own_got, sum_theirs, sum_theirs_got)
    chip = lax.axis_index("chip")
    values = around(sums, "chip", chips, SIDE, lambda i, d: i // SIDE * SIDE + (i % SIDE + d) % SIDE)
    grad_tokens = run_spread(pre, after, common[4])
    values, grad_tokens = tie(values, grad_tokens)
    sums = run_fold(scalar(lax.rem(chip, SIDE)), values)
    values = around(sums, "chip", chips, chips // SIDE, lambda i, d: (i + d * SIDE) % chips)
    sums = run_fold(scalar(lax.div(chip, SIDE)), values)
    values = around_by_sides(sums, sequences)
    grad_conv, grad_decay, grad_skip = run_finish(core, scalar(lax.axis_index("dp")), values)
    return (
        out_tokens[None],
        grad_tokens[None],
        grad_step[None],
        grad_conv,
        grad_decay.reshape(HEADS),
        grad_skip.reshape(HEADS),
    )


def solution(mesh):
    dp, ctx = mesh.devices.shape
    fine = Mesh(mesh.devices.reshape(dp, ctx // 2, 2), ALL)
    seq = P("dp", CTX, None)
    rate = P("dp", None, CTX)
    in_specs = (seq, P(), rate, P(), P(), seq)
    out_specs = (seq, seq, rate, P(), P(), P())
    return jax.shard_map(local, mesh=fine, in_specs=in_specs, out_specs=out_specs, check_vma=False)
```

```python
import functools

import jax
import jax.numpy as jnp
from jax import lax
from jax.experimental import pallas as pl
from jax.experimental.pallas import tpu as pltpu
from jax.sharding import Mesh
from jax.sharding import PartitionSpec as P

HEADS = 64
HEAD_DIM = 64
GROUPS = 4
STATE = 128
TAPS = 4
T = 128
LANES = 128
WIDTH_X = HEADS * HEAD_DIM
WIDTH_B = GROUPS * STATE
CHANNELS = WIDTH_X + 2 * WIDTH_B
GROUP_X = WIDTH_X // GROUPS
PAIRS = HEADS // 2
GROUP_PAIRS = PAIRS // GROUPS
GROUP_HEADS = HEADS // GROUPS
HALF_PAIRS = PAIRS // 2
HALF_GROUPS = GROUPS // 2
F32 = jnp.float32
BF16 = jnp.bfloat16
EXACT = lax.Precision.HIGHEST
NN = (((1,), (0,)), ((), ()))
NT = (((1,), (1,)), ((), ()))
SUM_GROUP = 64
PACK_ROWS = 2 * STATE + 16


def dot(a, b, dims=NN):
    return lax.dot_general(a, b, dims, preferred_element_type=F32)


def exact_dot(a, b, dims=NN):
    return lax.dot_general(a, b, dims, precision=EXACT, preferred_element_type=F32)


def iota(shape, dim):
    return lax.broadcasted_iota(jnp.int32, shape, dim)


def sigmoid(v):
    return 0.5 + 0.5 * jnp.tanh(0.5 * v)


def split_two(v):
    high = v.astype(BF16)
    return high, (v - high.astype(F32)).astype(BF16)


def span(index, size):
    return pl.ds(pl.multiple_of(index * size, size), size)


def pin(value, space):
    return pltpu.with_memory_space_constraint(value, space)


def placed(space, shape, dtype):
    return space(shape, dtype)


def call(kernel, name, outs, specs, micros, scratch=(), mib=28, aliases=None):
    cost = pl.CostEstimate(
        flops=int(micros * 1e9), transcendentals=0, bytes_accessed=int(micros * 3.6e6)
    )
    blocks = {
        "s": pl.BlockSpec(memory_space=pltpu.SMEM),
        "v": pl.BlockSpec(memory_space=pltpu.VMEM),
        "V": pl.BlockSpec(memory_space=pltpu.VMEM),
        "h": pl.BlockSpec(memory_space=pltpu.HBM),
    }
    spaces = {"V": pltpu.VMEM, "h": pltpu.HBM}
    shapes = [
        placed(spaces[p], shape, dtype) if p in spaces else jax.ShapeDtypeStruct(shape, dtype)
        for p, shape, dtype in outs
    ]
    run = pl.pallas_call(
        kernel,
        out_shape=shapes,
        in_specs=[blocks[p] for p in specs],
        out_specs=[blocks[p] for p, _, _ in outs],
        scratch_shapes=list(scratch),
        input_output_aliases=aliases or {},
        cost_estimate=cost,
        compiler_params=pltpu.CompilerParams(vmem_limit_bytes=mib << 20),
        name=name,
    )

    def go(*args):
        return run(*[pin(a, spaces[p]) if p in spaces else a for a, p in zip(args, specs, strict=True)])

    return go


def start_all(pairs, sems):
    copies = [pltpu.make_async_copy(a, b, sems.at[i]) for i, (a, b) in enumerate(pairs)]
    for copy in copies:
        copy.start()
    return copies


def wait_all(copies):
    for copy in copies:
        copy.wait()


def DMA(*shape):
    return pltpu.SemaphoreType.DMA(shape)


def fill_window(win_ref, before, tokens):
    width = tokens.shape[1]
    win_ref[0:8, :width] = before
    win_ref[8 : 8 + T, :width] = tokens.astype(F32)


def pre_conv(win_ref, weights, lo):
    cols = slice(lo, lo + LANES)
    acc = weights[0:1, cols] * win_ref[5 : 5 + T, cols]
    for k in range(1, TAPS):
        acc = acc + weights[k : k + 1, cols] * win_ref[5 + k : 5 + k + T, cols]
    return acc


BLOCKS = CHANNELS // GROUP_X


ROW_DT, ROW_SEG, ROW_COLS, ROW_SCALE, ROW_TOT, ROW_SKIP, ROW_DECAY, SMALL_ROWS = (
    0, 64, 128, 256, 384, 416, 448, 512
)


def begin_kernel(raw_h, decay_log_h, skip_gain_h, tok_h, weight_h, g_h,
                 small_h, small_ref, tot_ref, x_ref, bc_ref, head_ref, weight_ref, g_ref,
                 raw_ref, decay_log_ref, skip_gain_ref, wide_ref, hold_ref, win_ref, sems):
    first = start_all(
        [(raw_h, raw_ref), (decay_log_h, decay_log_ref), (skip_gain_h, skip_gain_ref), (weight_h, weight_ref)],
        sems.at[0],
    )
    blocks = [pl.ds(i * GROUP_X, GROUP_X) for i in range(BLOCKS)]
    copies = start_all([(tok_h.at[:, at], hold_ref.at[:, at]) for at in blocks], sems.at[1])
    later = start_all([(g_h, g_ref)], sems.at[2])
    win_ref[0:8, :] = jnp.zeros((8, GROUP_X), F32)
    copies[0].wait()
    diagonal = iota((HEADS, HEADS), 0) == iota((HEADS, HEADS), 1)

    def column(row):
        return jnp.sum(jnp.where(diagonal, row, 0.0), axis=1, keepdims=True)

    wait_all(first)
    raw = raw_ref[...]
    dt = jnp.log1p(jnp.exp(raw))
    decay = -jnp.exp(column(decay_log_ref[...]))
    upper = (iota((T, T), 0) <= iota((T, T), 1)).astype(F32)
    seg = exact_dot(dt * decay, upper)
    total = seg[:, T - 1 : T]
    small_ref[ROW_DT : ROW_DT + HEADS] = dt
    small_ref[ROW_SEG : ROW_SEG + HEADS] = seg
    small_ref[ROW_COLS : ROW_COLS + T] = jnp.transpose(jnp.concatenate([seg, dt], axis=0))
    small_ref[ROW_SCALE : ROW_SCALE + T] = jnp.transpose(
        jnp.concatenate([jnp.exp(seg), jnp.exp(total - seg) * dt], axis=0)
    )
    left = iota((PAIRS, LANES), 1) < HEAD_DIM

    def paired(col):
        wide_ref[...] = jnp.broadcast_to(col, (HEADS, LANES))
        return jnp.where(left, wide_ref[pl.ds(0, PAIRS, 2), :], wide_ref[pl.ds(1, PAIRS, 2), :])

    tot = paired(total)
    tot_ref[...] = tot
    small_ref[ROW_TOT : ROW_TOT + PAIRS] = tot
    small_ref[ROW_SKIP : ROW_SKIP + PAIRS] = paired(column(skip_gain_ref[...]))
    small_ref[ROW_DECAY : ROW_DECAY + HEADS] = jnp.broadcast_to(decay, (HEADS, LANES))
    save = start_all([(small_ref, small_h)], sems.at[0])
    for i in range(BLOCKS):
        if i:
            copies[i].wait()
        cols = slice(i * GROUP_X, (i + 1) * GROUP_X)
        win_ref[8 : 8 + T, :] = hold_ref[:, cols].astype(F32)
        for lo in range(0, GROUP_X, LANES):
            at = i * GROUP_X + lo
            pre = pre_conv(win_ref, weight_ref[:, cols], lo)
            mixed = (pre * sigmoid(pre)).astype(BF16)
            head_ref[:, at : at + LANES] = pre[0:8]
            if at < WIDTH_X:
                x_ref[:, at : at + LANES] = mixed
            else:
                bc_ref[:, at - WIDTH_X : at - WIDTH_X + LANES] = mixed
    wait_all(save + later)


def run_begin(raw, decay_log, skip_gain, tokens, weight, cot):
    out = [
        ("h", (SMALL_ROWS, LANES), F32),
        ("V", (SMALL_ROWS, LANES), F32),
        ("V", (PAIRS, LANES), F32),
        ("V", (T, WIDTH_X), BF16),
        ("V", (T, 2 * WIDTH_B), BF16),
        ("V", (8, CHANNELS), F32),
        ("V", (TAPS, CHANNELS), F32),
        ("V", (T, WIDTH_X), BF16),
    ]
    scratch = [
        pltpu.VMEM((HEADS, T), F32),
        pltpu.VMEM((1, HEADS), F32),
        pltpu.VMEM((1, HEADS), F32),
        pltpu.VMEM((HEADS, LANES), F32),
        pltpu.VMEM((T, CHANNELS), BF16),
        pltpu.VMEM((8 + T, GROUP_X), F32),
        DMA(3, BLOCKS),
    ]
    return call(begin_kernel, "begin", out, "hhhhhh", 4, scratch, mib=8)(
        raw, decay_log, skip_gain, tokens, weight, cot
    )


def rolled(cols, group):
    return pltpu.roll(cols, (LANES - group * GROUP_HEADS) % LANES, 1)


def widen(cols, base, pair):
    first = iota((T, LANES), 1) < HEAD_DIM
    at = base + 2 * pair
    return jnp.where(first, cols[:, at : at + 1], cols[:, at + 1 : at + 2])


def widen_two(cols, base, pair):
    return jnp.concatenate([widen(cols, base, pair), widen(cols, base, pair + 1)], axis=1)


def fill_half(half, x_ref, bc_ref, g_ref, scale, dst_ref):
    for jj in range(HALF_GROUPS):
        j = half * HALF_GROUPS + jj
        b_flip = jnp.transpose(bc_ref[:, span(j, STATE)].astype(F32)).astype(BF16)
        c_flip = jnp.transpose(bc_ref[:, span(GROUPS + j, STATE)].astype(F32)).astype(BF16)
        cols = rolled(scale, j)
        for q in range(0, GROUP_PAIRS, 2):
            lanes = pl.ds(pl.multiple_of(j * GROUP_X + q * LANES, 2 * LANES), 2 * LANES)
            xw = (x_ref[:, lanes].astype(F32) * widen_two(cols, HEADS, q)).astype(BF16)
            gw = (g_ref[:, lanes].astype(F32) * widen_two(cols, 0, q)).astype(BF16)
            state = dot(b_flip, xw).astype(BF16)
            grad = dot(c_flip, gw).astype(BF16)
            for k in range(2):
                at = jj * GROUP_PAIRS + q + k
                dst_ref[0, at] = state[:, k * LANES : (k + 1) * LANES]
                dst_ref[1, at] = grad[:, k * LANES : (k + 1) * LANES]


def enter_kernel(core_ref, x0_ref, bc0_ref, head_ref, halo_ref, weight_ref, g_ref, small_ref,
                 x_h, bc_h, before_h, x_ref, bc_ref, out_ref, before_ref, sems):
    half = 1 - core_ref[0]
    row = iota((8, GROUP_X), 0)
    for i in range(BLOCKS):
        cols = slice(i * GROUP_X, (i + 1) * GROUP_X)
        halo = halo_ref[:, cols].astype(F32)
        weight = weight_ref[:, cols]
        pre = head_ref[:, cols]
        before = jnp.zeros((8, GROUP_X), F32)
        for t in range(TAPS - 1):
            extra = jnp.zeros((1, GROUP_X), F32)
            for k in range(TAPS - 1 - t):
                extra = extra + weight[k : k + 1] * halo[t + k : t + k + 1]
            pre = pre + jnp.where(row == t, extra, 0.0)
            before = before + jnp.where(row == t + 5, halo[t : t + 1], 0.0)
        before_ref[:, cols] = before
        fixed = pre * sigmoid(pre)
        src, dst, at = (x0_ref, x_ref, cols) if i < GROUPS else (bc0_ref, bc_ref, slice(0, GROUP_X))
        rest = src[0:16, at].astype(F32)
        dst[16:T, at] = src[16:T, at]
        dst[0:16, at] = jnp.concatenate([fixed, rest[8:16]], axis=0).astype(BF16)
    saves = start_all([(x_ref, x_h), (bc_ref, bc_h), (before_ref, before_h)], sems)
    fill_half(half, x_ref, bc_ref, g_ref, small_ref[ROW_SCALE : ROW_SCALE + T], out_ref)
    wait_all(saves)


def run_enter(core, x0, bc0, head, halo, weight, cot, small):
    out = [
        ("h", (T, WIDTH_X), BF16),
        ("h", (T, 2 * WIDTH_B), BF16),
        ("h", (8, CHANNELS), F32),
        ("V", (T, WIDTH_X), BF16),
        ("V", (T, 2 * WIDTH_B), BF16),
        ("V", (2, HALF_PAIRS, STATE, LANES), BF16),
    ]
    scratch = [pltpu.VMEM((8, CHANNELS), F32), DMA(3)]
    return call(enter_kernel, "enter", out, "sVVVvVVV", 3, scratch, mib=6)(
        core, x0, bc0, head, halo, weight, cot, small
    )


def own_kernel(core_ref, x_ref, bc_ref, g_ref, small_ref, own_ref):
    fill_half(core_ref[0], x_ref, bc_ref, g_ref, small_ref[ROW_SCALE : ROW_SCALE + T], own_ref)


def run_own(core, x, bc, cot, small):
    out = [("V", (2, HALF_PAIRS, STATE, LANES), BF16)]
    return call(own_kernel, "own", out, "sVVVV", 3, mib=6)(core, x, bc, cot, small)[0]


STEP_PAIRS = 4
STEPS = HALF_PAIRS // STEP_PAIRS


def pack_kernel(core_ref, own_ref, got_ref, tot_ref, other_ref,
                out_h, left_h, right_h, tots_h, out_ref, sems):
    saves = start_all(
        [(tot_ref, tots_h.at[pl.ds(0, PAIRS)]), (other_ref, tots_h.at[pl.ds(PAIRS, PAIRS)])], sems.at[0]
    )
    second = core_ref[0] == 1

    def keep(first_ref, last_ref):
        return [
            pltpu.make_async_copy(first_ref.at[0], left_h, sems.at[0, 2]),
            pltpu.make_async_copy(last_ref.at[1], right_h, sems.at[0, 3]),
        ]

    @pl.when(second)
    def _():
        for copy in keep(got_ref, own_ref):
            copy.start()

    @pl.when(jnp.logical_not(second))
    def _():
        for copy in keep(own_ref, got_ref):
            copy.start()

    saves += keep(own_ref, got_ref)
    outs = []
    for i in range(HALF_PAIRS):
        at = core_ref[0] * HALF_PAIRS + i
        tot = tot_ref[pl.ds(at, 1), :]
        other = other_ref[pl.ds(at, 1), :]
        one = jnp.ones_like(tot)
        by_own = jnp.exp(tot)
        by_other = jnp.exp(other)
        state = (
            jnp.where(second, one, by_other) * own_ref[0, i].astype(F32)
            + jnp.where(second, by_own, one) * got_ref[0, i].astype(F32)
        )
        grad = (
            jnp.where(second, by_other, one) * own_ref[1, i].astype(F32)
            + jnp.where(second, one, by_own) * got_ref[1, i].astype(F32)
        )
        out_ref[i, 0:STATE, :] = state.astype(BF16)
        out_ref[i, STATE : 2 * STATE, :] = grad.astype(BF16)
        both = tot + other
        high = both.astype(BF16).astype(F32)
        mid = (both - high).astype(BF16).astype(F32)
        low = both - high - mid
        row = iota((16, LANES), 0)
        wide = jnp.where(row == 0, high, jnp.where(row == 1, mid, jnp.where(row == 2, low, 0.0)))
        out_ref[i, 2 * STATE : PACK_ROWS, :] = wide.astype(BF16)
        if i % STEP_PAIRS == STEP_PAIRS - 1:
            done = pl.ds(i + 1 - STEP_PAIRS, STEP_PAIRS)
            copy = pltpu.make_async_copy(out_ref.at[done], out_h.at[done], sems.at[1, i // STEP_PAIRS])
            copy.start()
            outs.append(copy)
    wait_all(outs + saves)


def run_pack(core, own, got, tot, other):
    half = (HALF_PAIRS, STATE, LANES)
    packed = (HALF_PAIRS, PACK_ROWS, LANES)
    out = [("h", packed, BF16), ("h", half, BF16), ("h", half, BF16), ("h", (2 * PAIRS, LANES), F32)]
    scratch = [pltpu.VMEM(packed, BF16), DMA(2, STEPS)]
    return call(pack_kernel, "pack", out, "sVvVv", 2, scratch, mib=8)(core, own, got, tot, other)


def chain_kernel(chips, per, in_ref, out_ref):
    for q in range(per):
        def decay(k):
            rows = in_ref[k * per + q, 2 * STATE : PACK_ROWS, :].astype(F32)
            return jnp.exp(rows[0:1] + rows[1:2] + rows[2:3])

        carry = jnp.zeros((STATE, LANES), F32)
        for k in range(chips):
            out_ref[k * per + q, 0:STATE, :] = carry.astype(BF16)
            if k < chips - 1:
                carry = decay(k) * carry + in_ref[k * per + q, 0:STATE, :].astype(F32)
        carry = jnp.zeros((STATE, LANES), F32)
        for k in reversed(range(chips)):
            out_ref[k * per + q, STATE : 2 * STATE, :] = carry.astype(BF16)
            if k > 0:
                carry = decay(k) * carry + in_ref[k * per + q, STATE : 2 * STATE, :].astype(F32)


def run_chain(chips, packed):
    kernel = functools.partial(chain_kernel, chips, HALF_PAIRS // chips)
    out = [("v", (HALF_PAIRS, 2 * STATE, LANES), BF16)]
    return call(kernel, "chain", out, "v", 1, mib=8)(packed)[0]


HALF_X = HALF_GROUPS * GROUP_X
HALF_B = 2 * HALF_GROUPS * STATE

NEAR = [
    ("V", (T, GROUP_X), BF16),
    ("V", (T, GROUP_X), BF16),
    ("V", (T, GROUP_X), F32),
    ("V", (T, GROUP_X), F32),
    ("V", (T, GROUP_X + 2 * STATE), F32),
    ("V", (T, GROUP_X + 2 * STATE), BF16),
    ("V", (T, 2 * STATE), BF16),
    ("V", (T, 2 * STATE), F32),
]
COMMON = [
    ("V", (8, CHANNELS), F32),
    ("V", (SMALL_ROWS, LANES), F32),
    ("V", (HEADS, T), F32),
    ("V", (PAIRS, LANES), F32),
    ("V", (TAPS, CHANNELS), F32),
]
FETCHES = 6 + 8


def fetch_group(j, far, near, sems):
    x_h, g_h, y_h, gx_h, slope_h, tok_h, bc_h, gbc_h = far
    x_v, g_v, y_v, gx_v, slope_v, tok_v, bc_v, gbc_v = near
    wide = pl.ds(0, GROUP_X)
    pairs = [
        (a.at[:, span(j, GROUP_X)], b.at[:, wide])
        for a, b in ((x_h, x_v), (g_h, g_v), (y_h, y_v), (gx_h, gx_v), (slope_h, slope_v), (tok_h, tok_v))
    ]
    for base in range(2):
        at = span(base * GROUPS + j, STATE)
        off = span(WIDTH_X // STATE + base * GROUPS + j, STATE)
        thin = pl.ds(base * STATE, STATE)
        tail = pl.ds(GROUP_X + base * STATE, STATE)
        pairs += [
            (bc_h.at[:, at], bc_v.at[:, thin]),
            (gbc_h.at[:, at], gbc_v.at[:, thin]),
            (slope_h.at[:, off], slope_v.at[:, tail]),
            (tok_h.at[:, off], tok_v.at[:, tail]),
        ]
    return start_all(pairs, sems)


def unpack_kernel(core_ref, back_ref, left_h, right_h, tots_h, *rest):
    far, rest = rest[: len(NEAR)], rest[len(NEAR) :]
    common_far, rest = rest[: len(COMMON)], rest[len(COMMON) :]
    mine_ref, send_ref, *rest = rest
    near = [rest[i * len(NEAR) : (i + 1) * len(NEAR)] for i in range(HALF_GROUPS)]
    rest = rest[HALF_GROUPS * len(NEAR) :]
    common, rest = rest[: len(COMMON)], rest[len(COMMON) :]
    left_ref, right_ref, tots_ref, sems, fetch_sems = rest
    first = start_all([(tots_h, tots_ref)], sems.at[STEPS])
    steps = []
    for step in range(STEPS):
        at = pl.ds(step * STEP_PAIRS, STEP_PAIRS)
        steps.append(
            start_all([(left_h.at[at], left_ref.at[at]), (right_h.at[at], right_ref.at[at])], sems.at[step])
        )
    fetches = start_all(list(zip(common_far, common)), fetch_sems.at[HALF_GROUPS])
    for jj in range(HALF_GROUPS):
        fetches += fetch_group(core_ref[0] * HALF_GROUPS + jj, far, near[jj], fetch_sems.at[jj])
    wait_all(first)
    second = core_ref[0] == 1
    for i in range(HALF_PAIRS):
        if i % STEP_PAIRS == 0:
            wait_all(steps[i // STEP_PAIRS])
        at = core_ref[0] * HALF_PAIRS + i
        tot = tots_ref[pl.ds(at, 1), :]
        other = tots_ref[pl.ds(PAIRS + at, 1), :]
        decay_zero = jnp.exp(jnp.where(second, other, tot))
        decay_one = jnp.exp(jnp.where(second, tot, other))
        state_zero = back_ref[i, 0:STATE, :].astype(F32)
        grad_one = back_ref[i, STATE : 2 * STATE, :].astype(F32)
        state_one = decay_zero * state_zero + left_ref[i].astype(F32)
        grad_zero = decay_one * grad_one + right_ref[i].astype(F32)
        mine_ref[0, i] = jnp.where(second, state_one, state_zero).astype(BF16)
        mine_ref[1, i] = jnp.where(second, grad_one, grad_zero).astype(BF16)
        send_ref[0, i] = jnp.where(second, state_zero, state_one).astype(BF16)
        send_ref[1, i] = jnp.where(second, grad_zero, grad_one).astype(BF16)
    wait_all(fetches)


def run_unpack(core, back, left, right, tots, far, common):
    half = (2, HALF_PAIRS, STATE, LANES)
    out = [("V", half, BF16)] * 2 + NEAR * HALF_GROUPS + COMMON
    scratch = [
        pltpu.VMEM(half[1:], BF16),
        pltpu.VMEM(half[1:], BF16),
        pltpu.VMEM((2 * PAIRS, LANES), F32),
        DMA(STEPS + 1, 2),
        DMA(HALF_GROUPS + 1, FETCHES),
    ]
    specs = "svhhh" + "h" * (len(NEAR) + len(COMMON))
    outs = call(unpack_kernel, "unpack", out, specs, 3, scratch, mib=8)(
        core, back, left, right, tots, *far, *common
    )
    at = 2 + HALF_GROUPS * len(NEAR)
    return outs[0], outs[1], outs[2:at], outs[at:]


def by_lane_half(v):
    first = iota(v.shape, 1) < HEAD_DIM
    wide = v.astype(F32)
    return jnp.concatenate(
        [jnp.where(first, wide, 0.0).astype(BF16), jnp.where(first, 0.0, wide).astype(BF16)], axis=0
    )


def inner_kernel(x_h, bc_h, g_h, small_h, y_h, gbc_h, skips_h,
                 x_ref, bc_ref, g_ref, small_ref, y_ref, gbc_ref, skips_ref, sems):
    first = start_all([(bc_h, bc_ref), (small_h, small_ref)], sems.at[0])

    def loads(j):
        at = span(j, GROUP_X)
        return [
            pltpu.make_async_copy(x_h.at[:, at], x_ref.at[:, at], sems.at[1, j]),
            pltpu.make_async_copy(g_h.at[:, at], g_ref.at[:, at], sems.at[2, j]),
        ]

    def store(j):
        at = span(j, GROUP_X)
        return pltpu.make_async_copy(y_ref.at[:, at], y_h.at[:, at], sems.at[3, j])

    for j in range(GROUPS):
        for copy in loads(j):
            copy.start()
    wait_all(first)
    lower = iota((T, T), 0) >= iota((T, T), 1)

    @pl.loop(0, GROUPS)
    def _(j):
        wait_all(loads(j))
        b = bc_ref[:, span(j, STATE)]
        c = bc_ref[:, span(GROUPS + j, STATE)]
        seg = small_ref[pl.ds(pl.multiple_of(ROW_SEG + j * GROUP_HEADS, GROUP_HEADS), GROUP_HEADS), :]
        dt = small_ref[pl.ds(pl.multiple_of(ROW_DT + j * GROUP_HEADS, GROUP_HEADS), GROUP_HEADS), :]
        scores = dot(c, b, NT)
        cols = rolled(small_ref[ROW_COLS : ROW_COLS + T], j)
        total = jnp.zeros((T, T), F32)
        skips = []
        for i in range(GROUP_PAIRS):
            lanes = pl.ds(pl.multiple_of(j * GROUP_X + i * LANES, LANES), LANES)
            x = x_ref[:, lanes]
            g = g_ref[:, lanes]
            skips.append(jnp.sum(g.astype(F32) * x.astype(F32), axis=0, keepdims=True))
            inner = dot(by_lane_half(g), x, NT)
            weights = []
            for k in range(2):
                h = 2 * i + k
                spread = cols[:, h : h + 1] - seg[h : h + 1, :]
                kernel = jnp.exp(jnp.where(lower, spread, -1e30)) * dt[h : h + 1, :]
                total = total + kernel * inner[k * T : (k + 1) * T]
                weights.append((kernel * scores).astype(BF16))
            y_ref[:, lanes] = dot(jnp.concatenate(weights, axis=1), by_lane_half(x))
        skips_ref[span(j, GROUP_PAIRS), :] = jnp.concatenate(skips, axis=0)
        gbc_ref[:, span(GROUPS + j, STATE)] = dot(total.astype(BF16), b)
        gbc_ref[:, span(j, STATE)] = dot(jnp.transpose(total).astype(BF16), c)
        store(j).start()

    last = start_all([(gbc_ref, gbc_h), (skips_ref, skips_h)], sems.at[0])
    for j in range(GROUPS):
        store(j).wait()
    wait_all(last)


def run_inner(x, bc, cot, small):
    out = [("h", (T, WIDTH_X), F32), ("h", (T, 2 * WIDTH_B), F32), ("h", (PAIRS, LANES), F32)]
    scratch = [
        pltpu.VMEM((T, WIDTH_X), BF16),
        pltpu.VMEM((T, 2 * WIDTH_B), BF16),
        pltpu.VMEM((T, WIDTH_X), BF16),
        pltpu.VMEM((SMALL_ROWS, LANES), F32),
        pltpu.VMEM((T, WIDTH_X), F32),
        pltpu.VMEM((T, 2 * WIDTH_B), F32),
        pltpu.VMEM((PAIRS, LANES), F32),
        DMA(4, GROUPS),
    ]
    return call(inner_kernel, "inner", out, "hhhh", 4, scratch, mib=16)(x, bc, cot, small)


def slopes_kernel(bc_h, g_h, small_h, tok_h, before_h, weight_h, gx_h, slope_h,
                  bc_ref, g_ref, small_ref, tok_ref, before_ref, weight_ref, gx_ref, slope_ref, win_ref, sems):
    first = start_all(
        [(bc_h, bc_ref), (small_h, small_ref), (before_h, before_ref), (weight_h, weight_ref), (tok_h, tok_ref)],
        sems.at[0],
    )

    def load(j):
        at = span(j, GROUP_X)
        return pltpu.make_async_copy(g_h.at[:, at], g_ref.at[:, at], sems.at[1, j])

    def store(j):
        at = span(j, GROUP_X)
        return pltpu.make_async_copy(gx_ref.at[:, at], gx_h.at[:, at], sems.at[2, j])

    def store_slope(i):
        at = span(i, GROUP_X)
        return pltpu.make_async_copy(slope_ref.at[:, at], slope_h.at[:, at], sems.at[3, i])

    for j in range(GROUPS):
        load(j).start()
    wait_all(first)
    upper = iota((T, T), 0) <= iota((T, T), 1)

    @pl.loop(0, GROUPS)
    def _(j):
        load(j).wait()
        b = bc_ref[:, span(j, STATE)]
        c = bc_ref[:, span(GROUPS + j, STATE)]
        seg = small_ref[pl.ds(pl.multiple_of(ROW_SEG + j * GROUP_HEADS, GROUP_HEADS), GROUP_HEADS), :]
        scores = jnp.transpose(dot(c, b, NT))
        cols = rolled(small_ref[ROW_COLS : ROW_COLS + T], j)
        for i in range(GROUP_PAIRS):
            lanes = pl.ds(pl.multiple_of(j * GROUP_X + i * LANES, LANES), LANES)
            weights = []
            for k in range(2):
                h = 2 * i + k
                spread = seg[h : h + 1, :] - cols[:, h : h + 1]
                kernel = jnp.exp(jnp.where(upper, spread, -1e30)) * cols[:, HEADS + h : HEADS + h + 1]
                weights.append((kernel * scores).astype(BF16))
            gx_ref[:, lanes] = dot(jnp.concatenate(weights, axis=1), by_lane_half(g_ref[:, lanes]))
        store(j).start()

    @pl.loop(0, BLOCKS)
    def _(i):
        cols = span(i, GROUP_X)
        fill_window(win_ref, before_ref[:, cols], tok_ref[:, cols])
        weights = weight_ref[:, cols]
        for lo in range(0, GROUP_X, LANES):
            pre = pre_conv(win_ref, weights, lo)
            s = sigmoid(pre)
            at = pl.ds(pl.multiple_of(i * GROUP_X + lo, LANES), LANES)
            slope_ref[:, at] = s * (1.0 + pre * (1.0 - s))
        store_slope(i).start()

    for j in range(GROUPS):
        store(j).wait()
    for i in range(BLOCKS):
        store_slope(i).wait()


def run_slopes(bc, cot, small, tokens, before, weight):
    out = [("h", (T, WIDTH_X), F32), ("h", (T, CHANNELS), F32)]
    scratch = [
        pltpu.VMEM((T, 2 * WIDTH_B), BF16),
        pltpu.VMEM((T, WIDTH_X), BF16),
        pltpu.VMEM((SMALL_ROWS, LANES), F32),
        pltpu.VMEM((T, CHANNELS), BF16),
        pltpu.VMEM((8, CHANNELS), F32),
        pltpu.VMEM((TAPS, CHANNELS), F32),
        pltpu.VMEM((T, WIDTH_X), F32),
        pltpu.VMEM((T, CHANNELS), F32),
        pltpu.VMEM((8 + T, GROUP_X), F32),
        DMA(4, BLOCKS),
    ]
    return call(slopes_kernel, "slopes", out, "hhhhhh", 6, scratch, mib=16)(
        bc, cot, small, tokens, before, weight
    )


def leave_kernel(theirs, core_ref, state_ref, *rest):
    rest = list(rest)

    def take(count):
        taken = rest[:count]
        del rest[:count]
        return taken

    sets = [take(len(NEAR)) for _ in range(HALF_GROUPS)]
    before_ref, small_ref, raw_ref, skips_ref, _ = take(len(COMMON))
    half = 1 - core_ref[0] if theirs else core_ref[0]
    fetches = []
    if theirs:
        pre_own_ref, _, _ = take(3)
        out_h, step_h, pre_h, sum_ref, first_ref = take(5)
        head_ref, pre_ref, out_ref, step_ref, win_ref, sems = rest
        own = core_ref[0]
        head_ref[:, span(own, HALF_X)] = pre_own_ref[0:8, 0:HALF_X]
        size = HALF_GROUPS * STATE
        for base in range(2):
            at = HALF_X + base * size
            head_ref[:, span(WIDTH_X // size + 2 * base + own, size)] = pre_own_ref[0:8, at : at + size]
    else:
        far = take(len(NEAR))
        out_h, step_h, pre_ref, sum_ref = take(4)
        after = [take(len(NEAR)) for _ in range(HALF_GROUPS)]
        out_ref, step_ref, win_ref, sems = rest
        for jj in range(HALF_GROUPS):
            fetches += fetch_group((1 - half) * HALF_GROUPS + jj, far, after[jj], sems.at[2 + jj])
    last = iota((8, 2 * LANES), 0) == 7
    lower = (iota((T, T), 0) >= iota((T, T), 1)).astype(F32)

    def tap_sums(grad_pre, lo):
        width = grad_pre.shape[1]
        return [
            jnp.sum(grad_pre * win_ref[5 + k : 5 + k + T, lo : lo + width], axis=0, keepdims=True)
            for k in range(TAPS)
        ]

    def by_rows(sums):
        return [s[:, lo : lo + LANES] for lo in range(0, sums[0].shape[1], LANES) for s in sums]

    saves = []

    def save(src, dst):
        copy = pltpu.make_async_copy(src, dst, sems.at[len(saves) // 8, len(saves) % 8])
        copy.start()
        saves.append(copy)

    for jj in range(HALF_GROUPS):
        j = half * HALF_GROUPS + jj
        x_ref, g_ref, y_ref, gx_ref, slope_ref, tok_ref, bc_ref, gbc_ref = sets[jj]
        b = bc_ref[:, 0:STATE]
        c = bc_ref[:, STATE:]
        grad_b = gbc_ref[:, 0:STATE]
        grad_c = gbc_ref[:, STATE:]
        cols = rolled(small_ref[ROW_SCALE : ROW_SCALE + T], j)
        skip_rows = small_ref[pl.ds(pl.multiple_of(ROW_SKIP + j * GROUP_PAIRS, GROUP_PAIRS), GROUP_PAIRS), :]
        tot_rows = small_ref[pl.ds(pl.multiple_of(ROW_TOT + j * GROUP_PAIRS, GROUP_PAIRS), GROUP_PAIRS), :]
        seg_grad = jnp.zeros((GROUP_HEADS, T), F32)
        dt_grad = jnp.zeros((GROUP_HEADS, T), F32)
        skips = [skips_ref[span(j, GROUP_PAIRS), :]]
        terms = []
        fill_window(win_ref, before_ref[:, span(j, GROUP_X)], tok_ref[:, 0:GROUP_X])
        for q in range(0, GROUP_PAIRS, 2):
            lanes = slice(q * LANES, (q + 2) * LANES)
            wide = slice(jj * GROUP_X + q * LANES, jj * GROUP_X + (q + 2) * LANES)
            rise = widen_two(cols, 0, q)
            keep = widen_two(cols, HEADS, q)
            at = jj * GROUP_PAIRS + q
            state = jnp.concatenate([state_ref[0, at], state_ref[0, at + 1]], axis=1)
            exits = jnp.concatenate([state_ref[1, at], state_ref[1, at + 1]], axis=1)
            skip = jnp.concatenate([skip_rows[q : q + 1], skip_rows[q + 1 : q + 2]], axis=1)
            tot = jnp.concatenate([tot_rows[q : q + 1], tot_rows[q + 1 : q + 2]], axis=1)
            x = x_ref[:, lanes].astype(F32)
            g = g_ref[:, lanes].astype(F32)
            y = y_ref[:, lanes] + rise * dot(c, state)
            through = keep * dot(b, exits)
            gx = gx_ref[:, lanes] + through
            grad_c = grad_c + dot((g * rise).astype(BF16), state, NT)
            grad_b = grad_b + dot((x * keep).astype(BF16), exits, NT)
            out_ref[:, wide] = (y + skip * x).astype(BF16)
            grad_pre = (gx + skip * g) * slope_ref[:, lanes]
            pre_ref[:, wide] = grad_pre
            if theirs:
                at = pl.ds(pl.multiple_of(j * GROUP_X + q * LANES, 2 * LANES), 2 * LANES)
                head_ref[:, at] = grad_pre[0:8]
            terms += by_rows(tap_sums(grad_pre, q * LANES))
            x_gx = x * gx
            end = jnp.sum(x * through, axis=0, keepdims=True) + jnp.exp(tot) * jnp.sum(
                exits.astype(F32) * state.astype(F32), axis=0, keepdims=True
            )
            moved = g * y - x_gx
            moved = jnp.concatenate([moved[: T - 8], moved[T - 8 :] + jnp.where(last, end, 0.0)], axis=0)
            pick = (
                iota((GROUP_HEADS, 2 * LANES), 0)
                == 2 * q + iota((GROUP_HEADS, 2 * LANES), 1) // HEAD_DIM
            ).astype(F32).astype(BF16)
            for part in split_two(moved):
                seg_grad = seg_grad + dot(pick, part, NT)
            for part in split_two(x_gx):
                dt_grad = dt_grad + dot(pick, part, NT)
            if q % 4 == 2:
                size = GROUP_X // 2
                near_at = pl.ds(jj * GROUP_X + (q // 4) * size, size)
                far_at = span(2 * j + q // 4, size)
                save(out_ref.at[:, near_at], out_h.at[:, far_at])
                if theirs:
                    save(pre_ref.at[:, near_at], pre_h.at[:, near_at])
        for grad, base in ((grad_b, 0), (grad_c, 1)):
            at = HALF_X + (base * HALF_GROUPS + jj) * STATE
            tail = slice(GROUP_X + base * STATE, GROUP_X + (base + 1) * STATE)
            far_at = span(WIDTH_X // STATE + base * GROUPS + j, STATE)
            fill_window(win_ref, before_ref[:, far_at], tok_ref[:, tail])
            grad_pre = grad * slope_ref[:, tail]
            pre_ref[:, at : at + STATE] = grad_pre
            if theirs:
                head_ref[:, far_at] = grad_pre[0:8]
                save(pre_ref.at[:, pl.ds(at, STATE)], pre_h.at[:, pl.ds(at, STATE)])
            terms += tap_sums(grad_pre, 0)
        heads = span(j, GROUP_HEADS)
        behind = exact_dot(seg_grad, lower)
        dt = small_ref[pl.ds(pl.multiple_of(ROW_DT + j * GROUP_HEADS, GROUP_HEADS), GROUP_HEADS), :]
        decay = small_ref[pl.ds(pl.multiple_of(ROW_DECAY + j * GROUP_HEADS, GROUP_HEADS), GROUP_HEADS), :]
        near = pl.ds(jj * GROUP_HEADS, GROUP_HEADS)
        step_ref[near, :] = (dt_grad / dt + decay * behind) * sigmoid(raw_ref[heads, :])
        save(step_ref.at[near], step_h.at[heads])
        rows = jj * SUM_GROUP
        sum_ref[rows : rows + SUM_GROUP, :] = jnp.concatenate(terms + skips + [dt * behind * decay], axis=0)
    wait_all(fetches)
    if theirs:
        first_ref[...] = head_ref[0 : TAPS - 1, :].astype(BF16)
    wait_all(saves)


def run_leave(core, state, near, common, far, before_out):
    theirs = before_out is not None
    out = [
        ("h", (T, WIDTH_X), BF16),
        ("h", (HEADS, T), F32),
        ("h" if theirs else "V", (T, HALF_X + HALF_B), F32),
        ("V", (HALF_GROUPS * SUM_GROUP, LANES), F32),
    ]
    scratch = [
        pltpu.VMEM((T, HALF_X), BF16),
        pltpu.VMEM((HALF_GROUPS * GROUP_HEADS, T), F32),
        pltpu.VMEM((8 + T, GROUP_X), F32),
        DMA(2 + HALF_GROUPS, FETCHES),
    ]
    args = [core, state, *near, *common, *far]
    specs = "s" + ("v" if theirs else "V") + "V" * (len(near) + len(COMMON)) + "h" * len(far)
    aliases = {}
    if theirs:
        done, pre_own = before_out
        args += [pre_own]
        aliases = {len(args) + i: i for i in range(2)}
        args += done
        specs += "Vhh"
        out += [("V", (TAPS - 1, CHANNELS), BF16)]
        scratch = [pltpu.VMEM((8, CHANNELS), F32), pltpu.VMEM((T, HALF_X + HALF_B), F32)] + scratch
    else:
        out += NEAR * HALF_GROUPS
    kernel = functools.partial(leave_kernel, theirs)
    outs = call(kernel, "leave", out, specs, 5, scratch, mib=8, aliases=aliases)(*args)
    return outs[:2], outs[2], outs[3], outs[4:]


def spread_kernel(core_ref, own_ref, theirs_h, halo_ref, weight_ref, out_h, theirs_ref, out_ref, win_ref, sems):
    load = start_all([(theirs_h, theirs_ref)], sems.at[pl.ds(8, 1)])
    saves = []
    size = HALF_GROUPS * STATE
    for side, pre_ref in enumerate((own_ref, theirs_ref)):
        half = 1 - core_ref[0] if side else core_ref[0]
        if side:
            wait_all(load)
        blocks = [(jj * GROUP_X, span(half * HALF_GROUPS + jj, GROUP_X), GROUP_X) for jj in range(HALF_GROUPS)]
        blocks += [
            (HALF_X + base * size, span(WIDTH_X // size + 2 * base + half, size), size) for base in range(2)
        ]
        for near, far, width in blocks:
            win_ref[0:T, 0:width] = pre_ref[:, near : near + width]
            win_ref[T : T + TAPS - 1, 0:width] = halo_ref[:, far].astype(F32)
            weights = weight_ref[:, far]
            base = side * (HALF_X + HALF_B) + near
            for lo in range(0, width, LANES):
                at = slice(lo, lo + LANES)
                acc = weights[0:1, at] * win_ref[3 : 3 + T, at]
                for k in range(1, TAPS):
                    acc = acc + weights[k : k + 1, at] * win_ref[3 - k : 3 - k + T, at]
                out_ref[:, base + lo : base + lo + LANES] = acc.astype(BF16)
            copy = pltpu.make_async_copy(out_ref.at[:, pl.ds(base, width)], out_h.at[:, far], sems.at[len(saves)])
            copy.start()
            saves.append(copy)
    wait_all(saves)


def run_spread(core, own, theirs, halo, weight):
    out = [("h", (T, CHANNELS), BF16)]
    scratch = [
        pltpu.VMEM((T, HALF_X + HALF_B), F32),
        pltpu.VMEM((T, CHANNELS), BF16),
        pltpu.VMEM((T + 8, GROUP_X), F32),
        DMA(9),
    ]
    return call(spread_kernel, "spread", out, "sVhvV", 3, scratch, mib=8)(core, own, theirs, halo, weight)[0]


CONV_ROWS = TAPS * (CHANNELS // LANES)
CONV_GROUP = CONV_ROWS // GROUPS
SEND_ROWS = CONV_ROWS + 16


def write_send(out_ref, conv, thin):
    high = thin.astype(BF16).astype(F32)
    low = thin - high
    row = iota((16, LANES), 0)
    out_ref[0:CONV_ROWS, :] = conv.astype(BF16)
    out_ref[CONV_ROWS:SEND_ROWS, :] = jnp.where(row == 0, high, jnp.where(row == 1, low, 0.0)).astype(BF16)


def read_send(value):
    wide = value.astype(F32)
    return wide[0:CONV_ROWS], wide[CONV_ROWS : CONV_ROWS + 1] + wide[CONV_ROWS + 1 : CONV_ROWS + 2]


def merge_kernel(core_ref, own_ref, own_got_ref, theirs_ref, theirs_got_ref, out_ref):
    thin = jnp.zeros((8, LANES), F32)
    left = iota((8, LANES), 1) < HEAD_DIM
    count = HEADS // 2
    parts = []
    for side, (mine, other) in enumerate(((own_ref, theirs_got_ref), (theirs_ref, own_got_ref))):
        half = 1 - core_ref[0] if side else core_ref[0]
        total = mine[...] + other[...]
        rows, skips, decays = [], [], []
        for jj in range(HALF_GROUPS):
            at = jj * SUM_GROUP
            rows.append(total[at : at + CONV_GROUP])
            skips.append(total[at + CONV_GROUP : at + SUM_GROUP - GROUP_HEADS])
            decays.append(total[at + SUM_GROUP - GROUP_HEADS : at + SUM_GROUP])
        skips = jnp.concatenate(skips, axis=0)
        even = exact_dot(jnp.where(left, 1.0, 0.0), skips, NT)
        odd = exact_dot(jnp.where(left, 0.0, 1.0), skips, NT)
        decay = exact_dot(jnp.ones((8, LANES), F32), jnp.concatenate(decays, axis=0), NT)
        for part, step, shift in ((even, 2, 0), (odd, 2, 1), (decay, 1, HEADS)):
            size = part.shape[1]
            spot = (iota((size, LANES), 1) == step * iota((size, LANES), 0) + shift + half * count).astype(F32)
            thin = thin + exact_dot(part, spot)
        parts.append(jnp.concatenate(rows, axis=0))
    first = core_ref[0] == 0
    conv = jnp.concatenate(
        [jnp.where(first, parts[0], parts[1]), jnp.where(first, parts[1], parts[0])], axis=0
    )
    write_send(out_ref, conv, thin[0:1])


def run_merge(core, own, own_got, theirs, theirs_got):
    out = [("v", (SEND_ROWS, LANES), BF16)]
    return call(merge_kernel, "merge", out, "svvvv", 1, mib=4)(core, own, own_got, theirs, theirs_got)[0]


def ring_sum(core_ref, me_ref, refs, hold_ref):
    count = len(refs)
    sides = (count - 1) // 2
    hold_ref[0] = refs[0][...]
    for k in range(1, sides + 1):
        mine = jnp.where(core_ref[0] == 0, k, count - k)
        hold_ref[mine] = refs[k][...]
        hold_ref[count - mine] = refs[sides + k][...]
    if count % 2 == 0:
        hold_ref[count // 2] = refs[count - 1][...]
    conv, thin = read_send(hold_ref[lax.rem(me_ref[0], count)])
    for k in range(1, count):
        more, little = read_send(hold_ref[lax.rem(me_ref[0] + count - k, count)])
        conv, thin = conv + more, thin + little
    return conv, thin


def fold_kernel(core_ref, me_ref, *rest):
    *refs, out_ref, hold_ref = rest
    write_send(out_ref, *ring_sum(core_ref, me_ref, refs, hold_ref))


def run_fold(core, me, values):
    out = [("v", (SEND_ROWS, LANES), BF16)]
    scratch = [pltpu.VMEM((len(values), SEND_ROWS, LANES), BF16)]
    return call(fold_kernel, "fold", out, "ss" + "v" * len(values), 1, scratch, mib=4)(core, me, *values)[0]


def finish_kernel(core_ref, me_ref, *rest):
    *refs, conv_ref, decay_ref, skip_ref, hold_ref = rest
    conv, thin = ring_sum(core_ref, me_ref, refs, hold_ref)
    for i in range(CHANNELS // LANES):
        if i < PAIRS:
            row = CONV_GROUP * (i // GROUP_PAIRS) + TAPS * (i % GROUP_PAIRS)
        else:
            kind, group = divmod(i - PAIRS, GROUPS)
            row = CONV_GROUP * group + TAPS * (GROUP_PAIRS + kind)
        conv_ref[:, i * LANES : (i + 1) * LANES] = conv[row : row + TAPS]
    skip_ref[...] = thin[:, 0:HEADS]
    decay_ref[...] = thin[:, HEADS:]


def run_finish(core, me, values):
    out = [("v", (TAPS, CHANNELS), F32), ("v", (1, HEADS), F32), ("v", (1, HEADS), F32)]
    scratch = [pltpu.VMEM((len(values), SEND_ROWS, LANES), BF16)]
    return call(finish_kernel, "finish", out, "ss" + "v" * len(values), 1, scratch, mib=4)(core, me, *values)


CTX = ("chip", "core")
ALL = ("dp", "chip", "core")


def all_to_all(value, axis):
    return lax.all_to_all(value, axis, 0, 0, tiled=True)


def tie(*values):
    return lax.optimization_barrier(values)


SIDE = 4


def around(value, axis, size, ring, move):
    def hear(first, second):
        return lax.ppermute(
            value,
            (axis, "core"),
            [(2 * i + side, 2 * move(i, d) + side) for i in range(size) for side, d in enumerate((first, second))],
        )

    middle = [hear(ring // 2, ring // 2)] if ring % 2 == 0 else []
    heard = [hear(k, ring - k) for k in range(1, (ring - 1) // 2 + 1)]
    swapped = [lax.ppermute(part, "core", [(0, 1), (1, 0)]) for part in heard]
    return [value] + heard + swapped + middle


def scalar(value):
    return value.astype(jnp.int32).reshape(1)


def local(conv_input, conv_weight, step_raw, decay_log, skip_gain, cotangent):
    chips = lax.axis_size("chip")
    devices = 2 * chips
    sequences = lax.axis_size("dp")
    tokens = conv_input[0]
    raw = step_raw[0]
    cot = cotangent[0]
    core = lax.axis_index("core").astype(jnp.int32).reshape(1)
    swap = [(0, 1), (1, 0)]
    halo = lax.ppermute(tokens[T - TAPS + 1 :], CTX, [(i, i + 1) for i in range(devices - 1)])
    small, small_near, tot, x0, bc0, head, weight_near, cot_near = run_begin(
        raw, decay_log.reshape(1, HEADS), skip_gain.reshape(1, HEADS), tokens, conv_weight, cot
    )
    other = lax.ppermute(tot, "core", swap)
    x, bc, before, x_near, bc_near, out = run_enter(
        core, x0, bc0, head, halo, weight_near, cot_near, small_near
    )
    got_near = lax.ppermute(out, "core", swap)
    own_near = run_own(core, x_near, bc_near, cot_near, small_near)
    packed, left, right, tots = run_pack(core, own_near, got_near, tot, other)
    heard = all_to_all(packed, "chip")
    y, gbc, skips = run_inner(x, bc, cot, small)
    heard, y, gbc, skips = tie(heard, y, gbc, skips)
    chained = run_chain(chips, heard)
    late, chained = tie(bc, chained)
    back = all_to_all(chained, "chip")
    gx, slope = run_slopes(late, cot, small, tokens, before, conv_weight)
    back, gx, slope = tie(back, gx, slope)
    far = (x, cot, y, gx, slope, tokens, bc, gbc)
    mine, send, near, common = run_unpack(
        core, back, left, right, tots, far, (before, small, raw, skips, conv_weight)
    )
    theirs = lax.ppermute(send, "core", swap)
    half, pre_own, sum_own, near = run_leave(core, mine, near, common, far, None)
    sum_own_got = lax.ppermute(sum_own, "core", swap)
    (out_tokens, grad_step), pre_theirs, sum_theirs, (first,) = run_leave(
        core, theirs, near, common, (), (half, pre_own)
    )
    sum_theirs_got = lax.ppermute(sum_theirs, "core", swap)
    after = lax.ppermute(first, CTX, [(i + 1, i) for i in range(devices - 1)])
    sums = run_merge(core, sum_own, sum_own_got, sum_theirs, sum_theirs_got)
    chip, sequence = lax.axis_index("chip"), lax.axis_index("dp")
    rows = chips // SIDE
    values = around(sums, "chip", chips, SIDE, lambda i, d: i // SIDE * SIDE + (i % SIDE + d) % SIDE)
    values, after = tie(values, after)
    sums = run_fold(core, scalar(lax.rem(chip, SIDE)), values)
    values = around(sums, "chip", chips, rows, lambda i, d: (i + d * SIDE) % chips)
    grad_tokens = run_spread(core, pre_own, pre_theirs, after, common[4])
    values, grad_tokens = tie(values, grad_tokens)
    sums = run_fold(core, scalar(lax.div(chip, SIDE)), values)
    near = 2 if sequences % 2 == 0 else 1
    if near > 1:
        values = around(sums, "dp", sequences, near, lambda i, d: i // 2 * 2 + (i % 2 + d) % 2)
        sums = run_fold(core, scalar(lax.rem(sequence, near)), values)
    values = around(sums, "dp", sequences, sequences // near, lambda i, d: (i + d * near) % sequences)
    grad_conv, grad_decay, grad_skip = run_finish(core, scalar(lax.div(sequence, near)), values)
    return (
        out_tokens[None],
        grad_tokens[None],
        grad_step[None],
        grad_conv,
        grad_decay.reshape(HEADS),
        grad_skip.reshape(HEADS),
    )


def solution(mesh):
    dp, ctx = mesh.devices.shape
    fine = Mesh(mesh.devices.reshape(dp, ctx // 2, 2), ALL)
    seq = P("dp", CTX, None)
    rate = P("dp", None, CTX)
    in_specs = (seq, P(), rate, P(), P(), seq)
    out_specs = (seq, seq, rate, P(), P(), P())
    return jax.shard_map(local, mesh=fine, in_specs=in_specs, out_specs=out_specs, check_vma=False)
```

```python
import functools

import jax
import jax.numpy as jnp
from jax import lax
from jax.experimental import pallas as pl
from jax.experimental.pallas import tpu as pltpu
from jax.sharding import Mesh
from jax.sharding import PartitionSpec as P

HEADS = 64
HEAD_DIM = 64
GROUPS = 4
STATE = 128
TAPS = 4
T = 128
LANES = 128
WIDTH_X = HEADS * HEAD_DIM
WIDTH_B = GROUPS * STATE
CHANNELS = WIDTH_X + 2 * WIDTH_B
GROUP_X = WIDTH_X // GROUPS
PAIRS = HEADS // 2
GROUP_PAIRS = PAIRS // GROUPS
GROUP_HEADS = HEADS // GROUPS
HALF_PAIRS = PAIRS // 2
HALF_GROUPS = GROUPS // 2
F32 = jnp.float32
BF16 = jnp.bfloat16
EXACT = lax.Precision.HIGHEST
NN = (((1,), (0,)), ((), ()))
NT = (((1,), (1,)), ((), ()))
SUM_GROUP = 64
PACK_ROWS = 2 * STATE + 16


def dot(a, b, dims=NN):
    return lax.dot_general(a, b, dims, preferred_element_type=F32)


def exact_dot(a, b, dims=NN):
    return lax.dot_general(a, b, dims, precision=EXACT, preferred_element_type=F32)


def iota(shape, dim):
    return lax.broadcasted_iota(jnp.int32, shape, dim)


def sigmoid(v):
    return 0.5 + 0.5 * jnp.tanh(0.5 * v)


def split_two(v):
    high = v.astype(BF16)
    return high, (v - high.astype(F32)).astype(BF16)


def span(index, size):
    return pl.ds(pl.multiple_of(index * size, size), size)


def pin(value, space):
    return pltpu.with_memory_space_constraint(value, space)


def placed(space, shape, dtype):
    return space(shape, dtype)


def call(kernel, name, outs, specs, micros, scratch=(), mib=28, aliases=None):
    cost = pl.CostEstimate(
        flops=int(micros * 1e9), transcendentals=0, bytes_accessed=int(micros * 3.6e6)
    )
    blocks = {
        "s": pl.BlockSpec(memory_space=pltpu.SMEM),
        "v": pl.BlockSpec(memory_space=pltpu.VMEM),
        "V": pl.BlockSpec(memory_space=pltpu.VMEM),
        "h": pl.BlockSpec(memory_space=pltpu.HBM),
    }
    spaces = {"V": pltpu.VMEM, "h": pltpu.HBM}
    shapes = [
        placed(spaces[p], shape, dtype) if p in spaces else jax.ShapeDtypeStruct(shape, dtype)
        for p, shape, dtype in outs
    ]
    run = pl.pallas_call(
        kernel,
        out_shape=shapes,
        in_specs=[blocks[p] for p in specs],
        out_specs=[blocks[p] for p, _, _ in outs],
        scratch_shapes=list(scratch),
        input_output_aliases=aliases or {},
        cost_estimate=cost,
        compiler_params=pltpu.CompilerParams(vmem_limit_bytes=mib << 20),
        name=name,
    )

    def go(*args):
        return run(*[pin(a, spaces[p]) if p in spaces else a for a, p in zip(args, specs, strict=True)])

    return go


def start_all(pairs, sems):
    copies = [pltpu.make_async_copy(a, b, sems.at[i]) for i, (a, b) in enumerate(pairs)]
    for copy in copies:
        copy.start()
    return copies


def wait_all(copies):
    for copy in copies:
        copy.wait()


def DMA(*shape):
    return pltpu.SemaphoreType.DMA(shape)


def fill_window(win_ref, before, tokens):
    width = tokens.shape[1]
    win_ref[0:8, :width] = before
    win_ref[8 : 8 + T, :width] = tokens.astype(F32)


def pre_conv(win_ref, weights, lo):
    cols = slice(lo, lo + LANES)
    acc = weights[0:1, cols] * win_ref[5 : 5 + T, cols]
    for k in range(1, TAPS):
        acc = acc + weights[k : k + 1, cols] * win_ref[5 + k : 5 + k + T, cols]
    return acc


BLOCKS = CHANNELS // GROUP_X


ROW_DT, ROW_SEG, ROW_COLS, ROW_SCALE, ROW_TOT, ROW_SKIP, ROW_DECAY, SMALL_ROWS = (
    0, 64, 128, 256, 384, 416, 448, 512
)


def begin_kernel(raw_h, decay_log_h, skip_gain_h, tok_h, weight_h, g_h,
                 small_h, small_ref, tot_ref, x_ref, bc_ref, head_ref, weight_ref, g_ref,
                 raw_ref, decay_log_ref, skip_gain_ref, wide_ref, hold_ref, win_ref, sems):
    first = start_all(
        [(raw_h, raw_ref), (decay_log_h, decay_log_ref), (skip_gain_h, skip_gain_ref), (weight_h, weight_ref)],
        sems.at[0],
    )
    blocks = [pl.ds(i * GROUP_X, GROUP_X) for i in range(BLOCKS)]
    copies = start_all([(tok_h.at[:, at], hold_ref.at[:, at]) for at in blocks], sems.at[1])
    later = start_all([(g_h, g_ref)], sems.at[2])
    win_ref[0:8, :] = jnp.zeros((8, GROUP_X), F32)
    copies[0].wait()
    diagonal = iota((HEADS, HEADS), 0) == iota((HEADS, HEADS), 1)

    def column(row):
        return jnp.sum(jnp.where(diagonal, row, 0.0), axis=1, keepdims=True)

    wait_all(first)
    raw = raw_ref[...]
    dt = jnp.log1p(jnp.exp(raw))
    decay = -jnp.exp(column(decay_log_ref[...]))
    upper = (iota((T, T), 0) <= iota((T, T), 1)).astype(F32)
    seg = exact_dot(dt * decay, upper)
    total = seg[:, T - 1 : T]
    small_ref[ROW_DT : ROW_DT + HEADS] = dt
    small_ref[ROW_SEG : ROW_SEG + HEADS] = seg
    small_ref[ROW_COLS : ROW_COLS + T] = jnp.transpose(jnp.concatenate([seg, dt], axis=0))
    small_ref[ROW_SCALE : ROW_SCALE + T] = jnp.transpose(
        jnp.concatenate([jnp.exp(seg), jnp.exp(total - seg) * dt], axis=0)
    )
    left = iota((PAIRS, LANES), 1) < HEAD_DIM

    def paired(col):
        wide_ref[...] = jnp.broadcast_to(col, (HEADS, LANES))
        return jnp.where(left, wide_ref[pl.ds(0, PAIRS, 2), :], wide_ref[pl.ds(1, PAIRS, 2), :])

    tot = paired(total)
    tot_ref[...] = tot
    small_ref[ROW_TOT : ROW_TOT + PAIRS] = tot
    small_ref[ROW_SKIP : ROW_SKIP + PAIRS] = paired(column(skip_gain_ref[...]))
    small_ref[ROW_DECAY : ROW_DECAY + HEADS] = jnp.broadcast_to(decay, (HEADS, LANES))
    save = start_all([(small_ref, small_h)], sems.at[0])
    for i in range(BLOCKS):
        if i:
            copies[i].wait()
        cols = slice(i * GROUP_X, (i + 1) * GROUP_X)
        win_ref[8 : 8 + T, :] = hold_ref[:, cols].astype(F32)
        for lo in range(0, GROUP_X, LANES):
            at = i * GROUP_X + lo
            pre = pre_conv(win_ref, weight_ref[:, cols], lo)
            mixed = (pre * sigmoid(pre)).astype(BF16)
            head_ref[:, at : at + LANES] = pre[0:8]
            if at < WIDTH_X:
                x_ref[:, at : at + LANES] = mixed
            else:
                bc_ref[:, at - WIDTH_X : at - WIDTH_X + LANES] = mixed
    wait_all(save + later)


def run_begin(raw, decay_log, skip_gain, tokens, weight, cot):
    out = [
        ("h", (SMALL_ROWS, LANES), F32),
        ("V", (SMALL_ROWS, LANES), F32),
        ("V", (PAIRS, LANES), F32),
        ("V", (T, WIDTH_X), BF16),
        ("V", (T, 2 * WIDTH_B), BF16),
        ("V", (8, CHANNELS), F32),
        ("V", (TAPS, CHANNELS), F32),
        ("V", (T, WIDTH_X), BF16),
    ]
    scratch = [
        pltpu.VMEM((HEADS, T), F32),
        pltpu.VMEM((1, HEADS), F32),
        pltpu.VMEM((1, HEADS), F32),
        pltpu.VMEM((HEADS, LANES), F32),
        pltpu.VMEM((T, CHANNELS), BF16),
        pltpu.VMEM((8 + T, GROUP_X), F32),
        DMA(3, BLOCKS),
    ]
    return call(begin_kernel, "begin", out, "hhhhhh", 4, scratch, mib=8)(
        raw, decay_log, skip_gain, tokens, weight, cot
    )


def rolled(cols, group):
    return pltpu.roll(cols, (LANES - group * GROUP_HEADS) % LANES, 1)


def widen(cols, base, pair):
    first = iota((T, LANES), 1) < HEAD_DIM
    at = base + 2 * pair
    return jnp.where(first, cols[:, at : at + 1], cols[:, at + 1 : at + 2])


def widen_two(cols, base, pair):
    return jnp.concatenate([widen(cols, base, pair), widen(cols, base, pair + 1)], axis=1)


def fill_half(half, x_ref, bc_ref, g_ref, scale, dst_ref):
    for jj in range(HALF_GROUPS):
        j = half * HALF_GROUPS + jj
        b_flip = jnp.transpose(bc_ref[:, span(j, STATE)].astype(F32)).astype(BF16)
        c_flip = jnp.transpose(bc_ref[:, span(GROUPS + j, STATE)].astype(F32)).astype(BF16)
        cols = rolled(scale, j)
        for q in range(0, GROUP_PAIRS, 2):
            lanes = pl.ds(pl.multiple_of(j * GROUP_X + q * LANES, 2 * LANES), 2 * LANES)
            xw = (x_ref[:, lanes].astype(F32) * widen_two(cols, HEADS, q)).astype(BF16)
            gw = (g_ref[:, lanes].astype(F32) * widen_two(cols, 0, q)).astype(BF16)
            state = dot(b_flip, xw).astype(BF16)
            grad = dot(c_flip, gw).astype(BF16)
            for k in range(2):
                at = jj * GROUP_PAIRS + q + k
                dst_ref[0, at] = state[:, k * LANES : (k + 1) * LANES]
                dst_ref[1, at] = grad[:, k * LANES : (k + 1) * LANES]


def enter_kernel(core_ref, x0_ref, bc0_ref, head_ref, halo_ref, weight_ref, g_ref, small_ref,
                 x_h, bc_h, before_h, x_ref, bc_ref, out_ref, before_ref, sems):
    half = 1 - core_ref[0]
    row = iota((8, GROUP_X), 0)
    for i in range(BLOCKS):
        cols = slice(i * GROUP_X, (i + 1) * GROUP_X)
        halo = halo_ref[:, cols].astype(F32)
        weight = weight_ref[:, cols]
        pre = head_ref[:, cols]
        before = jnp.zeros((8, GROUP_X), F32)
        for t in range(TAPS - 1):
            extra = jnp.zeros((1, GROUP_X), F32)
            for k in range(TAPS - 1 - t):
                extra = extra + weight[k : k + 1] * halo[t + k : t + k + 1]
            pre = pre + jnp.where(row == t, extra, 0.0)
            before = before + jnp.where(row == t + 5, halo[t : t + 1], 0.0)
        before_ref[:, cols] = before
        fixed = pre * sigmoid(pre)
        src, dst, at = (x0_ref, x_ref, cols) if i < GROUPS else (bc0_ref, bc_ref, slice(0, GROUP_X))
        rest = src[0:16, at].astype(F32)
        dst[16:T, at] = src[16:T, at]
        dst[0:16, at] = jnp.concatenate([fixed, rest[8:16]], axis=0).astype(BF16)
    saves = start_all([(x_ref, x_h), (bc_ref, bc_h), (before_ref, before_h)], sems)
    fill_half(half, x_ref, bc_ref, g_ref, small_ref[ROW_SCALE : ROW_SCALE + T], out_ref)
    wait_all(saves)


def run_enter(core, x0, bc0, head, halo, weight, cot, small):
    out = [
        ("h", (T, WIDTH_X), BF16),
        ("h", (T, 2 * WIDTH_B), BF16),
        ("h", (8, CHANNELS), F32),
        ("V", (T, WIDTH_X), BF16),
        ("V", (T, 2 * WIDTH_B), BF16),
        ("V", (2, HALF_PAIRS, STATE, LANES), BF16),
    ]
    scratch = [pltpu.VMEM((8, CHANNELS), F32), DMA(3)]
    return call(enter_kernel, "enter", out, "sVVVvVVV", 3, scratch, mib=6)(
        core, x0, bc0, head, halo, weight, cot, small
    )


def own_kernel(core_ref, x_ref, bc_ref, g_ref, small_ref, own_ref):
    fill_half(core_ref[0], x_ref, bc_ref, g_ref, small_ref[ROW_SCALE : ROW_SCALE + T], own_ref)


def run_own(core, x, bc, cot, small):
    out = [("V", (2, HALF_PAIRS, STATE, LANES), BF16)]
    return call(own_kernel, "own", out, "sVVVV", 3, mib=6)(core, x, bc, cot, small)[0]


STEP_PAIRS = 4
STEPS = HALF_PAIRS // STEP_PAIRS


def pack_kernel(core_ref, own_ref, got_ref, tot_ref, other_ref,
                out_h, left_h, right_h, tots_h, out_ref, sems):
    saves = start_all(
        [(tot_ref, tots_h.at[pl.ds(0, PAIRS)]), (other_ref, tots_h.at[pl.ds(PAIRS, PAIRS)])], sems.at[0]
    )
    second = core_ref[0] == 1

    def keep(first_ref, last_ref):
        return [
            pltpu.make_async_copy(first_ref.at[0], left_h, sems.at[0, 2]),
            pltpu.make_async_copy(last_ref.at[1], right_h, sems.at[0, 3]),
        ]

    @pl.when(second)
    def _():
        for copy in keep(got_ref, own_ref):
            copy.start()

    @pl.when(jnp.logical_not(second))
    def _():
        for copy in keep(own_ref, got_ref):
            copy.start()

    saves += keep(own_ref, got_ref)
    outs = []
    for i in range(HALF_PAIRS):
        at = core_ref[0] * HALF_PAIRS + i
        tot = tot_ref[pl.ds(at, 1), :]
        other = other_ref[pl.ds(at, 1), :]
        one = jnp.ones_like(tot)
        by_own = jnp.exp(tot)
        by_other = jnp.exp(other)
        state = (
            jnp.where(second, one, by_other) * own_ref[0, i].astype(F32)
            + jnp.where(second, by_own, one) * got_ref[0, i].astype(F32)
        )
        grad = (
            jnp.where(second, by_other, one) * own_ref[1, i].astype(F32)
            + jnp.where(second, one, by_own) * got_ref[1, i].astype(F32)
        )
        out_ref[i, 0:STATE, :] = state.astype(BF16)
        out_ref[i, STATE : 2 * STATE, :] = grad.astype(BF16)
        both = tot + other
        high = both.astype(BF16).astype(F32)
        mid = (both - high).astype(BF16).astype(F32)
        low = both - high - mid
        row = iota((16, LANES), 0)
        wide = jnp.where(row == 0, high, jnp.where(row == 1, mid, jnp.where(row == 2, low, 0.0)))
        out_ref[i, 2 * STATE : PACK_ROWS, :] = wide.astype(BF16)
        if i % STEP_PAIRS == STEP_PAIRS - 1:
            done = pl.ds(i + 1 - STEP_PAIRS, STEP_PAIRS)
            copy = pltpu.make_async_copy(out_ref.at[done], out_h.at[done], sems.at[1, i // STEP_PAIRS])
            copy.start()
            outs.append(copy)
    wait_all(outs + saves)


def run_pack(core, own, got, tot, other):
    half = (HALF_PAIRS, STATE, LANES)
    packed = (HALF_PAIRS, PACK_ROWS, LANES)
    out = [("h", packed, BF16), ("h", half, BF16), ("h", half, BF16), ("h", (2 * PAIRS, LANES), F32)]
    scratch = [pltpu.VMEM(packed, BF16), DMA(2, STEPS)]
    return call(pack_kernel, "pack", out, "sVvVv", 2, scratch, mib=8)(core, own, got, tot, other)


def chain_kernel(chips, per, in_ref, out_ref):
    for q in range(per):
        def decay(k):
            rows = in_ref[k * per + q, 2 * STATE : PACK_ROWS, :].astype(F32)
            return jnp.exp(rows[0:1] + rows[1:2] + rows[2:3])

        carry = jnp.zeros((STATE, LANES), F32)
        for k in range(chips):
            out_ref[k * per + q, 0:STATE, :] = carry.astype(BF16)
            if k < chips - 1:
                carry = decay(k) * carry + in_ref[k * per + q, 0:STATE, :].astype(F32)
        carry = jnp.zeros((STATE, LANES), F32)
        for k in reversed(range(chips)):
            out_ref[k * per + q, STATE : 2 * STATE, :] = carry.astype(BF16)
            if k > 0:
                carry = decay(k) * carry + in_ref[k * per + q, STATE : 2 * STATE, :].astype(F32)


def run_chain(chips, packed):
    kernel = functools.partial(chain_kernel, chips, HALF_PAIRS // chips)
    out = [("v", (HALF_PAIRS, 2 * STATE, LANES), BF16)]
    return call(kernel, "chain", out, "v", 1, mib=8)(packed)[0]


HALF_X = HALF_GROUPS * GROUP_X
HALF_B = 2 * HALF_GROUPS * STATE

NEAR = [
    ("V", (T, GROUP_X), BF16),
    ("V", (T, GROUP_X), BF16),
    ("V", (T, GROUP_X), F32),
    ("V", (T, GROUP_X), F32),
    ("V", (T, GROUP_X + 2 * STATE), F32),
    ("V", (T, GROUP_X + 2 * STATE), BF16),
    ("V", (T, 2 * STATE), BF16),
    ("V", (T, 2 * STATE), F32),
]
COMMON = [
    ("V", (8, CHANNELS), F32),
    ("V", (SMALL_ROWS, LANES), F32),
    ("V", (HEADS, T), F32),
    ("V", (PAIRS, LANES), F32),
    ("V", (TAPS, CHANNELS), F32),
]
FETCHES = 6 + 8


def fetch_group(j, far, near, sems):
    x_h, g_h, y_h, gx_h, slope_h, tok_h, bc_h, gbc_h = far
    x_v, g_v, y_v, gx_v, slope_v, tok_v, bc_v, gbc_v = near
    wide = pl.ds(0, GROUP_X)
    pairs = [
        (a.at[:, span(j, GROUP_X)], b.at[:, wide])
        for a, b in ((x_h, x_v), (g_h, g_v), (y_h, y_v), (gx_h, gx_v), (slope_h, slope_v), (tok_h, tok_v))
    ]
    for base in range(2):
        at = span(base * GROUPS + j, STATE)
        off = span(WIDTH_X // STATE + base * GROUPS + j, STATE)
        thin = pl.ds(base * STATE, STATE)
        tail = pl.ds(GROUP_X + base * STATE, STATE)
        pairs += [
            (bc_h.at[:, at], bc_v.at[:, thin]),
            (gbc_h.at[:, at], gbc_v.at[:, thin]),
            (slope_h.at[:, off], slope_v.at[:, tail]),
            (tok_h.at[:, off], tok_v.at[:, tail]),
        ]
    return start_all(pairs, sems)


def unpack_kernel(core_ref, back_ref, left_h, right_h, tots_h, *rest):
    far, rest = rest[: len(NEAR)], rest[len(NEAR) :]
    common_far, rest = rest[: len(COMMON)], rest[len(COMMON) :]
    mine_ref, send_ref, *rest = rest
    near = [rest[i * len(NEAR) : (i + 1) * len(NEAR)] for i in range(HALF_GROUPS)]
    rest = rest[HALF_GROUPS * len(NEAR) :]
    common, rest = rest[: len(COMMON)], rest[len(COMMON) :]
    left_ref, right_ref, tots_ref, sems, fetch_sems = rest
    first = start_all([(tots_h, tots_ref)], sems.at[STEPS])
    steps = []
    for step in range(STEPS):
        at = pl.ds(step * STEP_PAIRS, STEP_PAIRS)
        steps.append(
            start_all([(left_h.at[at], left_ref.at[at]), (right_h.at[at], right_ref.at[at])], sems.at[step])
        )
    fetches = start_all(list(zip(common_far, common)), fetch_sems.at[HALF_GROUPS])
    for jj in range(HALF_GROUPS):
        fetches += fetch_group(core_ref[0] * HALF_GROUPS + jj, far, near[jj], fetch_sems.at[jj])
    wait_all(first)
    second = core_ref[0] == 1
    for i in range(HALF_PAIRS):
        if i % STEP_PAIRS == 0:
            wait_all(steps[i // STEP_PAIRS])
        at = core_ref[0] * HALF_PAIRS + i
        tot = tots_ref[pl.ds(at, 1), :]
        other = tots_ref[pl.ds(PAIRS + at, 1), :]
        decay_zero = jnp.exp(jnp.where(second, other, tot))
        decay_one = jnp.exp(jnp.where(second, tot, other))
        state_zero = back_ref[i, 0:STATE, :].astype(F32)
        grad_one = back_ref[i, STATE : 2 * STATE, :].astype(F32)
        state_one = decay_zero * state_zero + left_ref[i].astype(F32)
        grad_zero = decay_one * grad_one + right_ref[i].astype(F32)
        mine_ref[0, i] = jnp.where(second, state_one, state_zero).astype(BF16)
        mine_ref[1, i] = jnp.where(second, grad_one, grad_zero).astype(BF16)
        send_ref[0, i] = jnp.where(second, state_zero, state_one).astype(BF16)
        send_ref[1, i] = jnp.where(second, grad_zero, grad_one).astype(BF16)
    wait_all(fetches)


def run_unpack(core, back, left, right, tots, far, common):
    half = (2, HALF_PAIRS, STATE, LANES)
    out = [("V", half, BF16)] * 2 + NEAR * HALF_GROUPS + COMMON
    scratch = [
        pltpu.VMEM(half[1:], BF16),
        pltpu.VMEM(half[1:], BF16),
        pltpu.VMEM((2 * PAIRS, LANES), F32),
        DMA(STEPS + 1, 2),
        DMA(HALF_GROUPS + 1, FETCHES),
    ]
    specs = "svhhh" + "h" * (len(NEAR) + len(COMMON))
    outs = call(unpack_kernel, "unpack", out, specs, 3, scratch, mib=8)(
        core, back, left, right, tots, *far, *common
    )
    at = 2 + HALF_GROUPS * len(NEAR)
    return outs[0], outs[1], outs[2:at], outs[at:]


def by_lane_half(v):
    first = iota(v.shape, 1) < HEAD_DIM
    wide = v.astype(F32)
    return jnp.concatenate(
        [jnp.where(first, wide, 0.0).astype(BF16), jnp.where(first, 0.0, wide).astype(BF16)], axis=0
    )


def inner_kernel(x_h, bc_h, g_h, small_h, y_h, gbc_h, skips_h,
                 x_ref, bc_ref, g_ref, small_ref, y_ref, gbc_ref, skips_ref, sems):
    first = start_all([(bc_h, bc_ref), (small_h, small_ref)], sems.at[0])

    def loads(j):
        at = span(j, GROUP_X)
        return [
            pltpu.make_async_copy(x_h.at[:, at], x_ref.at[:, at], sems.at[1, j]),
            pltpu.make_async_copy(g_h.at[:, at], g_ref.at[:, at], sems.at[2, j]),
        ]

    def store(j):
        at = span(j, GROUP_X)
        return pltpu.make_async_copy(y_ref.at[:, at], y_h.at[:, at], sems.at[3, j])

    for j in range(GROUPS):
        for copy in loads(j):
            copy.start()
    wait_all(first)
    lower = iota((T, T), 0) >= iota((T, T), 1)

    @pl.loop(0, GROUPS)
    def _(j):
        wait_all(loads(j))
        b = bc_ref[:, span(j, STATE)]
        c = bc_ref[:, span(GROUPS + j, STATE)]
        seg = small_ref[pl.ds(pl.multiple_of(ROW_SEG + j * GROUP_HEADS, GROUP_HEADS), GROUP_HEADS), :]
        dt = small_ref[pl.ds(pl.multiple_of(ROW_DT + j * GROUP_HEADS, GROUP_HEADS), GROUP_HEADS), :]
        scores = dot(c, b, NT)
        cols = rolled(small_ref[ROW_COLS : ROW_COLS + T], j)
        total = jnp.zeros((T, T), F32)
        skips = []
        for i in range(GROUP_PAIRS):
            lanes = pl.ds(pl.multiple_of(j * GROUP_X + i * LANES, LANES), LANES)
            x = x_ref[:, lanes]
            g = g_ref[:, lanes]
            skips.append(jnp.sum(g.astype(F32) * x.astype(F32), axis=0, keepdims=True))
            inner = dot(by_lane_half(g), x, NT)
            weights = []
            for k in range(2):
                h = 2 * i + k
                spread = cols[:, h : h + 1] - seg[h : h + 1, :]
                kernel = jnp.exp(jnp.where(lower, spread, -1e30)) * dt[h : h + 1, :]
                total = total + kernel * inner[k * T : (k + 1) * T]
                weights.append((kernel * scores).astype(BF16))
            y_ref[:, lanes] = dot(jnp.concatenate(weights, axis=1), by_lane_half(x))
        skips_ref[span(j, GROUP_PAIRS), :] = jnp.concatenate(skips, axis=0)
        gbc_ref[:, span(GROUPS + j, STATE)] = dot(total.astype(BF16), b)
        gbc_ref[:, span(j, STATE)] = dot(jnp.transpose(total).astype(BF16), c)
        store(j).start()

    last = start_all([(gbc_ref, gbc_h), (skips_ref, skips_h)], sems.at[0])
    for j in range(GROUPS):
        store(j).wait()
    wait_all(last)


def run_inner(x, bc, cot, small):
    out = [("h", (T, WIDTH_X), F32), ("h", (T, 2 * WIDTH_B), F32), ("h", (PAIRS, LANES), F32)]
    scratch = [
        pltpu.VMEM((T, WIDTH_X), BF16),
        pltpu.VMEM((T, 2 * WIDTH_B), BF16),
        pltpu.VMEM((T, WIDTH_X), BF16),
        pltpu.VMEM((SMALL_ROWS, LANES), F32),
        pltpu.VMEM((T, WIDTH_X), F32),
        pltpu.VMEM((T, 2 * WIDTH_B), F32),
        pltpu.VMEM((PAIRS, LANES), F32),
        DMA(4, GROUPS),
    ]
    return call(inner_kernel, "inner", out, "hhhh", 4, scratch, mib=16)(x, bc, cot, small)


def slopes_kernel(bc_h, g_h, small_h, tok_h, before_h, weight_h, gx_h, slope_h,
                  bc_ref, g_ref, small_ref, tok_ref, before_ref, weight_ref, gx_ref, slope_ref, win_ref, sems):
    first = start_all(
        [(bc_h, bc_ref), (small_h, small_ref), (before_h, before_ref), (weight_h, weight_ref), (tok_h, tok_ref)],
        sems.at[0],
    )

    def load(j):
        at = span(j, GROUP_X)
        return pltpu.make_async_copy(g_h.at[:, at], g_ref.at[:, at], sems.at[1, j])

    def store(j):
        at = span(j, GROUP_X)
        return pltpu.make_async_copy(gx_ref.at[:, at], gx_h.at[:, at], sems.at[2, j])

    def store_slope(i):
        at = span(i, GROUP_X)
        return pltpu.make_async_copy(slope_ref.at[:, at], slope_h.at[:, at], sems.at[3, i])

    for j in range(GROUPS):
        load(j).start()
    wait_all(first)
    upper = iota((T, T), 0) <= iota((T, T), 1)

    @pl.loop(0, GROUPS)
    def _(j):
        load(j).wait()
        b = bc_ref[:, span(j, STATE)]
        c = bc_ref[:, span(GROUPS + j, STATE)]
        seg = small_ref[pl.ds(pl.multiple_of(ROW_SEG + j * GROUP_HEADS, GROUP_HEADS), GROUP_HEADS), :]
        scores = jnp.transpose(dot(c, b, NT))
        cols = rolled(small_ref[ROW_COLS : ROW_COLS + T], j)
        for i in range(GROUP_PAIRS):
            lanes = pl.ds(pl.multiple_of(j * GROUP_X + i * LANES, LANES), LANES)
            weights = []
            for k in range(2):
                h = 2 * i + k
                spread = seg[h : h + 1, :] - cols[:, h : h + 1]
                kernel = jnp.exp(jnp.where(upper, spread, -1e30)) * cols[:, HEADS + h : HEADS + h + 1]
                weights.append((kernel * scores).astype(BF16))
            gx_ref[:, lanes] = dot(jnp.concatenate(weights, axis=1), by_lane_half(g_ref[:, lanes]))
        store(j).start()

    @pl.loop(0, BLOCKS)
    def _(i):
        cols = span(i, GROUP_X)
        fill_window(win_ref, before_ref[:, cols], tok_ref[:, cols])
        weights = weight_ref[:, cols]
        for lo in range(0, GROUP_X, LANES):
            pre = pre_conv(win_ref, weights, lo)
            s = sigmoid(pre)
            at = pl.ds(pl.multiple_of(i * GROUP_X + lo, LANES), LANES)
            slope_ref[:, at] = s * (1.0 + pre * (1.0 - s))
        store_slope(i).start()

    for j in range(GROUPS):
        store(j).wait()
    for i in range(BLOCKS):
        store_slope(i).wait()


def run_slopes(bc, cot, small, tokens, before, weight):
    out = [("h", (T, WIDTH_X), F32), ("h", (T, CHANNELS), F32)]
    scratch = [
        pltpu.VMEM((T, 2 * WIDTH_B), BF16),
        pltpu.VMEM((T, WIDTH_X), BF16),
        pltpu.VMEM((SMALL_ROWS, LANES), F32),
        pltpu.VMEM((T, CHANNELS), BF16),
        pltpu.VMEM((8, CHANNELS), F32),
        pltpu.VMEM((TAPS, CHANNELS), F32),
        pltpu.VMEM((T, WIDTH_X), F32),
        pltpu.VMEM((T, CHANNELS), F32),
        pltpu.VMEM((8 + T, GROUP_X), F32),
        DMA(4, BLOCKS),
    ]
    return call(slopes_kernel, "slopes", out, "hhhhhh", 6, scratch, mib=16)(
        bc, cot, small, tokens, before, weight
    )


def leave_kernel(theirs, core_ref, state_ref, *rest):
    rest = list(rest)

    def take(count):
        taken = rest[:count]
        del rest[:count]
        return taken

    sets = [take(len(NEAR)) for _ in range(HALF_GROUPS)]
    before_ref, small_ref, raw_ref, skips_ref, _ = take(len(COMMON))
    half = 1 - core_ref[0] if theirs else core_ref[0]
    fetches = []
    if theirs:
        pre_own_ref, _, _ = take(3)
        out_h, step_h, pre_h, sum_ref, first_ref = take(5)
        head_ref, pre_ref, out_ref, step_ref, win_ref, sems = rest
        own = core_ref[0]
        head_ref[:, span(own, HALF_X)] = pre_own_ref[0:8, 0:HALF_X]
        size = HALF_GROUPS * STATE
        for base in range(2):
            at = HALF_X + base * size
            head_ref[:, span(WIDTH_X // size + 2 * base + own, size)] = pre_own_ref[0:8, at : at + size]
    else:
        far = take(len(NEAR))
        out_h, step_h, pre_ref, sum_ref = take(4)
        after = [take(len(NEAR)) for _ in range(HALF_GROUPS)]
        out_ref, step_ref, win_ref, sems = rest
        for jj in range(HALF_GROUPS):
            fetches += fetch_group((1 - half) * HALF_GROUPS + jj, far, after[jj], sems.at[2 + jj])
    last = iota((8, 2 * LANES), 0) == 7
    lower = (iota((T, T), 0) >= iota((T, T), 1)).astype(F32)

    def tap_sums(grad_pre, lo):
        width = grad_pre.shape[1]
        return [
            jnp.sum(grad_pre * win_ref[5 + k : 5 + k + T, lo : lo + width], axis=0, keepdims=True)
            for k in range(TAPS)
        ]

    def by_rows(sums):
        return [s[:, lo : lo + LANES] for lo in range(0, sums[0].shape[1], LANES) for s in sums]

    saves = []

    def save(src, dst):
        copy = pltpu.make_async_copy(src, dst, sems.at[len(saves) // 8, len(saves) % 8])
        copy.start()
        saves.append(copy)

    for jj in range(HALF_GROUPS):
        j = half * HALF_GROUPS + jj
        x_ref, g_ref, y_ref, gx_ref, slope_ref, tok_ref, bc_ref, gbc_ref = sets[jj]
        b = bc_ref[:, 0:STATE]
        c = bc_ref[:, STATE:]
        grad_b = gbc_ref[:, 0:STATE]
        grad_c = gbc_ref[:, STATE:]
        cols = rolled(small_ref[ROW_SCALE : ROW_SCALE + T], j)
        skip_rows = small_ref[pl.ds(pl.multiple_of(ROW_SKIP + j * GROUP_PAIRS, GROUP_PAIRS), GROUP_PAIRS), :]
        tot_rows = small_ref[pl.ds(pl.multiple_of(ROW_TOT + j * GROUP_PAIRS, GROUP_PAIRS), GROUP_PAIRS), :]
        seg_grad = jnp.zeros((GROUP_HEADS, T), F32)
        dt_grad = jnp.zeros((GROUP_HEADS, T), F32)
        skips = [skips_ref[span(j, GROUP_PAIRS), :]]
        terms = []
        fill_window(win_ref, before_ref[:, span(j, GROUP_X)], tok_ref[:, 0:GROUP_X])
        for q in range(0, GROUP_PAIRS, 2):
            lanes = slice(q * LANES, (q + 2) * LANES)
            wide = slice(jj * GROUP_X + q * LANES, jj * GROUP_X + (q + 2) * LANES)
            rise = widen_two(cols, 0, q)
            keep = widen_two(cols, HEADS, q)
            at = jj * GROUP_PAIRS + q
            state = jnp.concatenate([state_ref[0, at], state_ref[0, at + 1]], axis=1)
            exits = jnp.concatenate([state_ref[1, at], state_ref[1, at + 1]], axis=1)
            skip = jnp.concatenate([skip_rows[q : q + 1], skip_rows[q + 1 : q + 2]], axis=1)
            tot = jnp.concatenate([tot_rows[q : q + 1], tot_rows[q + 1 : q + 2]], axis=1)
            x = x_ref[:, lanes].astype(F32)
            g = g_ref[:, lanes].astype(F32)
            y = y_ref[:, lanes] + rise * dot(c, state)
            through = keep * dot(b, exits)
            gx = gx_ref[:, lanes] + through
            grad_c = grad_c + dot((g * rise).astype(BF16), state, NT)
            grad_b = grad_b + dot((x * keep).astype(BF16), exits, NT)
            out_ref[:, wide] = (y + skip * x).astype(BF16)
            grad_pre = (gx + skip * g) * slope_ref[:, lanes]
            pre_ref[:, wide] = grad_pre
            if theirs:
                at = pl.ds(pl.multiple_of(j * GROUP_X + q * LANES, 2 * LANES), 2 * LANES)
                head_ref[:, at] = grad_pre[0:8]
            terms += by_rows(tap_sums(grad_pre, q * LANES))
            x_gx = x * gx
            end = jnp.sum(x * through, axis=0, keepdims=True) + jnp.exp(tot) * jnp.sum(
                exits.astype(F32) * state.astype(F32), axis=0, keepdims=True
            )
            moved = g * y - x_gx
            moved = jnp.concatenate([moved[: T - 8], moved[T - 8 :] + jnp.where(last, end, 0.0)], axis=0)
            pick = (
                iota((GROUP_HEADS, 2 * LANES), 0)
                == 2 * q + iota((GROUP_HEADS, 2 * LANES), 1) // HEAD_DIM
            ).astype(F32).astype(BF16)
            for part in split_two(moved):
                seg_grad = seg_grad + dot(pick, part, NT)
            for part in split_two(x_gx):
                dt_grad = dt_grad + dot(pick, part, NT)
            if q % 4 == 2:
                size = GROUP_X // 2
                near_at = pl.ds(jj * GROUP_X + (q // 4) * size, size)
                far_at = span(2 * j + q // 4, size)
                save(out_ref.at[:, near_at], out_h.at[:, far_at])
                if theirs:
                    save(pre_ref.at[:, near_at], pre_h.at[:, near_at])
        for grad, base in ((grad_b, 0), (grad_c, 1)):
            at = HALF_X + (base * HALF_GROUPS + jj) * STATE
            tail = slice(GROUP_X + base * STATE, GROUP_X + (base + 1) * STATE)
            far_at = span(WIDTH_X // STATE + base * GROUPS + j, STATE)
            fill_window(win_ref, before_ref[:, far_at], tok_ref[:, tail])
            grad_pre = grad * slope_ref[:, tail]
            pre_ref[:, at : at + STATE] = grad_pre
            if theirs:
                head_ref[:, far_at] = grad_pre[0:8]
                save(pre_ref.at[:, pl.ds(at, STATE)], pre_h.at[:, pl.ds(at, STATE)])
            terms += tap_sums(grad_pre, 0)
        heads = span(j, GROUP_HEADS)
        behind = exact_dot(seg_grad, lower)
        dt = small_ref[pl.ds(pl.multiple_of(ROW_DT + j * GROUP_HEADS, GROUP_HEADS), GROUP_HEADS), :]
        decay = small_ref[pl.ds(pl.multiple_of(ROW_DECAY + j * GROUP_HEADS, GROUP_HEADS), GROUP_HEADS), :]
        near = pl.ds(jj * GROUP_HEADS, GROUP_HEADS)
        step_ref[near, :] = (dt_grad / dt + decay * behind) * sigmoid(raw_ref[heads, :])
        save(step_ref.at[near], step_h.at[heads])
        rows = jj * SUM_GROUP
        sum_ref[rows : rows + SUM_GROUP, :] = jnp.concatenate(terms + skips + [dt * behind * decay], axis=0)
    wait_all(fetches)
    if theirs:
        first_ref[...] = head_ref[0 : TAPS - 1, :].astype(BF16)
    wait_all(saves)


def run_leave(core, state, near, common, far, before_out):
    theirs = before_out is not None
    out = [
        ("h", (T, WIDTH_X), BF16),
        ("h", (HEADS, T), F32),
        ("h" if theirs else "V", (T, HALF_X + HALF_B), F32),
        ("V", (HALF_GROUPS * SUM_GROUP, LANES), F32),
    ]
    scratch = [
        pltpu.VMEM((T, HALF_X), BF16),
        pltpu.VMEM((HALF_GROUPS * GROUP_HEADS, T), F32),
        pltpu.VMEM((8 + T, GROUP_X), F32),
        DMA(2 + HALF_GROUPS, FETCHES),
    ]
    args = [core, state, *near, *common, *far]
    specs = "s" + ("v" if theirs else "V") + "V" * (len(near) + len(COMMON)) + "h" * len(far)
    aliases = {}
    if theirs:
        done, pre_own = before_out
        args += [pre_own]
        aliases = {len(args) + i: i for i in range(2)}
        args += done
        specs += "Vhh"
        out += [("V", (TAPS - 1, CHANNELS), BF16)]
        scratch = [pltpu.VMEM((8, CHANNELS), F32), pltpu.VMEM((T, HALF_X + HALF_B), F32)] + scratch
    else:
        out += NEAR * HALF_GROUPS
    kernel = functools.partial(leave_kernel, theirs)
    outs = call(kernel, "leave", out, specs, 5, scratch, mib=8, aliases=aliases)(*args)
    return outs[:2], outs[2], outs[3], outs[4:]


def spread_kernel(core_ref, own_ref, theirs_h, halo_ref, weight_ref, out_h, theirs_ref, out_ref, win_ref, sems):
    load = start_all([(theirs_h, theirs_ref)], sems.at[pl.ds(8, 1)])
    saves = []
    size = HALF_GROUPS * STATE
    for side, pre_ref in enumerate((own_ref, theirs_ref)):
        half = 1 - core_ref[0] if side else core_ref[0]
        if side:
            wait_all(load)
        blocks = [(jj * GROUP_X, span(half * HALF_GROUPS + jj, GROUP_X), GROUP_X) for jj in range(HALF_GROUPS)]
        blocks += [
            (HALF_X + base * size, span(WIDTH_X // size + 2 * base + half, size), size) for base in range(2)
        ]
        for near, far, width in blocks:
            win_ref[0:T, 0:width] = pre_ref[:, near : near + width]
            win_ref[T : T + TAPS - 1, 0:width] = halo_ref[:, far].astype(F32)
            weights = weight_ref[:, far]
            base = side * (HALF_X + HALF_B) + near
            for lo in range(0, width, LANES):
                at = slice(lo, lo + LANES)
                acc = weights[0:1, at] * win_ref[3 : 3 + T, at]
                for k in range(1, TAPS):
                    acc = acc + weights[k : k + 1, at] * win_ref[3 - k : 3 - k + T, at]
                out_ref[:, base + lo : base + lo + LANES] = acc.astype(BF16)
            copy = pltpu.make_async_copy(out_ref.at[:, pl.ds(base, width)], out_h.at[:, far], sems.at[len(saves)])
            copy.start()
            saves.append(copy)
    wait_all(saves)


def run_spread(core, own, theirs, halo, weight):
    out = [("h", (T, CHANNELS), BF16)]
    scratch = [
        pltpu.VMEM((T, HALF_X + HALF_B), F32),
        pltpu.VMEM((T, CHANNELS), BF16),
        pltpu.VMEM((T + 8, GROUP_X), F32),
        DMA(9),
    ]
    return call(spread_kernel, "spread", out, "sVhvV", 3, scratch, mib=8)(core, own, theirs, halo, weight)[0]


CONV_ROWS = TAPS * (CHANNELS // LANES)
CONV_GROUP = CONV_ROWS // GROUPS
SEND_ROWS = CONV_ROWS + 16


def write_send(out_ref, conv, thin):
    high = thin.astype(BF16).astype(F32)
    low = thin - high
    row = iota((16, LANES), 0)
    out_ref[0:CONV_ROWS, :] = conv.astype(BF16)
    out_ref[CONV_ROWS:SEND_ROWS, :] = jnp.where(row == 0, high, jnp.where(row == 1, low, 0.0)).astype(BF16)


def read_send(value):
    wide = value.astype(F32)
    return wide[0:CONV_ROWS], wide[CONV_ROWS : CONV_ROWS + 1] + wide[CONV_ROWS + 1 : CONV_ROWS + 2]


def merge_kernel(core_ref, own_ref, own_got_ref, theirs_ref, theirs_got_ref, out_ref):
    thin = jnp.zeros((8, LANES), F32)
    left = iota((8, LANES), 1) < HEAD_DIM
    count = HEADS // 2
    parts = []
    for side, (mine, other) in enumerate(((own_ref, theirs_got_ref), (theirs_ref, own_got_ref))):
        half = 1 - core_ref[0] if side else core_ref[0]
        total = mine[...] + other[...]
        rows, skips, decays = [], [], []
        for jj in range(HALF_GROUPS):
            at = jj * SUM_GROUP
            rows.append(total[at : at + CONV_GROUP])
            skips.append(total[at + CONV_GROUP : at + SUM_GROUP - GROUP_HEADS])
            decays.append(total[at + SUM_GROUP - GROUP_HEADS : at + SUM_GROUP])
        skips = jnp.concatenate(skips, axis=0)
        even = exact_dot(jnp.where(left, 1.0, 0.0), skips, NT)
        odd = exact_dot(jnp.where(left, 0.0, 1.0), skips, NT)
        decay = exact_dot(jnp.ones((8, LANES), F32), jnp.concatenate(decays, axis=0), NT)
        for part, step, shift in ((even, 2, 0), (odd, 2, 1), (decay, 1, HEADS)):
            size = part.shape[1]
            spot = (iota((size, LANES), 1) == step * iota((size, LANES), 0) + shift + half * count).astype(F32)
            thin = thin + exact_dot(part, spot)
        parts.append(jnp.concatenate(rows, axis=0))
    first = core_ref[0] == 0
    conv = jnp.concatenate(
        [jnp.where(first, parts[0], parts[1]), jnp.where(first, parts[1], parts[0])], axis=0
    )
    write_send(out_ref, conv, thin[0:1])


def run_merge(core, own, own_got, theirs, theirs_got):
    out = [("v", (SEND_ROWS, LANES), BF16)]
    return call(merge_kernel, "merge", out, "svvvv", 1, mib=4)(core, own, own_got, theirs, theirs_got)[0]


def ring_sum(core_ref, me_ref, refs, hold_ref):
    count = len(refs)
    sides = (count - 1) // 2
    hold_ref[0] = refs[0][...]
    for k in range(1, sides + 1):
        mine = jnp.where(core_ref[0] == 0, k, count - k)
        hold_ref[mine] = refs[k][...]
        hold_ref[count - mine] = refs[sides + k][...]
    if count % 2 == 0:
        hold_ref[count // 2] = refs[count - 1][...]
    conv, thin = read_send(hold_ref[lax.rem(me_ref[0], count)])
    for k in range(1, count):
        more, little = read_send(hold_ref[lax.rem(me_ref[0] + count - k, count)])
        conv, thin = conv + more, thin + little
    return conv, thin


def fold_kernel(core_ref, me_ref, *rest):
    *refs, out_ref, hold_ref = rest
    write_send(out_ref, *ring_sum(core_ref, me_ref, refs, hold_ref))


def run_fold(core, me, values):
    out = [("v", (SEND_ROWS, LANES), BF16)]
    scratch = [pltpu.VMEM((len(values), SEND_ROWS, LANES), BF16)]
    return call(fold_kernel, "fold", out, "ss" + "v" * len(values), 1, scratch, mib=4)(core, me, *values)[0]


def finish_kernel(core_ref, me_ref, *rest):
    *refs, conv_ref, decay_ref, skip_ref, hold_ref = rest
    conv, thin = ring_sum(core_ref, me_ref, refs, hold_ref)
    for i in range(CHANNELS // LANES):
        if i < PAIRS:
            row = CONV_GROUP * (i // GROUP_PAIRS) + TAPS * (i % GROUP_PAIRS)
        else:
            kind, group = divmod(i - PAIRS, GROUPS)
            row = CONV_GROUP * group + TAPS * (GROUP_PAIRS + kind)
        conv_ref[:, i * LANES : (i + 1) * LANES] = conv[row : row + TAPS]
    skip_ref[...] = thin[:, 0:HEADS]
    decay_ref[...] = thin[:, HEADS:]


def run_finish(core, me, values):
    out = [("v", (TAPS, CHANNELS), F32), ("v", (1, HEADS), F32), ("v", (1, HEADS), F32)]
    scratch = [pltpu.VMEM((len(values), SEND_ROWS, LANES), BF16)]
    return call(finish_kernel, "finish", out, "ss" + "v" * len(values), 1, scratch, mib=4)(core, me, *values)


CTX = ("chip", "core")
ALL = ("dp", "chip", "core")


def all_to_all(value, axis):
    return lax.all_to_all(value, axis, 0, 0, tiled=True)


def tie(*values):
    return lax.optimization_barrier(values)


SIDE = 4


def around(value, axis, size, ring, move):
    def hear(first, second):
        return lax.ppermute(
            value,
            (axis, "core"),
            [(2 * i + side, 2 * move(i, d) + side) for i in range(size) for side, d in enumerate((first, second))],
        )

    middle = [hear(ring // 2, ring // 2)] if ring % 2 == 0 else []
    heard = [hear(k, ring - k) for k in range(1, (ring - 1) // 2 + 1)]
    swapped = [lax.ppermute(part, "core", [(0, 1), (1, 0)]) for part in heard]
    return [value] + heard + swapped + middle


def scalar(value):
    return value.astype(jnp.int32).reshape(1)


def local(conv_input, conv_weight, step_raw, decay_log, skip_gain, cotangent):
    chips = lax.axis_size("chip")
    devices = 2 * chips
    sequences = lax.axis_size("dp")
    tokens = conv_input[0]
    raw = step_raw[0]
    cot = cotangent[0]
    core = lax.axis_index("core").astype(jnp.int32).reshape(1)
    swap = [(0, 1), (1, 0)]
    halo = lax.ppermute(tokens[T - TAPS + 1 :], CTX, [(i, i + 1) for i in range(devices - 1)])
    small, small_near, tot, x0, bc0, head, weight_near, cot_near = run_begin(
        raw, decay_log.reshape(1, HEADS), skip_gain.reshape(1, HEADS), tokens, conv_weight, cot
    )
    other = lax.ppermute(tot, "core", swap)
    x, bc, before, x_near, bc_near, out = run_enter(
        core, x0, bc0, head, halo, weight_near, cot_near, small_near
    )
    got_near = lax.ppermute(out, "core", swap)
    own_near = run_own(core, x_near, bc_near, cot_near, small_near)
    packed, left, right, tots = run_pack(core, own_near, got_near, tot, other)
    heard = all_to_all(packed, "chip")
    y, gbc, skips = run_inner(x, bc, cot, small)
    heard, y, gbc, skips = tie(heard, y, gbc, skips)
    chained = run_chain(chips, heard)
    late, chained = tie(bc, chained)
    back = all_to_all(chained, "chip")
    gx, slope = run_slopes(late, cot, small, tokens, before, conv_weight)
    back, gx, slope = tie(back, gx, slope)
    far = (x, cot, y, gx, slope, tokens, bc, gbc)
    mine, send, near, common = run_unpack(
        core, back, left, right, tots, far, (before, small, raw, skips, conv_weight)
    )
    theirs = lax.ppermute(send, "core", swap)
    half, pre_own, sum_own, near = run_leave(core, mine, near, common, far, None)
    sum_own_got = lax.ppermute(sum_own, "core", swap)
    (out_tokens, grad_step), pre_theirs, sum_theirs, (first,) = run_leave(
        core, theirs, near, common, (), (half, pre_own)
    )
    sum_theirs_got = lax.ppermute(sum_theirs, "core", swap)
    after = lax.ppermute(first, CTX, [(i + 1, i) for i in range(devices - 1)])
    sums = run_merge(core, sum_own, sum_own_got, sum_theirs, sum_theirs_got)
    chip, sequence = lax.axis_index("chip"), lax.axis_index("dp")
    rows = chips // SIDE
    values = around(sums, "chip", chips, SIDE, lambda i, d: i // SIDE * SIDE + (i % SIDE + d) % SIDE)
    grad_tokens = run_spread(core, pre_own, pre_theirs, after, common[4])
    values, grad_tokens = tie(values, grad_tokens)
    sums = run_fold(core, scalar(lax.rem(chip, SIDE)), values)
    values = around(sums, "chip", chips, rows, lambda i, d: (i + d * SIDE) % chips)
    sums = run_fold(core, scalar(lax.div(chip, SIDE)), values)
    near = 2 if sequences % 2 == 0 else 1
    if near > 1:
        values = around(sums, "dp", sequences, near, lambda i, d: i // 2 * 2 + (i % 2 + d) % 2)
        sums = run_fold(core, scalar(lax.rem(sequence, near)), values)
    values = around(sums, "dp", sequences, sequences // near, lambda i, d: (i + d * near) % sequences)
    grad_conv, grad_decay, grad_skip = run_finish(core, scalar(lax.div(sequence, near)), values)
    return (
        out_tokens[None],
        grad_tokens[None],
        grad_step[None],
        grad_conv,
        grad_decay.reshape(HEADS),
        grad_skip.reshape(HEADS),
    )


def solution(mesh):
    dp, ctx = mesh.devices.shape
    fine = Mesh(mesh.devices.reshape(dp, ctx // 2, 2), ALL)
    seq = P("dp", CTX, None)
    rate = P("dp", None, CTX)
    in_specs = (seq, P(), rate, P(), P(), seq)
    out_specs = (seq, seq, rate, P(), P(), P())
    return jax.shard_map(local, mesh=fine, in_specs=in_specs, out_specs=out_specs, check_vma=False)
```

```python
import functools

import jax
import jax.numpy as jnp
from jax import lax
from jax.experimental import pallas as pl
from jax.experimental.pallas import tpu as pltpu
from jax.sharding import Mesh
from jax.sharding import PartitionSpec as P

HEADS = 64
HEAD_DIM = 64
GROUPS = 4
STATE = 128
TAPS = 4
T = 128
LANES = 128
WIDTH_X = HEADS * HEAD_DIM
WIDTH_B = GROUPS * STATE
CHANNELS = WIDTH_X + 2 * WIDTH_B
GROUP_X = WIDTH_X // GROUPS
PAIRS = HEADS // 2
GROUP_PAIRS = PAIRS // GROUPS
GROUP_HEADS = HEADS // GROUPS
HALF_PAIRS = PAIRS // 2
HALF_GROUPS = GROUPS // 2
F32 = jnp.float32
BF16 = jnp.bfloat16
EXACT = lax.Precision.HIGHEST
NN = (((1,), (0,)), ((), ()))
NT = (((1,), (1,)), ((), ()))
SUM_GROUP = 64
PACK_ROWS = 2 * STATE + 16


def dot(a, b, dims=NN):
    return lax.dot_general(a, b, dims, preferred_element_type=F32)


def exact_dot(a, b, dims=NN):
    return lax.dot_general(a, b, dims, precision=EXACT, preferred_element_type=F32)


def iota(shape, dim):
    return lax.broadcasted_iota(jnp.int32, shape, dim)


def sigmoid(v):
    return 0.5 + 0.5 * jnp.tanh(0.5 * v)


def split_two(v):
    high = v.astype(BF16)
    return high, (v - high.astype(F32)).astype(BF16)


def span(index, size):
    return pl.ds(pl.multiple_of(index * size, size), size)


def pin(value, space):
    return pltpu.with_memory_space_constraint(value, space)


def placed(space, shape, dtype):
    return space(shape, dtype)


def call(kernel, name, outs, specs, micros, scratch=(), mib=28, aliases=None):
    cost = pl.CostEstimate(
        flops=int(micros * 1e9), transcendentals=0, bytes_accessed=int(micros * 3.6e6)
    )
    blocks = {
        "s": pl.BlockSpec(memory_space=pltpu.SMEM),
        "v": pl.BlockSpec(memory_space=pltpu.VMEM),
        "V": pl.BlockSpec(memory_space=pltpu.VMEM),
        "h": pl.BlockSpec(memory_space=pltpu.HBM),
    }
    spaces = {"V": pltpu.VMEM, "h": pltpu.HBM}
    shapes = [
        placed(spaces[p], shape, dtype) if p in spaces else jax.ShapeDtypeStruct(shape, dtype)
        for p, shape, dtype in outs
    ]
    run = pl.pallas_call(
        kernel,
        out_shape=shapes,
        in_specs=[blocks[p] for p in specs],
        out_specs=[blocks[p] for p, _, _ in outs],
        scratch_shapes=list(scratch),
        input_output_aliases=aliases or {},
        cost_estimate=cost,
        compiler_params=pltpu.CompilerParams(vmem_limit_bytes=mib << 20),
        name=name,
    )

    def go(*args):
        return run(*[pin(a, spaces[p]) if p in spaces else a for a, p in zip(args, specs, strict=True)])

    return go


def start_all(pairs, sems):
    copies = [pltpu.make_async_copy(a, b, sems.at[i]) for i, (a, b) in enumerate(pairs)]
    for copy in copies:
        copy.start()
    return copies


def wait_all(copies):
    for copy in copies:
        copy.wait()


def DMA(*shape):
    return pltpu.SemaphoreType.DMA(shape)


def fill_window(win_ref, before, tokens):
    width = tokens.shape[1]
    win_ref[0:8, :width] = before
    win_ref[8 : 8 + T, :width] = tokens.astype(F32)


def pre_conv(win_ref, weights, lo):
    cols = slice(lo, lo + LANES)
    rows = win_ref[0 : 8 + T, cols]
    acc = weights[TAPS - 1 : TAPS, cols] * rows[8:]
    for k in range(TAPS - 1):
        acc = acc + weights[k : k + 1, cols] * pltpu.roll(rows, TAPS - 1 - k, 0)[8:]
    return acc


BLOCKS = CHANNELS // GROUP_X


ROW_DT, ROW_SEG, ROW_COLS, ROW_SCALE, ROW_TOT, ROW_SKIP, ROW_DECAY, SMALL_ROWS = (
    0, 64, 128, 256, 384, 416, 448, 512
)


def begin_kernel(raw_h, decay_log_h, skip_gain_h, tok_h, weight_h, g_h,
                 small_h, small_ref, tot_ref, x_ref, bc_ref, head_ref, weight_ref, g_ref,
                 raw_ref, decay_log_ref, skip_gain_ref, wide_ref, hold_ref, win_ref, sems):
    first = start_all(
        [(raw_h, raw_ref), (decay_log_h, decay_log_ref), (skip_gain_h, skip_gain_ref), (weight_h, weight_ref)],
        sems.at[0],
    )
    blocks = [pl.ds(i * GROUP_X, GROUP_X) for i in range(BLOCKS)]
    copies = start_all([(tok_h.at[:, at], hold_ref.at[:, at]) for at in blocks], sems.at[1])
    later = start_all([(g_h, g_ref)], sems.at[2])
    win_ref[0:8, :] = jnp.zeros((8, GROUP_X), F32)
    copies[0].wait()
    diagonal = iota((HEADS, HEADS), 0) == iota((HEADS, HEADS), 1)

    def column(row):
        return jnp.sum(jnp.where(diagonal, row, 0.0), axis=1, keepdims=True)

    wait_all(first)
    raw = raw_ref[...]
    dt = jnp.log1p(jnp.exp(raw))
    decay = -jnp.exp(column(decay_log_ref[...]))
    upper = (iota((T, T), 0) <= iota((T, T), 1)).astype(F32)
    seg = exact_dot(dt * decay, upper)
    total = seg[:, T - 1 : T]
    small_ref[ROW_DT : ROW_DT + HEADS] = dt
    small_ref[ROW_SEG : ROW_SEG + HEADS] = seg
    small_ref[ROW_COLS : ROW_COLS + T] = jnp.transpose(jnp.concatenate([seg, dt], axis=0))
    small_ref[ROW_SCALE : ROW_SCALE + T] = jnp.transpose(
        jnp.concatenate([jnp.exp(seg), jnp.exp(total - seg) * dt], axis=0)
    )
    left = iota((PAIRS, LANES), 1) < HEAD_DIM

    def paired(col):
        wide_ref[...] = jnp.broadcast_to(col, (HEADS, LANES))
        return jnp.where(left, wide_ref[pl.ds(0, PAIRS, 2), :], wide_ref[pl.ds(1, PAIRS, 2), :])

    tot = paired(total)
    tot_ref[...] = tot
    small_ref[ROW_TOT : ROW_TOT + PAIRS] = tot
    small_ref[ROW_SKIP : ROW_SKIP + PAIRS] = paired(column(skip_gain_ref[...]))
    small_ref[ROW_DECAY : ROW_DECAY + HEADS] = jnp.broadcast_to(decay, (HEADS, LANES))
    save = start_all([(small_ref, small_h)], sems.at[0])
    for i in range(BLOCKS):
        if i:
            copies[i].wait()
        cols = slice(i * GROUP_X, (i + 1) * GROUP_X)
        win_ref[8 : 8 + T, :] = hold_ref[:, cols].astype(F32)
        for lo in range(0, GROUP_X, LANES):
            at = i * GROUP_X + lo
            pre = pre_conv(win_ref, weight_ref[:, cols], lo)
            mixed = (pre * sigmoid(pre)).astype(BF16)
            head_ref[:, at : at + LANES] = pre[0:8]
            if at < WIDTH_X:
                x_ref[:, at : at + LANES] = mixed
            else:
                bc_ref[:, at - WIDTH_X : at - WIDTH_X + LANES] = mixed
    wait_all(save + later)


def run_begin(raw, decay_log, skip_gain, tokens, weight, cot):
    out = [
        ("h", (SMALL_ROWS, LANES), F32),
        ("V", (SMALL_ROWS, LANES), F32),
        ("V", (PAIRS, LANES), F32),
        ("V", (T, WIDTH_X), BF16),
        ("V", (T, 2 * WIDTH_B), BF16),
        ("V", (8, CHANNELS), F32),
        ("V", (TAPS, CHANNELS), F32),
        ("V", (T, WIDTH_X), BF16),
    ]
    scratch = [
        pltpu.VMEM((HEADS, T), F32),
        pltpu.VMEM((1, HEADS), F32),
        pltpu.VMEM((1, HEADS), F32),
        pltpu.VMEM((HEADS, LANES), F32),
        pltpu.VMEM((T, CHANNELS), BF16),
        pltpu.VMEM((8 + T, GROUP_X), F32),
        DMA(3, BLOCKS),
    ]
    return call(begin_kernel, "begin", out, "hhhhhh", 4, scratch, mib=8)(
        raw, decay_log, skip_gain, tokens, weight, cot
    )


def rolled(cols, group):
    return pltpu.roll(cols, (LANES - group * GROUP_HEADS) % LANES, 1)


def widen(cols, base, pair):
    first = iota((T, LANES), 1) < HEAD_DIM
    at = base + 2 * pair
    return jnp.where(first, cols[:, at : at + 1], cols[:, at + 1 : at + 2])


def widen_two(cols, base, pair):
    return jnp.concatenate([widen(cols, base, pair), widen(cols, base, pair + 1)], axis=1)


def fill_half(half, x_ref, bc_ref, g_ref, scale, dst_ref):
    for jj in range(HALF_GROUPS):
        j = half * HALF_GROUPS + jj
        b_flip = jnp.transpose(bc_ref[:, span(j, STATE)].astype(F32)).astype(BF16)
        c_flip = jnp.transpose(bc_ref[:, span(GROUPS + j, STATE)].astype(F32)).astype(BF16)
        cols = rolled(scale, j)
        for q in range(0, GROUP_PAIRS, 2):
            lanes = pl.ds(pl.multiple_of(j * GROUP_X + q * LANES, 2 * LANES), 2 * LANES)
            xw = (x_ref[:, lanes].astype(F32) * widen_two(cols, HEADS, q)).astype(BF16)
            gw = (g_ref[:, lanes].astype(F32) * widen_two(cols, 0, q)).astype(BF16)
            state = dot(b_flip, xw).astype(BF16)
            grad = dot(c_flip, gw).astype(BF16)
            for k in range(2):
                at = jj * GROUP_PAIRS + q + k
                dst_ref[0, at] = state[:, k * LANES : (k + 1) * LANES]
                dst_ref[1, at] = grad[:, k * LANES : (k + 1) * LANES]


def enter_kernel(core_ref, x0_ref, bc0_ref, head_ref, halo_ref, weight_ref, g_ref, small_ref,
                 x_h, bc_h, before_h, x_ref, bc_ref, out_ref, before_ref, sems):
    half = 1 - core_ref[0]
    row = iota((8, GROUP_X), 0)
    for i in range(BLOCKS):
        cols = slice(i * GROUP_X, (i + 1) * GROUP_X)
        halo = halo_ref[:, cols].astype(F32)
        weight = weight_ref[:, cols]
        pre = head_ref[:, cols]
        before = jnp.zeros((8, GROUP_X), F32)
        for t in range(TAPS - 1):
            extra = jnp.zeros((1, GROUP_X), F32)
            for k in range(TAPS - 1 - t):
                extra = extra + weight[k : k + 1] * halo[t + k : t + k + 1]
            pre = pre + jnp.where(row == t, extra, 0.0)
            before = before + jnp.where(row == t + 5, halo[t : t + 1], 0.0)
        before_ref[:, cols] = before
        fixed = pre * sigmoid(pre)
        src, dst, at = (x0_ref, x_ref, cols) if i < GROUPS else (bc0_ref, bc_ref, slice(0, GROUP_X))
        rest = src[0:16, at].astype(F32)
        dst[16:T, at] = src[16:T, at]
        dst[0:16, at] = jnp.concatenate([fixed, rest[8:16]], axis=0).astype(BF16)
    saves = start_all([(x_ref, x_h), (bc_ref, bc_h), (before_ref, before_h)], sems)
    fill_half(half, x_ref, bc_ref, g_ref, small_ref[ROW_SCALE : ROW_SCALE + T], out_ref)
    wait_all(saves)


def run_enter(core, x0, bc0, head, halo, weight, cot, small):
    out = [
        ("h", (T, WIDTH_X), BF16),
        ("h", (T, 2 * WIDTH_B), BF16),
        ("h", (8, CHANNELS), F32),
        ("V", (T, WIDTH_X), BF16),
        ("V", (T, 2 * WIDTH_B), BF16),
        ("V", (2, HALF_PAIRS, STATE, LANES), BF16),
    ]
    scratch = [pltpu.VMEM((8, CHANNELS), F32), DMA(3)]
    return call(enter_kernel, "enter", out, "sVVVvVVV", 3, scratch, mib=6)(
        core, x0, bc0, head, halo, weight, cot, small
    )


def own_kernel(core_ref, x_ref, bc_ref, g_ref, small_ref, own_ref):
    fill_half(core_ref[0], x_ref, bc_ref, g_ref, small_ref[ROW_SCALE : ROW_SCALE + T], own_ref)


def run_own(core, x, bc, cot, small):
    out = [("V", (2, HALF_PAIRS, STATE, LANES), BF16)]
    return call(own_kernel, "own", out, "sVVVV", 3, mib=6)(core, x, bc, cot, small)[0]


STEP_PAIRS = 4
STEPS = HALF_PAIRS // STEP_PAIRS


def pack_kernel(core_ref, own_ref, got_ref, tot_ref, other_ref,
                out_h, left_h, right_h, tots_h, out_ref, sems):
    saves = start_all(
        [(tot_ref, tots_h.at[pl.ds(0, PAIRS)]), (other_ref, tots_h.at[pl.ds(PAIRS, PAIRS)])], sems.at[0]
    )
    second = core_ref[0] == 1

    def keep(first_ref, last_ref):
        return [
            pltpu.make_async_copy(first_ref.at[0], left_h, sems.at[0, 2]),
            pltpu.make_async_copy(last_ref.at[1], right_h, sems.at[0, 3]),
        ]

    @pl.when(second)
    def _():
        for copy in keep(got_ref, own_ref):
            copy.start()

    @pl.when(jnp.logical_not(second))
    def _():
        for copy in keep(own_ref, got_ref):
            copy.start()

    saves += keep(own_ref, got_ref)
    outs = []
    for i in range(HALF_PAIRS):
        at = core_ref[0] * HALF_PAIRS + i
        tot = tot_ref[pl.ds(at, 1), :]
        other = other_ref[pl.ds(at, 1), :]
        one = jnp.ones_like(tot)
        by_own = jnp.exp(tot)
        by_other = jnp.exp(other)
        state = (
            jnp.where(second, one, by_other) * own_ref[0, i].astype(F32)
            + jnp.where(second, by_own, one) * got_ref[0, i].astype(F32)
        )
        grad = (
            jnp.where(second, by_other, one) * own_ref[1, i].astype(F32)
            + jnp.where(second, one, by_own) * got_ref[1, i].astype(F32)
        )
        out_ref[i, 0:STATE, :] = state.astype(BF16)
        out_ref[i, STATE : 2 * STATE, :] = grad.astype(BF16)
        both = tot + other
        high = both.astype(BF16).astype(F32)
        mid = (both - high).astype(BF16).astype(F32)
        low = both - high - mid
        row = iota((16, LANES), 0)
        wide = jnp.where(row == 0, high, jnp.where(row == 1, mid, jnp.where(row == 2, low, 0.0)))
        out_ref[i, 2 * STATE : PACK_ROWS, :] = wide.astype(BF16)
        if i % STEP_PAIRS == STEP_PAIRS - 1:
            done = pl.ds(i + 1 - STEP_PAIRS, STEP_PAIRS)
            copy = pltpu.make_async_copy(out_ref.at[done], out_h.at[done], sems.at[1, i // STEP_PAIRS])
            copy.start()
            outs.append(copy)
    wait_all(outs + saves)


def run_pack(core, own, got, tot, other):
    half = (HALF_PAIRS, STATE, LANES)
    packed = (HALF_PAIRS, PACK_ROWS, LANES)
    out = [("h", packed, BF16), ("h", half, BF16), ("h", half, BF16), ("h", (2 * PAIRS, LANES), F32)]
    scratch = [pltpu.VMEM(packed, BF16), DMA(2, STEPS)]
    return call(pack_kernel, "pack", out, "sVvVv", 2, scratch, mib=8)(core, own, got, tot, other)


def chain_kernel(chips, per, in_ref, out_ref):
    for q in range(per):
        def decay(k):
            rows = in_ref[k * per + q, 2 * STATE : PACK_ROWS, :].astype(F32)
            return jnp.exp(rows[0:1] + rows[1:2] + rows[2:3])

        carry = jnp.zeros((STATE, LANES), F32)
        for k in range(chips):
            out_ref[k * per + q, 0:STATE, :] = carry.astype(BF16)
            if k < chips - 1:
                carry = decay(k) * carry + in_ref[k * per + q, 0:STATE, :].astype(F32)
        carry = jnp.zeros((STATE, LANES), F32)
        for k in reversed(range(chips)):
            out_ref[k * per + q, STATE : 2 * STATE, :] = carry.astype(BF16)
            if k > 0:
                carry = decay(k) * carry + in_ref[k * per + q, STATE : 2 * STATE, :].astype(F32)


def run_chain(chips, packed):
    kernel = functools.partial(chain_kernel, chips, HALF_PAIRS // chips)
    out = [("v", (HALF_PAIRS, 2 * STATE, LANES), BF16)]
    return call(kernel, "chain", out, "v", 1, mib=8)(packed)[0]


HALF_X = HALF_GROUPS * GROUP_X
HALF_B = 2 * HALF_GROUPS * STATE

NEAR = [
    ("V", (T, GROUP_X), BF16),
    ("V", (T, GROUP_X), BF16),
    ("V", (T, GROUP_X), F32),
    ("V", (T, GROUP_X), F32),
    ("V", (T, GROUP_X + 2 * STATE), F32),
    ("V", (T, GROUP_X + 2 * STATE), BF16),
    ("V", (T, 2 * STATE), BF16),
    ("V", (T, 2 * STATE), F32),
]
COMMON = [
    ("V", (8, CHANNELS), F32),
    ("V", (SMALL_ROWS, LANES), F32),
    ("V", (HEADS, T), F32),
    ("V", (PAIRS, LANES), F32),
    ("V", (TAPS, CHANNELS), F32),
]
FETCHES = 6 + 8


def fetch_group(j, far, near, sems):
    x_h, g_h, y_h, gx_h, slope_h, tok_h, bc_h, gbc_h = far
    x_v, g_v, y_v, gx_v, slope_v, tok_v, bc_v, gbc_v = near
    wide = pl.ds(0, GROUP_X)
    pairs = [
        (a.at[:, span(j, GROUP_X)], b.at[:, wide])
        for a, b in ((x_h, x_v), (g_h, g_v), (y_h, y_v), (gx_h, gx_v), (slope_h, slope_v), (tok_h, tok_v))
    ]
    for base in range(2):
        at = span(base * GROUPS + j, STATE)
        off = span(WIDTH_X // STATE + base * GROUPS + j, STATE)
        thin = pl.ds(base * STATE, STATE)
        tail = pl.ds(GROUP_X + base * STATE, STATE)
        pairs += [
            (bc_h.at[:, at], bc_v.at[:, thin]),
            (gbc_h.at[:, at], gbc_v.at[:, thin]),
            (slope_h.at[:, off], slope_v.at[:, tail]),
            (tok_h.at[:, off], tok_v.at[:, tail]),
        ]
    return start_all(pairs, sems)


def unpack_kernel(core_ref, back_ref, left_h, right_h, tots_h, *rest):
    far, rest = rest[: len(NEAR)], rest[len(NEAR) :]
    common_far, rest = rest[: len(COMMON)], rest[len(COMMON) :]
    mine_ref, send_ref, *rest = rest
    near = [rest[i * len(NEAR) : (i + 1) * len(NEAR)] for i in range(HALF_GROUPS)]
    rest = rest[HALF_GROUPS * len(NEAR) :]
    common, rest = rest[: len(COMMON)], rest[len(COMMON) :]
    left_ref, right_ref, tots_ref, sems, fetch_sems = rest
    first = start_all([(tots_h, tots_ref)], sems.at[STEPS])
    steps = []
    for step in range(STEPS):
        at = pl.ds(step * STEP_PAIRS, STEP_PAIRS)
        steps.append(
            start_all([(left_h.at[at], left_ref.at[at]), (right_h.at[at], right_ref.at[at])], sems.at[step])
        )
    fetches = start_all(list(zip(common_far, common)), fetch_sems.at[HALF_GROUPS])
    for jj in range(HALF_GROUPS):
        fetches += fetch_group(core_ref[0] * HALF_GROUPS + jj, far, near[jj], fetch_sems.at[jj])
    wait_all(first)
    second = core_ref[0] == 1
    for i in range(HALF_PAIRS):
        if i % STEP_PAIRS == 0:
            wait_all(steps[i // STEP_PAIRS])
        at = core_ref[0] * HALF_PAIRS + i
        tot = tots_ref[pl.ds(at, 1), :]
        other = tots_ref[pl.ds(PAIRS + at, 1), :]
        decay_zero = jnp.exp(jnp.where(second, other, tot))
        decay_one = jnp.exp(jnp.where(second, tot, other))
        state_zero = back_ref[i, 0:STATE, :].astype(F32)
        grad_one = back_ref[i, STATE : 2 * STATE, :].astype(F32)
        state_one = decay_zero * state_zero + left_ref[i].astype(F32)
        grad_zero = decay_one * grad_one + right_ref[i].astype(F32)
        mine_ref[0, i] = jnp.where(second, state_one, state_zero).astype(BF16)
        mine_ref[1, i] = jnp.where(second, grad_one, grad_zero).astype(BF16)
        send_ref[0, i] = jnp.where(second, state_zero, state_one).astype(BF16)
        send_ref[1, i] = jnp.where(second, grad_zero, grad_one).astype(BF16)
    wait_all(fetches)


def run_unpack(core, back, left, right, tots, far, common):
    half = (2, HALF_PAIRS, STATE, LANES)
    out = [("V", half, BF16)] * 2 + NEAR * HALF_GROUPS + COMMON
    scratch = [
        pltpu.VMEM(half[1:], BF16),
        pltpu.VMEM(half[1:], BF16),
        pltpu.VMEM((2 * PAIRS, LANES), F32),
        DMA(STEPS + 1, 2),
        DMA(HALF_GROUPS + 1, FETCHES),
    ]
    specs = "svhhh" + "h" * (len(NEAR) + len(COMMON))
    outs = call(unpack_kernel, "unpack", out, specs, 3, scratch, mib=8)(
        core, back, left, right, tots, *far, *common
    )
    at = 2 + HALF_GROUPS * len(NEAR)
    return outs[0], outs[1], outs[2:at], outs[at:]


def by_lane_half(v):
    first = iota(v.shape, 1) < HEAD_DIM
    wide = v.astype(F32)
    return jnp.concatenate(
        [jnp.where(first, wide, 0.0).astype(BF16), jnp.where(first, 0.0, wide).astype(BF16)], axis=0
    )


def inner_kernel(x_h, bc_h, g_h, small_h, y_h, gbc_h, skips_h,
                 x_ref, bc_ref, g_ref, small_ref, y_ref, gbc_ref, skips_ref, sems):
    first = start_all([(bc_h, bc_ref), (small_h, small_ref)], sems.at[0])

    def loads(j):
        at = span(j, GROUP_X)
        return [
            pltpu.make_async_copy(x_h.at[:, at], x_ref.at[:, at], sems.at[1, j]),
            pltpu.make_async_copy(g_h.at[:, at], g_ref.at[:, at], sems.at[2, j]),
        ]

    def store(j):
        at = span(j, GROUP_X)
        return pltpu.make_async_copy(y_ref.at[:, at], y_h.at[:, at], sems.at[3, j])

    for j in range(GROUPS):
        for copy in loads(j):
            copy.start()
    wait_all(first)
    lower = iota((T, T), 0) >= iota((T, T), 1)

    @pl.loop(0, GROUPS)
    def _(j):
        wait_all(loads(j))
        b = bc_ref[:, span(j, STATE)]
        c = bc_ref[:, span(GROUPS + j, STATE)]
        seg = small_ref[pl.ds(pl.multiple_of(ROW_SEG + j * GROUP_HEADS, GROUP_HEADS), GROUP_HEADS), :]
        dt = small_ref[pl.ds(pl.multiple_of(ROW_DT + j * GROUP_HEADS, GROUP_HEADS), GROUP_HEADS), :]
        scores = dot(c, b, NT)
        cols = rolled(small_ref[ROW_COLS : ROW_COLS + T], j)
        total = jnp.zeros((T, T), F32)
        skips = []
        for i in range(GROUP_PAIRS):
            lanes = pl.ds(pl.multiple_of(j * GROUP_X + i * LANES, LANES), LANES)
            x = x_ref[:, lanes]
            g = g_ref[:, lanes]
            skips.append(jnp.sum(g.astype(F32) * x.astype(F32), axis=0, keepdims=True))
            inner = dot(by_lane_half(g), x, NT)
            weights = []
            for k in range(2):
                h = 2 * i + k
                spread = cols[:, h : h + 1] - seg[h : h + 1, :]
                kernel = jnp.exp(jnp.where(lower, spread, -1e30)) * dt[h : h + 1, :]
                total = total + kernel * inner[k * T : (k + 1) * T]
                weights.append((kernel * scores).astype(BF16))
            y_ref[:, lanes] = dot(jnp.concatenate(weights, axis=1), by_lane_half(x))
        skips_ref[span(j, GROUP_PAIRS), :] = jnp.concatenate(skips, axis=0)
        gbc_ref[:, span(GROUPS + j, STATE)] = dot(total.astype(BF16), b)
        gbc_ref[:, span(j, STATE)] = dot(jnp.transpose(total).astype(BF16), c)
        store(j).start()

    last = start_all([(gbc_ref, gbc_h), (skips_ref, skips_h)], sems.at[0])
    for j in range(GROUPS):
        store(j).wait()
    wait_all(last)


def run_inner(x, bc, cot, small):
    out = [("h", (T, WIDTH_X), F32), ("h", (T, 2 * WIDTH_B), F32), ("h", (PAIRS, LANES), F32)]
    scratch = [
        pltpu.VMEM((T, WIDTH_X), BF16),
        pltpu.VMEM((T, 2 * WIDTH_B), BF16),
        pltpu.VMEM((T, WIDTH_X), BF16),
        pltpu.VMEM((SMALL_ROWS, LANES), F32),
        pltpu.VMEM((T, WIDTH_X), F32),
        pltpu.VMEM((T, 2 * WIDTH_B), F32),
        pltpu.VMEM((PAIRS, LANES), F32),
        DMA(4, GROUPS),
    ]
    return call(inner_kernel, "inner", out, "hhhh", 4, scratch, mib=16)(x, bc, cot, small)


def slopes_kernel(bc_h, g_h, small_h, tok_h, before_h, weight_h, gx_h, slope_h,
                  bc_ref, g_ref, small_ref, tok_ref, before_ref, weight_ref, gx_ref, slope_ref, win_ref, sems):
    first = start_all(
        [(bc_h, bc_ref), (small_h, small_ref), (before_h, before_ref), (weight_h, weight_ref), (tok_h, tok_ref)],
        sems.at[0],
    )

    def load(j):
        at = span(j, GROUP_X)
        return pltpu.make_async_copy(g_h.at[:, at], g_ref.at[:, at], sems.at[1, j])

    def store(j):
        at = span(j, GROUP_X)
        return pltpu.make_async_copy(gx_ref.at[:, at], gx_h.at[:, at], sems.at[2, j])

    def store_slope(i):
        at = span(i, GROUP_X)
        return pltpu.make_async_copy(slope_ref.at[:, at], slope_h.at[:, at], sems.at[3, i])

    for j in range(GROUPS):
        load(j).start()
    wait_all(first)
    upper = iota((T, T), 0) <= iota((T, T), 1)

    @pl.loop(0, GROUPS)
    def _(j):
        load(j).wait()
        b = bc_ref[:, span(j, STATE)]
        c = bc_ref[:, span(GROUPS + j, STATE)]
        seg = small_ref[pl.ds(pl.multiple_of(ROW_SEG + j * GROUP_HEADS, GROUP_HEADS), GROUP_HEADS), :]
        scores = jnp.transpose(dot(c, b, NT))
        cols = rolled(small_ref[ROW_COLS : ROW_COLS + T], j)
        for i in range(GROUP_PAIRS):
            lanes = pl.ds(pl.multiple_of(j * GROUP_X + i * LANES, LANES), LANES)
            weights = []
            for k in range(2):
                h = 2 * i + k
                spread = seg[h : h + 1, :] - cols[:, h : h + 1]
                kernel = jnp.exp(jnp.where(upper, spread, -1e30)) * cols[:, HEADS + h : HEADS + h + 1]
                weights.append((kernel * scores).astype(BF16))
            gx_ref[:, lanes] = dot(jnp.concatenate(weights, axis=1), by_lane_half(g_ref[:, lanes]))
        store(j).start()

    @pl.loop(0, BLOCKS)
    def _(i):
        cols = span(i, GROUP_X)
        fill_window(win_ref, before_ref[:, cols], tok_ref[:, cols])
        weights = weight_ref[:, cols]
        for lo in range(0, GROUP_X, LANES):
            pre = pre_conv(win_ref, weights, lo)
            s = sigmoid(pre)
            at = pl.ds(pl.multiple_of(i * GROUP_X + lo, LANES), LANES)
            slope_ref[:, at] = s * (1.0 + pre * (1.0 - s))
        store_slope(i).start()

    for j in range(GROUPS):
        store(j).wait()
    for i in range(BLOCKS):
        store_slope(i).wait()


def run_slopes(bc, cot, small, tokens, before, weight):
    out = [("h", (T, WIDTH_X), F32), ("h", (T, CHANNELS), F32)]
    scratch = [
        pltpu.VMEM((T, 2 * WIDTH_B), BF16),
        pltpu.VMEM((T, WIDTH_X), BF16),
        pltpu.VMEM((SMALL_ROWS, LANES), F32),
        pltpu.VMEM((T, CHANNELS), BF16),
        pltpu.VMEM((8, CHANNELS), F32),
        pltpu.VMEM((TAPS, CHANNELS), F32),
        pltpu.VMEM((T, WIDTH_X), F32),
        pltpu.VMEM((T, CHANNELS), F32),
        pltpu.VMEM((8 + T, GROUP_X), F32),
        DMA(4, BLOCKS),
    ]
    return call(slopes_kernel, "slopes", out, "hhhhhh", 6, scratch, mib=16)(
        bc, cot, small, tokens, before, weight
    )


def leave_kernel(theirs, core_ref, state_ref, *rest):
    rest = list(rest)

    def take(count):
        taken = rest[:count]
        del rest[:count]
        return taken

    sets = [take(len(NEAR)) for _ in range(HALF_GROUPS)]
    before_ref, small_ref, raw_ref, skips_ref, _ = take(len(COMMON))
    half = 1 - core_ref[0] if theirs else core_ref[0]
    fetches = []
    if theirs:
        pre_own_ref, _, _ = take(3)
        out_h, step_h, pre_h, sum_ref, first_ref = take(5)
        head_ref, pre_ref, out_ref, step_ref, win_ref, sems = rest
        own = core_ref[0]
        head_ref[:, span(own, HALF_X)] = pre_own_ref[0:8, 0:HALF_X]
        size = HALF_GROUPS * STATE
        for base in range(2):
            at = HALF_X + base * size
            head_ref[:, span(WIDTH_X // size + 2 * base + own, size)] = pre_own_ref[0:8, at : at + size]
    else:
        far = take(len(NEAR))
        out_h, step_h, pre_ref, sum_ref = take(4)
        after = [take(len(NEAR)) for _ in range(HALF_GROUPS)]
        out_ref, step_ref, win_ref, sems = rest
        for jj in range(HALF_GROUPS):
            fetches += fetch_group((1 - half) * HALF_GROUPS + jj, far, after[jj], sems.at[2 + jj])
    last = iota((8, 2 * LANES), 0) == 7
    lower = (iota((T, T), 0) >= iota((T, T), 1)).astype(F32)

    def tap_sums(grad_pre, lo):
        rows = win_ref[0 : 8 + T, lo : lo + grad_pre.shape[1]]
        moved = [pltpu.roll(rows, TAPS - 1 - k, 0)[8:] for k in range(TAPS - 1)] + [rows[8:]]
        return [jnp.sum(grad_pre * part, axis=0, keepdims=True) for part in moved]

    def by_rows(sums):
        return [s[:, lo : lo + LANES] for lo in range(0, sums[0].shape[1], LANES) for s in sums]

    saves = []

    def save(src, dst):
        copy = pltpu.make_async_copy(src, dst, sems.at[len(saves) // 8, len(saves) % 8])
        copy.start()
        saves.append(copy)

    for jj in range(HALF_GROUPS):
        j = half * HALF_GROUPS + jj
        x_ref, g_ref, y_ref, gx_ref, slope_ref, tok_ref, bc_ref, gbc_ref = sets[jj]
        b = bc_ref[:, 0:STATE]
        c = bc_ref[:, STATE:]
        grad_b = gbc_ref[:, 0:STATE]
        grad_c = gbc_ref[:, STATE:]
        cols = rolled(small_ref[ROW_SCALE : ROW_SCALE + T], j)
        skip_rows = small_ref[pl.ds(pl.multiple_of(ROW_SKIP + j * GROUP_PAIRS, GROUP_PAIRS), GROUP_PAIRS), :]
        tot_rows = small_ref[pl.ds(pl.multiple_of(ROW_TOT + j * GROUP_PAIRS, GROUP_PAIRS), GROUP_PAIRS), :]
        seg_grad = jnp.zeros((GROUP_HEADS, T), F32)
        dt_grad = jnp.zeros((GROUP_HEADS, T), F32)
        skips = [skips_ref[span(j, GROUP_PAIRS), :]]
        terms = []
        fill_window(win_ref, before_ref[:, span(j, GROUP_X)], tok_ref[:, 0:GROUP_X])
        for q in range(0, GROUP_PAIRS, 2):
            lanes = slice(q * LANES, (q + 2) * LANES)
            wide = slice(jj * GROUP_X + q * LANES, jj * GROUP_X + (q + 2) * LANES)
            rise = widen_two(cols, 0, q)
            keep = widen_two(cols, HEADS, q)
            at = jj * GROUP_PAIRS + q
            state = jnp.concatenate([state_ref[0, at], state_ref[0, at + 1]], axis=1)
            exits = jnp.concatenate([state_ref[1, at], state_ref[1, at + 1]], axis=1)
            skip = jnp.concatenate([skip_rows[q : q + 1], skip_rows[q + 1 : q + 2]], axis=1)
            tot = jnp.concatenate([tot_rows[q : q + 1], tot_rows[q + 1 : q + 2]], axis=1)
            x = x_ref[:, lanes].astype(F32)
            g = g_ref[:, lanes].astype(F32)
            y = y_ref[:, lanes] + rise * dot(c, state)
            through = keep * dot(b, exits)
            gx = gx_ref[:, lanes] + through
            grad_c = grad_c + dot((g * rise).astype(BF16), state, NT)
            grad_b = grad_b + dot((x * keep).astype(BF16), exits, NT)
            out_ref[:, wide] = (y + skip * x).astype(BF16)
            grad_pre = (gx + skip * g) * slope_ref[:, lanes]
            pre_ref[:, wide] = grad_pre
            if theirs:
                at = pl.ds(pl.multiple_of(j * GROUP_X + q * LANES, 2 * LANES), 2 * LANES)
                head_ref[:, at] = grad_pre[0:8]
            terms += by_rows(tap_sums(grad_pre, q * LANES))
            x_gx = x * gx
            end = jnp.sum(x * through, axis=0, keepdims=True) + jnp.exp(tot) * jnp.sum(
                exits.astype(F32) * state.astype(F32), axis=0, keepdims=True
            )
            moved = g * y - x_gx
            moved = jnp.concatenate([moved[: T - 8], moved[T - 8 :] + jnp.where(last, end, 0.0)], axis=0)
            pick = (
                iota((GROUP_HEADS, 2 * LANES), 0)
                == 2 * q + iota((GROUP_HEADS, 2 * LANES), 1) // HEAD_DIM
            ).astype(F32).astype(BF16)
            for part in split_two(moved):
                seg_grad = seg_grad + dot(pick, part, NT)
            for part in split_two(x_gx):
                dt_grad = dt_grad + dot(pick, part, NT)
            if q % 4 == 2:
                size = GROUP_X // 2
                near_at = pl.ds(jj * GROUP_X + (q // 4) * size, size)
                far_at = span(2 * j + q // 4, size)
                save(out_ref.at[:, near_at], out_h.at[:, far_at])
                if theirs:
                    save(pre_ref.at[:, near_at], pre_h.at[:, near_at])
        for grad, base in ((grad_b, 0), (grad_c, 1)):
            at = HALF_X + (base * HALF_GROUPS + jj) * STATE
            tail = slice(GROUP_X + base * STATE, GROUP_X + (base + 1) * STATE)
            far_at = span(WIDTH_X // STATE + base * GROUPS + j, STATE)
            fill_window(win_ref, before_ref[:, far_at], tok_ref[:, tail])
            grad_pre = grad * slope_ref[:, tail]
            pre_ref[:, at : at + STATE] = grad_pre
            if theirs:
                head_ref[:, far_at] = grad_pre[0:8]
                save(pre_ref.at[:, pl.ds(at, STATE)], pre_h.at[:, pl.ds(at, STATE)])
            terms += tap_sums(grad_pre, 0)
        heads = span(j, GROUP_HEADS)
        behind = exact_dot(seg_grad, lower)
        dt = small_ref[pl.ds(pl.multiple_of(ROW_DT + j * GROUP_HEADS, GROUP_HEADS), GROUP_HEADS), :]
        decay = small_ref[pl.ds(pl.multiple_of(ROW_DECAY + j * GROUP_HEADS, GROUP_HEADS), GROUP_HEADS), :]
        near = pl.ds(jj * GROUP_HEADS, GROUP_HEADS)
        step_ref[near, :] = (dt_grad / dt + decay * behind) * sigmoid(raw_ref[heads, :])
        save(step_ref.at[near], step_h.at[heads])
        rows = jj * SUM_GROUP
        sum_ref[rows : rows + SUM_GROUP, :] = jnp.concatenate(terms + skips + [dt * behind * decay], axis=0)
    wait_all(fetches)
    if theirs:
        first_ref[...] = head_ref[0 : TAPS - 1, :].astype(BF16)
    wait_all(saves)


def run_leave(core, state, near, common, far, before_out):
    theirs = before_out is not None
    out = [
        ("h", (T, WIDTH_X), BF16),
        ("h", (HEADS, T), F32),
        ("h" if theirs else "V", (T, HALF_X + HALF_B), F32),
        ("V", (HALF_GROUPS * SUM_GROUP, LANES), F32),
    ]
    scratch = [
        pltpu.VMEM((T, HALF_X), BF16),
        pltpu.VMEM((HALF_GROUPS * GROUP_HEADS, T), F32),
        pltpu.VMEM((8 + T, GROUP_X), F32),
        DMA(2 + HALF_GROUPS, FETCHES),
    ]
    args = [core, state, *near, *common, *far]
    specs = "s" + ("v" if theirs else "V") + "V" * (len(near) + len(COMMON)) + "h" * len(far)
    aliases = {}
    if theirs:
        done, pre_own = before_out
        args += [pre_own]
        aliases = {len(args) + i: i for i in range(2)}
        args += done
        specs += "Vhh"
        out += [("V", (TAPS - 1, CHANNELS), BF16)]
        scratch = [pltpu.VMEM((8, CHANNELS), F32), pltpu.VMEM((T, HALF_X + HALF_B), F32)] + scratch
    else:
        out += NEAR * HALF_GROUPS
    kernel = functools.partial(leave_kernel, theirs)
    outs = call(kernel, "leave", out, specs, 5, scratch, mib=8, aliases=aliases)(*args)
    return outs[:2], outs[2], outs[3], outs[4:]


def spread_kernel(core_ref, own_ref, theirs_h, halo_ref, weight_ref, out_h, theirs_ref, out_ref, win_ref, sems):
    load = start_all([(theirs_h, theirs_ref)], sems.at[pl.ds(8, 1)])
    saves = []
    size = HALF_GROUPS * STATE
    for side, pre_ref in enumerate((own_ref, theirs_ref)):
        half = 1 - core_ref[0] if side else core_ref[0]
        if side:
            wait_all(load)
        blocks = [(jj * GROUP_X, span(half * HALF_GROUPS + jj, GROUP_X), GROUP_X) for jj in range(HALF_GROUPS)]
        blocks += [
            (HALF_X + base * size, span(WIDTH_X // size + 2 * base + half, size), size) for base in range(2)
        ]
        for near, far, width in blocks:
            win_ref[0:T, 0:width] = pre_ref[:, near : near + width]
            win_ref[T : T + TAPS - 1, 0:width] = halo_ref[:, far].astype(F32)
            weights = weight_ref[:, far]
            base = side * (HALF_X + HALF_B) + near
            for lo in range(0, width, LANES):
                at = slice(lo, lo + LANES)
                rows = win_ref[:, at]
                acc = weights[TAPS - 1 : TAPS, at] * rows[:T]
                for k in range(TAPS - 1):
                    acc = acc + weights[k : k + 1, at] * pltpu.roll(rows, T + 8 - (TAPS - 1 - k), 0)[:T]
                out_ref[:, base + lo : base + lo + LANES] = acc.astype(BF16)
            copy = pltpu.make_async_copy(out_ref.at[:, pl.ds(base, width)], out_h.at[:, far], sems.at[len(saves)])
            copy.start()
            saves.append(copy)
    wait_all(saves)


def run_spread(core, own, theirs, halo, weight):
    out = [("h", (T, CHANNELS), BF16)]
    scratch = [
        pltpu.VMEM((T, HALF_X + HALF_B), F32),
        pltpu.VMEM((T, CHANNELS), BF16),
        pltpu.VMEM((T + 8, GROUP_X), F32),
        DMA(9),
    ]
    return call(spread_kernel, "spread", out, "sVhvV", 3, scratch, mib=8)(core, own, theirs, halo, weight)[0]


CONV_ROWS = TAPS * (CHANNELS // LANES)
CONV_GROUP = CONV_ROWS // GROUPS
SEND_ROWS = CONV_ROWS + 16


def write_send(out_ref, conv, thin):
    high = thin.astype(BF16).astype(F32)
    low = thin - high
    row = iota((16, LANES), 0)
    out_ref[0:CONV_ROWS, :] = conv.astype(BF16)
    out_ref[CONV_ROWS:SEND_ROWS, :] = jnp.where(row == 0, high, jnp.where(row == 1, low, 0.0)).astype(BF16)


def read_send(value):
    wide = value.astype(F32)
    return wide[0:CONV_ROWS], wide[CONV_ROWS : CONV_ROWS + 1] + wide[CONV_ROWS + 1 : CONV_ROWS + 2]


def merge_kernel(core_ref, own_ref, own_got_ref, theirs_ref, theirs_got_ref, out_ref):
    thin = jnp.zeros((8, LANES), F32)
    left = iota((8, LANES), 1) < HEAD_DIM
    count = HEADS // 2
    parts = []
    for side, (mine, other) in enumerate(((own_ref, theirs_got_ref), (theirs_ref, own_got_ref))):
        half = 1 - core_ref[0] if side else core_ref[0]
        total = mine[...] + other[...]
        rows, skips, decays = [], [], []
        for jj in range(HALF_GROUPS):
            at = jj * SUM_GROUP
            rows.append(total[at : at + CONV_GROUP])
            skips.append(total[at + CONV_GROUP : at + SUM_GROUP - GROUP_HEADS])
            decays.append(total[at + SUM_GROUP - GROUP_HEADS : at + SUM_GROUP])
        skips = jnp.concatenate(skips, axis=0)
        even = exact_dot(jnp.where(left, 1.0, 0.0), skips, NT)
        odd = exact_dot(jnp.where(left, 0.0, 1.0), skips, NT)
        decay = exact_dot(jnp.ones((8, LANES), F32), jnp.concatenate(decays, axis=0), NT)
        for part, step, shift in ((even, 2, 0), (odd, 2, 1), (decay, 1, HEADS)):
            size = part.shape[1]
            spot = (iota((size, LANES), 1) == step * iota((size, LANES), 0) + shift + half * count).astype(F32)
            thin = thin + exact_dot(part, spot)
        parts.append(jnp.concatenate(rows, axis=0))
    first = core_ref[0] == 0
    conv = jnp.concatenate(
        [jnp.where(first, parts[0], parts[1]), jnp.where(first, parts[1], parts[0])], axis=0
    )
    write_send(out_ref, conv, thin[0:1])


def run_merge(core, own, own_got, theirs, theirs_got):
    out = [("v", (SEND_ROWS, LANES), BF16)]
    return call(merge_kernel, "merge", out, "svvvv", 1, mib=4)(core, own, own_got, theirs, theirs_got)[0]


def ring_sum(core_ref, me_ref, refs, hold_ref):
    count = len(refs)
    sides = (count - 1) // 2
    hold_ref[0] = refs[0][...]
    for k in range(1, sides + 1):
        mine = jnp.where(core_ref[0] == 0, k, count - k)
        hold_ref[mine] = refs[k][...]
        hold_ref[count - mine] = refs[sides + k][...]
    if count % 2 == 0:
        hold_ref[count // 2] = refs[count - 1][...]
    conv, thin = read_send(hold_ref[lax.rem(me_ref[0], count)])
    for k in range(1, count):
        more, little = read_send(hold_ref[lax.rem(me_ref[0] + count - k, count)])
        conv, thin = conv + more, thin + little
    return conv, thin


def fold_kernel(core_ref, me_ref, *rest):
    *refs, out_ref, hold_ref = rest
    write_send(out_ref, *ring_sum(core_ref, me_ref, refs, hold_ref))


def run_fold(core, me, values):
    out = [("v", (SEND_ROWS, LANES), BF16)]
    scratch = [pltpu.VMEM((len(values), SEND_ROWS, LANES), BF16)]
    return call(fold_kernel, "fold", out, "ss" + "v" * len(values), 1, scratch, mib=4)(core, me, *values)[0]


def finish_kernel(core_ref, me_ref, *rest):
    *refs, conv_ref, decay_ref, skip_ref, hold_ref = rest
    conv, thin = ring_sum(core_ref, me_ref, refs, hold_ref)
    for i in range(CHANNELS // LANES):
        if i < PAIRS:
            row = CONV_GROUP * (i // GROUP_PAIRS) + TAPS * (i % GROUP_PAIRS)
        else:
            kind, group = divmod(i - PAIRS, GROUPS)
            row = CONV_GROUP * group + TAPS * (GROUP_PAIRS + kind)
        conv_ref[:, i * LANES : (i + 1) * LANES] = conv[row : row + TAPS]
    skip_ref[...] = thin[:, 0:HEADS]
    decay_ref[...] = thin[:, HEADS:]


def run_finish(core, me, values):
    out = [("v", (TAPS, CHANNELS), F32), ("v", (1, HEADS), F32), ("v", (1, HEADS), F32)]
    scratch = [pltpu.VMEM((len(values), SEND_ROWS, LANES), BF16)]
    return call(finish_kernel, "finish", out, "ss" + "v" * len(values), 1, scratch, mib=4)(core, me, *values)


CTX = ("chip", "core")
ALL = ("dp", "chip", "core")


def all_to_all(value, axis):
    return lax.all_to_all(value, axis, 0, 0, tiled=True)


def tie(*values):
    return lax.optimization_barrier(values)


SIDE = 4


def around(value, axis, size, ring, move):
    def hear(first, second):
        return lax.ppermute(
            value,
            (axis, "core"),
            [(2 * i + side, 2 * move(i, d) + side) for i in range(size) for side, d in enumerate((first, second))],
        )

    middle = [hear(ring // 2, ring // 2)] if ring % 2 == 0 else []
    heard = [hear(k, ring - k) for k in range(1, (ring - 1) // 2 + 1)]
    swapped = [lax.ppermute(part, "core", [(0, 1), (1, 0)]) for part in heard]
    return [value] + heard + swapped + middle


def scalar(value):
    return value.astype(jnp.int32).reshape(1)


def local(conv_input, conv_weight, step_raw, decay_log, skip_gain, cotangent):
    chips = lax.axis_size("chip")
    devices = 2 * chips
    sequences = lax.axis_size("dp")
    tokens = conv_input[0]
    raw = step_raw[0]
    cot = cotangent[0]
    core = lax.axis_index("core").astype(jnp.int32).reshape(1)
    swap = [(0, 1), (1, 0)]
    halo = lax.ppermute(tokens[T - TAPS + 1 :], CTX, [(i, i + 1) for i in range(devices - 1)])
    small, small_near, tot, x0, bc0, head, weight_near, cot_near = run_begin(
        raw, decay_log.reshape(1, HEADS), skip_gain.reshape(1, HEADS), tokens, conv_weight, cot
    )
    other = lax.ppermute(tot, "core", swap)
    x, bc, before, x_near, bc_near, out = run_enter(
        core, x0, bc0, head, halo, weight_near, cot_near, small_near
    )
    got_near = lax.ppermute(out, "core", swap)
    own_near = run_own(core, x_near, bc_near, cot_near, small_near)
    packed, left, right, tots = run_pack(core, own_near, got_near, tot, other)
    heard = all_to_all(packed, "chip")
    y, gbc, skips = run_inner(x, bc, cot, small)
    heard, y, gbc, skips = tie(heard, y, gbc, skips)
    chained = run_chain(chips, heard)
    late, chained = tie(bc, chained)
    back = all_to_all(chained, "chip")
    gx, slope = run_slopes(late, cot, small, tokens, before, conv_weight)
    back, gx, slope = tie(back, gx, slope)
    far = (x, cot, y, gx, slope, tokens, bc, gbc)
    mine, send, near, common = run_unpack(
        core, back, left, right, tots, far, (before, small, raw, skips, conv_weight)
    )
    theirs = lax.ppermute(send, "core", swap)
    half, pre_own, sum_own, near = run_leave(core, mine, near, common, far, None)
    sum_own_got = lax.ppermute(sum_own, "core", swap)
    (out_tokens, grad_step), pre_theirs, sum_theirs, (first,) = run_leave(
        core, theirs, near, common, (), (half, pre_own)
    )
    sum_theirs_got = lax.ppermute(sum_theirs, "core", swap)
    sums = run_merge(core, sum_own, sum_own_got, sum_theirs, sum_theirs_got)
    chip, sequence = lax.axis_index("chip"), lax.axis_index("dp")
    rows = chips // SIDE
    values = around(sums, "chip", chips, SIDE, lambda i, d: i // SIDE * SIDE + (i % SIDE + d) % SIDE)
    sums = run_fold(core, scalar(lax.rem(chip, SIDE)), values)
    values = around(sums, "chip", chips, rows, lambda i, d: (i + d * SIDE) % chips)
    sums, first = tie(run_fold(core, scalar(lax.div(chip, SIDE)), values), first)
    after = lax.ppermute(first, CTX, [(i + 1, i) for i in range(devices - 1)])
    near = 2 if sequences % 2 == 0 else 1
    if near > 1:
        values = around(sums, "dp", sequences, near, lambda i, d: i // 2 * 2 + (i % 2 + d) % 2)
        sums = run_fold(core, scalar(lax.rem(sequence, near)), values)
    values = around(sums, "dp", sequences, sequences // near, lambda i, d: (i + d * near) % sequences)
    grad_tokens = run_spread(core, pre_own, pre_theirs, after, common[4])
    values, grad_tokens = tie(values, grad_tokens)
    grad_conv, grad_decay, grad_skip = run_finish(core, scalar(lax.div(sequence, near)), values)
    return (
        out_tokens[None],
        grad_tokens[None],
        grad_step[None],
        grad_conv,
        grad_decay.reshape(HEADS),
        grad_skip.reshape(HEADS),
    )


def solution(mesh):
    dp, ctx = mesh.devices.shape
    fine = Mesh(mesh.devices.reshape(dp, ctx // 2, 2), ALL)
    seq = P("dp", CTX, None)
    rate = P("dp", None, CTX)
    in_specs = (seq, P(), rate, P(), P(), seq)
    out_specs = (seq, seq, rate, P(), P(), P())
    return jax.shard_map(local, mesh=fine, in_specs=in_specs, out_specs=out_specs, check_vma=False)
```

```python
import functools

import jax
import jax.numpy as jnp
from jax import lax
from jax.experimental import pallas as pl
from jax.experimental.pallas import tpu as pltpu
from jax.sharding import Mesh
from jax.sharding import PartitionSpec as P

HEADS = 64
HEAD_DIM = 64
GROUPS = 4
STATE = 128
TAPS = 4
T = 128
LANES = 128
WIDTH_X = HEADS * HEAD_DIM
WIDTH_B = GROUPS * STATE
CHANNELS = WIDTH_X + 2 * WIDTH_B
GROUP_X = WIDTH_X // GROUPS
PAIRS = HEADS // 2
GROUP_PAIRS = PAIRS // GROUPS
GROUP_HEADS = HEADS // GROUPS
HALF_PAIRS = PAIRS // 2
HALF_GROUPS = GROUPS // 2
F32 = jnp.float32
BF16 = jnp.bfloat16
EXACT = lax.Precision.HIGHEST
NN = (((1,), (0,)), ((), ()))
NT = (((1,), (1,)), ((), ()))
SUM_GROUP = 64
PACK_ROWS = 2 * STATE + 16


def dot(a, b, dims=NN):
    return lax.dot_general(a, b, dims, preferred_element_type=F32)


def exact_dot(a, b, dims=NN):
    return lax.dot_general(a, b, dims, precision=EXACT, preferred_element_type=F32)


def iota(shape, dim):
    return lax.broadcasted_iota(jnp.int32, shape, dim)


def sigmoid(v):
    return 0.5 + 0.5 * jnp.tanh(0.5 * v)


def split_two(v):
    high = v.astype(BF16)
    return high, (v - high.astype(F32)).astype(BF16)


def span(index, size):
    return pl.ds(pl.multiple_of(index * size, size), size)


def pin(value, space):
    return pltpu.with_memory_space_constraint(value, space)


def placed(space, shape, dtype):
    return space(shape, dtype)


def call(kernel, name, outs, specs, micros, scratch=(), mib=28, aliases=None):
    cost = pl.CostEstimate(
        flops=int(micros * 1e9), transcendentals=0, bytes_accessed=int(micros * 3.6e6)
    )
    blocks = {
        "s": pl.BlockSpec(memory_space=pltpu.SMEM),
        "v": pl.BlockSpec(memory_space=pltpu.VMEM),
        "V": pl.BlockSpec(memory_space=pltpu.VMEM),
        "h": pl.BlockSpec(memory_space=pltpu.HBM),
    }
    spaces = {"V": pltpu.VMEM, "h": pltpu.HBM}
    shapes = [
        placed(spaces[p], shape, dtype) if p in spaces else jax.ShapeDtypeStruct(shape, dtype)
        for p, shape, dtype in outs
    ]
    run = pl.pallas_call(
        kernel,
        out_shape=shapes,
        in_specs=[blocks[p] for p in specs],
        out_specs=[blocks[p] for p, _, _ in outs],
        scratch_shapes=list(scratch),
        input_output_aliases=aliases or {},
        cost_estimate=cost,
        compiler_params=pltpu.CompilerParams(vmem_limit_bytes=mib << 20),
        name=name,
    )

    def go(*args):
        return run(*[pin(a, spaces[p]) if p in spaces else a for a, p in zip(args, specs, strict=True)])

    return go


def start_all(pairs, sems):
    copies = [pltpu.make_async_copy(a, b, sems.at[i]) for i, (a, b) in enumerate(pairs)]
    for copy in copies:
        copy.start()
    return copies


def wait_all(copies):
    for copy in copies:
        copy.wait()


def DMA(*shape):
    return pltpu.SemaphoreType.DMA(shape)


def fill_window(win_ref, before, tokens):
    width = tokens.shape[1]
    win_ref[0:8, :width] = before
    win_ref[8 : 8 + T, :width] = tokens.astype(F32)


def pre_conv(win_ref, weights, lo):
    cols = slice(lo, lo + LANES)
    rows = win_ref[0 : 8 + T, cols]
    acc = weights[TAPS - 1 : TAPS, cols] * rows[8:]
    for k in range(TAPS - 1):
        acc = acc + weights[k : k + 1, cols] * pltpu.roll(rows, TAPS - 1 - k, 0)[8:]
    return acc


BLOCKS = CHANNELS // GROUP_X


ROW_DT, ROW_SEG, ROW_COLS, ROW_SCALE, ROW_TOT, ROW_SKIP, ROW_DECAY, SMALL_ROWS = (
    0, 64, 128, 256, 384, 416, 448, 512
)


def begin_kernel(raw_h, decay_log_h, skip_gain_h, tok_h, weight_h, g_h,
                 small_h, small_ref, tot_ref, x_ref, bc_ref, head_ref, weight_ref, g_ref,
                 raw_ref, decay_log_ref, skip_gain_ref, wide_ref, hold_ref, win_ref, sems):
    first = start_all(
        [(raw_h, raw_ref), (decay_log_h, decay_log_ref), (skip_gain_h, skip_gain_ref), (weight_h, weight_ref)],
        sems.at[0],
    )
    blocks = [pl.ds(i * GROUP_X, GROUP_X) for i in range(BLOCKS)]
    copies = start_all([(tok_h.at[:, at], hold_ref.at[:, at]) for at in blocks], sems.at[1])
    later = start_all([(g_h, g_ref)], sems.at[2])
    win_ref[0:8, :] = jnp.zeros((8, GROUP_X), F32)
    copies[0].wait()
    diagonal = iota((HEADS, HEADS), 0) == iota((HEADS, HEADS), 1)

    def column(row):
        return jnp.sum(jnp.where(diagonal, row, 0.0), axis=1, keepdims=True)

    wait_all(first)
    raw = raw_ref[...]
    dt = jnp.log1p(jnp.exp(raw))
    decay = -jnp.exp(column(decay_log_ref[...]))
    upper = (iota((T, T), 0) <= iota((T, T), 1)).astype(F32)
    seg = exact_dot(dt * decay, upper)
    total = seg[:, T - 1 : T]
    small_ref[ROW_DT : ROW_DT + HEADS] = dt
    small_ref[ROW_SEG : ROW_SEG + HEADS] = seg
    small_ref[ROW_COLS : ROW_COLS + T] = jnp.transpose(jnp.concatenate([seg, dt], axis=0))
    small_ref[ROW_SCALE : ROW_SCALE + T] = jnp.transpose(
        jnp.concatenate([jnp.exp(seg), jnp.exp(total - seg) * dt], axis=0)
    )
    left = iota((PAIRS, LANES), 1) < HEAD_DIM

    def paired(col):
        wide_ref[...] = jnp.broadcast_to(col, (HEADS, LANES))
        return jnp.where(left, wide_ref[pl.ds(0, PAIRS, 2), :], wide_ref[pl.ds(1, PAIRS, 2), :])

    tot = paired(total)
    tot_ref[...] = tot
    small_ref[ROW_TOT : ROW_TOT + PAIRS] = tot
    small_ref[ROW_SKIP : ROW_SKIP + PAIRS] = paired(column(skip_gain_ref[...]))
    small_ref[ROW_DECAY : ROW_DECAY + HEADS] = jnp.broadcast_to(decay, (HEADS, LANES))
    save = start_all([(small_ref, small_h)], sems.at[0])
    for i in range(BLOCKS):
        if i:
            copies[i].wait()
        cols = slice(i * GROUP_X, (i + 1) * GROUP_X)
        win_ref[8 : 8 + T, :] = hold_ref[:, cols].astype(F32)
        for lo in range(0, GROUP_X, LANES):
            at = i * GROUP_X + lo
            pre = pre_conv(win_ref, weight_ref[:, cols], lo)
            mixed = (pre * sigmoid(pre)).astype(BF16)
            head_ref[:, at : at + LANES] = pre[0:8]
            if at < WIDTH_X:
                x_ref[:, at : at + LANES] = mixed
            else:
                bc_ref[:, at - WIDTH_X : at - WIDTH_X + LANES] = mixed
    wait_all(save + later)


def run_begin(raw, decay_log, skip_gain, tokens, weight, cot):
    out = [
        ("h", (SMALL_ROWS, LANES), F32),
        ("V", (SMALL_ROWS, LANES), F32),
        ("V", (PAIRS, LANES), F32),
        ("V", (T, WIDTH_X), BF16),
        ("V", (T, 2 * WIDTH_B), BF16),
        ("V", (8, CHANNELS), F32),
        ("V", (TAPS, CHANNELS), F32),
        ("V", (T, WIDTH_X), BF16),
    ]
    scratch = [
        pltpu.VMEM((HEADS, T), F32),
        pltpu.VMEM((1, HEADS), F32),
        pltpu.VMEM((1, HEADS), F32),
        pltpu.VMEM((HEADS, LANES), F32),
        pltpu.VMEM((T, CHANNELS), BF16),
        pltpu.VMEM((8 + T, GROUP_X), F32),
        DMA(3, BLOCKS),
    ]
    return call(begin_kernel, "begin", out, "hhhhhh", 4, scratch, mib=8)(
        raw, decay_log, skip_gain, tokens, weight, cot
    )


def rolled(cols, group):
    return pltpu.roll(cols, (LANES - group * GROUP_HEADS) % LANES, 1)


def widen(cols, base, pair):
    first = iota((T, LANES), 1) < HEAD_DIM
    at = base + 2 * pair
    return jnp.where(first, cols[:, at : at + 1], cols[:, at + 1 : at + 2])


def widen_two(cols, base, pair):
    return jnp.concatenate([widen(cols, base, pair), widen(cols, base, pair + 1)], axis=1)


def fill_half(half, x_ref, bc_ref, g_ref, scale, dst_ref):
    for jj in range(HALF_GROUPS):
        j = half * HALF_GROUPS + jj
        b_flip = jnp.transpose(bc_ref[:, span(j, STATE)].astype(F32)).astype(BF16)
        c_flip = jnp.transpose(bc_ref[:, span(GROUPS + j, STATE)].astype(F32)).astype(BF16)
        cols = rolled(scale, j)
        for q in range(0, GROUP_PAIRS, 2):
            lanes = pl.ds(pl.multiple_of(j * GROUP_X + q * LANES, 2 * LANES), 2 * LANES)
            xw = (x_ref[:, lanes].astype(F32) * widen_two(cols, HEADS, q)).astype(BF16)
            gw = (g_ref[:, lanes].astype(F32) * widen_two(cols, 0, q)).astype(BF16)
            state = dot(b_flip, xw).astype(BF16)
            grad = dot(c_flip, gw).astype(BF16)
            for k in range(2):
                at = jj * GROUP_PAIRS + q + k
                dst_ref[0, at] = state[:, k * LANES : (k + 1) * LANES]
                dst_ref[1, at] = grad[:, k * LANES : (k + 1) * LANES]


def enter_kernel(core_ref, x0_ref, bc0_ref, head_ref, halo_ref, weight_ref, g_ref, small_ref,
                 x_h, bc_h, before_h, x_ref, bc_ref, out_ref, before_ref, sems):
    half = 1 - core_ref[0]
    row = iota((8, GROUP_X), 0)
    for i in range(BLOCKS):
        cols = slice(i * GROUP_X, (i + 1) * GROUP_X)
        halo = halo_ref[:, cols].astype(F32)
        weight = weight_ref[:, cols]
        pre = head_ref[:, cols]
        before = jnp.zeros((8, GROUP_X), F32)
        for t in range(TAPS - 1):
            extra = jnp.zeros((1, GROUP_X), F32)
            for k in range(TAPS - 1 - t):
                extra = extra + weight[k : k + 1] * halo[t + k : t + k + 1]
            pre = pre + jnp.where(row == t, extra, 0.0)
            before = before + jnp.where(row == t + 5, halo[t : t + 1], 0.0)
        before_ref[:, cols] = before
        fixed = pre * sigmoid(pre)
        src, dst, at = (x0_ref, x_ref, cols) if i < GROUPS else (bc0_ref, bc_ref, slice(0, GROUP_X))
        rest = src[0:16, at].astype(F32)
        dst[16:T, at] = src[16:T, at]
        dst[0:16, at] = jnp.concatenate([fixed, rest[8:16]], axis=0).astype(BF16)
    saves = start_all([(x_ref, x_h), (bc_ref, bc_h), (before_ref, before_h)], sems)
    fill_half(half, x_ref, bc_ref, g_ref, small_ref[ROW_SCALE : ROW_SCALE + T], out_ref)
    wait_all(saves)


def run_enter(core, x0, bc0, head, halo, weight, cot, small):
    out = [
        ("h", (T, WIDTH_X), BF16),
        ("h", (T, 2 * WIDTH_B), BF16),
        ("h", (8, CHANNELS), F32),
        ("V", (T, WIDTH_X), BF16),
        ("V", (T, 2 * WIDTH_B), BF16),
        ("V", (2, HALF_PAIRS, STATE, LANES), BF16),
    ]
    scratch = [pltpu.VMEM((8, CHANNELS), F32), DMA(3)]
    return call(enter_kernel, "enter", out, "sVVVvVVV", 3, scratch, mib=6)(
        core, x0, bc0, head, halo, weight, cot, small
    )


def own_kernel(core_ref, x_ref, bc_ref, g_ref, small_ref, own_ref):
    fill_half(core_ref[0], x_ref, bc_ref, g_ref, small_ref[ROW_SCALE : ROW_SCALE + T], own_ref)


def run_own(core, x, bc, cot, small):
    out = [("V", (2, HALF_PAIRS, STATE, LANES), BF16)]
    return call(own_kernel, "own", out, "sVVVV", 3, mib=6)(core, x, bc, cot, small)[0]


STEP_PAIRS = 4
STEPS = HALF_PAIRS // STEP_PAIRS


def pack_kernel(core_ref, own_ref, got_ref, tot_ref, other_ref,
                out_h, left_h, right_h, tots_h, out_ref, sems):
    saves = start_all(
        [(tot_ref, tots_h.at[pl.ds(0, PAIRS)]), (other_ref, tots_h.at[pl.ds(PAIRS, PAIRS)])], sems.at[0]
    )
    second = core_ref[0] == 1

    def keep(first_ref, last_ref):
        return [
            pltpu.make_async_copy(first_ref.at[0], left_h, sems.at[0, 2]),
            pltpu.make_async_copy(last_ref.at[1], right_h, sems.at[0, 3]),
        ]

    @pl.when(second)
    def _():
        for copy in keep(got_ref, own_ref):
            copy.start()

    @pl.when(jnp.logical_not(second))
    def _():
        for copy in keep(own_ref, got_ref):
            copy.start()

    saves += keep(own_ref, got_ref)
    outs = []
    for i in range(HALF_PAIRS):
        at = core_ref[0] * HALF_PAIRS + i
        tot = tot_ref[pl.ds(at, 1), :]
        other = other_ref[pl.ds(at, 1), :]
        one = jnp.ones_like(tot)
        by_own = jnp.exp(tot)
        by_other = jnp.exp(other)
        state = (
            jnp.where(second, one, by_other) * own_ref[0, i].astype(F32)
            + jnp.where(second, by_own, one) * got_ref[0, i].astype(F32)
        )
        grad = (
            jnp.where(second, by_other, one) * own_ref[1, i].astype(F32)
            + jnp.where(second, one, by_own) * got_ref[1, i].astype(F32)
        )
        out_ref[i, 0:STATE, :] = state.astype(BF16)
        out_ref[i, STATE : 2 * STATE, :] = grad.astype(BF16)
        both = tot + other
        high = both.astype(BF16).astype(F32)
        mid = (both - high).astype(BF16).astype(F32)
        low = both - high - mid
        row = iota((16, LANES), 0)
        wide = jnp.where(row == 0, high, jnp.where(row == 1, mid, jnp.where(row == 2, low, 0.0)))
        out_ref[i, 2 * STATE : PACK_ROWS, :] = wide.astype(BF16)
        if i % STEP_PAIRS == STEP_PAIRS - 1:
            done = pl.ds(i + 1 - STEP_PAIRS, STEP_PAIRS)
            copy = pltpu.make_async_copy(out_ref.at[done], out_h.at[done], sems.at[1, i // STEP_PAIRS])
            copy.start()
            outs.append(copy)
    wait_all(outs + saves)


def run_pack(core, own, got, tot, other):
    half = (HALF_PAIRS, STATE, LANES)
    packed = (HALF_PAIRS, PACK_ROWS, LANES)
    out = [("h", packed, BF16), ("h", half, BF16), ("h", half, BF16), ("h", (2 * PAIRS, LANES), F32)]
    scratch = [pltpu.VMEM(packed, BF16), DMA(2, STEPS)]
    return call(pack_kernel, "pack", out, "sVvVv", 2, scratch, mib=8)(core, own, got, tot, other)


def chain_kernel(chips, per, in_ref, out_ref):
    for q in range(per):
        def decay(k):
            rows = in_ref[k * per + q, 2 * STATE : PACK_ROWS, :].astype(F32)
            return jnp.exp(rows[0:1] + rows[1:2] + rows[2:3])

        carry = jnp.zeros((STATE, LANES), F32)
        for k in range(chips):
            out_ref[k * per + q, 0:STATE, :] = carry.astype(BF16)
            if k < chips - 1:
                carry = decay(k) * carry + in_ref[k * per + q, 0:STATE, :].astype(F32)
        carry = jnp.zeros((STATE, LANES), F32)
        for k in reversed(range(chips)):
            out_ref[k * per + q, STATE : 2 * STATE, :] = carry.astype(BF16)
            if k > 0:
                carry = decay(k) * carry + in_ref[k * per + q, STATE : 2 * STATE, :].astype(F32)


def run_chain(chips, packed):
    kernel = functools.partial(chain_kernel, chips, HALF_PAIRS // chips)
    out = [("v", (HALF_PAIRS, 2 * STATE, LANES), BF16)]
    return call(kernel, "chain", out, "v", 1, mib=8)(packed)[0]


HALF_X = HALF_GROUPS * GROUP_X
HALF_B = 2 * HALF_GROUPS * STATE

NEAR = [
    ("V", (T, GROUP_X), BF16),
    ("V", (T, GROUP_X), BF16),
    ("V", (T, GROUP_X), F32),
    ("V", (T, GROUP_X), F32),
    ("V", (T, GROUP_X + 2 * STATE), F32),
    ("V", (T, GROUP_X + 2 * STATE), BF16),
    ("V", (T, 2 * STATE), BF16),
    ("V", (T, 2 * STATE), F32),
]
COMMON = [
    ("V", (8, CHANNELS), F32),
    ("V", (SMALL_ROWS, LANES), F32),
    ("V", (HEADS, T), F32),
    ("V", (PAIRS, LANES), F32),
    ("V", (TAPS, CHANNELS), F32),
]
FETCHES = 6 + 8


def fetch_group(j, far, near, sems):
    x_h, g_h, y_h, gx_h, slope_h, tok_h, bc_h, gbc_h = far
    x_v, g_v, y_v, gx_v, slope_v, tok_v, bc_v, gbc_v = near
    wide = pl.ds(0, GROUP_X)
    pairs = [
        (a.at[:, span(j, GROUP_X)], b.at[:, wide])
        for a, b in ((x_h, x_v), (g_h, g_v), (y_h, y_v), (gx_h, gx_v), (slope_h, slope_v), (tok_h, tok_v))
    ]
    for base in range(2):
        at = span(base * GROUPS + j, STATE)
        off = span(WIDTH_X // STATE + base * GROUPS + j, STATE)
        thin = pl.ds(base * STATE, STATE)
        tail = pl.ds(GROUP_X + base * STATE, STATE)
        pairs += [
            (bc_h.at[:, at], bc_v.at[:, thin]),
            (gbc_h.at[:, at], gbc_v.at[:, thin]),
            (slope_h.at[:, off], slope_v.at[:, tail]),
            (tok_h.at[:, off], tok_v.at[:, tail]),
        ]
    return start_all(pairs, sems)


def unpack_kernel(core_ref, back_ref, left_h, right_h, tots_h, *rest):
    far, rest = rest[: len(NEAR)], rest[len(NEAR) :]
    common_far, rest = rest[: len(COMMON)], rest[len(COMMON) :]
    mine_ref, send_ref, *rest = rest
    near = [rest[i * len(NEAR) : (i + 1) * len(NEAR)] for i in range(HALF_GROUPS)]
    rest = rest[HALF_GROUPS * len(NEAR) :]
    common, rest = rest[: len(COMMON)], rest[len(COMMON) :]
    left_ref, right_ref, tots_ref, sems, fetch_sems = rest
    first = start_all([(tots_h, tots_ref)], sems.at[STEPS])
    steps = []
    for step in range(STEPS):
        at = pl.ds(step * STEP_PAIRS, STEP_PAIRS)
        steps.append(
            start_all([(left_h.at[at], left_ref.at[at]), (right_h.at[at], right_ref.at[at])], sems.at[step])
        )
    fetches = start_all(list(zip(common_far, common)), fetch_sems.at[HALF_GROUPS])
    for jj in range(HALF_GROUPS):
        fetches += fetch_group(core_ref[0] * HALF_GROUPS + jj, far, near[jj], fetch_sems.at[jj])
    wait_all(first)
    second = core_ref[0] == 1
    for i in range(HALF_PAIRS):
        if i % STEP_PAIRS == 0:
            wait_all(steps[i // STEP_PAIRS])
        at = core_ref[0] * HALF_PAIRS + i
        tot = tots_ref[pl.ds(at, 1), :]
        other = tots_ref[pl.ds(PAIRS + at, 1), :]
        decay_zero = jnp.exp(jnp.where(second, other, tot))
        decay_one = jnp.exp(jnp.where(second, tot, other))
        state_zero = back_ref[i, 0:STATE, :].astype(F32)
        grad_one = back_ref[i, STATE : 2 * STATE, :].astype(F32)
        state_one = decay_zero * state_zero + left_ref[i].astype(F32)
        grad_zero = decay_one * grad_one + right_ref[i].astype(F32)
        mine_ref[0, i] = jnp.where(second, state_one, state_zero).astype(BF16)
        mine_ref[1, i] = jnp.where(second, grad_one, grad_zero).astype(BF16)
        send_ref[0, i] = jnp.where(second, state_zero, state_one).astype(BF16)
        send_ref[1, i] = jnp.where(second, grad_zero, grad_one).astype(BF16)
    wait_all(fetches)


def run_unpack(core, back, left, right, tots, far, common):
    half = (2, HALF_PAIRS, STATE, LANES)
    out = [("V", half, BF16)] * 2 + NEAR * HALF_GROUPS + COMMON
    scratch = [
        pltpu.VMEM(half[1:], BF16),
        pltpu.VMEM(half[1:], BF16),
        pltpu.VMEM((2 * PAIRS, LANES), F32),
        DMA(STEPS + 1, 2),
        DMA(HALF_GROUPS + 1, FETCHES),
    ]
    specs = "svhhh" + "h" * (len(NEAR) + len(COMMON))
    outs = call(unpack_kernel, "unpack", out, specs, 3, scratch, mib=8)(
        core, back, left, right, tots, *far, *common
    )
    at = 2 + HALF_GROUPS * len(NEAR)
    return outs[0], outs[1], outs[2:at], outs[at:]


def by_lane_half(v):
    first = iota(v.shape, 1) < HEAD_DIM
    wide = v.astype(F32)
    return jnp.concatenate(
        [jnp.where(first, wide, 0.0).astype(BF16), jnp.where(first, 0.0, wide).astype(BF16)], axis=0
    )


def inner_kernel(x_h, bc_h, g_h, small_h, y_h, gbc_h, skips_h,
                 x_ref, bc_ref, g_ref, small_ref, y_ref, gbc_ref, skips_ref, sems):
    first = start_all([(bc_h, bc_ref), (small_h, small_ref)], sems.at[0])

    def loads(j):
        at = span(j, GROUP_X)
        return [
            pltpu.make_async_copy(x_h.at[:, at], x_ref.at[:, at], sems.at[1, j]),
            pltpu.make_async_copy(g_h.at[:, at], g_ref.at[:, at], sems.at[2, j]),
        ]

    def store(j):
        at = span(j, GROUP_X)
        return pltpu.make_async_copy(y_ref.at[:, at], y_h.at[:, at], sems.at[3, j])

    for j in range(GROUPS):
        for copy in loads(j):
            copy.start()
    wait_all(first)
    lower = iota((T, T), 0) >= iota((T, T), 1)

    @pl.loop(0, GROUPS)
    def _(j):
        wait_all(loads(j))
        b = bc_ref[:, span(j, STATE)]
        c = bc_ref[:, span(GROUPS + j, STATE)]
        seg = small_ref[pl.ds(pl.multiple_of(ROW_SEG + j * GROUP_HEADS, GROUP_HEADS), GROUP_HEADS), :]
        dt = small_ref[pl.ds(pl.multiple_of(ROW_DT + j * GROUP_HEADS, GROUP_HEADS), GROUP_HEADS), :]
        scores = dot(c, b, NT)
        cols = rolled(small_ref[ROW_COLS : ROW_COLS + T], j)
        total = jnp.zeros((T, T), F32)
        skips = []
        for i in range(GROUP_PAIRS):
            lanes = pl.ds(pl.multiple_of(j * GROUP_X + i * LANES, LANES), LANES)
            x = x_ref[:, lanes]
            g = g_ref[:, lanes]
            skips.append(jnp.sum(g.astype(F32) * x.astype(F32), axis=0, keepdims=True))
            inner = dot(by_lane_half(g), x, NT)
            weights = []
            for k in range(2):
                h = 2 * i + k
                spread = cols[:, h : h + 1] - seg[h : h + 1, :]
                kernel = jnp.exp(jnp.where(lower, spread, -1e30)) * dt[h : h + 1, :]
                total = total + kernel * inner[k * T : (k + 1) * T]
                weights.append((kernel * scores).astype(BF16))
            y_ref[:, lanes] = dot(jnp.concatenate(weights, axis=1), by_lane_half(x))
        skips_ref[span(j, GROUP_PAIRS), :] = jnp.concatenate(skips, axis=0)
        gbc_ref[:, span(GROUPS + j, STATE)] = dot(total.astype(BF16), b)
        gbc_ref[:, span(j, STATE)] = dot(jnp.transpose(total).astype(BF16), c)
        store(j).start()

    last = start_all([(gbc_ref, gbc_h), (skips_ref, skips_h)], sems.at[0])
    for j in range(GROUPS):
        store(j).wait()
    wait_all(last)


def run_inner(x, bc, cot, small):
    out = [("h", (T, WIDTH_X), F32), ("h", (T, 2 * WIDTH_B), F32), ("h", (PAIRS, LANES), F32)]
    scratch = [
        pltpu.VMEM((T, WIDTH_X), BF16),
        pltpu.VMEM((T, 2 * WIDTH_B), BF16),
        pltpu.VMEM((T, WIDTH_X), BF16),
        pltpu.VMEM((SMALL_ROWS, LANES), F32),
        pltpu.VMEM((T, WIDTH_X), F32),
        pltpu.VMEM((T, 2 * WIDTH_B), F32),
        pltpu.VMEM((PAIRS, LANES), F32),
        DMA(4, GROUPS),
    ]
    return call(inner_kernel, "inner", out, "hhhh", 4, scratch, mib=16)(x, bc, cot, small)


def slopes_kernel(bc_h, g_h, small_h, tok_h, before_h, weight_h, gx_h, slope_h,
                  bc_ref, g_ref, small_ref, tok_ref, before_ref, weight_ref, gx_ref, slope_ref, win_ref, sems):
    first = start_all(
        [(bc_h, bc_ref), (small_h, small_ref), (before_h, before_ref), (weight_h, weight_ref), (tok_h, tok_ref)],
        sems.at[0],
    )

    def load(j):
        at = span(j, GROUP_X)
        return pltpu.make_async_copy(g_h.at[:, at], g_ref.at[:, at], sems.at[1, j])

    def store(j):
        at = span(j, GROUP_X)
        return pltpu.make_async_copy(gx_ref.at[:, at], gx_h.at[:, at], sems.at[2, j])

    def store_slope(i):
        at = span(i, GROUP_X)
        return pltpu.make_async_copy(slope_ref.at[:, at], slope_h.at[:, at], sems.at[3, i])

    for j in range(GROUPS):
        load(j).start()
    wait_all(first)
    upper = iota((T, T), 0) <= iota((T, T), 1)

    @pl.loop(0, GROUPS)
    def _(j):
        load(j).wait()
        b = bc_ref[:, span(j, STATE)]
        c = bc_ref[:, span(GROUPS + j, STATE)]
        seg = small_ref[pl.ds(pl.multiple_of(ROW_SEG + j * GROUP_HEADS, GROUP_HEADS), GROUP_HEADS), :]
        scores = jnp.transpose(dot(c, b, NT))
        cols = rolled(small_ref[ROW_COLS : ROW_COLS + T], j)
        for i in range(GROUP_PAIRS):
            lanes = pl.ds(pl.multiple_of(j * GROUP_X + i * LANES, LANES), LANES)
            weights = []
            for k in range(2):
                h = 2 * i + k
                spread = seg[h : h + 1, :] - cols[:, h : h + 1]
                kernel = jnp.exp(jnp.where(upper, spread, -1e30)) * cols[:, HEADS + h : HEADS + h + 1]
                weights.append((kernel * scores).astype(BF16))
            gx_ref[:, lanes] = dot(jnp.concatenate(weights, axis=1), by_lane_half(g_ref[:, lanes]))
        store(j).start()

    @pl.loop(0, BLOCKS)
    def _(i):
        cols = span(i, GROUP_X)
        fill_window(win_ref, before_ref[:, cols], tok_ref[:, cols])
        weights = weight_ref[:, cols]
        for lo in range(0, GROUP_X, LANES):
            pre = pre_conv(win_ref, weights, lo)
            s = sigmoid(pre)
            at = pl.ds(pl.multiple_of(i * GROUP_X + lo, LANES), LANES)
            slope_ref[:, at] = s * (1.0 + pre * (1.0 - s))
        store_slope(i).start()

    for j in range(GROUPS):
        store(j).wait()
    for i in range(BLOCKS):
        store_slope(i).wait()


def run_slopes(bc, cot, small, tokens, before, weight):
    out = [("h", (T, WIDTH_X), F32), ("h", (T, CHANNELS), F32)]
    scratch = [
        pltpu.VMEM((T, 2 * WIDTH_B), BF16),
        pltpu.VMEM((T, WIDTH_X), BF16),
        pltpu.VMEM((SMALL_ROWS, LANES), F32),
        pltpu.VMEM((T, CHANNELS), BF16),
        pltpu.VMEM((8, CHANNELS), F32),
        pltpu.VMEM((TAPS, CHANNELS), F32),
        pltpu.VMEM((T, WIDTH_X), F32),
        pltpu.VMEM((T, CHANNELS), F32),
        pltpu.VMEM((8 + T, GROUP_X), F32),
        DMA(4, BLOCKS),
    ]
    return call(slopes_kernel, "slopes", out, "hhhhhh", 6, scratch, mib=16)(
        bc, cot, small, tokens, before, weight
    )


def leave_kernel(theirs, core_ref, state_ref, *rest):
    rest = list(rest)

    def take(count):
        taken = rest[:count]
        del rest[:count]
        return taken

    sets = [take(len(NEAR)) for _ in range(HALF_GROUPS)]
    before_ref, small_ref, raw_ref, skips_ref, _ = take(len(COMMON))
    half = 1 - core_ref[0] if theirs else core_ref[0]
    fetches = []
    if theirs:
        pre_own_ref, _, _ = take(3)
        out_h, step_h, pre_h, sum_ref, first_ref = take(5)
        head_ref, pre_ref, out_ref, step_ref, win_ref, sems = rest
        own = core_ref[0]
        head_ref[:, span(own, HALF_X)] = pre_own_ref[0:8, 0:HALF_X]
        size = HALF_GROUPS * STATE
        for base in range(2):
            at = HALF_X + base * size
            head_ref[:, span(WIDTH_X // size + 2 * base + own, size)] = pre_own_ref[0:8, at : at + size]
    else:
        far = take(len(NEAR))
        out_h, step_h, pre_ref, sum_ref = take(4)
        after = [take(len(NEAR)) for _ in range(HALF_GROUPS)]
        out_ref, step_ref, win_ref, sems = rest
        for jj in range(HALF_GROUPS):
            fetches += fetch_group((1 - half) * HALF_GROUPS + jj, far, after[jj], sems.at[2 + jj])
    last = iota((8, 2 * LANES), 0) == 7
    lower = (iota((T, T), 0) >= iota((T, T), 1)).astype(F32)

    def tap_sums(grad_pre, lo):
        rows = win_ref[0 : 8 + T, lo : lo + grad_pre.shape[1]]
        moved = [pltpu.roll(rows, TAPS - 1 - k, 0)[8:] for k in range(TAPS - 1)] + [rows[8:]]
        return [jnp.sum(grad_pre * part, axis=0, keepdims=True) for part in moved]

    def by_rows(sums):
        return [s[:, lo : lo + LANES] for lo in range(0, sums[0].shape[1], LANES) for s in sums]

    saves = []

    def save(src, dst):
        copy = pltpu.make_async_copy(src, dst, sems.at[len(saves) // 8, len(saves) % 8])
        copy.start()
        saves.append(copy)

    for jj in range(HALF_GROUPS):
        j = half * HALF_GROUPS + jj
        x_ref, g_ref, y_ref, gx_ref, slope_ref, tok_ref, bc_ref, gbc_ref = sets[jj]
        b = bc_ref[:, 0:STATE]
        c = bc_ref[:, STATE:]
        grad_b = gbc_ref[:, 0:STATE]
        grad_c = gbc_ref[:, STATE:]
        cols = rolled(small_ref[ROW_SCALE : ROW_SCALE + T], j)
        skip_rows = small_ref[pl.ds(pl.multiple_of(ROW_SKIP + j * GROUP_PAIRS, GROUP_PAIRS), GROUP_PAIRS), :]
        tot_rows = small_ref[pl.ds(pl.multiple_of(ROW_TOT + j * GROUP_PAIRS, GROUP_PAIRS), GROUP_PAIRS), :]
        seg_grad = jnp.zeros((GROUP_HEADS, T), F32)
        dt_grad = jnp.zeros((GROUP_HEADS, T), F32)
        skips = [skips_ref[span(j, GROUP_PAIRS), :]]
        terms = []
        fill_window(win_ref, before_ref[:, span(j, GROUP_X)], tok_ref[:, 0:GROUP_X])
        for q in range(0, GROUP_PAIRS, 2):
            lanes = slice(q * LANES, (q + 2) * LANES)
            wide = slice(jj * GROUP_X + q * LANES, jj * GROUP_X + (q + 2) * LANES)
            rise = widen_two(cols, 0, q)
            keep = widen_two(cols, HEADS, q)
            at = jj * GROUP_PAIRS + q
            state = jnp.concatenate([state_ref[0, at], state_ref[0, at + 1]], axis=1)
            exits = jnp.concatenate([state_ref[1, at], state_ref[1, at + 1]], axis=1)
            skip = jnp.concatenate([skip_rows[q : q + 1], skip_rows[q + 1 : q + 2]], axis=1)
            tot = jnp.concatenate([tot_rows[q : q + 1], tot_rows[q + 1 : q + 2]], axis=1)
            x = x_ref[:, lanes].astype(F32)
            g = g_ref[:, lanes].astype(F32)
            y = y_ref[:, lanes] + rise * dot(c, state)
            through = keep * dot(b, exits)
            gx = gx_ref[:, lanes] + through
            grad_c = grad_c + dot((g * rise).astype(BF16), state, NT)
            grad_b = grad_b + dot((x * keep).astype(BF16), exits, NT)
            out_ref[:, wide] = (y + skip * x).astype(BF16)
            grad_pre = (gx + skip * g) * slope_ref[:, lanes]
            pre_ref[:, wide] = grad_pre
            if theirs:
                at = pl.ds(pl.multiple_of(j * GROUP_X + q * LANES, 2 * LANES), 2 * LANES)
                head_ref[:, at] = grad_pre[0:8]
            terms += by_rows(tap_sums(grad_pre, q * LANES))
            x_gx = x * gx
            end = jnp.sum(x * through, axis=0, keepdims=True) + jnp.exp(tot) * jnp.sum(
                exits.astype(F32) * state.astype(F32), axis=0, keepdims=True
            )
            moved = g * y - x_gx
            moved = jnp.concatenate([moved[: T - 8], moved[T - 8 :] + jnp.where(last, end, 0.0)], axis=0)
            pick = (
                iota((GROUP_HEADS, 2 * LANES), 0)
                == 2 * q + iota((GROUP_HEADS, 2 * LANES), 1) // HEAD_DIM
            ).astype(F32).astype(BF16)
            for part in split_two(moved):
                seg_grad = seg_grad + dot(pick, part, NT)
            for part in split_two(x_gx):
                dt_grad = dt_grad + dot(pick, part, NT)
            if q % 4 == 2:
                size = GROUP_X // 2
                near_at = pl.ds(jj * GROUP_X + (q // 4) * size, size)
                far_at = span(2 * j + q // 4, size)
                save(out_ref.at[:, near_at], out_h.at[:, far_at])
                if theirs:
                    save(pre_ref.at[:, near_at], pre_h.at[:, near_at])
        for grad, base in ((grad_b, 0), (grad_c, 1)):
            at = HALF_X + (base * HALF_GROUPS + jj) * STATE
            tail = slice(GROUP_X + base * STATE, GROUP_X + (base + 1) * STATE)
            far_at = span(WIDTH_X // STATE + base * GROUPS + j, STATE)
            fill_window(win_ref, before_ref[:, far_at], tok_ref[:, tail])
            grad_pre = grad * slope_ref[:, tail]
            pre_ref[:, at : at + STATE] = grad_pre
            if theirs:
                head_ref[:, far_at] = grad_pre[0:8]
                save(pre_ref.at[:, pl.ds(at, STATE)], pre_h.at[:, pl.ds(at, STATE)])
            terms += tap_sums(grad_pre, 0)
        heads = span(j, GROUP_HEADS)
        behind = exact_dot(seg_grad, lower)
        dt = small_ref[pl.ds(pl.multiple_of(ROW_DT + j * GROUP_HEADS, GROUP_HEADS), GROUP_HEADS), :]
        decay = small_ref[pl.ds(pl.multiple_of(ROW_DECAY + j * GROUP_HEADS, GROUP_HEADS), GROUP_HEADS), :]
        near = pl.ds(jj * GROUP_HEADS, GROUP_HEADS)
        step_ref[near, :] = (dt_grad / dt + decay * behind) * sigmoid(raw_ref[heads, :])
        save(step_ref.at[near], step_h.at[heads])
        rows = jj * SUM_GROUP
        sum_ref[rows : rows + SUM_GROUP, :] = jnp.concatenate(terms + skips + [dt * behind * decay], axis=0)
    wait_all(fetches)
    if theirs:
        first_ref[...] = head_ref[0 : TAPS - 1, :].astype(BF16)
    wait_all(saves)


def run_leave(core, state, near, common, far, before_out):
    theirs = before_out is not None
    out = [
        ("h", (T, WIDTH_X), BF16),
        ("h", (HEADS, T), F32),
        ("h" if theirs else "V", (T, HALF_X + HALF_B), F32),
        ("V", (HALF_GROUPS * SUM_GROUP, LANES), F32),
    ]
    scratch = [
        pltpu.VMEM((T, HALF_X), BF16),
        pltpu.VMEM((HALF_GROUPS * GROUP_HEADS, T), F32),
        pltpu.VMEM((8 + T, GROUP_X), F32),
        DMA(2 + HALF_GROUPS, FETCHES),
    ]
    args = [core, state, *near, *common, *far]
    specs = "s" + ("v" if theirs else "V") + "V" * (len(near) + len(COMMON)) + "h" * len(far)
    aliases = {}
    if theirs:
        done, pre_own = before_out
        args += [pre_own]
        aliases = {len(args) + i: i for i in range(2)}
        args += done
        specs += "Vhh"
        out += [("V", (TAPS - 1, CHANNELS), BF16)]
        scratch = [pltpu.VMEM((8, CHANNELS), F32), pltpu.VMEM((T, HALF_X + HALF_B), F32)] + scratch
    else:
        out += NEAR * HALF_GROUPS
    kernel = functools.partial(leave_kernel, theirs)
    outs = call(kernel, "leave", out, specs, 5, scratch, mib=8, aliases=aliases)(*args)
    return outs[:2], outs[2], outs[3], outs[4:]


def spread_kernel(core_ref, chip_ref, own_ref, theirs_h, swap_ref, near_ref, far_ref, weight_ref, out_h,
                  theirs_ref, halo_ref, out_ref, win_ref, sems):
    load = start_all([(theirs_h, theirs_ref)], sems.at[pl.ds(8, 1)])
    edge = lax.rem(chip_ref[0], SIDE) == SIDE - 1
    last = (chip_ref[0] == chip_ref[1] - 1).astype(F32)
    rows = jnp.where(edge, far_ref[SEND_ROWS:, :].astype(F32), near_ref[SEND_ROWS:, :].astype(F32)) * (1.0 - last)
    for i in range(CHANNELS // LANES):
        cols = slice(i * LANES, (i + 1) * LANES)
        across = rows[i * (TAPS - 1) : (i + 1) * (TAPS - 1)]
        halo_ref[0 : TAPS - 1, cols] = jnp.where(core_ref[0] == 0, swap_ref[:, cols].astype(F32), across)
    saves = []
    size = HALF_GROUPS * STATE
    for side, pre_ref in enumerate((own_ref, theirs_ref)):
        half = 1 - core_ref[0] if side else core_ref[0]
        if side:
            wait_all(load)
        blocks = [(jj * GROUP_X, span(half * HALF_GROUPS + jj, GROUP_X), GROUP_X) for jj in range(HALF_GROUPS)]
        blocks += [
            (HALF_X + base * size, span(WIDTH_X // size + 2 * base + half, size), size) for base in range(2)
        ]
        for near, far, width in blocks:
            win_ref[0:T, 0:width] = pre_ref[:, near : near + width]
            win_ref[T : T + 8, 0:width] = halo_ref[:, far]
            weights = weight_ref[:, far]
            base = side * (HALF_X + HALF_B) + near
            for lo in range(0, width, LANES):
                at = slice(lo, lo + LANES)
                rows = win_ref[:, at]
                acc = weights[TAPS - 1 : TAPS, at] * rows[:T]
                for k in range(TAPS - 1):
                    acc = acc + weights[k : k + 1, at] * pltpu.roll(rows, T + 8 - (TAPS - 1 - k), 0)[:T]
                out_ref[:, base + lo : base + lo + LANES] = acc.astype(BF16)
            copy = pltpu.make_async_copy(out_ref.at[:, pl.ds(base, width)], out_h.at[:, far], sems.at[len(saves)])
            copy.start()
            saves.append(copy)
    wait_all(saves)


def run_spread(core, chip, own, theirs, swapped, near, far, weight):
    out = [("h", (T, CHANNELS), BF16)]
    scratch = [
        pltpu.VMEM((T, HALF_X + HALF_B), F32),
        pltpu.VMEM((8, CHANNELS), F32),
        pltpu.VMEM((T, CHANNELS), BF16),
        pltpu.VMEM((T + 8, GROUP_X), F32),
        DMA(9),
    ]
    return call(spread_kernel, "spread", out, "ssVhvvvV", 3, scratch, mib=8)(
        core, chip, own, theirs, swapped, near, far, weight
    )[0]


CONV_ROWS = TAPS * (CHANNELS // LANES)
CONV_GROUP = CONV_ROWS // GROUPS
SEND_ROWS = CONV_ROWS + 16
PLUS_ROWS = SEND_ROWS + 128


def write_send(out_ref, conv, thin):
    high = thin.astype(BF16).astype(F32)
    low = thin - high
    row = iota((16, LANES), 0)
    out_ref[0:CONV_ROWS, :] = conv.astype(BF16)
    out_ref[CONV_ROWS:SEND_ROWS, :] = jnp.where(row == 0, high, jnp.where(row == 1, low, 0.0)).astype(BF16)


def read_send(value):
    wide = value.astype(F32)
    return wide[0:CONV_ROWS], wide[CONV_ROWS : CONV_ROWS + 1] + wide[CONV_ROWS + 1 : CONV_ROWS + 2]


def merge_kernel(core_ref, own_ref, own_got_ref, theirs_ref, theirs_got_ref, swap_ref, out_ref, plus_ref):
    thin = jnp.zeros((8, LANES), F32)
    left = iota((8, LANES), 1) < HEAD_DIM
    count = HEADS // 2
    parts = []
    for side, (mine, other) in enumerate(((own_ref, theirs_got_ref), (theirs_ref, own_got_ref))):
        half = 1 - core_ref[0] if side else core_ref[0]
        total = mine[...] + other[...]
        rows, skips, decays = [], [], []
        for jj in range(HALF_GROUPS):
            at = jj * SUM_GROUP
            rows.append(total[at : at + CONV_GROUP])
            skips.append(total[at + CONV_GROUP : at + SUM_GROUP - GROUP_HEADS])
            decays.append(total[at + SUM_GROUP - GROUP_HEADS : at + SUM_GROUP])
        skips = jnp.concatenate(skips, axis=0)
        even = exact_dot(jnp.where(left, 1.0, 0.0), skips, NT)
        odd = exact_dot(jnp.where(left, 0.0, 1.0), skips, NT)
        decay = exact_dot(jnp.ones((8, LANES), F32), jnp.concatenate(decays, axis=0), NT)
        for part, step, shift in ((even, 2, 0), (odd, 2, 1), (decay, 1, HEADS)):
            size = part.shape[1]
            spot = (iota((size, LANES), 1) == step * iota((size, LANES), 0) + shift + half * count).astype(F32)
            thin = thin + exact_dot(part, spot)
        parts.append(jnp.concatenate(rows, axis=0))
    first = core_ref[0] == 0
    conv = jnp.concatenate(
        [jnp.where(first, parts[0], parts[1]), jnp.where(first, parts[1], parts[0])], axis=0
    )
    write_send(out_ref, conv, thin[0:1])
    plus_ref[0:SEND_ROWS, :] = out_ref[...]
    rows = [swap_ref[:, i * LANES : (i + 1) * LANES].astype(F32) for i in range(CHANNELS // LANES)]
    rows.append(jnp.zeros((PLUS_ROWS - SEND_ROWS - (TAPS - 1) * (CHANNELS // LANES), LANES), F32))
    plus_ref[SEND_ROWS:PLUS_ROWS, :] = jnp.concatenate(rows, axis=0).astype(BF16)


def run_merge(core, own, own_got, theirs, theirs_got, swapped):
    out = [("v", (SEND_ROWS, LANES), BF16), ("v", (PLUS_ROWS, LANES), BF16)]
    return call(merge_kernel, "merge", out, "svvvvv", 1, mib=4)(core, own, own_got, theirs, theirs_got, swapped)


def ring_sum(me_ref, hold_ref):
    count = hold_ref.shape[0]
    conv, thin = read_send(hold_ref[lax.rem(me_ref[0], count)])
    for k in range(1, count):
        more, little = read_send(hold_ref[lax.rem(me_ref[0] + count - k, count)])
        conv, thin = conv + more, thin + little
    return conv, thin


def fold_kernel(me_ref, *rest):
    *refs, out_ref, plus_ref, hold_ref = rest
    for d, ref in enumerate(refs):
        hold_ref[d] = ref[0:SEND_ROWS, :]
    write_send(out_ref, *ring_sum(me_ref, hold_ref))
    plus_ref[0:SEND_ROWS, :] = out_ref[...]
    plus_ref[SEND_ROWS:PLUS_ROWS, :] = refs[-1][SEND_ROWS:PLUS_ROWS, :]


def run_fold(me, values):
    out = [("v", (SEND_ROWS, LANES), BF16), ("v", (PLUS_ROWS, LANES), BF16)]
    scratch = [pltpu.VMEM((len(values), SEND_ROWS, LANES), BF16)]
    return call(fold_kernel, "fold", out, "s" + "v" * len(values), 1, scratch, mib=4)(me, *values)


def finish_kernel(core_ref, me_ref, *rest):
    *refs, conv_ref, decay_ref, skip_ref, hold_ref = rest
    count = len(refs)
    sides = (count - 1) // 2
    hold_ref[0] = refs[0][...]
    for k in range(1, sides + 1):
        mine = jnp.where(core_ref[0] == 0, k, count - k)
        hold_ref[mine] = refs[k][...]
        hold_ref[count - mine] = refs[sides + k][...]
    if count % 2 == 0:
        hold_ref[count // 2] = refs[count - 1][...]
    conv, thin = ring_sum(me_ref, hold_ref)
    for i in range(CHANNELS // LANES):
        if i < PAIRS:
            row = CONV_GROUP * (i // GROUP_PAIRS) + TAPS * (i % GROUP_PAIRS)
        else:
            kind, group = divmod(i - PAIRS, GROUPS)
            row = CONV_GROUP * group + TAPS * (GROUP_PAIRS + kind)
        conv_ref[:, i * LANES : (i + 1) * LANES] = conv[row : row + TAPS]
    skip_ref[...] = thin[:, 0:HEADS]
    decay_ref[...] = thin[:, HEADS:]


def run_finish(core, me, values):
    out = [("v", (TAPS, CHANNELS), F32), ("v", (1, HEADS), F32), ("v", (1, HEADS), F32)]
    scratch = [pltpu.VMEM((len(values), SEND_ROWS, LANES), BF16)]
    return call(finish_kernel, "finish", out, "ss" + "v" * len(values), 1, scratch, mib=4)(core, me, *values)


CTX = ("chip", "core")
ALL = ("dp", "chip", "core")


def all_to_all(value, axis):
    return lax.all_to_all(value, axis, 0, 0, tiled=True)


def tie(*values):
    return lax.optimization_barrier(values)


SIDE = 4


def around(value, plus, axis, size, ring, move):
    return [value] + [
        lax.ppermute(plus if d == ring - 1 else value, axis, [(i, move(i, d)) for i in range(size)])
        for d in range(1, ring)
    ]


def around_by_sides(value, axis, size, ring, move):
    def hear(first, second):
        return lax.ppermute(
            value,
            (axis, "core"),
            [(2 * i + side, 2 * move(i, d) + side) for i in range(size) for side, d in enumerate((first, second))],
        )

    middle = [hear(ring // 2, ring // 2)] if ring % 2 == 0 else []
    heard = [hear(k, ring - k) for k in range(1, (ring - 1) // 2 + 1)]
    swapped = [lax.ppermute(part, "core", [(0, 1), (1, 0)]) for part in heard]
    return [value] + heard + swapped + middle


def scalar(value):
    return value.astype(jnp.int32).reshape(1)


def local(conv_input, conv_weight, step_raw, decay_log, skip_gain, cotangent):
    chips = lax.axis_size("chip")
    devices = 2 * chips
    sequences = lax.axis_size("dp")
    tokens = conv_input[0]
    raw = step_raw[0]
    cot = cotangent[0]
    core = lax.axis_index("core").astype(jnp.int32).reshape(1)
    swap = [(0, 1), (1, 0)]
    halo = lax.ppermute(tokens[T - TAPS + 1 :], CTX, [(i, i + 1) for i in range(devices - 1)])
    small, small_near, tot, x0, bc0, head, weight_near, cot_near = run_begin(
        raw, decay_log.reshape(1, HEADS), skip_gain.reshape(1, HEADS), tokens, conv_weight, cot
    )
    other = lax.ppermute(tot, "core", swap)
    x, bc, before, x_near, bc_near, out = run_enter(
        core, x0, bc0, head, halo, weight_near, cot_near, small_near
    )
    got_near = lax.ppermute(out, "core", swap)
    own_near = run_own(core, x_near, bc_near, cot_near, small_near)
    packed, left, right, tots = run_pack(core, own_near, got_near, tot, other)
    heard = all_to_all(packed, "chip")
    y, gbc, skips = run_inner(x, bc, cot, small)
    heard, y, gbc, skips = tie(heard, y, gbc, skips)
    chained = run_chain(chips, heard)
    late, chained = tie(bc, chained)
    back = all_to_all(chained, "chip")
    gx, slope = run_slopes(late, cot, small, tokens, before, conv_weight)
    back, gx, slope = tie(back, gx, slope)
    far = (x, cot, y, gx, slope, tokens, bc, gbc)
    mine, send, near, common = run_unpack(
        core, back, left, right, tots, far, (before, small, raw, skips, conv_weight)
    )
    theirs = lax.ppermute(send, "core", swap)
    half, pre_own, sum_own, near = run_leave(core, mine, near, common, far, None)
    sum_own_got = lax.ppermute(sum_own, "core", swap)
    (out_tokens, grad_step), pre_theirs, sum_theirs, (first,) = run_leave(
        core, theirs, near, common, (), (half, pre_own)
    )
    sum_theirs_got = lax.ppermute(sum_theirs, "core", swap)
    first_got = lax.ppermute(first, "core", swap)
    sums, plus = run_merge(core, sum_own, sum_own_got, sum_theirs, sum_theirs_got, first_got)
    chip, sequence = lax.axis_index("chip"), lax.axis_index("dp")
    rows = chips // SIDE
    values = around(sums, plus, "chip", chips, SIDE, lambda i, d: i // SIDE * SIDE + (i % SIDE + d) % SIDE)
    after_y = values[-1]
    sums, plus = run_fold(scalar(lax.rem(chip, SIDE)), values)
    after_x = plus
    if rows > 1:
        values = around(sums, plus, "chip", chips, rows, lambda i, d: (i + d * SIDE) % chips)
        after_x = values[-1]
        sums, _ = run_fold(scalar(lax.div(chip, SIDE)), values)
    values = around_by_sides(sums, "dp", sequences, sequences, lambda i, d: (i + d) % sequences)
    place = jnp.stack([chip.astype(jnp.int32), jnp.int32(chips)])
    grad_tokens = run_spread(core, place, pre_own, pre_theirs, first_got, after_y, after_x, common[4])
    values, grad_tokens = tie(values, grad_tokens)
    grad_conv, grad_decay, grad_skip = run_finish(core, scalar(sequence), values)
    return (
        out_tokens[None],
        grad_tokens[None],
        grad_step[None],
        grad_conv,
        grad_decay.reshape(HEADS),
        grad_skip.reshape(HEADS),
    )


def solution(mesh):
    dp, ctx = mesh.devices.shape
    fine = Mesh(mesh.devices.reshape(dp, ctx // 2, 2), ALL)
    seq = P("dp", CTX, None)
    rate = P("dp", None, CTX)
    in_specs = (seq, P(), rate, P(), P(), seq)
    out_specs = (seq, seq, rate, P(), P(), P())
    return jax.shard_map(local, mesh=fine, in_specs=in_specs, out_specs=out_specs, check_vma=False)
```

```python
import functools

import jax
import jax.numpy as jnp
from jax import lax
from jax.experimental import pallas as pl
from jax.experimental.pallas import tpu as pltpu
from jax.sharding import Mesh
from jax.sharding import PartitionSpec as P

HEADS = 64
HEAD_DIM = 64
GROUPS = 4
STATE = 128
TAPS = 4
T = 128
LANES = 128
WIDTH_X = HEADS * HEAD_DIM
WIDTH_B = GROUPS * STATE
CHANNELS = WIDTH_X + 2 * WIDTH_B
GROUP_X = WIDTH_X // GROUPS
PAIRS = HEADS // 2
GROUP_PAIRS = PAIRS // GROUPS
GROUP_HEADS = HEADS // GROUPS
HALF_PAIRS = PAIRS // 2
HALF_GROUPS = GROUPS // 2
F32 = jnp.float32
BF16 = jnp.bfloat16
EXACT = lax.Precision.HIGHEST
NN = (((1,), (0,)), ((), ()))
NT = (((1,), (1,)), ((), ()))
SUM_GROUP = 64
PACK_ROWS = 2 * STATE + 16


def dot(a, b, dims=NN):
    return lax.dot_general(a, b, dims, preferred_element_type=F32)


def exact_dot(a, b, dims=NN):
    return lax.dot_general(a, b, dims, precision=EXACT, preferred_element_type=F32)


def iota(shape, dim):
    return lax.broadcasted_iota(jnp.int32, shape, dim)


def sigmoid(v):
    return 0.5 + 0.5 * jnp.tanh(0.5 * v)


def split_two(v):
    high = v.astype(BF16)
    return high, (v - high.astype(F32)).astype(BF16)


def span(index, size):
    return pl.ds(pl.multiple_of(index * size, size), size)


def pin(value, space):
    return pltpu.with_memory_space_constraint(value, space)


def placed(space, shape, dtype):
    return space(shape, dtype)


def call(kernel, name, outs, specs, micros, scratch=(), mib=28, aliases=None):
    cost = pl.CostEstimate(
        flops=int(micros * 1e9), transcendentals=0, bytes_accessed=int(micros * 3.6e6)
    )
    blocks = {
        "s": pl.BlockSpec(memory_space=pltpu.SMEM),
        "v": pl.BlockSpec(memory_space=pltpu.VMEM),
        "V": pl.BlockSpec(memory_space=pltpu.VMEM),
        "h": pl.BlockSpec(memory_space=pltpu.HBM),
    }
    spaces = {"V": pltpu.VMEM, "h": pltpu.HBM}
    shapes = [
        placed(spaces[p], shape, dtype) if p in spaces else jax.ShapeDtypeStruct(shape, dtype)
        for p, shape, dtype in outs
    ]
    run = pl.pallas_call(
        kernel,
        out_shape=shapes,
        in_specs=[blocks[p] for p in specs],
        out_specs=[blocks[p] for p, _, _ in outs],
        scratch_shapes=list(scratch),
        input_output_aliases=aliases or {},
        cost_estimate=cost,
        compiler_params=pltpu.CompilerParams(vmem_limit_bytes=mib << 20),
        name=name,
    )

    def go(*args):
        return run(*[pin(a, spaces[p]) if p in spaces else a for a, p in zip(args, specs, strict=True)])

    return go


def start_all(pairs, sems):
    copies = [pltpu.make_async_copy(a, b, sems.at[i]) for i, (a, b) in enumerate(pairs)]
    for copy in copies:
        copy.start()
    return copies


def wait_all(copies):
    for copy in copies:
        copy.wait()


def DMA(*shape):
    return pltpu.SemaphoreType.DMA(shape)


def fill_window(win_ref, before, tokens):
    width = tokens.shape[1]
    win_ref[0:8, :width] = before
    win_ref[8 : 8 + T, :width] = tokens.astype(F32)


def pre_conv(win_ref, weights, lo):
    cols = slice(lo, lo + LANES)
    rows = win_ref[0 : 8 + T, cols]
    acc = weights[TAPS - 1 : TAPS, cols] * rows[8:]
    for k in range(TAPS - 1):
        acc = acc + weights[k : k + 1, cols] * pltpu.roll(rows, TAPS - 1 - k, 0)[8:]
    return acc


BLOCKS = CHANNELS // GROUP_X


ROW_DT, ROW_SEG, ROW_COLS, ROW_SCALE, ROW_TOT, ROW_SKIP, ROW_DECAY, SMALL_ROWS = (
    0, 64, 128, 256, 384, 416, 448, 512
)


def begin_kernel(raw_h, decay_log_h, skip_gain_h, tok_h, weight_h, g_h,
                 small_h, small_ref, tot_ref, x_ref, bc_ref, head_ref, weight_ref, g_ref,
                 raw_ref, decay_log_ref, skip_gain_ref, wide_ref, hold_ref, win_ref, sems):
    first = start_all(
        [(raw_h, raw_ref), (decay_log_h, decay_log_ref), (skip_gain_h, skip_gain_ref), (weight_h, weight_ref)],
        sems.at[0],
    )
    blocks = [pl.ds(i * GROUP_X, GROUP_X) for i in range(BLOCKS)]
    copies = start_all([(tok_h.at[:, at], hold_ref.at[:, at]) for at in blocks], sems.at[1])
    later = start_all([(g_h, g_ref)], sems.at[2])
    win_ref[0:8, :] = jnp.zeros((8, GROUP_X), F32)
    copies[0].wait()
    diagonal = iota((HEADS, HEADS), 0) == iota((HEADS, HEADS), 1)

    def column(row):
        return jnp.sum(jnp.where(diagonal, row, 0.0), axis=1, keepdims=True)

    wait_all(first)
    raw = raw_ref[...]
    dt = jnp.log1p(jnp.exp(raw))
    decay = -jnp.exp(column(decay_log_ref[...]))
    upper = (iota((T, T), 0) <= iota((T, T), 1)).astype(F32)
    seg = exact_dot(dt * decay, upper)
    total = seg[:, T - 1 : T]
    small_ref[ROW_DT : ROW_DT + HEADS] = dt
    small_ref[ROW_SEG : ROW_SEG + HEADS] = seg
    small_ref[ROW_COLS : ROW_COLS + T] = jnp.transpose(jnp.concatenate([seg, dt], axis=0))
    small_ref[ROW_SCALE : ROW_SCALE + T] = jnp.transpose(
        jnp.concatenate([jnp.exp(seg), jnp.exp(total - seg) * dt], axis=0)
    )
    left = iota((PAIRS, LANES), 1) < HEAD_DIM

    def paired(col):
        wide_ref[...] = jnp.broadcast_to(col, (HEADS, LANES))
        return jnp.where(left, wide_ref[pl.ds(0, PAIRS, 2), :], wide_ref[pl.ds(1, PAIRS, 2), :])

    tot = paired(total)
    tot_ref[...] = tot
    small_ref[ROW_TOT : ROW_TOT + PAIRS] = tot
    small_ref[ROW_SKIP : ROW_SKIP + PAIRS] = paired(column(skip_gain_ref[...]))
    small_ref[ROW_DECAY : ROW_DECAY + HEADS] = jnp.broadcast_to(decay, (HEADS, LANES))
    save = start_all([(small_ref, small_h)], sems.at[0])
    for i in range(BLOCKS):
        if i:
            copies[i].wait()
        cols = slice(i * GROUP_X, (i + 1) * GROUP_X)
        win_ref[8 : 8 + T, :] = hold_ref[:, cols].astype(F32)
        for lo in range(0, GROUP_X, LANES):
            at = i * GROUP_X + lo
            pre = pre_conv(win_ref, weight_ref[:, cols], lo)
            mixed = (pre * sigmoid(pre)).astype(BF16)
            head_ref[:, at : at + LANES] = pre[0:8]
            if at < WIDTH_X:
                x_ref[:, at : at + LANES] = mixed
            else:
                bc_ref[:, at - WIDTH_X : at - WIDTH_X + LANES] = mixed
    wait_all(save + later)


def run_begin(raw, decay_log, skip_gain, tokens, weight, cot):
    out = [
        ("h", (SMALL_ROWS, LANES), F32),
        ("V", (SMALL_ROWS, LANES), F32),
        ("V", (PAIRS, LANES), F32),
        ("V", (T, WIDTH_X), BF16),
        ("V", (T, 2 * WIDTH_B), BF16),
        ("V", (8, CHANNELS), F32),
        ("V", (TAPS, CHANNELS), F32),
        ("V", (T, WIDTH_X), BF16),
    ]
    scratch = [
        pltpu.VMEM((HEADS, T), F32),
        pltpu.VMEM((1, HEADS), F32),
        pltpu.VMEM((1, HEADS), F32),
        pltpu.VMEM((HEADS, LANES), F32),
        pltpu.VMEM((T, CHANNELS), BF16),
        pltpu.VMEM((8 + T, GROUP_X), F32),
        DMA(3, BLOCKS),
    ]
    return call(begin_kernel, "begin", out, "hhhhhh", 4, scratch, mib=8)(
        raw, decay_log, skip_gain, tokens, weight, cot
    )


def rolled(cols, group):
    return pltpu.roll(cols, (LANES - group * GROUP_HEADS) % LANES, 1)


def widen(cols, base, pair):
    first = iota((T, LANES), 1) < HEAD_DIM
    at = base + 2 * pair
    return jnp.where(first, cols[:, at : at + 1], cols[:, at + 1 : at + 2])


def widen_two(cols, base, pair):
    return jnp.concatenate([widen(cols, base, pair), widen(cols, base, pair + 1)], axis=1)


def fill_half(half, x_ref, bc_ref, g_ref, scale, dst_ref):
    for jj in range(HALF_GROUPS):
        j = half * HALF_GROUPS + jj
        b_flip = jnp.transpose(bc_ref[:, span(j, STATE)].astype(F32)).astype(BF16)
        c_flip = jnp.transpose(bc_ref[:, span(GROUPS + j, STATE)].astype(F32)).astype(BF16)
        cols = rolled(scale, j)
        for q in range(0, GROUP_PAIRS, 2):
            lanes = pl.ds(pl.multiple_of(j * GROUP_X + q * LANES, 2 * LANES), 2 * LANES)
            xw = (x_ref[:, lanes].astype(F32) * widen_two(cols, HEADS, q)).astype(BF16)
            gw = (g_ref[:, lanes].astype(F32) * widen_two(cols, 0, q)).astype(BF16)
            state = dot(b_flip, xw).astype(BF16)
            grad = dot(c_flip, gw).astype(BF16)
            for k in range(2):
                at = jj * GROUP_PAIRS + q + k
                dst_ref[0, at] = state[:, k * LANES : (k + 1) * LANES]
                dst_ref[1, at] = grad[:, k * LANES : (k + 1) * LANES]


def enter_kernel(core_ref, x0_ref, bc0_ref, head_ref, halo_ref, weight_ref, g_ref, small_ref,
                 x_h, bc_h, before_h, x_ref, bc_ref, out_ref, before_ref, sems):
    half = 1 - core_ref[0]
    row = iota((8, GROUP_X), 0)
    for i in range(BLOCKS):
        cols = slice(i * GROUP_X, (i + 1) * GROUP_X)
        halo = halo_ref[:, cols].astype(F32)
        weight = weight_ref[:, cols]
        pre = head_ref[:, cols]
        before = jnp.zeros((8, GROUP_X), F32)
        for t in range(TAPS - 1):
            extra = jnp.zeros((1, GROUP_X), F32)
            for k in range(TAPS - 1 - t):
                extra = extra + weight[k : k + 1] * halo[t + k : t + k + 1]
            pre = pre + jnp.where(row == t, extra, 0.0)
            before = before + jnp.where(row == t + 5, halo[t : t + 1], 0.0)
        before_ref[:, cols] = before
        fixed = pre * sigmoid(pre)
        src, dst, at = (x0_ref, x_ref, cols) if i < GROUPS else (bc0_ref, bc_ref, slice(0, GROUP_X))
        rest = src[0:16, at].astype(F32)
        dst[16:T, at] = src[16:T, at]
        dst[0:16, at] = jnp.concatenate([fixed, rest[8:16]], axis=0).astype(BF16)
    saves = start_all([(x_ref, x_h), (bc_ref, bc_h), (before_ref, before_h)], sems)
    fill_half(half, x_ref, bc_ref, g_ref, small_ref[ROW_SCALE : ROW_SCALE + T], out_ref)
    wait_all(saves)


def run_enter(core, x0, bc0, head, halo, weight, cot, small):
    out = [
        ("h", (T, WIDTH_X), BF16),
        ("h", (T, 2 * WIDTH_B), BF16),
        ("h", (8, CHANNELS), F32),
        ("V", (T, WIDTH_X), BF16),
        ("V", (T, 2 * WIDTH_B), BF16),
        ("V", (2, HALF_PAIRS, STATE, LANES), BF16),
    ]
    scratch = [pltpu.VMEM((8, CHANNELS), F32), DMA(3)]
    return call(enter_kernel, "enter", out, "sVVVvVVV", 3, scratch, mib=6)(
        core, x0, bc0, head, halo, weight, cot, small
    )


def own_kernel(core_ref, x_ref, bc_ref, g_ref, small_ref, own_ref):
    fill_half(core_ref[0], x_ref, bc_ref, g_ref, small_ref[ROW_SCALE : ROW_SCALE + T], own_ref)


def run_own(core, x, bc, cot, small):
    out = [("V", (2, HALF_PAIRS, STATE, LANES), BF16)]
    return call(own_kernel, "own", out, "sVVVV", 3, mib=6)(core, x, bc, cot, small)[0]


STEP_PAIRS = 4
STEPS = HALF_PAIRS // STEP_PAIRS


def pack_kernel(core_ref, own_ref, got_ref, tot_ref, other_ref,
                out_h, left_h, right_h, tots_h, out_ref, sems):
    saves = start_all(
        [(tot_ref, tots_h.at[pl.ds(0, PAIRS)]), (other_ref, tots_h.at[pl.ds(PAIRS, PAIRS)])], sems.at[0]
    )
    second = core_ref[0] == 1

    def keep(first_ref, last_ref):
        return [
            pltpu.make_async_copy(first_ref.at[0], left_h, sems.at[0, 2]),
            pltpu.make_async_copy(last_ref.at[1], right_h, sems.at[0, 3]),
        ]

    @pl.when(second)
    def _():
        for copy in keep(got_ref, own_ref):
            copy.start()

    @pl.when(jnp.logical_not(second))
    def _():
        for copy in keep(own_ref, got_ref):
            copy.start()

    saves += keep(own_ref, got_ref)
    outs = []
    for i in range(HALF_PAIRS):
        at = core_ref[0] * HALF_PAIRS + i
        tot = tot_ref[pl.ds(at, 1), :]
        other = other_ref[pl.ds(at, 1), :]
        one = jnp.ones_like(tot)
        by_own = jnp.exp(tot)
        by_other = jnp.exp(other)
        state = (
            jnp.where(second, one, by_other) * own_ref[0, i].astype(F32)
            + jnp.where(second, by_own, one) * got_ref[0, i].astype(F32)
        )
        grad = (
            jnp.where(second, by_other, one) * own_ref[1, i].astype(F32)
            + jnp.where(second, one, by_own) * got_ref[1, i].astype(F32)
        )
        out_ref[i, 0:STATE, :] = state.astype(BF16)
        out_ref[i, STATE : 2 * STATE, :] = grad.astype(BF16)
        both = tot + other
        high = both.astype(BF16).astype(F32)
        mid = (both - high).astype(BF16).astype(F32)
        low = both - high - mid
        row = iota((16, LANES), 0)
        wide = jnp.where(row == 0, high, jnp.where(row == 1, mid, jnp.where(row == 2, low, 0.0)))
        out_ref[i, 2 * STATE : PACK_ROWS, :] = wide.astype(BF16)
        if i % STEP_PAIRS == STEP_PAIRS - 1:
            done = pl.ds(i + 1 - STEP_PAIRS, STEP_PAIRS)
            copy = pltpu.make_async_copy(out_ref.at[done], out_h.at[done], sems.at[1, i // STEP_PAIRS])
            copy.start()
            outs.append(copy)
    wait_all(outs + saves)


def run_pack(core, own, got, tot, other):
    half = (HALF_PAIRS, STATE, LANES)
    packed = (HALF_PAIRS, PACK_ROWS, LANES)
    out = [("h", packed, BF16), ("h", half, BF16), ("h", half, BF16), ("h", (2 * PAIRS, LANES), F32)]
    scratch = [pltpu.VMEM(packed, BF16), DMA(2, STEPS)]
    return call(pack_kernel, "pack", out, "sVvVv", 2, scratch, mib=8)(core, own, got, tot, other)


def chain_kernel(chips, per, in_ref, out_ref):
    for q in range(per):
        def decay(k):
            rows = in_ref[k * per + q, 2 * STATE : PACK_ROWS, :].astype(F32)
            return jnp.exp(rows[0:1] + rows[1:2] + rows[2:3])

        carry = jnp.zeros((STATE, LANES), F32)
        for k in range(chips):
            out_ref[k * per + q, 0:STATE, :] = carry.astype(BF16)
            if k < chips - 1:
                carry = decay(k) * carry + in_ref[k * per + q, 0:STATE, :].astype(F32)
        carry = jnp.zeros((STATE, LANES), F32)
        for k in reversed(range(chips)):
            out_ref[k * per + q, STATE : 2 * STATE, :] = carry.astype(BF16)
            if k > 0:
                carry = decay(k) * carry + in_ref[k * per + q, STATE : 2 * STATE, :].astype(F32)


def run_chain(chips, packed):
    kernel = functools.partial(chain_kernel, chips, HALF_PAIRS // chips)
    out = [("v", (HALF_PAIRS, 2 * STATE, LANES), BF16)]
    return call(kernel, "chain", out, "v", 1, mib=8)(packed)[0]


HALF_X = HALF_GROUPS * GROUP_X
HALF_B = 2 * HALF_GROUPS * STATE

NEAR = [
    ("V", (T, GROUP_X), BF16),
    ("V", (T, GROUP_X), BF16),
    ("V", (T, GROUP_X), F32),
    ("V", (T, GROUP_X), F32),
    ("V", (T, GROUP_X + 2 * STATE), F32),
    ("V", (T, GROUP_X + 2 * STATE), BF16),
    ("V", (T, 2 * STATE), BF16),
    ("V", (T, 2 * STATE), F32),
]
COMMON = [
    ("V", (8, CHANNELS), F32),
    ("V", (SMALL_ROWS, LANES), F32),
    ("V", (HEADS, T), F32),
    ("V", (PAIRS, LANES), F32),
    ("V", (TAPS, CHANNELS), F32),
]
FETCHES = 6 + 8


def fetch_group(j, far, near, sems):
    x_h, g_h, y_h, gx_h, slope_h, tok_h, bc_h, gbc_h = far
    x_v, g_v, y_v, gx_v, slope_v, tok_v, bc_v, gbc_v = near
    wide = pl.ds(0, GROUP_X)
    pairs = [
        (a.at[:, span(j, GROUP_X)], b.at[:, wide])
        for a, b in ((x_h, x_v), (g_h, g_v), (y_h, y_v), (gx_h, gx_v), (slope_h, slope_v), (tok_h, tok_v))
    ]
    for base in range(2):
        at = span(base * GROUPS + j, STATE)
        off = span(WIDTH_X // STATE + base * GROUPS + j, STATE)
        thin = pl.ds(base * STATE, STATE)
        tail = pl.ds(GROUP_X + base * STATE, STATE)
        pairs += [
            (bc_h.at[:, at], bc_v.at[:, thin]),
            (gbc_h.at[:, at], gbc_v.at[:, thin]),
            (slope_h.at[:, off], slope_v.at[:, tail]),
            (tok_h.at[:, off], tok_v.at[:, tail]),
        ]
    return start_all(pairs, sems)


def unpack_kernel(core_ref, back_ref, left_h, right_h, tots_h, *rest):
    far, rest = rest[: len(NEAR)], rest[len(NEAR) :]
    common_far, rest = rest[: len(COMMON)], rest[len(COMMON) :]
    mine_ref, send_ref, *rest = rest
    near = [rest[i * len(NEAR) : (i + 1) * len(NEAR)] for i in range(HALF_GROUPS)]
    rest = rest[HALF_GROUPS * len(NEAR) :]
    common, rest = rest[: len(COMMON)], rest[len(COMMON) :]
    left_ref, right_ref, tots_ref, sems, fetch_sems = rest
    first = start_all([(tots_h, tots_ref)], sems.at[STEPS])
    steps = []
    for step in range(STEPS):
        at = pl.ds(step * STEP_PAIRS, STEP_PAIRS)
        steps.append(
            start_all([(left_h.at[at], left_ref.at[at]), (right_h.at[at], right_ref.at[at])], sems.at[step])
        )
    fetches = start_all(list(zip(common_far, common)), fetch_sems.at[HALF_GROUPS])
    for jj in range(HALF_GROUPS):
        fetches += fetch_group(core_ref[0] * HALF_GROUPS + jj, far, near[jj], fetch_sems.at[jj])
    wait_all(first)
    second = core_ref[0] == 1
    for i in range(HALF_PAIRS):
        if i % STEP_PAIRS == 0:
            wait_all(steps[i // STEP_PAIRS])
        at = core_ref[0] * HALF_PAIRS + i
        tot = tots_ref[pl.ds(at, 1), :]
        other = tots_ref[pl.ds(PAIRS + at, 1), :]
        decay_zero = jnp.exp(jnp.where(second, other, tot))
        decay_one = jnp.exp(jnp.where(second, tot, other))
        state_zero = back_ref[i, 0:STATE, :].astype(F32)
        grad_one = back_ref[i, STATE : 2 * STATE, :].astype(F32)
        state_one = decay_zero * state_zero + left_ref[i].astype(F32)
        grad_zero = decay_one * grad_one + right_ref[i].astype(F32)
        mine_ref[0, i] = jnp.where(second, state_one, state_zero).astype(BF16)
        mine_ref[1, i] = jnp.where(second, grad_one, grad_zero).astype(BF16)
        send_ref[0, i] = jnp.where(second, state_zero, state_one).astype(BF16)
        send_ref[1, i] = jnp.where(second, grad_zero, grad_one).astype(BF16)
    wait_all(fetches)


def run_unpack(core, back, left, right, tots, far, common):
    half = (2, HALF_PAIRS, STATE, LANES)
    out = [("V", half, BF16)] * 2 + NEAR * HALF_GROUPS + COMMON
    scratch = [
        pltpu.VMEM(half[1:], BF16),
        pltpu.VMEM(half[1:], BF16),
        pltpu.VMEM((2 * PAIRS, LANES), F32),
        DMA(STEPS + 1, 2),
        DMA(HALF_GROUPS + 1, FETCHES),
    ]
    specs = "svhhh" + "h" * (len(NEAR) + len(COMMON))
    outs = call(unpack_kernel, "unpack", out, specs, 3, scratch, mib=8)(
        core, back, left, right, tots, *far, *common
    )
    at = 2 + HALF_GROUPS * len(NEAR)
    return outs[0], outs[1], outs[2:at], outs[at:]


def by_lane_half(v):
    first = iota(v.shape, 1) < HEAD_DIM
    wide = v.astype(F32)
    return jnp.concatenate(
        [jnp.where(first, wide, 0.0).astype(BF16), jnp.where(first, 0.0, wide).astype(BF16)], axis=0
    )


def inner_kernel(x_h, bc_h, g_h, small_h, y_h, gbc_h, skips_h,
                 x_ref, bc_ref, g_ref, small_ref, y_ref, gbc_ref, skips_ref, sems):
    first = start_all([(bc_h, bc_ref), (small_h, small_ref)], sems.at[0])

    def loads(j):
        at = span(j, GROUP_X)
        return [
            pltpu.make_async_copy(x_h.at[:, at], x_ref.at[:, at], sems.at[1, j]),
            pltpu.make_async_copy(g_h.at[:, at], g_ref.at[:, at], sems.at[2, j]),
        ]

    def store(j):
        at = span(j, GROUP_X)
        return pltpu.make_async_copy(y_ref.at[:, at], y_h.at[:, at], sems.at[3, j])

    for j in range(GROUPS):
        for copy in loads(j):
            copy.start()
    wait_all(first)
    lower = iota((T, T), 0) >= iota((T, T), 1)

    @pl.loop(0, GROUPS)
    def _(j):
        wait_all(loads(j))
        b = bc_ref[:, span(j, STATE)]
        c = bc_ref[:, span(GROUPS + j, STATE)]
        seg = small_ref[pl.ds(pl.multiple_of(ROW_SEG + j * GROUP_HEADS, GROUP_HEADS), GROUP_HEADS), :]
        dt = small_ref[pl.ds(pl.multiple_of(ROW_DT + j * GROUP_HEADS, GROUP_HEADS), GROUP_HEADS), :]
        scores = dot(c, b, NT)
        cols = rolled(small_ref[ROW_COLS : ROW_COLS + T], j)
        total = jnp.zeros((T, T), F32)
        skips = []
        for i in range(GROUP_PAIRS):
            lanes = pl.ds(pl.multiple_of(j * GROUP_X + i * LANES, LANES), LANES)
            x = x_ref[:, lanes]
            g = g_ref[:, lanes]
            skips.append(jnp.sum(g.astype(F32) * x.astype(F32), axis=0, keepdims=True))
            inner = dot(by_lane_half(g), x, NT)
            weights = []
            for k in range(2):
                h = 2 * i + k
                spread = cols[:, h : h + 1] - seg[h : h + 1, :]
                kernel = jnp.exp(jnp.where(lower, spread, -1e30)) * dt[h : h + 1, :]
                total = total + kernel * inner[k * T : (k + 1) * T]
                weights.append((kernel * scores).astype(BF16))
            y_ref[:, lanes] = dot(jnp.concatenate(weights, axis=1), by_lane_half(x))
        skips_ref[span(j, GROUP_PAIRS), :] = jnp.concatenate(skips, axis=0)
        gbc_ref[:, span(GROUPS + j, STATE)] = dot(total.astype(BF16), b)
        gbc_ref[:, span(j, STATE)] = dot(jnp.transpose(total).astype(BF16), c)
        store(j).start()

    last = start_all([(gbc_ref, gbc_h), (skips_ref, skips_h)], sems.at[0])
    for j in range(GROUPS):
        store(j).wait()
    wait_all(last)


def run_inner(x, bc, cot, small):
    out = [("h", (T, WIDTH_X), F32), ("h", (T, 2 * WIDTH_B), F32), ("h", (PAIRS, LANES), F32)]
    scratch = [
        pltpu.VMEM((T, WIDTH_X), BF16),
        pltpu.VMEM((T, 2 * WIDTH_B), BF16),
        pltpu.VMEM((T, WIDTH_X), BF16),
        pltpu.VMEM((SMALL_ROWS, LANES), F32),
        pltpu.VMEM((T, WIDTH_X), F32),
        pltpu.VMEM((T, 2 * WIDTH_B), F32),
        pltpu.VMEM((PAIRS, LANES), F32),
        DMA(4, GROUPS),
    ]
    return call(inner_kernel, "inner", out, "hhhh", 4, scratch, mib=16)(x, bc, cot, small)


def slopes_kernel(bc_h, g_h, small_h, tok_h, before_h, weight_h, gx_h, slope_h,
                  bc_ref, g_ref, small_ref, tok_ref, before_ref, weight_ref, gx_ref, slope_ref, win_ref, sems):
    first = start_all(
        [(bc_h, bc_ref), (small_h, small_ref), (before_h, before_ref), (weight_h, weight_ref), (tok_h, tok_ref)],
        sems.at[0],
    )

    def load(j):
        at = span(j, GROUP_X)
        return pltpu.make_async_copy(g_h.at[:, at], g_ref.at[:, at], sems.at[1, j])

    def store(j):
        at = span(j, GROUP_X)
        return pltpu.make_async_copy(gx_ref.at[:, at], gx_h.at[:, at], sems.at[2, j])

    def store_slope(i):
        at = span(i, GROUP_X)
        return pltpu.make_async_copy(slope_ref.at[:, at], slope_h.at[:, at], sems.at[3, i])

    for j in range(GROUPS):
        load(j).start()
    wait_all(first)
    upper = iota((T, T), 0) <= iota((T, T), 1)

    @pl.loop(0, GROUPS)
    def _(j):
        load(j).wait()
        b = bc_ref[:, span(j, STATE)]
        c = bc_ref[:, span(GROUPS + j, STATE)]
        seg = small_ref[pl.ds(pl.multiple_of(ROW_SEG + j * GROUP_HEADS, GROUP_HEADS), GROUP_HEADS), :]
        scores = jnp.transpose(dot(c, b, NT))
        cols = rolled(small_ref[ROW_COLS : ROW_COLS + T], j)
        for i in range(GROUP_PAIRS):
            lanes = pl.ds(pl.multiple_of(j * GROUP_X + i * LANES, LANES), LANES)
            weights = []
            for k in range(2):
                h = 2 * i + k
                spread = seg[h : h + 1, :] - cols[:, h : h + 1]
                kernel = jnp.exp(jnp.where(upper, spread, -1e30)) * cols[:, HEADS + h : HEADS + h + 1]
                weights.append((kernel * scores).astype(BF16))
            gx_ref[:, lanes] = dot(jnp.concatenate(weights, axis=1), by_lane_half(g_ref[:, lanes]))
        store(j).start()

    @pl.loop(0, BLOCKS)
    def _(i):
        cols = span(i, GROUP_X)
        fill_window(win_ref, before_ref[:, cols], tok_ref[:, cols])
        weights = weight_ref[:, cols]
        for lo in range(0, GROUP_X, LANES):
            pre = pre_conv(win_ref, weights, lo)
            s = sigmoid(pre)
            at = pl.ds(pl.multiple_of(i * GROUP_X + lo, LANES), LANES)
            slope_ref[:, at] = s * (1.0 + pre * (1.0 - s))
        store_slope(i).start()

    for j in range(GROUPS):
        store(j).wait()
    for i in range(BLOCKS):
        store_slope(i).wait()


def run_slopes(bc, cot, small, tokens, before, weight):
    out = [("h", (T, WIDTH_X), F32), ("h", (T, CHANNELS), F32)]
    scratch = [
        pltpu.VMEM((T, 2 * WIDTH_B), BF16),
        pltpu.VMEM((T, WIDTH_X), BF16),
        pltpu.VMEM((SMALL_ROWS, LANES), F32),
        pltpu.VMEM((T, CHANNELS), BF16),
        pltpu.VMEM((8, CHANNELS), F32),
        pltpu.VMEM((TAPS, CHANNELS), F32),
        pltpu.VMEM((T, WIDTH_X), F32),
        pltpu.VMEM((T, CHANNELS), F32),
        pltpu.VMEM((8 + T, GROUP_X), F32),
        DMA(4, BLOCKS),
    ]
    return call(slopes_kernel, "slopes", out, "hhhhhh", 6, scratch, mib=16)(
        bc, cot, small, tokens, before, weight
    )


def leave_kernel(theirs, core_ref, state_ref, *rest):
    rest = list(rest)

    def take(count):
        taken = rest[:count]
        del rest[:count]
        return taken

    sets = [take(len(NEAR)) for _ in range(HALF_GROUPS)]
    before_ref, small_ref, raw_ref, skips_ref, _ = take(len(COMMON))
    half = 1 - core_ref[0] if theirs else core_ref[0]
    fetches = []
    if theirs:
        pre_own_ref, _, _ = take(3)
        out_h, step_h, pre_h, sum_ref, first_ref = take(5)
        head_ref, pre_ref, out_ref, step_ref, win_ref, sems = rest
        own = core_ref[0]
        head_ref[:, span(own, HALF_X)] = pre_own_ref[0:8, 0:HALF_X]
        size = HALF_GROUPS * STATE
        for base in range(2):
            at = HALF_X + base * size
            head_ref[:, span(WIDTH_X // size + 2 * base + own, size)] = pre_own_ref[0:8, at : at + size]
    else:
        far = take(len(NEAR))
        out_h, step_h, pre_ref, sum_ref = take(4)
        after = [take(len(NEAR)) for _ in range(HALF_GROUPS)]
        out_ref, step_ref, win_ref, sems = rest
        for jj in range(HALF_GROUPS):
            fetches += fetch_group((1 - half) * HALF_GROUPS + jj, far, after[jj], sems.at[2 + jj])
    last = iota((8, 2 * LANES), 0) == 7
    lower = (iota((T, T), 0) >= iota((T, T), 1)).astype(F32)

    def tap_sums(grad_pre, lo):
        rows = win_ref[0 : 8 + T, lo : lo + grad_pre.shape[1]]
        moved = [pltpu.roll(rows, TAPS - 1 - k, 0)[8:] for k in range(TAPS - 1)] + [rows[8:]]
        return [jnp.sum(grad_pre * part, axis=0, keepdims=True) for part in moved]

    def by_rows(sums):
        return [s[:, lo : lo + LANES] for lo in range(0, sums[0].shape[1], LANES) for s in sums]

    saves = []

    def save(src, dst):
        copy = pltpu.make_async_copy(src, dst, sems.at[len(saves) // 8, len(saves) % 8])
        copy.start()
        saves.append(copy)

    for jj in range(HALF_GROUPS):
        j = half * HALF_GROUPS + jj
        x_ref, g_ref, y_ref, gx_ref, slope_ref, tok_ref, bc_ref, gbc_ref = sets[jj]
        b = bc_ref[:, 0:STATE]
        c = bc_ref[:, STATE:]
        grad_b = gbc_ref[:, 0:STATE]
        grad_c = gbc_ref[:, STATE:]
        cols = rolled(small_ref[ROW_SCALE : ROW_SCALE + T], j)
        skip_rows = small_ref[pl.ds(pl.multiple_of(ROW_SKIP + j * GROUP_PAIRS, GROUP_PAIRS), GROUP_PAIRS), :]
        tot_rows = small_ref[pl.ds(pl.multiple_of(ROW_TOT + j * GROUP_PAIRS, GROUP_PAIRS), GROUP_PAIRS), :]
        seg_grad = jnp.zeros((GROUP_HEADS, T), F32)
        dt_grad = jnp.zeros((GROUP_HEADS, T), F32)
        skips = [skips_ref[span(j, GROUP_PAIRS), :]]
        terms = []
        fill_window(win_ref, before_ref[:, span(j, GROUP_X)], tok_ref[:, 0:GROUP_X])
        for q in range(0, GROUP_PAIRS, 2):
            lanes = slice(q * LANES, (q + 2) * LANES)
            wide = slice(jj * GROUP_X + q * LANES, jj * GROUP_X + (q + 2) * LANES)
            rise = widen_two(cols, 0, q)
            keep = widen_two(cols, HEADS, q)
            at = jj * GROUP_PAIRS + q
            state = jnp.concatenate([state_ref[0, at], state_ref[0, at + 1]], axis=1)
            exits = jnp.concatenate([state_ref[1, at], state_ref[1, at + 1]], axis=1)
            skip = jnp.concatenate([skip_rows[q : q + 1], skip_rows[q + 1 : q + 2]], axis=1)
            tot = jnp.concatenate([tot_rows[q : q + 1], tot_rows[q + 1 : q + 2]], axis=1)
            x = x_ref[:, lanes].astype(F32)
            g = g_ref[:, lanes].astype(F32)
            y = y_ref[:, lanes] + rise * dot(c, state)
            through = keep * dot(b, exits)
            gx = gx_ref[:, lanes] + through
            grad_c = grad_c + dot((g * rise).astype(BF16), state, NT)
            grad_b = grad_b + dot((x * keep).astype(BF16), exits, NT)
            out_ref[:, wide] = (y + skip * x).astype(BF16)
            grad_pre = (gx + skip * g) * slope_ref[:, lanes]
            pre_ref[:, wide] = grad_pre
            if theirs:
                at = pl.ds(pl.multiple_of(j * GROUP_X + q * LANES, 2 * LANES), 2 * LANES)
                head_ref[:, at] = grad_pre[0:8]
            terms += by_rows(tap_sums(grad_pre, q * LANES))
            x_gx = x * gx
            end = jnp.sum(x * through, axis=0, keepdims=True) + jnp.exp(tot) * jnp.sum(
                exits.astype(F32) * state.astype(F32), axis=0, keepdims=True
            )
            moved = g * y - x_gx
            moved = jnp.concatenate([moved[: T - 8], moved[T - 8 :] + jnp.where(last, end, 0.0)], axis=0)
            pick = (
                iota((GROUP_HEADS, 2 * LANES), 0)
                == 2 * q + iota((GROUP_HEADS, 2 * LANES), 1) // HEAD_DIM
            ).astype(F32).astype(BF16)
            for part in split_two(moved):
                seg_grad = seg_grad + dot(pick, part, NT)
            for part in split_two(x_gx):
                dt_grad = dt_grad + dot(pick, part, NT)
            if q % 4 == 2:
                size = GROUP_X // 2
                near_at = pl.ds(jj * GROUP_X + (q // 4) * size, size)
                far_at = span(2 * j + q // 4, size)
                save(out_ref.at[:, near_at], out_h.at[:, far_at])
                if theirs:
                    save(pre_ref.at[:, near_at], pre_h.at[:, near_at])
        for grad, base in ((grad_b, 0), (grad_c, 1)):
            at = HALF_X + (base * HALF_GROUPS + jj) * STATE
            tail = slice(GROUP_X + base * STATE, GROUP_X + (base + 1) * STATE)
            far_at = span(WIDTH_X // STATE + base * GROUPS + j, STATE)
            fill_window(win_ref, before_ref[:, far_at], tok_ref[:, tail])
            grad_pre = grad * slope_ref[:, tail]
            pre_ref[:, at : at + STATE] = grad_pre
            if theirs:
                head_ref[:, far_at] = grad_pre[0:8]
                save(pre_ref.at[:, pl.ds(at, STATE)], pre_h.at[:, pl.ds(at, STATE)])
            terms += tap_sums(grad_pre, 0)
        heads = span(j, GROUP_HEADS)
        behind = exact_dot(seg_grad, lower)
        dt = small_ref[pl.ds(pl.multiple_of(ROW_DT + j * GROUP_HEADS, GROUP_HEADS), GROUP_HEADS), :]
        decay = small_ref[pl.ds(pl.multiple_of(ROW_DECAY + j * GROUP_HEADS, GROUP_HEADS), GROUP_HEADS), :]
        near = pl.ds(jj * GROUP_HEADS, GROUP_HEADS)
        step_ref[near, :] = (dt_grad / dt + decay * behind) * sigmoid(raw_ref[heads, :])
        save(step_ref.at[near], step_h.at[heads])
        rows = jj * SUM_GROUP
        sum_ref[rows : rows + SUM_GROUP, :] = jnp.concatenate(terms + skips + [dt * behind * decay], axis=0)
    wait_all(fetches)
    if theirs:
        first_ref[...] = head_ref[0 : TAPS - 1, :].astype(BF16)
    wait_all(saves)


def run_leave(core, state, near, common, far, before_out):
    theirs = before_out is not None
    out = [
        ("h", (T, WIDTH_X), BF16),
        ("h", (HEADS, T), F32),
        ("h" if theirs else "V", (T, HALF_X + HALF_B), F32),
        ("V", (HALF_GROUPS * SUM_GROUP, LANES), F32),
    ]
    scratch = [
        pltpu.VMEM((T, HALF_X), BF16),
        pltpu.VMEM((HALF_GROUPS * GROUP_HEADS, T), F32),
        pltpu.VMEM((8 + T, GROUP_X), F32),
        DMA(2 + HALF_GROUPS, FETCHES),
    ]
    args = [core, state, *near, *common, *far]
    specs = "s" + ("v" if theirs else "V") + "V" * (len(near) + len(COMMON)) + "h" * len(far)
    aliases = {}
    if theirs:
        done, pre_own = before_out
        args += [pre_own]
        aliases = {len(args) + i: i for i in range(2)}
        args += done
        specs += "Vhh"
        out += [("V", (TAPS - 1, CHANNELS), BF16)]
        scratch = [pltpu.VMEM((8, CHANNELS), F32), pltpu.VMEM((T, HALF_X + HALF_B), F32)] + scratch
    else:
        out += NEAR * HALF_GROUPS
    kernel = functools.partial(leave_kernel, theirs)
    outs = call(kernel, "leave", out, specs, 5, scratch, mib=8, aliases=aliases)(*args)
    return outs[:2], outs[2], outs[3], outs[4:]


def spread_kernel(core_ref, own_ref, theirs_h, halo_ref, weight_ref, out_h, theirs_ref, out_ref, win_ref, sems):
    load = start_all([(theirs_h, theirs_ref)], sems.at[pl.ds(8, 1)])
    saves = []
    size = HALF_GROUPS * STATE
    for side, pre_ref in enumerate((own_ref, theirs_ref)):
        half = 1 - core_ref[0] if side else core_ref[0]
        if side:
            wait_all(load)
        blocks = [(jj * GROUP_X, span(half * HALF_GROUPS + jj, GROUP_X), GROUP_X) for jj in range(HALF_GROUPS)]
        blocks += [
            (HALF_X + base * size, span(WIDTH_X // size + 2 * base + half, size), size) for base in range(2)
        ]
        for near, far, width in blocks:
            win_ref[0:T, 0:width] = pre_ref[:, near : near + width]
            win_ref[T : T + TAPS - 1, 0:width] = halo_ref[:, far].astype(F32)
            weights = weight_ref[:, far]
            base = side * (HALF_X + HALF_B) + near
            for lo in range(0, width, LANES):
                at = slice(lo, lo + LANES)
                rows = win_ref[:, at]
                acc = weights[TAPS - 1 : TAPS, at] * rows[:T]
                for k in range(TAPS - 1):
                    acc = acc + weights[k : k + 1, at] * pltpu.roll(rows, T + 8 - (TAPS - 1 - k), 0)[:T]
                out_ref[:, base + lo : base + lo + LANES] = acc.astype(BF16)
            copy = pltpu.make_async_copy(out_ref.at[:, pl.ds(base, width)], out_h.at[:, far], sems.at[len(saves)])
            copy.start()
            saves.append(copy)
    wait_all(saves)


def run_spread(core, own, theirs, halo, weight):
    out = [("h", (T, CHANNELS), BF16)]
    scratch = [
        pltpu.VMEM((T, HALF_X + HALF_B), F32),
        pltpu.VMEM((T, CHANNELS), BF16),
        pltpu.VMEM((T + 8, GROUP_X), F32),
        DMA(9),
    ]
    return call(spread_kernel, "spread", out, "sVhvV", 3, scratch, mib=8)(core, own, theirs, halo, weight)[0]


CONV_ROWS = TAPS * (CHANNELS // LANES)
CONV_GROUP = CONV_ROWS // GROUPS
SEND_ROWS = CONV_ROWS + 16


def write_send(out_ref, conv, thin):
    high = thin.astype(BF16).astype(F32)
    low = thin - high
    row = iota((16, LANES), 0)
    out_ref[0:CONV_ROWS, :] = conv.astype(BF16)
    out_ref[CONV_ROWS:SEND_ROWS, :] = jnp.where(row == 0, high, jnp.where(row == 1, low, 0.0)).astype(BF16)


def read_send(value):
    wide = value.astype(F32)
    return wide[0:CONV_ROWS], wide[CONV_ROWS : CONV_ROWS + 1] + wide[CONV_ROWS + 1 : CONV_ROWS + 2]


def merge_kernel(core_ref, own_ref, own_got_ref, theirs_ref, theirs_got_ref, out_ref):
    thin = jnp.zeros((8, LANES), F32)
    left = iota((8, LANES), 1) < HEAD_DIM
    count = HEADS // 2
    parts = []
    for side, (mine, other) in enumerate(((own_ref, theirs_got_ref), (theirs_ref, own_got_ref))):
        half = 1 - core_ref[0] if side else core_ref[0]
        total = mine[...] + other[...]
        rows, skips, decays = [], [], []
        for jj in range(HALF_GROUPS):
            at = jj * SUM_GROUP
            rows.append(total[at : at + CONV_GROUP])
            skips.append(total[at + CONV_GROUP : at + SUM_GROUP - GROUP_HEADS])
            decays.append(total[at + SUM_GROUP - GROUP_HEADS : at + SUM_GROUP])
        skips = jnp.concatenate(skips, axis=0)
        even = exact_dot(jnp.where(left, 1.0, 0.0), skips, NT)
        odd = exact_dot(jnp.where(left, 0.0, 1.0), skips, NT)
        decay = exact_dot(jnp.ones((8, LANES), F32), jnp.concatenate(decays, axis=0), NT)
        for part, step, shift in ((even, 2, 0), (odd, 2, 1), (decay, 1, HEADS)):
            size = part.shape[1]
            spot = (iota((size, LANES), 1) == step * iota((size, LANES), 0) + shift + half * count).astype(F32)
            thin = thin + exact_dot(part, spot)
        parts.append(jnp.concatenate(rows, axis=0))
    first = core_ref[0] == 0
    conv = jnp.concatenate(
        [jnp.where(first, parts[0], parts[1]), jnp.where(first, parts[1], parts[0])], axis=0
    )
    write_send(out_ref, conv, thin[0:1])


def run_merge(core, own, own_got, theirs, theirs_got):
    out = [("v", (SEND_ROWS, LANES), BF16)]
    return call(merge_kernel, "merge", out, "svvvv", 1, mib=4)(core, own, own_got, theirs, theirs_got)[0]


def ring_sum(core_ref, me_ref, refs, hold_ref):
    count = len(refs)
    sides = (count - 1) // 2
    hold_ref[0] = refs[0][...]
    for k in range(1, sides + 1):
        mine = jnp.where(core_ref[0] == 0, k, count - k)
        hold_ref[mine] = refs[k][...]
        hold_ref[count - mine] = refs[sides + k][...]
    if count % 2 == 0:
        hold_ref[count // 2] = refs[count - 1][...]
    conv, thin = read_send(hold_ref[lax.rem(me_ref[0], count)])
    for k in range(1, count):
        more, little = read_send(hold_ref[lax.rem(me_ref[0] + count - k, count)])
        conv, thin = conv + more, thin + little
    return conv, thin


def fold_kernel(core_ref, me_ref, *rest):
    *refs, out_ref, hold_ref = rest
    write_send(out_ref, *ring_sum(core_ref, me_ref, refs, hold_ref))


def run_fold(core, me, values):
    out = [("v", (SEND_ROWS, LANES), BF16)]
    scratch = [pltpu.VMEM((len(values), SEND_ROWS, LANES), BF16)]
    return call(fold_kernel, "fold", out, "ss" + "v" * len(values), 1, scratch, mib=4)(core, me, *values)[0]


def finish_kernel(core_ref, me_ref, *rest):
    *refs, conv_ref, decay_ref, skip_ref, hold_ref = rest
    conv, thin = ring_sum(core_ref, me_ref, refs, hold_ref)
    for i in range(CHANNELS // LANES):
        if i < PAIRS:
            row = CONV_GROUP * (i // GROUP_PAIRS) + TAPS * (i % GROUP_PAIRS)
        else:
            kind, group = divmod(i - PAIRS, GROUPS)
            row = CONV_GROUP * group + TAPS * (GROUP_PAIRS + kind)
        conv_ref[:, i * LANES : (i + 1) * LANES] = conv[row : row + TAPS]
    skip_ref[...] = thin[:, 0:HEADS]
    decay_ref[...] = thin[:, HEADS:]


def run_finish(core, me, values):
    out = [("v", (TAPS, CHANNELS), F32), ("v", (1, HEADS), F32), ("v", (1, HEADS), F32)]
    scratch = [pltpu.VMEM((len(values), SEND_ROWS, LANES), BF16)]
    return call(finish_kernel, "finish", out, "ss" + "v" * len(values), 1, scratch, mib=4)(core, me, *values)


CTX = ("chip", "core")
ALL = ("dp", "chip", "core")


def all_to_all(value, axis):
    return lax.all_to_all(value, axis, 0, 0, tiled=True)


def tie(*values):
    return lax.optimization_barrier(values)


SIDE = 4


def around(value, axis, size, ring, move):
    def hear(first, second):
        return lax.ppermute(
            value,
            (axis, "core"),
            [(2 * i + side, 2 * move(i, d) + side) for i in range(size) for side, d in enumerate((first, second))],
        )

    middle = [hear(ring // 2, ring // 2)] if ring % 2 == 0 else []
    heard = [hear(k, ring - k) for k in range(1, (ring - 1) // 2 + 1)]
    swapped = [lax.ppermute(part, "core", [(0, 1), (1, 0)]) for part in heard]
    return [value] + heard + swapped + middle


def scalar(value):
    return value.astype(jnp.int32).reshape(1)


def local(conv_input, conv_weight, step_raw, decay_log, skip_gain, cotangent):
    chips = lax.axis_size("chip")
    devices = 2 * chips
    sequences = lax.axis_size("dp")
    tokens = conv_input[0]
    raw = step_raw[0]
    cot = cotangent[0]
    core = lax.axis_index("core").astype(jnp.int32).reshape(1)
    swap = [(0, 1), (1, 0)]
    halo = lax.ppermute(tokens[T - TAPS + 1 :], CTX, [(i, i + 1) for i in range(devices - 1)])
    small, small_near, tot, x0, bc0, head, weight_near, cot_near = run_begin(
        raw, decay_log.reshape(1, HEADS), skip_gain.reshape(1, HEADS), tokens, conv_weight, cot
    )
    other = lax.ppermute(tot, "core", swap)
    x, bc, before, x_near, bc_near, out = run_enter(
        core, x0, bc0, head, halo, weight_near, cot_near, small_near
    )
    got_near = lax.ppermute(out, "core", swap)
    own_near = run_own(core, x_near, bc_near, cot_near, small_near)
    packed, left, right, tots = run_pack(core, own_near, got_near, tot, other)
    heard = all_to_all(packed, "chip")
    y, gbc, skips = run_inner(x, bc, cot, small)
    heard, y, gbc, skips = tie(heard, y, gbc, skips)
    chained = run_chain(chips, heard)
    late, chained = tie(bc, chained)
    back = all_to_all(chained, "chip")
    gx, slope = run_slopes(late, cot, small, tokens, before, conv_weight)
    back, gx, slope = tie(back, gx, slope)
    far = (x, cot, y, gx, slope, tokens, bc, gbc)
    mine, send, near, common = run_unpack(
        core, back, left, right, tots, far, (before, small, raw, skips, conv_weight)
    )
    theirs = lax.ppermute(send, "core", swap)
    half, pre_own, sum_own, near = run_leave(core, mine, near, common, far, None)
    sum_own_got = lax.ppermute(sum_own, "core", swap)
    (out_tokens, grad_step), pre_theirs, sum_theirs, (first,) = run_leave(
        core, theirs, near, common, (), (half, pre_own)
    )
    sum_theirs_got = lax.ppermute(sum_theirs, "core", swap)
    after = lax.ppermute(first, CTX, [(i + 1, i) for i in range(devices - 1)])
    sums = run_merge(core, sum_own, sum_own_got, sum_theirs, sum_theirs_got)
    chip, sequence = lax.axis_index("chip"), lax.axis_index("dp")
    rows = chips // SIDE
    values = around(sums, "chip", chips, SIDE, lambda i, d: i // SIDE * SIDE + (i % SIDE + d) % SIDE)
    grad_tokens = run_spread(core, pre_own, pre_theirs, after, common[4])
    values, grad_tokens = tie(values, grad_tokens)
    sums = run_fold(core, scalar(lax.rem(chip, SIDE)), values)
    values = around(sums, "chip", chips, rows, lambda i, d: (i + d * SIDE) % chips)
    sums = run_fold(core, scalar(lax.div(chip, SIDE)), values)
    near = 2 if sequences % 2 == 0 else 1
    if near > 1:
        values = around(sums, "dp", sequences, near, lambda i, d: i // 2 * 2 + (i % 2 + d) % 2)
        sums = run_fold(core, scalar(lax.rem(sequence, near)), values)
    values = around(sums, "dp", sequences, sequences // near, lambda i, d: (i + d * near) % sequences)
    grad_conv, grad_decay, grad_skip = run_finish(core, scalar(lax.div(sequence, near)), values)
    return (
        out_tokens[None],
        grad_tokens[None],
        grad_step[None],
        grad_conv,
        grad_decay.reshape(HEADS),
        grad_skip.reshape(HEADS),
    )


def solution(mesh):
    dp, ctx = mesh.devices.shape
    fine = Mesh(mesh.devices.reshape(dp, ctx // 2, 2), ALL)
    seq = P("dp", CTX, None)
    rate = P("dp", None, CTX)
    in_specs = (seq, P(), rate, P(), P(), seq)
    out_specs = (seq, seq, rate, P(), P(), P())
    return jax.shard_map(local, mesh=fine, in_specs=in_specs, out_specs=out_specs, check_vma=False)
```

```python
import functools

import jax
import jax.numpy as jnp
from jax import lax
from jax.experimental import pallas as pl
from jax.experimental.pallas import tpu as pltpu
from jax.sharding import Mesh
from jax.sharding import PartitionSpec as P

HEADS = 64
HEAD_DIM = 64
GROUPS = 4
STATE = 128
TAPS = 4
T = 128
LANES = 128
WIDTH_X = HEADS * HEAD_DIM
WIDTH_B = GROUPS * STATE
CHANNELS = WIDTH_X + 2 * WIDTH_B
GROUP_X = WIDTH_X // GROUPS
PAIRS = HEADS // 2
GROUP_PAIRS = PAIRS // GROUPS
GROUP_HEADS = HEADS // GROUPS
HALF_PAIRS = PAIRS // 2
HALF_GROUPS = GROUPS // 2
F32 = jnp.float32
BF16 = jnp.bfloat16
EXACT = lax.Precision.HIGHEST
NN = (((1,), (0,)), ((), ()))
NT = (((1,), (1,)), ((), ()))
SUM_GROUP = 64
PACK_ROWS = 2 * STATE + 16


def dot(a, b, dims=NN):
    return lax.dot_general(a, b, dims, preferred_element_type=F32)


def exact_dot(a, b, dims=NN):
    return lax.dot_general(a, b, dims, precision=EXACT, preferred_element_type=F32)


def iota(shape, dim):
    return lax.broadcasted_iota(jnp.int32, shape, dim)


def sigmoid(v):
    return 0.5 + 0.5 * jnp.tanh(0.5 * v)


def split_two(v):
    high = v.astype(BF16)
    return high, (v - high.astype(F32)).astype(BF16)


def span(index, size):
    return pl.ds(pl.multiple_of(index * size, size), size)


def pin(value, space):
    return pltpu.with_memory_space_constraint(value, space)


def placed(space, shape, dtype):
    return space(shape, dtype)


def call(kernel, name, outs, specs, micros, scratch=(), mib=28, aliases=None):
    cost = pl.CostEstimate(
        flops=int(micros * 1e9), transcendentals=0, bytes_accessed=int(micros * 3.6e6)
    )
    blocks = {
        "s": pl.BlockSpec(memory_space=pltpu.SMEM),
        "v": pl.BlockSpec(memory_space=pltpu.VMEM),
        "V": pl.BlockSpec(memory_space=pltpu.VMEM),
        "h": pl.BlockSpec(memory_space=pltpu.HBM),
    }
    spaces = {"V": pltpu.VMEM, "h": pltpu.HBM}
    shapes = [
        placed(spaces[p], shape, dtype) if p in spaces else jax.ShapeDtypeStruct(shape, dtype)
        for p, shape, dtype in outs
    ]
    run = pl.pallas_call(
        kernel,
        out_shape=shapes,
        in_specs=[blocks[p] for p in specs],
        out_specs=[blocks[p] for p, _, _ in outs],
        scratch_shapes=list(scratch),
        input_output_aliases=aliases or {},
        cost_estimate=cost,
        compiler_params=pltpu.CompilerParams(vmem_limit_bytes=mib << 20),
        name=name,
    )

    def go(*args):
        return run(*[pin(a, spaces[p]) if p in spaces else a for a, p in zip(args, specs, strict=True)])

    return go


def start_all(pairs, sems):
    copies = [pltpu.make_async_copy(a, b, sems.at[i]) for i, (a, b) in enumerate(pairs)]
    for copy in copies:
        copy.start()
    return copies


def wait_all(copies):
    for copy in copies:
        copy.wait()


def DMA(*shape):
    return pltpu.SemaphoreType.DMA(shape)


def fill_window(win_ref, before, tokens):
    width = tokens.shape[1]
    win_ref[0:8, :width] = before
    win_ref[8 : 8 + T, :width] = tokens.astype(F32)


def pre_conv(win_ref, weights, lo):
    cols = slice(lo, lo + LANES)
    rows = win_ref[0 : 8 + T, cols]
    acc = weights[TAPS - 1 : TAPS, cols] * rows[8:]
    for k in range(TAPS - 1):
        acc = acc + weights[k : k + 1, cols] * pltpu.roll(rows, TAPS - 1 - k, 0)[8:]
    return acc


BLOCKS = CHANNELS // GROUP_X


ROW_DT, ROW_SEG, ROW_COLS, ROW_SCALE, ROW_TOT, ROW_SKIP, ROW_DECAY, SMALL_ROWS = (
    0, 64, 128, 256, 384, 416, 448, 512
)


def begin_kernel(raw_h, decay_log_h, skip_gain_h, tok_h, weight_h, g_h,
                 small_h, small_ref, tot_ref, x_ref, bc_ref, head_ref, weight_ref, g_ref,
                 raw_ref, decay_log_ref, skip_gain_ref, wide_ref, hold_ref, win_ref, sems):
    first = start_all(
        [(raw_h, raw_ref), (decay_log_h, decay_log_ref), (skip_gain_h, skip_gain_ref), (weight_h, weight_ref)],
        sems.at[0],
    )
    blocks = [pl.ds(i * GROUP_X, GROUP_X) for i in range(BLOCKS)]
    copies = start_all([(tok_h.at[:, at], hold_ref.at[:, at]) for at in blocks], sems.at[1])
    later = start_all([(g_h, g_ref)], sems.at[2])
    win_ref[0:8, :] = jnp.zeros((8, GROUP_X), F32)
    copies[0].wait()
    diagonal = iota((HEADS, HEADS), 0) == iota((HEADS, HEADS), 1)

    def column(row):
        return jnp.sum(jnp.where(diagonal, row, 0.0), axis=1, keepdims=True)

    wait_all(first)
    raw = raw_ref[...]
    dt = jnp.log1p(jnp.exp(raw))
    decay = -jnp.exp(column(decay_log_ref[...]))
    upper = (iota((T, T), 0) <= iota((T, T), 1)).astype(F32)
    seg = exact_dot(dt * decay, upper)
    total = seg[:, T - 1 : T]
    small_ref[ROW_DT : ROW_DT + HEADS] = dt
    small_ref[ROW_SEG : ROW_SEG + HEADS] = seg
    small_ref[ROW_COLS : ROW_COLS + T] = jnp.transpose(jnp.concatenate([seg, dt], axis=0))
    small_ref[ROW_SCALE : ROW_SCALE + T] = jnp.transpose(
        jnp.concatenate([jnp.exp(seg), jnp.exp(total - seg) * dt], axis=0)
    )
    left = iota((PAIRS, LANES), 1) < HEAD_DIM

    def paired(col):
        wide_ref[...] = jnp.broadcast_to(col, (HEADS, LANES))
        return jnp.where(left, wide_ref[pl.ds(0, PAIRS, 2), :], wide_ref[pl.ds(1, PAIRS, 2), :])

    tot = paired(total)
    tot_ref[...] = tot
    small_ref[ROW_TOT : ROW_TOT + PAIRS] = tot
    small_ref[ROW_SKIP : ROW_SKIP + PAIRS] = paired(column(skip_gain_ref[...]))
    small_ref[ROW_DECAY : ROW_DECAY + HEADS] = jnp.broadcast_to(decay, (HEADS, LANES))
    save = start_all([(small_ref, small_h)], sems.at[0])
    for i in range(BLOCKS):
        if i:
            copies[i].wait()
        cols = slice(i * GROUP_X, (i + 1) * GROUP_X)
        win_ref[8 : 8 + T, :] = hold_ref[:, cols].astype(F32)
        for lo in range(0, GROUP_X, LANES):
            at = i * GROUP_X + lo
            pre = pre_conv(win_ref, weight_ref[:, cols], lo)
            mixed = (pre * sigmoid(pre)).astype(BF16)
            head_ref[:, at : at + LANES] = pre[0:8]
            if at < WIDTH_X:
                x_ref[:, at : at + LANES] = mixed
            else:
                bc_ref[:, at - WIDTH_X : at - WIDTH_X + LANES] = mixed
    wait_all(save + later)


def run_begin(raw, decay_log, skip_gain, tokens, weight, cot):
    out = [
        ("h", (SMALL_ROWS, LANES), F32),
        ("V", (SMALL_ROWS, LANES), F32),
        ("V", (PAIRS, LANES), F32),
        ("V", (T, WIDTH_X), BF16),
        ("V", (T, 2 * WIDTH_B), BF16),
        ("V", (8, CHANNELS), F32),
        ("V", (TAPS, CHANNELS), F32),
        ("V", (T, WIDTH_X), BF16),
    ]
    scratch = [
        pltpu.VMEM((HEADS, T), F32),
        pltpu.VMEM((1, HEADS), F32),
        pltpu.VMEM((1, HEADS), F32),
        pltpu.VMEM((HEADS, LANES), F32),
        pltpu.VMEM((T, CHANNELS), BF16),
        pltpu.VMEM((8 + T, GROUP_X), F32),
        DMA(3, BLOCKS),
    ]
    return call(begin_kernel, "begin", out, "hhhhhh", 4, scratch, mib=8)(
        raw, decay_log, skip_gain, tokens, weight, cot
    )


def rolled(cols, group):
    return pltpu.roll(cols, (LANES - group * GROUP_HEADS) % LANES, 1)


def widen(cols, base, pair):
    first = iota((T, LANES), 1) < HEAD_DIM
    at = base + 2 * pair
    return jnp.where(first, cols[:, at : at + 1], cols[:, at + 1 : at + 2])


def widen_two(cols, base, pair):
    return jnp.concatenate([widen(cols, base, pair), widen(cols, base, pair + 1)], axis=1)


def fill_half(half, x_ref, bc_ref, g_ref, scale, dst_ref):
    for jj in range(HALF_GROUPS):
        j = half * HALF_GROUPS + jj
        b_flip = jnp.transpose(bc_ref[:, span(j, STATE)].astype(F32)).astype(BF16)
        c_flip = jnp.transpose(bc_ref[:, span(GROUPS + j, STATE)].astype(F32)).astype(BF16)
        cols = rolled(scale, j)
        for q in range(0, GROUP_PAIRS, 2):
            lanes = pl.ds(pl.multiple_of(j * GROUP_X + q * LANES, 2 * LANES), 2 * LANES)
            xw = (x_ref[:, lanes].astype(F32) * widen_two(cols, HEADS, q)).astype(BF16)
            gw = (g_ref[:, lanes].astype(F32) * widen_two(cols, 0, q)).astype(BF16)
            state = dot(b_flip, xw).astype(BF16)
            grad = dot(c_flip, gw).astype(BF16)
            for k in range(2):
                at = jj * GROUP_PAIRS + q + k
                dst_ref[0, at] = state[:, k * LANES : (k + 1) * LANES]
                dst_ref[1, at] = grad[:, k * LANES : (k + 1) * LANES]


def enter_kernel(core_ref, x0_ref, bc0_ref, head_ref, halo_ref, weight_ref, g_ref, small_ref,
                 x_h, bc_h, before_h, x_ref, bc_ref, out_ref, before_ref, sems):
    half = 1 - core_ref[0]
    row = iota((8, GROUP_X), 0)
    for i in range(BLOCKS):
        cols = slice(i * GROUP_X, (i + 1) * GROUP_X)
        halo = halo_ref[:, cols].astype(F32)
        weight = weight_ref[:, cols]
        pre = head_ref[:, cols]
        before = jnp.zeros((8, GROUP_X), F32)
        for t in range(TAPS - 1):
            extra = jnp.zeros((1, GROUP_X), F32)
            for k in range(TAPS - 1 - t):
                extra = extra + weight[k : k + 1] * halo[t + k : t + k + 1]
            pre = pre + jnp.where(row == t, extra, 0.0)
            before = before + jnp.where(row == t + 5, halo[t : t + 1], 0.0)
        before_ref[:, cols] = before
        fixed = pre * sigmoid(pre)
        src, dst, at = (x0_ref, x_ref, cols) if i < GROUPS else (bc0_ref, bc_ref, slice(0, GROUP_X))
        rest = src[0:16, at].astype(F32)
        dst[16:T, at] = src[16:T, at]
        dst[0:16, at] = jnp.concatenate([fixed, rest[8:16]], axis=0).astype(BF16)
    saves = start_all([(x_ref, x_h), (bc_ref, bc_h), (before_ref, before_h)], sems)
    fill_half(half, x_ref, bc_ref, g_ref, small_ref[ROW_SCALE : ROW_SCALE + T], out_ref)
    wait_all(saves)


def run_enter(core, x0, bc0, head, halo, weight, cot, small):
    out = [
        ("h", (T, WIDTH_X), BF16),
        ("h", (T, 2 * WIDTH_B), BF16),
        ("h", (8, CHANNELS), F32),
        ("V", (T, WIDTH_X), BF16),
        ("V", (T, 2 * WIDTH_B), BF16),
        ("V", (2, HALF_PAIRS, STATE, LANES), BF16),
    ]
    scratch = [pltpu.VMEM((8, CHANNELS), F32), DMA(3)]
    return call(enter_kernel, "enter", out, "sVVVvVVV", 3, scratch, mib=6)(
        core, x0, bc0, head, halo, weight, cot, small
    )


def own_kernel(core_ref, x_ref, bc_ref, g_ref, small_ref, own_ref):
    fill_half(core_ref[0], x_ref, bc_ref, g_ref, small_ref[ROW_SCALE : ROW_SCALE + T], own_ref)


def run_own(core, x, bc, cot, small):
    out = [("V", (2, HALF_PAIRS, STATE, LANES), BF16)]
    return call(own_kernel, "own", out, "sVVVV", 3, mib=6)(core, x, bc, cot, small)[0]


STEP_PAIRS = 4
STEPS = HALF_PAIRS // STEP_PAIRS


def pack_kernel(core_ref, own_ref, got_ref, tot_ref, other_ref,
                out_h, left_h, right_h, tots_h, out_ref, sems):
    saves = start_all(
        [(tot_ref, tots_h.at[pl.ds(0, PAIRS)]), (other_ref, tots_h.at[pl.ds(PAIRS, PAIRS)])], sems.at[0]
    )
    second = core_ref[0] == 1

    def keep(first_ref, last_ref):
        return [
            pltpu.make_async_copy(first_ref.at[0], left_h, sems.at[0, 2]),
            pltpu.make_async_copy(last_ref.at[1], right_h, sems.at[0, 3]),
        ]

    @pl.when(second)
    def _():
        for copy in keep(got_ref, own_ref):
            copy.start()

    @pl.when(jnp.logical_not(second))
    def _():
        for copy in keep(own_ref, got_ref):
            copy.start()

    saves += keep(own_ref, got_ref)
    outs = []
    for i in range(HALF_PAIRS):
        at = core_ref[0] * HALF_PAIRS + i
        tot = tot_ref[pl.ds(at, 1), :]
        other = other_ref[pl.ds(at, 1), :]
        one = jnp.ones_like(tot)
        by_own = jnp.exp(tot)
        by_other = jnp.exp(other)
        state = (
            jnp.where(second, one, by_other) * own_ref[0, i].astype(F32)
            + jnp.where(second, by_own, one) * got_ref[0, i].astype(F32)
        )
        grad = (
            jnp.where(second, by_other, one) * own_ref[1, i].astype(F32)
            + jnp.where(second, one, by_own) * got_ref[1, i].astype(F32)
        )
        out_ref[i, 0:STATE, :] = state.astype(BF16)
        out_ref[i, STATE : 2 * STATE, :] = grad.astype(BF16)
        both = tot + other
        high = both.astype(BF16).astype(F32)
        mid = (both - high).astype(BF16).astype(F32)
        low = both - high - mid
        row = iota((16, LANES), 0)
        wide = jnp.where(row == 0, high, jnp.where(row == 1, mid, jnp.where(row == 2, low, 0.0)))
        out_ref[i, 2 * STATE : PACK_ROWS, :] = wide.astype(BF16)
        if i % STEP_PAIRS == STEP_PAIRS - 1:
            done = pl.ds(i + 1 - STEP_PAIRS, STEP_PAIRS)
            copy = pltpu.make_async_copy(out_ref.at[done], out_h.at[done], sems.at[1, i // STEP_PAIRS])
            copy.start()
            outs.append(copy)
    wait_all(outs + saves)


def run_pack(core, own, got, tot, other):
    half = (HALF_PAIRS, STATE, LANES)
    packed = (HALF_PAIRS, PACK_ROWS, LANES)
    out = [("h", packed, BF16), ("h", half, BF16), ("h", half, BF16), ("h", (2 * PAIRS, LANES), F32)]
    scratch = [pltpu.VMEM(packed, BF16), DMA(2, STEPS)]
    return call(pack_kernel, "pack", out, "sVvVv", 2, scratch, mib=8)(core, own, got, tot, other)


def chain_kernel(chips, per, in_ref, out_ref):
    for q in range(per):
        def decay(k):
            rows = in_ref[k * per + q, 2 * STATE : PACK_ROWS, :].astype(F32)
            return jnp.exp(rows[0:1] + rows[1:2] + rows[2:3])

        carry = jnp.zeros((STATE, LANES), F32)
        for k in range(chips):
            out_ref[k * per + q, 0:STATE, :] = carry.astype(BF16)
            if k < chips - 1:
                carry = decay(k) * carry + in_ref[k * per + q, 0:STATE, :].astype(F32)
        carry = jnp.zeros((STATE, LANES), F32)
        for k in reversed(range(chips)):
            out_ref[k * per + q, STATE : 2 * STATE, :] = carry.astype(BF16)
            if k > 0:
                carry = decay(k) * carry + in_ref[k * per + q, STATE : 2 * STATE, :].astype(F32)


def run_chain(chips, packed):
    kernel = functools.partial(chain_kernel, chips, HALF_PAIRS // chips)
    out = [("v", (HALF_PAIRS, 2 * STATE, LANES), BF16)]
    return call(kernel, "chain", out, "v", 1, mib=8)(packed)[0]


HALF_X = HALF_GROUPS * GROUP_X
HALF_B = 2 * HALF_GROUPS * STATE

NEAR = [
    ("V", (T, GROUP_X), BF16),
    ("V", (T, GROUP_X), BF16),
    ("V", (T, GROUP_X), F32),
    ("V", (T, GROUP_X), F32),
    ("V", (T, GROUP_X + 2 * STATE), F32),
    ("V", (T, GROUP_X + 2 * STATE), BF16),
    ("V", (T, 2 * STATE), BF16),
    ("V", (T, 2 * STATE), F32),
]
COMMON = [
    ("V", (8, CHANNELS), F32),
    ("V", (SMALL_ROWS, LANES), F32),
    ("V", (HEADS, T), F32),
    ("V", (PAIRS, LANES), F32),
    ("V", (TAPS, CHANNELS), F32),
]
FETCHES = 6 + 8


def fetch_group(j, far, near, sems):
    x_h, g_h, y_h, gx_h, slope_h, tok_h, bc_h, gbc_h = far
    x_v, g_v, y_v, gx_v, slope_v, tok_v, bc_v, gbc_v = near
    wide = pl.ds(0, GROUP_X)
    pairs = [
        (a.at[:, span(j, GROUP_X)], b.at[:, wide])
        for a, b in ((x_h, x_v), (g_h, g_v), (y_h, y_v), (gx_h, gx_v), (slope_h, slope_v), (tok_h, tok_v))
    ]
    for base in range(2):
        at = span(base * GROUPS + j, STATE)
        off = span(WIDTH_X // STATE + base * GROUPS + j, STATE)
        thin = pl.ds(base * STATE, STATE)
        tail = pl.ds(GROUP_X + base * STATE, STATE)
        pairs += [
            (bc_h.at[:, at], bc_v.at[:, thin]),
            (gbc_h.at[:, at], gbc_v.at[:, thin]),
            (slope_h.at[:, off], slope_v.at[:, tail]),
            (tok_h.at[:, off], tok_v.at[:, tail]),
        ]
    return start_all(pairs, sems)


def unpack_kernel(core_ref, back_ref, left_h, right_h, tots_h, *rest):
    far, rest = rest[: len(NEAR)], rest[len(NEAR) :]
    common_far, rest = rest[: len(COMMON)], rest[len(COMMON) :]
    mine_ref, send_ref, *rest = rest
    near = [rest[i * len(NEAR) : (i + 1) * len(NEAR)] for i in range(HALF_GROUPS)]
    rest = rest[HALF_GROUPS * len(NEAR) :]
    common, rest = rest[: len(COMMON)], rest[len(COMMON) :]
    left_ref, right_ref, tots_ref, sems, fetch_sems = rest
    first = start_all([(tots_h, tots_ref)], sems.at[STEPS])
    steps = []
    for step in range(STEPS):
        at = pl.ds(step * STEP_PAIRS, STEP_PAIRS)
        steps.append(
            start_all([(left_h.at[at], left_ref.at[at]), (right_h.at[at], right_ref.at[at])], sems.at[step])
        )
    fetches = start_all(list(zip(common_far, common)), fetch_sems.at[HALF_GROUPS])
    for jj in range(HALF_GROUPS):
        fetches += fetch_group(core_ref[0] * HALF_GROUPS + jj, far, near[jj], fetch_sems.at[jj])
    wait_all(first)
    second = core_ref[0] == 1
    for i in range(HALF_PAIRS):
        if i % STEP_PAIRS == 0:
            wait_all(steps[i // STEP_PAIRS])
        at = core_ref[0] * HALF_PAIRS + i
        tot = tots_ref[pl.ds(at, 1), :]
        other = tots_ref[pl.ds(PAIRS + at, 1), :]
        decay_zero = jnp.exp(jnp.where(second, other, tot))
        decay_one = jnp.exp(jnp.where(second, tot, other))
        state_zero = back_ref[i, 0:STATE, :].astype(F32)
        grad_one = back_ref[i, STATE : 2 * STATE, :].astype(F32)
        state_one = decay_zero * state_zero + left_ref[i].astype(F32)
        grad_zero = decay_one * grad_one + right_ref[i].astype(F32)
        mine_ref[0, i] = jnp.where(second, state_one, state_zero).astype(BF16)
        mine_ref[1, i] = jnp.where(second, grad_one, grad_zero).astype(BF16)
        send_ref[0, i] = jnp.where(second, state_zero, state_one).astype(BF16)
        send_ref[1, i] = jnp.where(second, grad_zero, grad_one).astype(BF16)
    wait_all(fetches)


def run_unpack(core, back, left, right, tots, far, common):
    half = (2, HALF_PAIRS, STATE, LANES)
    out = [("V", half, BF16)] * 2 + NEAR * HALF_GROUPS + COMMON
    scratch = [
        pltpu.VMEM(half[1:], BF16),
        pltpu.VMEM(half[1:], BF16),
        pltpu.VMEM((2 * PAIRS, LANES), F32),
        DMA(STEPS + 1, 2),
        DMA(HALF_GROUPS + 1, FETCHES),
    ]
    specs = "svhhh" + "h" * (len(NEAR) + len(COMMON))
    outs = call(unpack_kernel, "unpack", out, specs, 3, scratch, mib=8)(
        core, back, left, right, tots, *far, *common
    )
    at = 2 + HALF_GROUPS * len(NEAR)
    return outs[0], outs[1], outs[2:at], outs[at:]


def by_lane_half(v):
    first = iota(v.shape, 1) < HEAD_DIM
    wide = v.astype(F32)
    return jnp.concatenate(
        [jnp.where(first, wide, 0.0).astype(BF16), jnp.where(first, 0.0, wide).astype(BF16)], axis=0
    )


def inner_kernel(x_h, bc_h, g_h, small_h, y_h, gbc_h, skips_h,
                 x_ref, bc_ref, g_ref, small_ref, y_ref, gbc_ref, skips_ref, sems):
    first = start_all([(bc_h, bc_ref), (small_h, small_ref)], sems.at[0])

    def loads(j):
        at = span(j, GROUP_X)
        return [
            pltpu.make_async_copy(x_h.at[:, at], x_ref.at[:, at], sems.at[1, j]),
            pltpu.make_async_copy(g_h.at[:, at], g_ref.at[:, at], sems.at[2, j]),
        ]

    def store(j):
        at = span(j, GROUP_X)
        return pltpu.make_async_copy(y_ref.at[:, at], y_h.at[:, at], sems.at[3, j])

    for j in range(GROUPS):
        for copy in loads(j):
            copy.start()
    wait_all(first)
    lower = iota((T, T), 0) >= iota((T, T), 1)

    @pl.loop(0, GROUPS)
    def _(j):
        wait_all(loads(j))
        b = bc_ref[:, span(j, STATE)]
        c = bc_ref[:, span(GROUPS + j, STATE)]
        seg = small_ref[pl.ds(pl.multiple_of(ROW_SEG + j * GROUP_HEADS, GROUP_HEADS), GROUP_HEADS), :]
        dt = small_ref[pl.ds(pl.multiple_of(ROW_DT + j * GROUP_HEADS, GROUP_HEADS), GROUP_HEADS), :]
        scores = dot(c, b, NT)
        cols = rolled(small_ref[ROW_COLS : ROW_COLS + T], j)
        total = jnp.zeros((T, T), F32)
        skips = []
        for i in range(GROUP_PAIRS):
            lanes = pl.ds(pl.multiple_of(j * GROUP_X + i * LANES, LANES), LANES)
            x = x_ref[:, lanes]
            g = g_ref[:, lanes]
            skips.append(jnp.sum(g.astype(F32) * x.astype(F32), axis=0, keepdims=True))
            inner = dot(by_lane_half(g), x, NT)
            weights = []
            for k in range(2):
                h = 2 * i + k
                spread = cols[:, h : h + 1] - seg[h : h + 1, :]
                kernel = jnp.exp(jnp.where(lower, spread, -1e30)) * dt[h : h + 1, :]
                total = total + kernel * inner[k * T : (k + 1) * T]
                weights.append((kernel * scores).astype(BF16))
            y_ref[:, lanes] = dot(jnp.concatenate(weights, axis=1), by_lane_half(x))
        skips_ref[span(j, GROUP_PAIRS), :] = jnp.concatenate(skips, axis=0)
        gbc_ref[:, span(GROUPS + j, STATE)] = dot(total.astype(BF16), b)
        gbc_ref[:, span(j, STATE)] = dot(jnp.transpose(total).astype(BF16), c)
        store(j).start()

    last = start_all([(gbc_ref, gbc_h), (skips_ref, skips_h)], sems.at[0])
    for j in range(GROUPS):
        store(j).wait()
    wait_all(last)


def run_inner(x, bc, cot, small):
    out = [("h", (T, WIDTH_X), F32), ("h", (T, 2 * WIDTH_B), F32), ("h", (PAIRS, LANES), F32)]
    scratch = [
        pltpu.VMEM((T, WIDTH_X), BF16),
        pltpu.VMEM((T, 2 * WIDTH_B), BF16),
        pltpu.VMEM((T, WIDTH_X), BF16),
        pltpu.VMEM((SMALL_ROWS, LANES), F32),
        pltpu.VMEM((T, WIDTH_X), F32),
        pltpu.VMEM((T, 2 * WIDTH_B), F32),
        pltpu.VMEM((PAIRS, LANES), F32),
        DMA(4, GROUPS),
    ]
    return call(inner_kernel, "inner", out, "hhhh", 4, scratch, mib=16)(x, bc, cot, small)


def slopes_kernel(bc_h, g_h, small_h, tok_h, before_h, weight_h, gx_h, slope_h,
                  bc_ref, g_ref, small_ref, tok_ref, before_ref, weight_ref, gx_ref, slope_ref, win_ref, sems):
    first = start_all(
        [(bc_h, bc_ref), (small_h, small_ref), (before_h, before_ref), (weight_h, weight_ref), (tok_h, tok_ref)],
        sems.at[0],
    )

    def load(j):
        at = span(j, GROUP_X)
        return pltpu.make_async_copy(g_h.at[:, at], g_ref.at[:, at], sems.at[1, j])

    def store(j):
        at = span(j, GROUP_X)
        return pltpu.make_async_copy(gx_ref.at[:, at], gx_h.at[:, at], sems.at[2, j])

    def store_slope(i):
        at = span(i, GROUP_X)
        return pltpu.make_async_copy(slope_ref.at[:, at], slope_h.at[:, at], sems.at[3, i])

    for j in range(GROUPS):
        load(j).start()
    wait_all(first)
    upper = iota((T, T), 0) <= iota((T, T), 1)

    @pl.loop(0, GROUPS)
    def _(j):
        load(j).wait()
        b = bc_ref[:, span(j, STATE)]
        c = bc_ref[:, span(GROUPS + j, STATE)]
        seg = small_ref[pl.ds(pl.multiple_of(ROW_SEG + j * GROUP_HEADS, GROUP_HEADS), GROUP_HEADS), :]
        scores = jnp.transpose(dot(c, b, NT))
        cols = rolled(small_ref[ROW_COLS : ROW_COLS + T], j)
        for i in range(GROUP_PAIRS):
            lanes = pl.ds(pl.multiple_of(j * GROUP_X + i * LANES, LANES), LANES)
            weights = []
            for k in range(2):
                h = 2 * i + k
                spread = seg[h : h + 1, :] - cols[:, h : h + 1]
                kernel = jnp.exp(jnp.where(upper, spread, -1e30)) * cols[:, HEADS + h : HEADS + h + 1]
                weights.append((kernel * scores).astype(BF16))
            gx_ref[:, lanes] = dot(jnp.concatenate(weights, axis=1), by_lane_half(g_ref[:, lanes]))
        store(j).start()

    @pl.loop(0, BLOCKS)
    def _(i):
        cols = span(i, GROUP_X)
        fill_window(win_ref, before_ref[:, cols], tok_ref[:, cols])
        weights = weight_ref[:, cols]
        for lo in range(0, GROUP_X, LANES):
            pre = pre_conv(win_ref, weights, lo)
            s = sigmoid(pre)
            at = pl.ds(pl.multiple_of(i * GROUP_X + lo, LANES), LANES)
            slope_ref[:, at] = s * (1.0 + pre * (1.0 - s))
        store_slope(i).start()

    for j in range(GROUPS):
        store(j).wait()
    for i in range(BLOCKS):
        store_slope(i).wait()


def run_slopes(bc, cot, small, tokens, before, weight):
    out = [("h", (T, WIDTH_X), F32), ("h", (T, CHANNELS), F32)]
    scratch = [
        pltpu.VMEM((T, 2 * WIDTH_B), BF16),
        pltpu.VMEM((T, WIDTH_X), BF16),
        pltpu.VMEM((SMALL_ROWS, LANES), F32),
        pltpu.VMEM((T, CHANNELS), BF16),
        pltpu.VMEM((8, CHANNELS), F32),
        pltpu.VMEM((TAPS, CHANNELS), F32),
        pltpu.VMEM((T, WIDTH_X), F32),
        pltpu.VMEM((T, CHANNELS), F32),
        pltpu.VMEM((8 + T, GROUP_X), F32),
        DMA(4, BLOCKS),
    ]
    return call(slopes_kernel, "slopes", out, "hhhhhh", 6, scratch, mib=16)(
        bc, cot, small, tokens, before, weight
    )


def leave_kernel(theirs, core_ref, state_ref, *rest):
    rest = list(rest)

    def take(count):
        taken = rest[:count]
        del rest[:count]
        return taken

    sets = [take(len(NEAR)) for _ in range(HALF_GROUPS)]
    before_ref, small_ref, raw_ref, skips_ref, _ = take(len(COMMON))
    half = 1 - core_ref[0] if theirs else core_ref[0]
    fetches = []
    if theirs:
        pre_own_ref, _, _ = take(3)
        out_h, step_h, pre_h, sum_ref, first_ref = take(5)
        head_ref, pre_ref, out_ref, step_ref, win_ref, sems = rest
        own = core_ref[0]
        head_ref[:, span(own, HALF_X)] = pre_own_ref[0:8, 0:HALF_X]
        size = HALF_GROUPS * STATE
        for base in range(2):
            at = HALF_X + base * size
            head_ref[:, span(WIDTH_X // size + 2 * base + own, size)] = pre_own_ref[0:8, at : at + size]
    else:
        far = take(len(NEAR))
        out_h, step_h, pre_ref, sum_ref = take(4)
        after = [take(len(NEAR)) for _ in range(HALF_GROUPS)]
        out_ref, step_ref, win_ref, sems = rest
        for jj in range(HALF_GROUPS):
            fetches += fetch_group((1 - half) * HALF_GROUPS + jj, far, after[jj], sems.at[2 + jj])
    last = iota((8, 2 * LANES), 0) == 7
    lower = (iota((T, T), 0) >= iota((T, T), 1)).astype(F32)

    def tap_sums(grad_pre, lo):
        rows = win_ref[0 : 8 + T, lo : lo + grad_pre.shape[1]]
        moved = [pltpu.roll(rows, TAPS - 1 - k, 0)[8:] for k in range(TAPS - 1)] + [rows[8:]]
        return [jnp.sum(grad_pre * part, axis=0, keepdims=True) for part in moved]

    def by_rows(sums):
        return [s[:, lo : lo + LANES] for lo in range(0, sums[0].shape[1], LANES) for s in sums]

    saves = []

    def save(src, dst):
        copy = pltpu.make_async_copy(src, dst, sems.at[len(saves) // 8, len(saves) % 8])
        copy.start()
        saves.append(copy)

    for jj in range(HALF_GROUPS):
        j = half * HALF_GROUPS + jj
        x_ref, g_ref, y_ref, gx_ref, slope_ref, tok_ref, bc_ref, gbc_ref = sets[jj]
        b = bc_ref[:, 0:STATE]
        c = bc_ref[:, STATE:]
        grad_b = gbc_ref[:, 0:STATE]
        grad_c = gbc_ref[:, STATE:]
        cols = rolled(small_ref[ROW_SCALE : ROW_SCALE + T], j)
        skip_rows = small_ref[pl.ds(pl.multiple_of(ROW_SKIP + j * GROUP_PAIRS, GROUP_PAIRS), GROUP_PAIRS), :]
        tot_rows = small_ref[pl.ds(pl.multiple_of(ROW_TOT + j * GROUP_PAIRS, GROUP_PAIRS), GROUP_PAIRS), :]
        seg_grad = jnp.zeros((GROUP_HEADS, T), F32)
        dt_grad = jnp.zeros((GROUP_HEADS, T), F32)
        skips = [skips_ref[span(j, GROUP_PAIRS), :]]
        terms = []
        fill_window(win_ref, before_ref[:, span(j, GROUP_X)], tok_ref[:, 0:GROUP_X])
        for q in range(0, GROUP_PAIRS, 2):
            lanes = slice(q * LANES, (q + 2) * LANES)
            wide = slice(jj * GROUP_X + q * LANES, jj * GROUP_X + (q + 2) * LANES)
            rise = widen_two(cols, 0, q)
            keep = widen_two(cols, HEADS, q)
            at = jj * GROUP_PAIRS + q
            state = jnp.concatenate([state_ref[0, at], state_ref[0, at + 1]], axis=1)
            exits = jnp.concatenate([state_ref[1, at], state_ref[1, at + 1]], axis=1)
            skip = jnp.concatenate([skip_rows[q : q + 1], skip_rows[q + 1 : q + 2]], axis=1)
            tot = jnp.concatenate([tot_rows[q : q + 1], tot_rows[q + 1 : q + 2]], axis=1)
            x = x_ref[:, lanes].astype(F32)
            g = g_ref[:, lanes].astype(F32)
            y = y_ref[:, lanes] + rise * dot(c, state)
            through = keep * dot(b, exits)
            gx = gx_ref[:, lanes] + through
            grad_c = grad_c + dot((g * rise).astype(BF16), state, NT)
            grad_b = grad_b + dot((x * keep).astype(BF16), exits, NT)
            out_ref[:, wide] = (y + skip * x).astype(BF16)
            grad_pre = (gx + skip * g) * slope_ref[:, lanes]
            pre_ref[:, wide] = grad_pre
            if theirs:
                at = pl.ds(pl.multiple_of(j * GROUP_X + q * LANES, 2 * LANES), 2 * LANES)
                head_ref[:, at] = grad_pre[0:8]
            terms += by_rows(tap_sums(grad_pre, q * LANES))
            x_gx = x * gx
            end = jnp.sum(x * through, axis=0, keepdims=True) + jnp.exp(tot) * jnp.sum(
                exits.astype(F32) * state.astype(F32), axis=0, keepdims=True
            )
            moved = g * y - x_gx
            moved = jnp.concatenate([moved[: T - 8], moved[T - 8 :] + jnp.where(last, end, 0.0)], axis=0)
            pick = (
                iota((GROUP_HEADS, 2 * LANES), 0)
                == 2 * q + iota((GROUP_HEADS, 2 * LANES), 1) // HEAD_DIM
            ).astype(F32).astype(BF16)
            for part in split_two(moved):
                seg_grad = seg_grad + dot(pick, part, NT)
            for part in split_two(x_gx):
                dt_grad = dt_grad + dot(pick, part, NT)
            if q % 4 == 2:
                size = GROUP_X // 2
                near_at = pl.ds(jj * GROUP_X + (q // 4) * size, size)
                far_at = span(2 * j + q // 4, size)
                save(out_ref.at[:, near_at], out_h.at[:, far_at])
                if theirs:
                    save(pre_ref.at[:, near_at], pre_h.at[:, near_at])
        for grad, base in ((grad_b, 0), (grad_c, 1)):
            at = HALF_X + (base * HALF_GROUPS + jj) * STATE
            tail = slice(GROUP_X + base * STATE, GROUP_X + (base + 1) * STATE)
            far_at = span(WIDTH_X // STATE + base * GROUPS + j, STATE)
            fill_window(win_ref, before_ref[:, far_at], tok_ref[:, tail])
            grad_pre = grad * slope_ref[:, tail]
            pre_ref[:, at : at + STATE] = grad_pre
            if theirs:
                head_ref[:, far_at] = grad_pre[0:8]
                save(pre_ref.at[:, pl.ds(at, STATE)], pre_h.at[:, pl.ds(at, STATE)])
            terms += tap_sums(grad_pre, 0)
        heads = span(j, GROUP_HEADS)
        behind = exact_dot(seg_grad, lower)
        dt = small_ref[pl.ds(pl.multiple_of(ROW_DT + j * GROUP_HEADS, GROUP_HEADS), GROUP_HEADS), :]
        decay = small_ref[pl.ds(pl.multiple_of(ROW_DECAY + j * GROUP_HEADS, GROUP_HEADS), GROUP_HEADS), :]
        near = pl.ds(jj * GROUP_HEADS, GROUP_HEADS)
        step_ref[near, :] = (dt_grad / dt + decay * behind) * sigmoid(raw_ref[heads, :])
        save(step_ref.at[near], step_h.at[heads])
        rows = jj * SUM_GROUP
        sum_ref[rows : rows + SUM_GROUP, :] = jnp.concatenate(terms + skips + [dt * behind * decay], axis=0)
    wait_all(fetches)
    if theirs:
        first_ref[...] = head_ref[0 : TAPS - 1, :].astype(BF16)
    wait_all(saves)


def run_leave(core, state, near, common, far, before_out):
    theirs = before_out is not None
    out = [
        ("h", (T, WIDTH_X), BF16),
        ("h", (HEADS, T), F32),
        ("h" if theirs else "V", (T, HALF_X + HALF_B), F32),
        ("V", (HALF_GROUPS * SUM_GROUP, LANES), F32),
    ]
    scratch = [
        pltpu.VMEM((T, HALF_X), BF16),
        pltpu.VMEM((HALF_GROUPS * GROUP_HEADS, T), F32),
        pltpu.VMEM((8 + T, GROUP_X), F32),
        DMA(2 + HALF_GROUPS, FETCHES),
    ]
    args = [core, state, *near, *common, *far]
    specs = "s" + ("v" if theirs else "V") + "V" * (len(near) + len(COMMON)) + "h" * len(far)
    aliases = {}
    if theirs:
        done, pre_own = before_out
        args += [pre_own]
        aliases = {len(args) + i: i for i in range(2)}
        args += done
        specs += "Vhh"
        out += [("V", (TAPS - 1, CHANNELS), BF16)]
        scratch = [pltpu.VMEM((8, CHANNELS), F32), pltpu.VMEM((T, HALF_X + HALF_B), F32)] + scratch
    else:
        out += NEAR * HALF_GROUPS
    kernel = functools.partial(leave_kernel, theirs)
    outs = call(kernel, "leave", out, specs, 5, scratch, mib=8, aliases=aliases)(*args)
    return outs[:2], outs[2], outs[3], outs[4:]


def spread_kernel(core_ref, own_ref, theirs_h, halo_ref, weight_ref, out_h, theirs_ref, out_ref, win_ref, sems):
    load = start_all([(theirs_h, theirs_ref)], sems.at[pl.ds(8, 1)])
    saves = []
    size = HALF_GROUPS * STATE
    for side, pre_ref in enumerate((own_ref, theirs_ref)):
        half = 1 - core_ref[0] if side else core_ref[0]
        if side:
            wait_all(load)
        blocks = [(jj * GROUP_X, span(half * HALF_GROUPS + jj, GROUP_X), GROUP_X) for jj in range(HALF_GROUPS)]
        blocks += [
            (HALF_X + base * size, span(WIDTH_X // size + 2 * base + half, size), size) for base in range(2)
        ]
        for near, far, width in blocks:
            win_ref[0:T, 0:width] = pre_ref[:, near : near + width]
            win_ref[T : T + TAPS - 1, 0:width] = halo_ref[:, far].astype(F32)
            weights = weight_ref[:, far]
            base = side * (HALF_X + HALF_B) + near
            for lo in range(0, width, LANES):
                at = slice(lo, lo + LANES)
                rows = win_ref[:, at]
                acc = weights[TAPS - 1 : TAPS, at] * rows[:T]
                for k in range(TAPS - 1):
                    acc = acc + weights[k : k + 1, at] * pltpu.roll(rows, T + 8 - (TAPS - 1 - k), 0)[:T]
                out_ref[:, base + lo : base + lo + LANES] = acc.astype(BF16)
            copy = pltpu.make_async_copy(out_ref.at[:, pl.ds(base, width)], out_h.at[:, far], sems.at[len(saves)])
            copy.start()
            saves.append(copy)
    wait_all(saves)


def run_spread(core, own, theirs, halo, weight):
    out = [("h", (T, CHANNELS), BF16)]
    scratch = [
        pltpu.VMEM((T, HALF_X + HALF_B), F32),
        pltpu.VMEM((T, CHANNELS), BF16),
        pltpu.VMEM((T + 8, GROUP_X), F32),
        DMA(9),
    ]
    return call(spread_kernel, "spread", out, "sVhvV", 3, scratch, mib=8)(core, own, theirs, halo, weight)[0]


CONV_ROWS = TAPS * (CHANNELS // LANES)
CONV_GROUP = CONV_ROWS // GROUPS
SEND_ROWS = CONV_ROWS + 16


def write_send(out_ref, conv, thin):
    high = thin.astype(BF16).astype(F32)
    low = thin - high
    row = iota((16, LANES), 0)
    out_ref[0:CONV_ROWS, :] = conv.astype(BF16)
    out_ref[CONV_ROWS:SEND_ROWS, :] = jnp.where(row == 0, high, jnp.where(row == 1, low, 0.0)).astype(BF16)


def read_send(value):
    wide = value.astype(F32)
    return wide[0:CONV_ROWS], wide[CONV_ROWS : CONV_ROWS + 1] + wide[CONV_ROWS + 1 : CONV_ROWS + 2]


def merge_kernel(core_ref, own_ref, own_got_ref, theirs_ref, theirs_got_ref, out_ref):
    thin = jnp.zeros((8, LANES), F32)
    left = iota((8, LANES), 1) < HEAD_DIM
    count = HEADS // 2
    parts = []
    for side, (mine, other) in enumerate(((own_ref, theirs_got_ref), (theirs_ref, own_got_ref))):
        half = 1 - core_ref[0] if side else core_ref[0]
        total = mine[...] + other[...]
        rows, skips, decays = [], [], []
        for jj in range(HALF_GROUPS):
            at = jj * SUM_GROUP
            rows.append(total[at : at + CONV_GROUP])
            skips.append(total[at + CONV_GROUP : at + SUM_GROUP - GROUP_HEADS])
            decays.append(total[at + SUM_GROUP - GROUP_HEADS : at + SUM_GROUP])
        skips = jnp.concatenate(skips, axis=0)
        even = exact_dot(jnp.where(left, 1.0, 0.0), skips, NT)
        odd = exact_dot(jnp.where(left, 0.0, 1.0), skips, NT)
        decay = exact_dot(jnp.ones((8, LANES), F32), jnp.concatenate(decays, axis=0), NT)
        for part, step, shift in ((even, 2, 0), (odd, 2, 1), (decay, 1, HEADS)):
            size = part.shape[1]
            spot = (iota((size, LANES), 1) == step * iota((size, LANES), 0) + shift + half * count).astype(F32)
            thin = thin + exact_dot(part, spot)
        parts.append(jnp.concatenate(rows, axis=0))
    first = core_ref[0] == 0
    conv = jnp.concatenate(
        [jnp.where(first, parts[0], parts[1]), jnp.where(first, parts[1], parts[0])], axis=0
    )
    write_send(out_ref, conv, thin[0:1])


def run_merge(core, own, own_got, theirs, theirs_got):
    out = [("v", (SEND_ROWS, LANES), BF16)]
    return call(merge_kernel, "merge", out, "svvvv", 1, mib=4)(core, own, own_got, theirs, theirs_got)[0]


def ring_sum(core_ref, me_ref, refs, hold_ref):
    count = len(refs)
    sides = (count - 1) // 2
    hold_ref[0] = refs[0][...]
    for k in range(1, sides + 1):
        mine = jnp.where(core_ref[0] == 0, k, count - k)
        hold_ref[mine] = refs[k][...]
        hold_ref[count - mine] = refs[sides + k][...]
    if count % 2 == 0:
        hold_ref[count // 2] = refs[count - 1][...]
    conv, thin = read_send(hold_ref[lax.rem(me_ref[0], count)])
    for k in range(1, count):
        more, little = read_send(hold_ref[lax.rem(me_ref[0] + count - k, count)])
        conv, thin = conv + more, thin + little
    return conv, thin


def fold_kernel(core_ref, me_ref, *rest):
    *refs, out_ref, hold_ref = rest
    write_send(out_ref, *ring_sum(core_ref, me_ref, refs, hold_ref))


def run_fold(core, me, values):
    out = [("v", (SEND_ROWS, LANES), BF16)]
    scratch = [pltpu.VMEM((len(values), SEND_ROWS, LANES), BF16)]
    return call(fold_kernel, "fold", out, "ss" + "v" * len(values), 1, scratch, mib=4)(core, me, *values)[0]


def finish_kernel(core_ref, me_ref, *rest):
    *refs, conv_ref, decay_ref, skip_ref, hold_ref = rest
    conv, thin = ring_sum(core_ref, me_ref, refs, hold_ref)
    for i in range(CHANNELS // LANES):
        if i < PAIRS:
            row = CONV_GROUP * (i // GROUP_PAIRS) + TAPS * (i % GROUP_PAIRS)
        else:
            kind, group = divmod(i - PAIRS, GROUPS)
            row = CONV_GROUP * group + TAPS * (GROUP_PAIRS + kind)
        conv_ref[:, i * LANES : (i + 1) * LANES] = conv[row : row + TAPS]
    skip_ref[...] = thin[:, 0:HEADS]
    decay_ref[...] = thin[:, HEADS:]


def run_finish(core, me, values):
    out = [("v", (TAPS, CHANNELS), F32), ("v", (1, HEADS), F32), ("v", (1, HEADS), F32)]
    scratch = [pltpu.VMEM((len(values), SEND_ROWS, LANES), BF16)]
    return call(finish_kernel, "finish", out, "ss" + "v" * len(values), 1, scratch, mib=4)(core, me, *values)


CTX = ("chip", "core")
ALL = ("dp", "chip", "core")


def all_to_all(value, axis):
    return lax.all_to_all(value, axis, 0, 0, tiled=True)


def tie(*values):
    return lax.optimization_barrier(values)


SIDE = 4


def around(value, axis, size, ring, move):
    def hear(first, second):
        return lax.ppermute(
            value,
            (axis, "core"),
            [(2 * i + side, 2 * move(i, d) + side) for i in range(size) for side, d in enumerate((first, second))],
        )

    middle = [hear(ring // 2, ring // 2)] if ring % 2 == 0 else []
    heard = [hear(k, ring - k) for k in range(1, (ring - 1) // 2 + 1)]
    swapped = [lax.ppermute(part, "core", [(0, 1), (1, 0)]) for part in heard]
    return [value] + heard + swapped + middle


def scalar(value):
    return value.astype(jnp.int32).reshape(1)


def local(conv_input, conv_weight, step_raw, decay_log, skip_gain, cotangent):
    chips = lax.axis_size("chip")
    devices = 2 * chips
    sequences = lax.axis_size("dp")
    tokens = conv_input[0]
    raw = step_raw[0]
    cot = cotangent[0]
    core = lax.axis_index("core").astype(jnp.int32).reshape(1)
    swap = [(0, 1), (1, 0)]
    halo = lax.ppermute(tokens[T - TAPS + 1 :], CTX, [(i, i + 1) for i in range(devices - 1)])
    small, small_near, tot, x0, bc0, head, weight_near, cot_near = run_begin(
        raw, decay_log.reshape(1, HEADS), skip_gain.reshape(1, HEADS), tokens, conv_weight, cot
    )
    other = lax.ppermute(tot, "core", swap)
    x, bc, before, x_near, bc_near, out = run_enter(
        core, x0, bc0, head, halo, weight_near, cot_near, small_near
    )
    got_near = lax.ppermute(out, "core", swap)
    own_near = run_own(core, x_near, bc_near, cot_near, small_near)
    packed, left, right, tots = run_pack(core, own_near, got_near, tot, other)
    heard = all_to_all(packed, "chip")
    y, gbc, skips = run_inner(x, bc, cot, small)
    heard, y, gbc, skips = tie(heard, y, gbc, skips)
    chained = run_chain(chips, heard)
    late, chained = tie(bc, chained)
    back = all_to_all(chained, "chip")
    gx, slope = run_slopes(late, cot, small, tokens, before, conv_weight)
    back, gx, slope = tie(back, gx, slope)
    far = (x, cot, y, gx, slope, tokens, bc, gbc)
    mine, send, near, common = run_unpack(
        core, back, left, right, tots, far, (before, small, raw, skips, conv_weight)
    )
    theirs = lax.ppermute(send, "core", swap)
    half, pre_own, sum_own, near = run_leave(core, mine, near, common, far, None)
    sum_own_got = lax.ppermute(sum_own, "core", swap)
    (out_tokens, grad_step), pre_theirs, sum_theirs, (first,) = run_leave(
        core, theirs, near, common, (), (half, pre_own)
    )
    sum_theirs_got = lax.ppermute(sum_theirs, "core", swap)
    after = lax.ppermute(first, CTX, [(i + 1, i) for i in range(devices - 1)])
    sums = run_merge(core, sum_own, sum_own_got, sum_theirs, sum_theirs_got)
    chip, sequence = lax.axis_index("chip"), lax.axis_index("dp")
    rows = chips // SIDE
    values = around(sums, "chip", chips, SIDE, lambda i, d: i // SIDE * SIDE + (i % SIDE + d) % SIDE)
    grad_tokens = run_spread(core, pre_own, pre_theirs, after, common[4])
    values, grad_tokens = tie(values, grad_tokens)
    sums = run_fold(core, scalar(lax.rem(chip, SIDE)), values)
    values = around(sums, "chip", chips, rows, lambda i, d: (i + d * SIDE) % chips)
    sums = run_fold(core, scalar(lax.div(chip, SIDE)), values)
    near = 1
    if near > 1:
        values = around(sums, "dp", sequences, near, lambda i, d: i // 2 * 2 + (i % 2 + d) % 2)
        sums = run_fold(core, scalar(lax.rem(sequence, near)), values)
    values = around(sums, "dp", sequences, sequences // near, lambda i, d: (i + d * near) % sequences)
    grad_conv, grad_decay, grad_skip = run_finish(core, scalar(lax.div(sequence, near)), values)
    return (
        out_tokens[None],
        grad_tokens[None],
        grad_step[None],
        grad_conv,
        grad_decay.reshape(HEADS),
        grad_skip.reshape(HEADS),
    )


def solution(mesh):
    dp, ctx = mesh.devices.shape
    fine = Mesh(mesh.devices.reshape(dp, ctx // 2, 2), ALL)
    seq = P("dp", CTX, None)
    rate = P("dp", None, CTX)
    in_specs = (seq, P(), rate, P(), P(), seq)
    out_specs = (seq, seq, rate, P(), P(), P())
    return jax.shard_map(local, mesh=fine, in_specs=in_specs, out_specs=out_specs, check_vma=False)
```
